32 devices in a mesh: dp: 8 (over y, x, core), seq: 4 (over z).
Axes of the slice: x: 2, y: 2, z: 4, core: 2. Of those that a mesh axis runs over, the one named last changes fastest.
Arguments:
- frames: bfloat16 [8, 1024, 1536], P('dp', 'seq'), may hold values from -100 to 100
- time_token: bfloat16 [8, 1536], P('dp'), may hold values from -6 to 6
- cond_ids: int32 [8, 128], P('dp'), may hold values from 0 to 16383
- cond_mask: int32 [8, 128], P('dp'), may hold values from 0 to 1, as said below
- lengths: int32 [8], P('dp'), may hold values from 108 to 1024, as said below
- cond_table: bfloat16 [16384, 768], P('seq'), may hold values from -10 to 10
- cotangent: bfloat16 [8, 1024, 1536], P('dp', 'seq'), may hold values from -6 to 6
- attn_weight: float32 [1536, 9216], P(('dp', 'seq')), may hold values from -1 to 1
- cross_weight: float32 [768, 3072], P(('dp', 'seq')), may hold values from -0.21875 to 0.21875
- norm_param: float32 [6, 1536], P(None, ('dp', 'seq')), may hold values from -2 to 3
- ff_weight: float32 [1536, 18432], P(('dp', 'seq')), may hold values from -0.5 to 0.5
- attn_first: float32 [1536, 9216], P(('dp', 'seq')), may hold values from -0.0004272461 to 0.0004272461
- attn_second: float32 [1536, 9216], P(('dp', 'seq')), may hold values from 5.5758966e-09 to 2.2303587e-08
- cross_first: float32 [768, 3072], P(('dp', 'seq')), may hold values from -0.0004272461 to 0.0004272461
- cross_second: float32 [768, 3072], P(('dp', 'seq')), may hold values from 5.5758966e-09 to 2.2303587e-08
- norm_first: float32 [6, 1536], P(None, ('dp', 'seq')), may hold values from -0.0024414062 to 0.0024414062
- norm_second: float32 [6, 1536], P(None, ('dp', 'seq')), may hold values from 2.0073227e-07 to 8.029291e-07
- ff_first: float32 [1536, 18432], P(('dp', 'seq')), may hold values from -0.0008544922 to 0.0008544922
- ff_second: float32 [1536, 18432], P(('dp', 'seq')), may hold values from 2.2303587e-08 to 8.9214346e-08
Outputs:
- layer_out: bfloat16 [8, 1024, 1536], P('dp', 'seq')
- frames_grad: float32 [8, 1024, 1536], P('dp', 'seq')
- grad_norm: float32 [], replicated
- attn_new: float32 [1536, 9216], P(('dp', 'seq'))
- cross_new: float32 [768, 3072], P(('dp', 'seq'))
- norm_new: float32 [6, 1536], P(None, ('dp', 'seq'))
- ff_new: float32 [1536, 18432], P(('dp', 'seq'))
- attn_first_new: float32 [1536, 9216], P(('dp', 'seq'))
- cross_first_new: float32 [768, 3072], P(('dp', 'seq'))
- norm_first_new: float32 [6, 1536], P(None, ('dp', 'seq'))
- ff_first_new: float32 [1536, 18432], P(('dp', 'seq'))
- attn_second_new: float32 [1536, 9216], P(('dp', 'seq'))
- cross_second_new: float32 [768, 3072], P(('dp', 'seq'))
- norm_second_new: float32 [6, 1536], P(None, ('dp', 'seq'))
- ff_second_new: float32 [1536, 18432], P(('dp', 'seq'))
The draws below stay inside these ranges and needn't reach their ends.
Inputs may be any that keep to these rules, and one draw needn't show every extreme that they name: `lengths`: one clip of every draw has exactly 1024 frames and another exactly max(1, 108). `cond_mask`: each clip's present tokens form a leading run of 16 or more positions; some clip has exactly 16.
All inputs are finite; a program needn't handle non-finite values.
Results may differ from the reference program's by a relative error of at most 0.03.
Values may be sent and summed in bfloat16 or wider, within the bound.
A program may use at most 832 MiB of HBM per device.

```python
import math
import jax
import jax.numpy as jnp
import numpy as np
from jax import lax

D = 1536
HDIM = 64
FF = 6144
E = 768
CVOCAB = 16384
CTOK = 128
FRAMES = 1024
UPDATE_STEP = 10
CLIPS = 8
PARAMS = 44835840


def ramp_scales(count, low_end, ratio):
    steps = jnp.arange(count, dtype=jnp.float32) / max(count - 1, 1)
    return low_end * ratio ** steps


def draw_frames(key, part):
    key = jax.random.fold_in(key, 11)
    keys = jax.random.split(key, 3)
    shape = (CLIPS, FRAMES, D)
    base = jax.random.truncated_normal(keys[0], -4.0, 4.0, shape, jnp.float32)
    row_scale = jnp.exp(jax.random.uniform(keys[1], (CLIPS, FRAMES, 1), jnp.float32, math.log(0.5), math.log(5.0)))
    col_scale = jnp.exp(jax.random.uniform(keys[2], (1, 1, D), jnp.float32, math.log(0.5), math.log(2.0)))
    return (base * row_scale * col_scale).astype(jnp.bfloat16)


def draw_norm_param(key, part):
    key = jax.random.fold_in(key, 31)
    keys = jax.random.split(key, 2)
    jitter = jnp.exp(jax.random.uniform(keys[0], (3, D), jnp.float32, math.log(0.8), math.log(1.25)))
    gains = ramp_scales(D, 0.55, 3.0)[None, :] * jitter
    biases = 0.3 * jax.random.truncated_normal(keys[1], -4.0, 4.0, (3, D), jnp.float32)
    return jnp.stack([gains[0], biases[0], gains[1], biases[1], gains[2], biases[2]], axis=0)


def draw_cond_table(key, part):
    key = jax.random.fold_in(key, 41)
    base = jax.random.truncated_normal(key, -4.0, 4.0, (CVOCAB, E), jnp.float32)
    column = ramp_scales(E, 0.55, 3.0)
    return (base * column[None, :]).astype(jnp.bfloat16)


def draw_attn_weight(key, part):
    key = jax.random.fold_in(key, 51)
    factors = jnp.array([1.0, 1.0, 1.0, FRAMES ** 0.5 / 4.0, 1.0, CTOK ** 0.5 / 2.0], jnp.float32)
    column = jnp.repeat(factors, D) / D ** 0.5
    base = jax.random.truncated_normal(key, -4.0, 4.0, (D, 6 * D), jnp.float32)
    return base * column[None, :]


def draw_ff_weight(key, part):
    key = jax.random.fold_in(key, 61)
    factors = jnp.array([D ** (-0.5), D ** (-0.5), FF ** (-0.5)], jnp.float32)
    column = jnp.repeat(factors, FF)
    base = jax.random.truncated_normal(key, -4.0, 4.0, (D, 3 * FF), jnp.float32)
    return base * column[None, :]


def draw_lengths(key, part):
    key = jax.random.fold_in(key, 71)
    keys = jax.random.split(key, 5)
    shortest = max(1, FRAMES * 108 // 1024)
    cut_point = FRAMES * 7 // 10
    is_short = jax.random.randint(keys[0], (CLIPS,), 0, 4) == 0
    longer = jax.random.randint(keys[1], (CLIPS,), cut_point + 1, FRAMES + 1)
    shorter = jax.random.randint(keys[2], (CLIPS,), shortest, cut_point + 1)
    drawn = jnp.where(is_short, shorter, longer)
    first_pick = jax.random.randint(keys[3], (), 0, CLIPS)
    second_pick = (first_pick + 1 + jax.random.randint(keys[4], (), 0, CLIPS - 1)) % CLIPS
    index_row = jnp.arange(CLIPS, dtype=jnp.int32)
    drawn = jnp.where(index_row == first_pick, FRAMES, drawn)
    drawn = jnp.where(index_row == second_pick, shortest, drawn)
    return drawn.astype(jnp.int32)


def draw_cond_mask(key, part):
    key = jax.random.fold_in(key, 81)
    keys = jax.random.split(key, 2)
    least = CTOK // 8
    present = jax.random.randint(keys[0], (CLIPS,), least, CTOK + 1)
    pick = jax.random.randint(keys[1], (), 0, CLIPS)
    present = jnp.where(jnp.arange(CLIPS, dtype=jnp.int32) == pick, least, present)
    return (jnp.arange(CTOK, dtype=jnp.int32)[None, :] < present[:, None]).astype(jnp.int32)


def set_ends(values, own_key, smallest, top_value):
    longest = values.shape.index(max(values.shape))
    spots = []
    for shift in (0, 1):
        where = [jax.random.randint(jax.random.fold_in(own_key, axis), (), 0, length) for axis, length in enumerate(values.shape)]
        where[longest] = (where[longest] + shift) % values.shape[longest]
        spots.append(tuple(where))
    return values.at[spots[0]].set(smallest).at[spots[1]].set(top_value)


def block_scale(rng, extent, shards, low, largest):
    loudness, own = 1.0, jax.random.fold_in(rng, 6)
    for dim, shards_of in shards:
        steps = jnp.exp(jax.random.uniform(jax.random.fold_in(own, dim), (shards_of,), jnp.float32, low / len(shards), largest / len(shards)))
        loudness = loudness * jnp.repeat(steps, extent[dim] // shards_of).reshape([-1 if axis == dim else 1 for axis in range(len(extent))])
    return loudness


def rank_table(number_of, slope):
    weights = [(1 << 20) // math.isqrt(standing ** slope) + 1 for standing in range(1, number_of + 1)]
    deviation = 1 + sum(weights) // (1 << 30)
    return np.cumsum(np.array([max(1, weight // deviation) for weight in weights]))


def ranked_ids(rng, dims, number_of, skew):
    grid = rank_table(number_of, skew)
    lot = jax.random.randint(jax.random.fold_in(rng, 1), dims, 0, int(grid[number_of - 1]))
    standing = jnp.searchsorted(jnp.asarray(grid, jnp.int32), lot, side="right")
    return jax.random.permutation(jax.random.fold_in(rng, 2), number_of)[standing].astype(jnp.int32)


def normal_values(own_key, dims, scale, most, shards=(), kind=jnp.bfloat16):
    level = block_scale(own_key, dims, shards, -0.22, 0.18) if shards else 1.0
    values = jax.random.normal(own_key, dims, jnp.float32) * scale * level
    return jnp.minimum(jnp.maximum(values, -most), most).astype(kind)


def setup_inputs(seed: int = 0) -> dict:
    splits = jax.random.split(jax.random.key(seed), 20)
    frames = draw_frames(jax.random.fold_in(splits[19], 71), 0)
    time_token = normal_values(splits[1], (CLIPS, D), 1.0, 6.0, ((0, 8),))
    cond_ids = set_ends(ranked_ids(splits[2], (CLIPS, CTOK), CVOCAB, 2), jax.random.fold_in(splits[2], 3), 0, CVOCAB - 1).astype(jnp.int32)
    cond_mask = draw_cond_mask(jax.random.fold_in(splits[19], 71), 0)
    lengths = draw_lengths(jax.random.fold_in(splits[19], 71), 0)
    cond_table = draw_cond_table(jax.random.fold_in(splits[19], 71), 0)
    cotangent = normal_values(splits[6], (CLIPS, FRAMES, D), 1.0, 6.0, ((0, 8), (1, 4)))
    attn_weight = draw_attn_weight(jax.random.fold_in(splits[19], 71), 0)
    cross_weight = normal_values(splits[8], (E, 2 * D), E ** -0.5, 0.21875, ((0, 32),), jnp.float32)
    norm_param = draw_norm_param(jax.random.fold_in(splits[19], 71), 0)
    ff_weight = draw_ff_weight(jax.random.fold_in(splits[19], 71), 0)
    attn_first = normal_values(splits[11], (D, 6 * D), (0.5 * PARAMS ** -0.5), 0.0004272461, ((0, 32),), jnp.float32)
    attn_second = jnp.clip(jnp.exp(math.log(2.2303586533212183e-08) - 1.3862944 * jax.random.uniform(splits[12], (D, 6 * D), jnp.float32) ** block_scale(splits[12], (D, 6 * D), ((0, 32),), -0.2, 0.2)), 5.575896633303046e-09, 2.2303586533212183e-08)
    cross_first = normal_values(splits[13], (E, 2 * D), (0.5 * PARAMS ** -0.5), 0.0004272461, ((0, 32),), jnp.float32)
    cross_second = jnp.clip(jnp.exp(math.log(2.2303586533212183e-08) - 1.3862944 * jax.random.uniform(splits[14], (E, 2 * D), jnp.float32) ** block_scale(splits[14], (E, 2 * D), ((0, 32),), -0.2, 0.2)), 5.575896633303046e-09, 2.2303586533212183e-08)
    norm_first = normal_values(splits[15], (6, D), (3.0 * PARAMS ** -0.5), 0.0024414062, ((1, 32),), jnp.float32)
    norm_second = jnp.clip(jnp.exp(math.log(8.029290938793565e-07) - 1.3862944 * jax.random.uniform(splits[16], (6, D), jnp.float32) ** block_scale(splits[16], (6, D), ((1, 32),), -0.2, 0.2)), 2.0073227346983913e-07, 8.029290938793565e-07)
    ff_first = normal_values(splits[17], (D, 3 * FF), (1.0 * PARAMS ** -0.5), 0.0008544922, ((0, 32),), jnp.float32)
    ff_second = jnp.clip(jnp.exp(math.log(8.921434613284873e-08) - 1.3862944 * jax.random.uniform(splits[18], (D, 3 * FF), jnp.float32) ** block_scale(splits[18], (D, 3 * FF), ((0, 32),), -0.2, 0.2)), 2.2303586533212183e-08, 8.921434613284873e-08)
    return dict(frames=frames, time_token=time_token, cond_ids=cond_ids, cond_mask=cond_mask, lengths=lengths, cond_table=cond_table, cotangent=cotangent, attn_weight=attn_weight, cross_weight=cross_weight, norm_param=norm_param, ff_weight=ff_weight, attn_first=attn_first, attn_second=attn_second, cross_first=cross_first, cross_second=cross_second, norm_first=norm_first, norm_second=norm_second, ff_first=ff_first, ff_second=ff_second)


@jax.custom_vjp
def low(v):
    return lax.optimization_barrier(v.astype(jnp.bfloat16)).astype(jnp.float32)

@jax.custom_vjp
def low_back(v):
    return v

def low_keep(v):
    return (low(v), None)

def low_pass(kept, grad):
    return (grad,)

def back_keep(v):
    return (v, None)

def back_low(kept, grad):
    return (low(grad),)
low.defvjp(low_keep, low_pass)
low_back.defvjp(back_keep, back_low)
norm_eps = 1e-05
beta_first = 0.5
beta_second = 0.5
adam_eps = 1e-08
matrix_decay = 0.01
matrix_rate = 0.03
gain_rate = 0.25
clip_limit = 1.0
masked_score = -1e+30
highest = lax.Precision.HIGHEST

def matmul(left_mat, right_mat):
    return jnp.dot(left_mat, right_mat, precision=highest, preferred_element_type=jnp.float32)

def matmul_transposed(left_mat, right_mat):
    return lax.dot_general(left_mat, right_mat, (((1,), (1,)), ((), ())), precision=highest, preferred_element_type=jnp.float32)

def layer_norm(values, gain_row, bias_row):
    center = values - lax.optimization_barrier(jnp.mean(values, axis=-1, keepdims=True))
    spread = lax.optimization_barrier(jnp.mean(center * center, axis=-1, keepdims=True))
    return center * lax.rsqrt(spread + norm_eps) * gain_row + bias_row

def rotary_tables(positions, head_size):
    half_size = head_size // 2
    frequency = 10000.0 ** (-jnp.arange(half_size, dtype=jnp.float32) / half_size)
    angles = positions.astype(jnp.float32)[:, None] * frequency[None, :]
    return (jnp.cos(angles)[:, None, :], jnp.sin(angles)[:, None, :])

def rotate(values, cosine_table, sine_table):
    half_size = values.shape[-1] // 2
    first_half = values[..., :half_size]
    second_half = values[..., half_size:]
    return jnp.concatenate([first_half * cosine_table - second_half * sine_table, second_half * cosine_table + first_half * sine_table], axis=-1)

def attention(queries, all_keys, all_values, key_keep):
    score_scale = HDIM ** (-0.5)
    scores = low_back(jnp.einsum('qhd,khd->hqk', queries, all_keys, precision=highest, preferred_element_type=jnp.float32) * score_scale)
    scores = jnp.where(key_keep[None, None, :], scores, masked_score)
    top_score = lax.optimization_barrier(jnp.max(scores, axis=-1, keepdims=True))
    expo = jnp.exp(scores - top_score)
    probs = low(expo / lax.optimization_barrier(jnp.sum(expo, axis=-1, keepdims=True)))
    mixed = jnp.einsum('hqk,khd->qhd', probs, all_values, precision=highest, preferred_element_type=jnp.float32)
    return low(low_back(mixed.reshape(queries.shape[0], -1)))

def clip_layer(attn_low, cross_low, norm_low, ff_low, clip_frames, stamp, cond, cond_row, length):
    frame_count, wide = clip_frames.shape
    head_count = wide // HDIM
    hidden_width = ff_low.shape[1] // 3
    positions = jnp.arange(frame_count, dtype=jnp.int32)
    cosine_table, sine_table = rotary_tables(positions, HDIM)
    head_shape = (frame_count, head_count, HDIM)
    normed_one = low(layer_norm(clip_frames, norm_low[0], norm_low[1]))
    projected = matmul(normed_one, attn_low[:, :3 * wide])
    query_raw = low_back(projected[:, :wide]).reshape(head_shape)
    key_raw = low_back(projected[:, wide:2 * wide]).reshape(head_shape)
    own_values = low(low_back(projected[:, 2 * wide:])).reshape(head_shape)
    queries = low(rotate(query_raw, cosine_table, sine_table))
    own_keys = low(rotate(key_raw, cosine_table, sine_table))
    stamp_normed = low(layer_norm(stamp[None, :], norm_low[0], norm_low[1]))
    stamp_pair = matmul(stamp_normed, attn_low[:, wide:3 * wide])
    stamp_key = low(stamp_pair[:, :wide]).reshape(1, head_count, HDIM)
    stamp_value = low(stamp_pair[:, wide:]).reshape(1, head_count, HDIM)
    all_keys = jnp.concatenate([stamp_key, own_keys], axis=0)
    all_values = jnp.concatenate([stamp_value, own_values], axis=0)
    key_keep = jnp.concatenate([jnp.ones((1,), bool), positions < length])
    self_mixed = attention(queries, all_keys, all_values, key_keep)
    resid_one = clip_frames + low_back(matmul_transposed(self_mixed, attn_low[:, 3 * wide:4 * wide]))
    normed_two = low(layer_norm(resid_one, norm_low[2], norm_low[3]))
    cross_query = low(low_back(matmul(normed_two, attn_low[:, 4 * wide:5 * wide]))).reshape(head_shape)
    cond_pair = matmul(cond, cross_low)
    cond_shape = (cond.shape[0], head_count, HDIM)
    cross_keys = low(cond_pair[:, :wide]).reshape(cond_shape)
    cross_values = low(cond_pair[:, wide:]).reshape(cond_shape)
    cross_mixed = attention(cross_query, cross_keys, cross_values, cond_row > 0)
    resid_two = resid_one + low_back(matmul_transposed(cross_mixed, attn_low[:, 5 * wide:]))
    normed_three = low(layer_norm(resid_two, norm_low[4], norm_low[5]))
    gate_up = matmul(normed_three, ff_low[:, :2 * hidden_width])
    gate_val = low_back(gate_up[:, :hidden_width])
    up_val = low_back(gate_up[:, hidden_width:])
    hidden = low(jax.nn.silu(gate_val) * up_val)
    branch = matmul_transposed(hidden, ff_low[:, 2 * hidden_width:])
    return resid_two + low_back(branch)

def adam_step(weight, first, second, gradient, step_rate, decay_rate):
    first_new = beta_first * first + (1.0 - beta_first) * gradient
    second_new = beta_second * second + (1.0 - beta_second) * gradient * gradient
    fix_first = 1.0 - beta_first ** UPDATE_STEP
    fix_second = 1.0 - beta_second ** UPDATE_STEP
    normed_step = first_new / fix_first / (jnp.sqrt(second_new / fix_second) + adam_eps)
    return (weight - step_rate * (normed_step + decay_rate * weight), first_new, second_new)

def reference(frames, time_token, cond_ids, cond_mask, lengths, cond_table, cotangent, attn_weight, cross_weight, norm_param, ff_weight, attn_first, attn_second, cross_first, cross_second, norm_first, norm_second, ff_first, ff_second):
    cond = jnp.take(cond_table, cond_ids, axis=0).astype(jnp.float32)
    frames_float = frames.astype(jnp.float32)
    stamps = time_token.astype(jnp.float32)
    layer_fn = jax.checkpoint(clip_layer)

    def whole(frames_in, attn_in, cross_in, norm_in, ff_in):
        attn_low = low(attn_in)
        cross_low = low(cross_in)
        norm_low = low(norm_in)
        ff_low = low(ff_in)

        def one_clip(carry, inputs):
            clip_frames, stamp, cond_clip, cond_row, length = inputs
            return (carry, layer_fn(attn_low, cross_low, norm_low, ff_low, clip_frames, stamp, cond_clip, cond_row, length))
        _, result = lax.scan(one_clip, jnp.zeros((), jnp.float32), (frames_in, stamps, cond, cond_mask, lengths))
        return result
    result, pullback = jax.vjp(whole, frames_float, attn_weight, cross_weight, norm_param, ff_weight)
    frame_keep = jnp.arange(FRAMES, dtype=jnp.int32)[None, :] < lengths[:, None]
    out_grad = cotangent.astype(jnp.float32) * frame_keep[..., None].astype(jnp.float32)
    frames_grad, attn_grad, cross_grad, norm_grad, ff_grad = pullback(out_grad)
    total_sq = jnp.sum(attn_grad * attn_grad) + jnp.sum(cross_grad * cross_grad) + jnp.sum(norm_grad * norm_grad) + jnp.sum(ff_grad * ff_grad)
    grad_norm = jnp.sqrt(total_sq)
    factor = jnp.minimum(1.0, clip_limit / grad_norm)
    attn_new, attn_first_new, attn_second_new = adam_step(attn_weight, attn_first, attn_second, attn_grad * factor, matrix_rate, matrix_decay)
    cross_new, cross_first_new, cross_second_new = adam_step(cross_weight, cross_first, cross_second, cross_grad * factor, matrix_rate, matrix_decay)
    norm_new, norm_first_new, norm_second_new = adam_step(norm_param, norm_first, norm_second, norm_grad * factor, gain_rate, 0.0)
    ff_new, ff_first_new, ff_second_new = adam_step(ff_weight, ff_first, ff_second, ff_grad * factor, matrix_rate, matrix_decay)
    return (result.astype(jnp.bfloat16), frames_grad, grad_norm, attn_new, cross_new, norm_new, ff_new, attn_first_new, cross_first_new, norm_first_new, ff_first_new, attn_second_new, cross_second_new, norm_second_new, ff_second_new)
```

```python
import functools

import jax
import jax.numpy as jnp
from jax import lax
from jax.experimental import pallas as pl
from jax.experimental.pallas import tpu as pltpu
from jax.sharding import PartitionSpec as P

HEADS = 24
HDIM = 64
FF = 6144
UPDATE_STEP = 10


norm_eps = 1e-05
beta_first = 0.5
beta_second = 0.5
adam_eps = 1e-08
matrix_decay = 0.01
matrix_rate = 0.03
gain_rate = 0.25
clip_limit = 1.0
masked_score = -1e30


def layer_norm(values, gain_row, bias_row):
    center = values - jnp.mean(values, axis=-1, keepdims=True)
    spread = jnp.mean(center * center, axis=-1, keepdims=True)
    return center * lax.rsqrt(spread + norm_eps) * gain_row + bias_row


def rotary_tables(positions, head_size):
    half_size = head_size // 2
    frequency = 10000.0 ** (-jnp.arange(half_size, dtype=jnp.float32) / half_size)
    angles = positions.astype(jnp.float32)[:, None] * frequency[None, :]
    return (jnp.cos(angles)[:, None, :], jnp.sin(angles)[:, None, :])


def rotate(values, cosine_table, sine_table):
    half_size = values.shape[-1] // 2
    first_half = values[..., :half_size]
    second_half = values[..., half_size:]
    return jnp.concatenate(
        [
            first_half * cosine_table - second_half * sine_table,
            second_half * cosine_table + first_half * sine_table,
        ],
        axis=-1,
    )


def outer_sum(left_mat, right_mat):
    return lax.dot_general(
        left_mat, right_mat, (((0,), (0,)), ((), ())), preferred_element_type=jnp.float32
    )


def times_transposed(left_mat, right_mat):
    return lax.dot_general(
        left_mat, right_mat, (((1,), (1,)), ((), ())), preferred_element_type=jnp.float32
    )


def split_parts(values):
    upper = values.astype(jnp.bfloat16)
    lower = (values - upper.astype(jnp.float32)).astype(jnp.bfloat16)
    return (upper, lower)


def split_outer(left_low, right_full):
    upper, lower = split_parts(right_full)
    return outer_sum(left_low, upper) + outer_sum(left_low, lower)


def split_times_transposed(left_full, right_low):
    upper, lower = split_parts(left_full)
    return times_transposed(upper, right_low) + times_transposed(lower, right_low)


def self_scores(queries, keys, stamp_key, keep):
    score_scale = HDIM ** (-0.5)
    frame_part = (
        jnp.einsum("cqhd,ckhd->chqk", queries, keys, preferred_element_type=jnp.float32)
        * score_scale
    )
    frame_part = jnp.where(keep[:, None, None, :], frame_part, masked_score)
    stamp_part = (
        jnp.einsum("cqhd,chd->chq", queries, stamp_key, preferred_element_type=jnp.float32)
        * score_scale
    )
    return (frame_part, stamp_part)


def self_forward(queries, keys, values, stamp_key, stamp_value, keep):
    frame_scores, stamp_scores = self_scores(queries, keys, stamp_key, keep)
    top_score = jnp.maximum(jnp.max(frame_scores, axis=-1), stamp_scores)
    frame_expo = jnp.exp(frame_scores - top_score[..., None])
    stamp_expo = jnp.exp(stamp_scores - top_score)
    denom = jnp.sum(frame_expo, axis=-1) + stamp_expo
    self_lse = top_score + jnp.log(denom)
    frame_prob = (frame_expo / denom[..., None]).astype(jnp.bfloat16)
    stamp_prob = (stamp_expo / denom).astype(jnp.bfloat16)
    mixed = jnp.einsum(
        "chqk,ckhd->cqhd", frame_prob, values, preferred_element_type=jnp.float32
    ) + jnp.einsum("chq,chd->cqhd", stamp_prob, stamp_value, preferred_element_type=jnp.float32)
    return (mixed, self_lse)


def self_backward(queries, keys, values, stamp_key, stamp_value, keep, self_lse, grad_mixed):
    score_scale = HDIM ** (-0.5)
    frame_scores, stamp_scores = self_scores(queries, keys, stamp_key, keep)
    frame_prob = jnp.exp(frame_scores - self_lse[..., None])
    stamp_prob = jnp.exp(stamp_scores - self_lse)
    grad_frame_prob = jnp.einsum(
        "cqhd,ckhd->chqk", grad_mixed, values, preferred_element_type=jnp.float32
    )
    grad_stamp_prob = jnp.einsum(
        "cqhd,chd->chq", grad_mixed, stamp_value, preferred_element_type=jnp.float32
    )
    delta = jnp.sum(frame_prob * grad_frame_prob, axis=-1) + stamp_prob * grad_stamp_prob
    grad_frame_scores = (frame_prob * (grad_frame_prob - delta[..., None])).astype(jnp.bfloat16)
    grad_stamp_scores = (stamp_prob * (grad_stamp_prob - delta)).astype(jnp.bfloat16)
    grad_queries = (
        jnp.einsum("chqk,ckhd->cqhd", grad_frame_scores, keys, preferred_element_type=jnp.float32)
        + jnp.einsum(
            "chq,chd->cqhd", grad_stamp_scores, stamp_key, preferred_element_type=jnp.float32
        )
    ) * score_scale
    key_part = (
        jnp.einsum(
            "chqk,cqhd->ckhd", grad_frame_scores, queries, preferred_element_type=jnp.float32
        )
        * score_scale
    )
    value_part = jnp.einsum(
        "chqk,cqhd->ckhd",
        frame_prob.astype(jnp.bfloat16),
        grad_mixed,
        preferred_element_type=jnp.float32,
    )
    grad_stamp_key = (
        jnp.einsum("chq,cqhd->chd", grad_stamp_scores, queries, preferred_element_type=jnp.float32)
        * score_scale
    )
    grad_stamp_value = jnp.einsum(
        "chq,cqhd->chd",
        stamp_prob.astype(jnp.bfloat16),
        grad_mixed,
        preferred_element_type=jnp.float32,
    )
    return (grad_queries, key_part, value_part, grad_stamp_key, grad_stamp_value)


def cross_scores(query, keys, keep):
    score_scale = HDIM ** (-0.5)
    scores = (
        jnp.einsum("cqhd,ckhd->chqk", query, keys, preferred_element_type=jnp.float32) * score_scale
    )
    return jnp.where(keep[:, None, None, :], scores, masked_score)


def cross_forward(query, keys, values, keep):
    scores = cross_scores(query, keys, keep)
    top_score = jnp.max(scores, axis=-1)
    expo = jnp.exp(scores - top_score[..., None])
    denom = jnp.sum(expo, axis=-1)
    cross_lse = top_score + jnp.log(denom)
    prob = (expo / denom[..., None]).astype(jnp.bfloat16)
    mixed = jnp.einsum("chqk,ckhd->cqhd", prob, values, preferred_element_type=jnp.float32)
    return (mixed, cross_lse)


def cross_backward(query, keys, values, keep, cross_lse, grad_mixed):
    score_scale = HDIM ** (-0.5)
    prob = jnp.exp(cross_scores(query, keys, keep) - cross_lse[..., None])
    grad_prob = jnp.einsum(
        "cqhd,ckhd->chqk", grad_mixed, values, preferred_element_type=jnp.float32
    )
    delta = jnp.sum(prob * grad_prob, axis=-1)
    grad_scores = (prob * (grad_prob - delta[..., None])).astype(jnp.bfloat16)
    grad_query = (
        jnp.einsum("chqk,ckhd->cqhd", grad_scores, keys, preferred_element_type=jnp.float32)
        * score_scale
    )
    grad_keys = (
        jnp.einsum("chqk,cqhd->ckhd", grad_scores, query, preferred_element_type=jnp.float32)
        * score_scale
    )
    grad_values = jnp.einsum(
        "chqk,cqhd->ckhd", prob.astype(jnp.bfloat16), grad_mixed, preferred_element_type=jnp.float32
    )
    return (grad_query, grad_keys, grad_values)


def adam_step(weight, first, second, gradient, step_rate, decay_rate):
    first_new = beta_first * first + (1.0 - beta_first) * gradient
    second_new = beta_second * second + (1.0 - beta_second) * gradient * gradient
    fix_first = 1.0 - beta_first**UPDATE_STEP
    fix_second = 1.0 - beta_second**UPDATE_STEP
    normed_step = first_new / fix_first / (jnp.sqrt(second_new / fix_second) + adam_eps)
    return (weight - step_rate * (normed_step + decay_rate * weight), first_new, second_new)


def per_device(
    frames,
    time_token,
    cond_ids,
    cond_mask,
    lengths,
    cond_table,
    cotangent,
    attn_weight,
    cross_weight,
    norm_param,
    ff_weight,
    attn_first,
    attn_second,
    cross_first,
    cross_second,
    norm_first,
    norm_second,
    ff_first,
    ff_second,
):
    clip_count, frame_rows, wide = frames.shape
    hidden_width = FF
    token_count = clip_count * frame_rows
    seq_count = lax.axis_size("seq")
    seq_frames = frame_rows * seq_count
    seq_place = lax.axis_index("seq")
    vocab_rows = cond_table.shape[0]
    relative = cond_ids - seq_place * vocab_rows
    inside = (relative >= 0) & (relative < vocab_rows)
    picked = jnp.take(cond_table, jnp.clip(relative, 0, vocab_rows - 1), axis=0).astype(jnp.float32)
    picked = jnp.where(inside[..., None], picked, 0.0)
    cond = lax.psum(picked.astype(jnp.bfloat16), "seq")
    cond_count = cond.shape[1]
    cond_flat = cond.reshape(clip_count * cond_count, cond.shape[2])
    cond_width = cond.shape[2]
    cond_keep = cond_mask > 0
    attn_low = attn_weight.astype(jnp.bfloat16)
    cross_low = cross_weight.astype(jnp.bfloat16)
    norm_low = norm_param.astype(jnp.bfloat16)
    ff_low = ff_weight.astype(jnp.bfloat16)
    stream = frames.astype(jnp.float32).reshape(token_count, wide)
    stamps = time_token.astype(jnp.float32)
    positions = seq_place * frame_rows + jnp.arange(frame_rows)
    key_keep = jnp.arange(seq_frames)[None, :] < lengths[:, None]
    frame_valid = (positions[None, :] < lengths[:, None]).reshape(token_count)
    grad_out = cotangent.astype(jnp.float32).reshape(token_count, wide) * frame_valid[
        :, None
    ].astype(jnp.float32)
    grad_out_low = grad_out.astype(jnp.bfloat16)
    piece_heads = HEADS // seq_count
    piece_wide = wide // seq_count
    piece_ff = hidden_width // seq_count
    group_rows = clip_count * seq_frames

    def pieces():
        norm_copies = jnp.tile(norm_low[None], (1, 1, seq_count))
        moved_attn, moved_cross, moved_ff, moved_norm = (
            lax.all_to_all(
                attn_low.reshape(-1, 6, wide), "seq", split_axis=2, concat_axis=0, tiled=True
            ),
            lax.all_to_all(
                cross_low.reshape(-1, 2, wide), "seq", split_axis=2, concat_axis=0, tiled=True
            ),
            lax.all_to_all(
                ff_low.reshape(-1, 3, hidden_width), "seq", split_axis=2, concat_axis=0, tiled=True
            ),
            lax.all_to_all(norm_copies, "seq", split_axis=2, concat_axis=0, tiled=True),
        )
        attn_cols, cross_cols, ff_cols, norm_blocks = (
            lax.all_gather(moved_attn, "dp", axis=0, tiled=True),
            lax.all_gather(moved_cross, "dp", axis=0, tiled=True),
            lax.all_gather(moved_ff, "dp", axis=0, tiled=True),
            lax.all_gather(moved_norm, "dp", axis=0, tiled=True),
        )
        gains = norm_blocks.transpose(1, 0, 2).reshape(6, wide).astype(jnp.float32)
        return (attn_cols, cross_cols, ff_cols, gains)

    def collect(rows):
        whole = lax.all_gather(
            rows.reshape(clip_count, frame_rows, wide), "seq", axis=1, tiled=True
        )
        return whole.reshape(group_rows, wide)

    def spread(partial_value):
        mine = lax.psum_scatter(
            partial_value.reshape(clip_count, seq_frames, wide).astype(jnp.bfloat16),
            "seq",
            scatter_dimension=1,
            tiled=True,
        ).astype(jnp.float32)
        return mine.reshape(token_count, wide)

    attn_cols, cross_cols, ff_cols, gain_rows = pieces()
    group_shape = (clip_count, seq_frames, piece_heads, HDIM)
    cosine_table, sine_table = rotary_tables(jnp.arange(seq_frames), HDIM)
    normed_one = layer_norm(stream, gain_rows[0], gain_rows[1]).astype(jnp.bfloat16)
    group_one = collect(normed_one)
    projected = jnp.dot(
        group_one,
        attn_cols[:, :3].reshape(wide, 3 * piece_wide),
        preferred_element_type=jnp.float32,
    )
    queries = rotate(
        projected[:, :piece_wide].reshape(group_shape), cosine_table, sine_table
    ).astype(jnp.bfloat16)
    all_keys = rotate(
        projected[:, piece_wide : 2 * piece_wide].reshape(group_shape), cosine_table, sine_table
    ).astype(jnp.bfloat16)
    all_values = projected[:, 2 * piece_wide :].astype(jnp.bfloat16).reshape(group_shape)
    stamp_normed = layer_norm(stamps, gain_rows[0], gain_rows[1]).astype(jnp.bfloat16)
    stamp_pair = jnp.dot(
        stamp_normed,
        attn_cols[:, 1:3].reshape(wide, 2 * piece_wide),
        preferred_element_type=jnp.float32,
    )
    stamp_key = (
        stamp_pair[:, :piece_wide].astype(jnp.bfloat16).reshape(clip_count, piece_heads, HDIM)
    )
    stamp_value = (
        stamp_pair[:, piece_wide:].astype(jnp.bfloat16).reshape(clip_count, piece_heads, HDIM)
    )
    self_mixed, self_lse = self_forward(
        queries, all_keys, all_values, stamp_key, stamp_value, key_keep
    )
    self_low = self_mixed.astype(jnp.bfloat16).reshape(group_rows, piece_wide)
    resid_one = stream + spread(times_transposed(self_low, attn_cols[:, 3]))
    normed_two = layer_norm(resid_one, gain_rows[2], gain_rows[3]).astype(jnp.bfloat16)
    group_two = collect(normed_two)
    cross_query = jnp.dot(group_two, attn_cols[:, 4], preferred_element_type=jnp.float32)
    cross_query = cross_query.astype(jnp.bfloat16).reshape(group_shape)
    cond_pair = jnp.dot(
        cond_flat,
        cross_cols.reshape(cond_width, 2 * piece_wide),
        preferred_element_type=jnp.float32,
    )
    cond_shape = (clip_count, cond_count, piece_heads, HDIM)
    cross_keys = cond_pair[:, :piece_wide].astype(jnp.bfloat16).reshape(cond_shape)
    cross_values = cond_pair[:, piece_wide:].astype(jnp.bfloat16).reshape(cond_shape)
    cross_mixed, cross_lse = cross_forward(cross_query, cross_keys, cross_values, cond_keep)
    cross_low_out = cross_mixed.astype(jnp.bfloat16).reshape(group_rows, piece_wide)
    resid_two = resid_one + spread(times_transposed(cross_low_out, attn_cols[:, 5]))
    normed_three = layer_norm(resid_two, gain_rows[4], gain_rows[5]).astype(jnp.bfloat16)
    group_three = collect(normed_three)
    gate_up = jnp.dot(
        group_three, ff_cols[:, :2].reshape(wide, 2 * piece_ff), preferred_element_type=jnp.float32
    )
    gate_val = gate_up[:, :piece_ff]
    up_val = gate_up[:, piece_ff:]
    hidden = (jax.nn.silu(gate_val) * up_val).astype(jnp.bfloat16)
    branch = spread(times_transposed(hidden, ff_cols[:, 2]))
    layer_out = (resid_two + branch).astype(jnp.bfloat16).reshape(clip_count, frame_rows, wide)
    attn_cols, cross_cols, ff_cols, gain_rows = pieces()
    group_grad_out = collect(grad_out_low)
    grad_hidden = jnp.dot(group_grad_out, ff_cols[:, 2], preferred_element_type=jnp.float32)
    sigmoid_gate = jax.nn.sigmoid(gate_val)
    grad_gate = grad_hidden * up_val * sigmoid_gate * (1.0 + gate_val * (1.0 - sigmoid_gate))
    grad_up = grad_hidden * gate_val * sigmoid_gate
    grad_gate_up = jnp.concatenate([grad_gate, grad_up], axis=1).astype(jnp.bfloat16)
    grad_normed_three = spread(
        times_transposed(grad_gate_up, ff_cols[:, :2].reshape(wide, 2 * piece_ff))
    )
    _, norm_three_back = jax.vjp(layer_norm, resid_two, gain_rows[4], gain_rows[5])
    grad_two_part, grad_gain_three, grad_bias_three = norm_three_back(grad_normed_three)
    grad_two = grad_out + grad_two_part
    grad_cross_branch = grad_two.astype(jnp.bfloat16)
    group_cross_branch = collect(grad_cross_branch)
    grad_cross_mixed = jnp.dot(
        group_cross_branch, attn_cols[:, 5], preferred_element_type=jnp.float32
    )
    grad_cross_mixed = grad_cross_mixed.astype(jnp.bfloat16).reshape(group_shape)
    grad_cross_query, grad_cross_keys, grad_cross_values = cross_backward(
        cross_query, cross_keys, cross_values, cond_keep, cross_lse, grad_cross_mixed
    )
    grad_cross_query = grad_cross_query.astype(jnp.bfloat16).reshape(group_rows, piece_wide)
    grad_normed_two = spread(times_transposed(grad_cross_query, attn_cols[:, 4]))
    _, norm_two_back = jax.vjp(layer_norm, resid_one, gain_rows[2], gain_rows[3])
    grad_one_part, grad_gain_two, grad_bias_two = norm_two_back(grad_normed_two)
    grad_one = grad_two + grad_one_part
    grad_self_branch = grad_one.astype(jnp.bfloat16)
    group_self_branch = collect(grad_self_branch)
    grad_self_mixed = jnp.dot(
        group_self_branch, attn_cols[:, 3], preferred_element_type=jnp.float32
    )
    grad_self_mixed = grad_self_mixed.astype(jnp.bfloat16).reshape(group_shape)
    grad_queries, key_part, value_part, grad_stamp_key, grad_stamp_value = self_backward(
        queries, all_keys, all_values, stamp_key, stamp_value, key_keep, self_lse, grad_self_mixed
    )
    grad_query_raw = (
        rotate(grad_queries, cosine_table, -sine_table)
        .astype(jnp.bfloat16)
        .reshape(group_rows, piece_wide)
    )
    grad_key_raw = (
        rotate(key_part, cosine_table, -sine_table)
        .astype(jnp.bfloat16)
        .reshape(group_rows, piece_wide)
    )
    grad_value = value_part.astype(jnp.bfloat16).reshape(group_rows, piece_wide)
    grad_project = jnp.concatenate([grad_query_raw, grad_key_raw, grad_value], axis=1)
    grad_normed_one = spread(
        times_transposed(grad_project, attn_cols[:, :3].reshape(wide, 3 * piece_wide))
    )
    stamp_grad = jnp.concatenate(
        [
            grad_stamp_key.reshape(clip_count, piece_wide),
            grad_stamp_value.reshape(clip_count, piece_wide),
        ],
        axis=1,
    )
    grad_stamp_normed = split_times_transposed(
        stamp_grad, attn_cols[:, 1:3].reshape(wide, 2 * piece_wide)
    )
    _, norm_one_back = jax.vjp(layer_norm, stream, gain_rows[0], gain_rows[1])
    grad_zero_part, grad_gain_one, grad_bias_one = norm_one_back(grad_normed_one)
    _, norm_stamp_back = jax.vjp(layer_norm, stamps, gain_rows[0], gain_rows[1])
    _, grad_gain_stamp, grad_bias_stamp = norm_stamp_back(grad_stamp_normed)
    frames_grad = (grad_one + grad_zero_part).reshape(clip_count, frame_rows, wide)
    project_grad = outer_sum(group_one, grad_project)
    stamp_weight_grad = split_outer(stamp_normed, stamp_grad)
    attn_piece = jnp.stack(
        [
            project_grad[:, :piece_wide],
            project_grad[:, piece_wide : 2 * piece_wide] + stamp_weight_grad[:, :piece_wide],
            project_grad[:, 2 * piece_wide :] + stamp_weight_grad[:, piece_wide:],
            outer_sum(group_self_branch, self_low),
            outer_sum(group_two, grad_cross_query),
            outer_sum(group_cross_branch, cross_low_out),
        ],
        axis=1,
    )
    cond_grad = jnp.concatenate(
        [
            grad_cross_keys.reshape(clip_count * cond_count, piece_wide),
            grad_cross_values.reshape(clip_count * cond_count, piece_wide),
        ],
        axis=1,
    )
    cross_piece = split_outer(cond_flat, cond_grad).reshape(cond_width, 2, piece_wide)
    ff_piece = jnp.stack(
        [
            outer_sum(group_three, grad_gate_up[:, :piece_ff]),
            outer_sum(group_three, grad_gate_up[:, piece_ff:]),
            outer_sum(group_grad_out, hidden),
        ],
        axis=1,
    )
    norm_grad = jnp.stack(
        [
            grad_gain_one + grad_gain_stamp,
            grad_bias_one + grad_bias_stamp,
            grad_gain_two,
            grad_bias_two,
            grad_gain_three,
            grad_bias_three,
        ],
        axis=0,
    )
    norm_column = norm_grad.T[:, :, None]
    summed_attn, summed_cross, summed_ff, summed_norm = (
        lax.psum_scatter(
            attn_piece.astype(jnp.bfloat16), "dp", scatter_dimension=0, tiled=True
        ).astype(jnp.float32),
        lax.psum_scatter(
            cross_piece.astype(jnp.bfloat16), "dp", scatter_dimension=0, tiled=True
        ).astype(jnp.float32),
        lax.psum_scatter(
            ff_piece.astype(jnp.bfloat16), "dp", scatter_dimension=0, tiled=True
        ).astype(jnp.float32),
        lax.psum_scatter(
            norm_column.astype(jnp.bfloat16), "dp", scatter_dimension=0, tiled=True
        ).astype(jnp.float32),
    )
    owned_attn, owned_cross, owned_ff, owned_norm = (
        lax.all_to_all(
            summed_attn.astype(jnp.bfloat16), "seq", split_axis=0, concat_axis=2, tiled=True
        ).astype(summed_attn.dtype),
        lax.all_to_all(
            summed_cross.astype(jnp.bfloat16), "seq", split_axis=0, concat_axis=2, tiled=True
        ).astype(summed_cross.dtype),
        lax.all_to_all(
            summed_ff.astype(jnp.bfloat16), "seq", split_axis=0, concat_axis=2, tiled=True
        ).astype(summed_ff.dtype),
        lax.all_to_all(
            summed_norm.astype(jnp.bfloat16), "seq", split_axis=0, concat_axis=2, tiled=True
        ).astype(summed_norm.dtype),
    )
    attn_reduced = owned_attn.reshape(owned_attn.shape[0], 6 * wide)
    cross_reduced = owned_cross.reshape(owned_cross.shape[0], 2 * wide)
    ff_reduced = owned_ff.reshape(owned_ff.shape[0], 3 * hidden_width)
    norm_reduced = jnp.sum(owned_norm, axis=2).T
    local_squares = (
        jnp.sum(attn_reduced * attn_reduced)
        + jnp.sum(cross_reduced * cross_reduced)
        + jnp.sum(norm_reduced * norm_reduced)
        + jnp.sum(ff_reduced * ff_reduced)
    )
    total_squares = lax.psum(local_squares, ("dp", "seq"))
    grad_norm = jnp.sqrt(total_squares)
    factor = jnp.minimum(1.0, clip_limit / grad_norm)
    attn_new, attn_first_new, attn_second_new = adam_step(
        attn_weight, attn_first, attn_second, attn_reduced * factor, matrix_rate, matrix_decay
    )
    cross_new, cross_first_new, cross_second_new = adam_step(
        cross_weight, cross_first, cross_second, cross_reduced * factor, matrix_rate, matrix_decay
    )
    norm_new, norm_first_new, norm_second_new = adam_step(
        norm_param, norm_first, norm_second, norm_reduced * factor, gain_rate, 0.0
    )
    ff_new, ff_first_new, ff_second_new = adam_step(
        ff_weight, ff_first, ff_second, ff_reduced * factor, matrix_rate, matrix_decay
    )
    return (
        layer_out,
        frames_grad,
        grad_norm,
        attn_new,
        cross_new,
        norm_new,
        ff_new,
        attn_first_new,
        cross_first_new,
        norm_first_new,
        ff_first_new,
        attn_second_new,
        cross_second_new,
        norm_second_new,
        ff_second_new,
    )


MESH = pl.DeviceIdType.MESH
DMA = pltpu.SemaphoreType.DMA
VMEM_LIMIT = 60 * 2**20


def plane_fits(mesh):
    return mesh.shape["dp"] == 8 and mesh.shape["dp"] % mesh.shape["seq"] == 0


def plane_places():
    place = lax.axis_index("dp")
    return (place, lax.axis_index("seq"), lambda mask: jnp.bitwise_xor(place, mask))


def greet(partners):
    barrier = pltpu.get_barrier_semaphore()
    for partner in partners:
        pl.semaphore_signal(barrier, inc=1, device_id=partner, device_id_type=MESH)
    pl.semaphore_wait(barrier, len(partners))


def remote(source, goal, send_sem, recv_sem, device):
    return pltpu.make_async_remote_copy(
        src_ref=source,
        dst_ref=goal,
        send_sem=send_sem,
        recv_sem=recv_sem,
        device_id=device,
        device_id_type=MESH,
    )


def communicating(collective_id):
    return pltpu.CompilerParams(
        has_side_effects=True, collective_id=collective_id, vmem_limit_bytes=VMEM_LIMIT
    )


def any_spec():
    return pl.BlockSpec(memory_space=pl.ANY)


def gather_body(clips, rows, sub, own_ref, all_ref, send_sem, recv_sem, local_sem):
    place, depth, flip = plane_places()
    core, beside_x, beside_y, across = flip(1), flip(2), flip(4), flip(6)
    greet([(core, depth), (beside_x, depth), (beside_y, depth)])
    chunks = [(clip, part) for clip in range(clips) for part in range(rows // sub)]
    count = len(chunks)
    half = count // 2
    sends = []

    def view(slot, index):
        clip, part = chunks[index]
        return all_ref.at[clip, slot, pl.ds(part * sub, sub)]

    def own(index):
        clip, part = chunks[index]
        return own_ref.at[clip, pl.ds(part * sub, sub)]

    def send(source, slot, index, device):
        copy = remote(
            source,
            view(slot, index),
            send_sem.at[len(sends)],
            recv_sem.at[slot, index],
            (device, depth),
        )
        copy.start()
        sends.append(copy)

    def arrived(slot, index):
        block = view(slot, index)
        remote(
            block, block, send_sem.at[0], recv_sem.at[slot, index], (core, depth)
        ).wait_recv()

    x_order = list(range(count))
    y_order = list(range(half, count)) + list(range(half))
    for step in range(count):
        send(own(x_order[step]), place, x_order[step], beside_x)
        send(own(y_order[step]), place, y_order[step], beside_y)
    stays = []
    for clip in range(clips):
        copy = pltpu.make_async_copy(
            own_ref.at[clip], all_ref.at[clip, place], local_sem.at[clip]
        )
        copy.start()
        stays.append(copy)
    for index in range(count):
        send(own(index), place, index, core)
    for step in range(count):
        x_index, y_index = x_order[step], y_order[step]
        arrived(beside_x, x_index)
        if x_index < half:
            send(view(beside_x, x_index), beside_x, x_index, beside_y)
        send(view(beside_x, x_index), beside_x, x_index, core)
        arrived(beside_y, y_index)
        if y_index >= half:
            send(view(beside_y, y_index), beside_y, y_index, beside_x)
        send(view(beside_y, y_index), beside_y, y_index, core)
    for step in range(half):
        for index in (x_order[step], y_order[step]):
            arrived(across, index)
            send(view(across, index), across, index, core)
    for slot in (core, flip(3), flip(5), flip(7)):
        for index in range(count):
            arrived(slot, index)
    for copy in stays:
        copy.wait()
    for copy in sends:
        copy.wait_send()


def plane_gather(own_rows, collective_id, sub=64):
    clips, rows, wide = own_rows.shape
    count = clips * (rows // sub)
    return pl.pallas_call(
        functools.partial(gather_body, clips, rows, sub),
        out_shape=jax.ShapeDtypeStruct((clips, 8, rows, wide), own_rows.dtype),
        in_specs=[any_spec()],
        out_specs=any_spec(),
        scratch_shapes=[DMA((7 * count,)), DMA((8, count)), DMA((clips,))],
        compiler_params=communicating(collective_id),
    )(own_rows)


def reduce_body(
    clips, rows, sub, part_ref, sum_ref, pair, held, turn, from_x, from_y, *sems
):
    send_sem, core_sem, turn_sem, x_sem, y_sem = sems
    place, depth, flip = plane_places()
    core, beside_x, beside_y = flip(1), flip(2), flip(4)
    greet([(core, depth), (beside_x, depth), (beside_y, depth)])
    chunks = [(clip, part) for clip in range(clips) for part in range(rows // sub)]
    count = len(chunks)
    half = count // 2
    sends = []

    def send(source, goal, recv_sem, device):
        copy = remote(source, goal, send_sem.at[len(sends)], recv_sem, (device, depth))
        copy.start()
        sends.append(copy)

    def arrived(block, recv_sem):
        remote(block, block, send_sem.at[0], recv_sem, (core, depth)).wait_recv()

    def term(slot, index):
        clip, part = chunks[index]
        return part_ref.at[clip, slot, pl.ds(part * sub, sub)]

    for chip in (3, 1, 2, 0):
        for index in range(count):
            send(
                term(flip((2 * chip) ^ 1), index),
                pair.at[index, chip],
                core_sem.at[index, chip],
                core,
            )

    def total(*blocks):
        return sum(block[...].astype(jnp.float32) for block in blocks)

    def combine(chip, index):
        arrived(pair.at[index, chip], core_sem.at[index, chip])
        held[index, chip] = total(term(flip(2 * chip), index), pair.at[index, chip]).astype(
            held.dtype
        )

    for low in range(half):
        high = half + low
        combine(3, low)
        send(held.at[low, 3], turn.at[low], turn_sem.at[low], beside_x)
        combine(3, high)
        send(held.at[high, 3], turn.at[high], turn_sem.at[high], beside_y)
    for low in range(half):
        high = half + low
        combine(1, low)
        send(held.at[low, 1], from_x.at[low], x_sem.at[low], beside_x)
        combine(2, high)
        send(held.at[high, 2], from_y.at[high], y_sem.at[high], beside_y)
    for low in range(half):
        high = half + low
        combine(2, low)
        arrived(turn.at[low], turn_sem.at[low])
        held[low, 2] = total(held.at[low, 2], turn.at[low]).astype(held.dtype)
        send(held.at[low, 2], from_y.at[low], y_sem.at[low], beside_y)
        combine(1, high)
        arrived(turn.at[high], turn_sem.at[high])
        held[high, 1] = total(held.at[high, 1], turn.at[high]).astype(held.dtype)
        send(held.at[high, 1], from_x.at[high], x_sem.at[high], beside_x)
    for index in range(count):
        clip, part = chunks[index]
        arrived(pair.at[index, 0], core_sem.at[index, 0])
        arrived(from_x.at[index], x_sem.at[index])
        arrived(from_y.at[index], y_sem.at[index])
        sum_ref[clip, pl.ds(part * sub, sub)] = total(
            term(place, index), pair.at[index, 0], from_x.at[index], from_y.at[index]
        )
    for copy in sends:
        copy.wait_send()


def plane_reduce(terms, collective_id, sub=64):
    clips, _, rows, wide = terms.shape
    count = clips * (rows // sub)
    kind = terms.dtype
    return pl.pallas_call(
        functools.partial(reduce_body, clips, rows, sub),
        out_shape=jax.ShapeDtypeStruct((clips, rows, wide), jnp.float32),
        in_specs=[pl.BlockSpec(memory_space=pltpu.VMEM)],
        out_specs=pl.BlockSpec(memory_space=pltpu.VMEM),
        scratch_shapes=[
            pltpu.VMEM((count, 4, sub, wide), kind),
            pltpu.VMEM((count, 4, sub, wide), kind),
            pltpu.VMEM((count, sub, wide), kind),
            pltpu.VMEM((count, sub, wide), kind),
            pltpu.VMEM((count, sub, wide), kind),
            DMA((7 * count,)),
            DMA((count, 4)),
            DMA((count,)),
            DMA((count,)),
            DMA((count,)),
        ],
        compiler_params=communicating(collective_id),
    )(terms)


def greet_cross(group, planes):
    place, depth, flip = plane_places()
    greet(
        [(flip(mask), depth) for mask in range(1, group)]
        + [(place, lax.rem(depth + step, planes)) for step in range(1, planes)]
    )


def inward_body(group, planes, own_ref, kept_ref, mid, *sems):
    near_send, near_recv, far_send, far_recv, local_sem = sems
    place, depth, flip = plane_places()
    per = group // planes
    greet_cross(group, planes)
    first = []
    for mask in range(1, group):
        other = flip(mask)
        copy = remote(
            own_ref.at[other],
            mid.at[place],
            near_send.at[mask],
            near_recv.at[mask],
            (other, depth),
        )
        copy.start()
        first.append(copy)
    second = []
    for mask in range(group):
        source = flip(mask)
        goal, slot = lax.div(source, per), lax.rem(source, per)
        block = own_ref.at[place]
        if mask:
            first[mask - 1].wait_recv()
            block = mid.at[source]
        away = remote(
            block,
            kept_ref.at[slot, depth],
            far_send.at[mask],
            far_recv.at[slot, depth],
            (place, goal),
        )
        stay = pltpu.make_async_copy(block, kept_ref.at[slot, depth], local_sem.at[mask])
        pl.when(goal != depth)(away.start)
        pl.when(goal == depth)(stay.start)
        second.append((goal, away, stay))
    for slot in range(per):
        for origin in range(planes):
            block = kept_ref.at[slot, origin]
            pl.when(origin != depth)(
                remote(
                    block,
                    block,
                    far_send.at[0],
                    far_recv.at[slot, origin],
                    (place, lax.rem(depth + 1, planes)),
                ).wait_recv
            )
    for goal, away, stay in second:
        pl.when(goal != depth)(away.wait_send)
        pl.when(goal == depth)(stay.wait)
    for copy in first:
        copy.wait_send()


def inward(rows_of_clip, planes, collective_id):
    group, rows, wide = rows_of_clip.shape
    kept, _ = pl.pallas_call(
        functools.partial(inward_body, group, planes),
        out_shape=[
            jax.ShapeDtypeStruct((group // planes, planes, rows, wide), rows_of_clip.dtype),
            jax.ShapeDtypeStruct((group, rows, wide), rows_of_clip.dtype),
        ],
        in_specs=[any_spec()],
        out_specs=[any_spec()] * 2,
        scratch_shapes=[
            DMA((group,)),
            DMA((group,)),
            DMA((group,)),
            DMA((group // planes, planes)),
            DMA((group,)),
        ],
        compiler_params=communicating(collective_id),
    )(rows_of_clip)
    return kept


def outward_body(group, planes, kept_ref, own_ref, mid, *sems):
    far_send, far_recv, near_send, near_recv, local_sem = sems
    place, depth, flip = plane_places()
    per = group // planes
    greet_cross(group, planes)
    first = []
    for step in range(1, planes):
        origin = lax.rem(depth + step, planes)
        for slot in range(per):
            clip = per * depth + slot
            copy = remote(
                kept_ref.at[slot, origin],
                mid.at[clip],
                far_send.at[slot, step],
                far_recv.at[clip],
                (place, origin),
            )
            copy.start()
            first.append(copy)
    second = []

    def hand_over(block, clip):
        index = len(second)
        away = remote(
            block, own_ref.at[place], near_send.at[index], near_recv.at[place], (clip, depth)
        )
        stay = pltpu.make_async_copy(block, own_ref.at[place], local_sem.at[index])
        pl.when(clip != place)(away.start)
        pl.when(clip == place)(stay.start)
        second.append((clip, away, stay))

    for slot in range(per):
        hand_over(kept_ref.at[slot, depth], per * depth + slot)
    for step in range(1, planes):
        source = lax.rem(depth + step, planes)
        for slot in range(per):
            clip = per * source + slot
            block = mid.at[clip]
            remote(
                block, block, far_send.at[0, 0], far_recv.at[clip], (place, source)
            ).wait_recv()
            hand_over(block, clip)
    for mask in range(1, group):
        other = flip(mask)
        block = own_ref.at[other]
        remote(block, block, near_send.at[0], near_recv.at[other], (other, depth)).wait_recv()
    for clip, away, stay in second:
        pl.when(clip != place)(away.wait_send)
        pl.when(clip == place)(stay.wait)
    for copy in first:
        copy.wait_send()


def outward(kept_rows, collective_id):
    per, planes, rows, wide = kept_rows.shape
    group = per * planes
    own, _ = pl.pallas_call(
        functools.partial(outward_body, group, planes),
        out_shape=[jax.ShapeDtypeStruct((group, rows, wide), kept_rows.dtype)] * 2,
        in_specs=[any_spec()],
        out_specs=[any_spec()] * 2,
        scratch_shapes=[
            DMA((per, planes)),
            DMA((group,)),
            DMA((group,)),
            DMA((group,)),
            DMA((group,)),
        ],
        compiler_params=communicating(collective_id),
    )(kept_rows)
    return own


def swap_body(own_ref, kept_ref, send_sem, recv_sem, local_sem):
    place, depth, flip = plane_places()
    masks = (6, 7, 2, 3, 4, 5, 1)
    greet([(flip(mask), depth) for mask in masks])
    copies = []
    for mask in masks:
        other = flip(mask)
        copy = remote(
            own_ref.at[other],
            kept_ref.at[place],
            send_sem.at[mask],
            recv_sem.at[mask],
            (other, depth),
        )
        copy.start()
        copies.append(copy)
    stay = pltpu.make_async_copy(own_ref.at[place], kept_ref.at[place], local_sem)
    stay.start()
    stay.wait()
    for copy in copies:
        copy.wait()


def plane_swap(blocks, collective_id):
    return pl.pallas_call(
        swap_body,
        out_shape=jax.ShapeDtypeStruct(blocks.shape, blocks.dtype),
        in_specs=[any_spec()],
        out_specs=any_spec(),
        scratch_shapes=[DMA((8,)), DMA((8,)), DMA(())],
        compiler_params=communicating(collective_id),
    )(blocks)


def plane_device(
    frames,
    time_token,
    cond_ids,
    cond_mask,
    lengths,
    cond_table,
    cotangent,
    attn_weight,
    cross_weight,
    norm_param,
    ff_weight,
    attn_first,
    attn_second,
    cross_first,
    cross_second,
    norm_first,
    norm_second,
    ff_first,
    ff_second,
):
    group, planes = lax.axis_size("dp"), lax.axis_size("seq")
    place, depth = lax.axis_index("dp"), lax.axis_index("seq")
    clips = group // planes
    _, frame_rows, wide = frames.shape
    piece = frame_rows // group
    seq_frames = frame_rows * planes
    own_rows = planes * piece
    heads = HEADS // group
    head_wide = heads * HDIM
    ff_wide = FF // group
    owned = wide // (group * planes)
    cond_count, cond_wide = cond_ids.shape[1], cond_table.shape[1]
    cond_owned = cross_weight.shape[0]

    def to_plane_order(values):
        lead = values.shape[:-1]
        return jnp.swapaxes(values.reshape(lead + (group, planes, owned)), -3, -2).reshape(
            lead + (wide,)
        )

    def to_whole_order(values):
        lead = values.shape[:-1]
        return jnp.swapaxes(values.reshape(lead + (planes, group, owned)), -3, -2).reshape(
            lead + (wide,)
        )

    attn_low = attn_weight.astype(jnp.bfloat16).reshape(owned, 6, group, head_wide)
    attn_cut = attn_low.transpose(2, 0, 1, 3).reshape(group, owned, 6 * head_wide)
    cross_low = cross_weight.astype(jnp.bfloat16).reshape(cond_owned, 2, group, head_wide)
    cross_cut = cross_low.transpose(2, 0, 1, 3).reshape(group, owned, -1)
    ff_low = ff_weight.astype(jnp.bfloat16).reshape(owned, 3, group, ff_wide)
    ff_cut = ff_low.transpose(2, 0, 1, 3).reshape(group, owned, 3 * ff_wide)
    attn_mine = plane_swap(jnp.concatenate([attn_cut, cross_cut], axis=2), 1)
    ff_mine = plane_swap(ff_cut, 2)

    def over_planes(block):
        return lax.all_gather(block.reshape(group * owned, -1), "seq", axis=0, tiled=True)

    w_qkv = over_planes(attn_mine[:, :, : 3 * head_wide])
    w_rest = over_planes(attn_mine[:, :, 3 * head_wide :])
    w_gate_up = over_planes(ff_mine[:, :, : 2 * ff_wide])
    w_down = over_planes(ff_mine[:, :, 2 * ff_wide :])
    w_self_out = w_rest[:, :head_wide]
    w_cross_query = w_rest[:, head_wide : 2 * head_wide]
    w_cross_out = w_rest[:, 2 * head_wide : 3 * head_wide]
    w_cond = w_rest[:, 3 * head_wide :].reshape(planes, group, cond_owned, -1)
    w_cond = jnp.swapaxes(w_cond, 0, 1).reshape(cond_wide, 2 * head_wide)
    norm_all = lax.all_gather(norm_param.astype(jnp.bfloat16), ("dp", "seq"), axis=0)
    norm_all = norm_all.reshape(group, planes, 6, owned).transpose(2, 1, 0, 3)
    gain_rows = norm_all.reshape(6, wide).astype(jnp.float32)

    def of_plane(values):
        everyone = lax.all_gather(values, "dp", axis=0, tiled=True)
        return lax.dynamic_slice_in_dim(everyone, depth * clips, clips, axis=0)

    clip_lengths = of_plane(lengths)
    cond_keep = of_plane(cond_mask) > 0
    stamps = to_plane_order(of_plane(time_token)).astype(jnp.float32)
    vocab_rows = cond_table.shape[0]
    relative = cond_ids - depth * vocab_rows
    inside = (relative >= 0) & (relative < vocab_rows)
    picked = jnp.take(cond_table, jnp.clip(relative, 0, vocab_rows - 1), axis=0)
    picked = jnp.where(inside[..., None], picked, jnp.zeros((), picked.dtype))
    cond = of_plane(lax.psum(picked, "seq"))
    cond_flat = cond.reshape(clips * cond_count, cond_wide)

    positions = depth * frame_rows + jnp.arange(frame_rows)
    frame_valid = (positions[None, :] < lengths[:, None]).astype(cotangent.dtype)
    stream = inward(to_plane_order(frames).reshape(group, piece, wide), planes, 3)
    stream = stream.reshape(clips, own_rows, wide).astype(jnp.float32)
    masked = to_plane_order(cotangent * frame_valid[..., None])
    grad_out_low = inward(masked.reshape(group, piece, wide), planes, 4)
    grad_out_low = grad_out_low.reshape(clips, own_rows, wide)
    grad_out = grad_out_low.astype(jnp.float32)

    group_rows = clips * seq_frames
    row_place = jnp.arange(seq_frames)
    row_owner, row_rest = row_place // own_rows, row_place % own_rows
    true_place = (row_rest // piece) * frame_rows + row_owner * piece + row_rest % piece
    key_keep = true_place[None, :] < clip_lengths[:, None]
    cosine_table, sine_table = rotary_tables(true_place, HDIM)
    group_shape = (clips, seq_frames, heads, HDIM)

    def collect(rows, collective_id):
        return plane_gather(rows, collective_id).reshape(group_rows, wide)

    def spread(partial_value, collective_id):
        terms = partial_value.astype(jnp.bfloat16).reshape(clips, group, own_rows, wide)
        return plane_reduce(terms, collective_id)

    normed_one = layer_norm(stream, gain_rows[0], gain_rows[1]).astype(jnp.bfloat16)
    group_one = collect(normed_one, 5)
    projected = jnp.dot(group_one, w_qkv, preferred_element_type=jnp.float32)
    queries = rotate(
        projected[:, :head_wide].reshape(group_shape), cosine_table, sine_table
    ).astype(jnp.bfloat16)
    all_keys = rotate(
        projected[:, head_wide : 2 * head_wide].reshape(group_shape), cosine_table, sine_table
    ).astype(jnp.bfloat16)
    all_values = projected[:, 2 * head_wide :].astype(jnp.bfloat16).reshape(group_shape)
    stamp_normed = layer_norm(stamps, gain_rows[0], gain_rows[1]).astype(jnp.bfloat16)
    stamp_pair = jnp.dot(stamp_normed, w_qkv[:, head_wide:], preferred_element_type=jnp.float32)
    stamp_pair = stamp_pair.astype(jnp.bfloat16)
    stamp_key = stamp_pair[:, :head_wide].reshape(clips, heads, HDIM)
    stamp_value = stamp_pair[:, head_wide:].reshape(clips, heads, HDIM)
    self_mixed, self_lse = self_forward(
        queries, all_keys, all_values, stamp_key, stamp_value, key_keep
    )
    self_low = self_mixed.astype(jnp.bfloat16).reshape(group_rows, head_wide)
    resid_one = stream + spread(times_transposed(self_low, w_self_out), 6)
    normed_two = layer_norm(resid_one, gain_rows[2], gain_rows[3]).astype(jnp.bfloat16)
    group_two = collect(normed_two, 7)
    cross_query = jnp.dot(group_two, w_cross_query, preferred_element_type=jnp.float32)
    cross_query = cross_query.astype(jnp.bfloat16).reshape(group_shape)
    cond_pair = jnp.dot(cond_flat, w_cond, preferred_element_type=jnp.float32)
    cond_pair = cond_pair.astype(jnp.bfloat16)
    cond_shape = (clips, cond_count, heads, HDIM)
    cross_keys = cond_pair[:, :head_wide].reshape(cond_shape)
    cross_values = cond_pair[:, head_wide:].reshape(cond_shape)
    cross_mixed, cross_lse = cross_forward(cross_query, cross_keys, cross_values, cond_keep)
    cross_out = cross_mixed.astype(jnp.bfloat16).reshape(group_rows, head_wide)
    resid_two = resid_one + spread(times_transposed(cross_out, w_cross_out), 8)
    normed_three = layer_norm(resid_two, gain_rows[4], gain_rows[5]).astype(jnp.bfloat16)
    group_three = collect(normed_three, 9)
    group_grad_out = collect(grad_out_low, 10)
    gate_up = jnp.dot(group_three, w_gate_up, preferred_element_type=jnp.float32)
    gate_val, up_val = gate_up[:, :ff_wide], gate_up[:, ff_wide:]
    hidden = (jax.nn.silu(gate_val) * up_val).astype(jnp.bfloat16)
    branch = spread(times_transposed(hidden, w_down), 11)
    layer_out = (resid_two + branch).astype(jnp.bfloat16)
    layer_out = outward(layer_out.reshape(clips, planes, piece, wide), 12)
    layer_out = to_whole_order(layer_out.reshape(frames.shape))

    grad_hidden = jnp.dot(group_grad_out, w_down, preferred_element_type=jnp.float32)
    sigmoid_gate = jax.nn.sigmoid(gate_val)
    grad_gate = grad_hidden * up_val * sigmoid_gate * (1.0 + gate_val * (1.0 - sigmoid_gate))
    grad_up = grad_hidden * gate_val * sigmoid_gate
    grad_gate_up = jnp.concatenate([grad_gate, grad_up], axis=1).astype(jnp.bfloat16)
    grad_normed_three = spread(times_transposed(grad_gate_up, w_gate_up), 13)

    def over_rows(block):
        return lax.psum_scatter(
            block.astype(jnp.bfloat16), "seq", scatter_dimension=0, tiled=True
        ).reshape(group, owned, -1)

    ff_piece = jnp.concatenate(
        [outer_sum(group_three, grad_gate_up), outer_sum(group_grad_out, hidden)], axis=1
    )
    ff_owned = plane_swap(over_rows(ff_piece), 14)
    ff_reduced = ff_owned.reshape(group, owned, 3, ff_wide).transpose(1, 2, 0, 3)
    ff_reduced = ff_reduced.reshape(owned, 3 * FF).astype(jnp.float32)

    _, norm_three_back = jax.vjp(layer_norm, resid_two, gain_rows[4], gain_rows[5])
    grad_two_part, grad_gain_three, grad_bias_three = norm_three_back(grad_normed_three)
    grad_two = grad_out + grad_two_part
    group_cross_branch = collect(grad_two.astype(jnp.bfloat16), 15)
    grad_cross_mixed = jnp.dot(group_cross_branch, w_cross_out, preferred_element_type=jnp.float32)
    grad_cross_mixed = grad_cross_mixed.astype(jnp.bfloat16).reshape(group_shape)
    grad_cross_query, grad_cross_keys, grad_cross_values = cross_backward(
        cross_query, cross_keys, cross_values, cond_keep, cross_lse, grad_cross_mixed
    )
    grad_cross_query = grad_cross_query.astype(jnp.bfloat16).reshape(group_rows, head_wide)
    grad_normed_two = spread(times_transposed(grad_cross_query, w_cross_query), 16)
    _, norm_two_back = jax.vjp(layer_norm, resid_one, gain_rows[2], gain_rows[3])
    grad_one_part, grad_gain_two, grad_bias_two = norm_two_back(grad_normed_two)
    grad_one = grad_two + grad_one_part
    group_self_branch = collect(grad_one.astype(jnp.bfloat16), 17)
    grad_self_mixed = jnp.dot(group_self_branch, w_self_out, preferred_element_type=jnp.float32)
    grad_self_mixed = grad_self_mixed.astype(jnp.bfloat16).reshape(group_shape)
    cond_grad = jnp.concatenate(
        [
            grad_cross_keys.reshape(clips * cond_count, head_wide),
            grad_cross_values.reshape(clips * cond_count, head_wide),
        ],
        axis=1,
    )
    cross_piece = split_outer(cond_flat, cond_grad)
    cross_piece = cross_piece.reshape(group, planes, cond_owned, 2 * head_wide)
    cross_piece = jnp.swapaxes(cross_piece, 0, 1).reshape(wide, head_wide)
    rest_piece = jnp.concatenate(
        [
            outer_sum(group_self_branch, self_low),
            outer_sum(group_two, grad_cross_query),
            outer_sum(group_cross_branch, cross_out),
            cross_piece,
        ],
        axis=1,
    )
    rest_rows = over_rows(rest_piece)
    grad_queries, key_part, value_part, grad_stamp_key, grad_stamp_value = self_backward(
        queries, all_keys, all_values, stamp_key, stamp_value, key_keep, self_lse, grad_self_mixed
    )

    def turn_back(values):
        turned = rotate(values, cosine_table, -sine_table).astype(jnp.bfloat16)
        return turned.reshape(group_rows, head_wide)

    grad_value = value_part.astype(jnp.bfloat16).reshape(group_rows, head_wide)
    grad_project = jnp.concatenate(
        [turn_back(grad_queries), turn_back(key_part), grad_value], axis=1
    )
    grad_normed_one = spread(times_transposed(grad_project, w_qkv), 18)
    stamp_grad = jnp.concatenate(
        [
            grad_stamp_key.reshape(clips, head_wide),
            grad_stamp_value.reshape(clips, head_wide),
        ],
        axis=1,
    )
    grad_stamp_normed = split_times_transposed(stamp_grad, w_qkv[:, head_wide:])
    qkv_piece = outer_sum(group_one, grad_project)
    stamp_weight_grad = split_outer(stamp_normed, stamp_grad)
    qkv_piece = jnp.concatenate(
        [qkv_piece[:, :head_wide], qkv_piece[:, head_wide:] + stamp_weight_grad], axis=1
    )
    qkv_rows = over_rows(qkv_piece)
    attn_owned = plane_swap(jnp.concatenate([qkv_rows, rest_rows], axis=2), 19)
    cross_reduced = attn_owned[:, :, 6 * head_wide :].reshape(group, cond_owned, 2, head_wide)
    cross_reduced = cross_reduced.transpose(1, 2, 0, 3).reshape(cross_weight.shape)
    cross_reduced = cross_reduced.astype(jnp.float32)
    attn_reduced = attn_owned[:, :, : 6 * head_wide].reshape(group, owned, 6, head_wide)
    attn_reduced = attn_reduced.transpose(1, 2, 0, 3).reshape(attn_weight.shape)
    attn_reduced = attn_reduced.astype(jnp.float32)

    _, norm_one_back = jax.vjp(layer_norm, stream, gain_rows[0], gain_rows[1])
    grad_zero_part, grad_gain_one, grad_bias_one = norm_one_back(grad_normed_one)
    _, norm_stamp_back = jax.vjp(layer_norm, stamps, gain_rows[0], gain_rows[1])
    _, grad_gain_stamp, grad_bias_stamp = norm_stamp_back(grad_stamp_normed)
    frames_grad = (grad_one + grad_zero_part).astype(jnp.bfloat16)
    frames_grad = outward(frames_grad.reshape(clips, planes, piece, wide), 20)
    frames_grad = to_whole_order(frames_grad.reshape(frames.shape)).astype(jnp.float32)
    norm_grad = jnp.stack(
        [
            grad_gain_one + grad_gain_stamp,
            grad_bias_one + grad_bias_stamp,
            grad_gain_two,
            grad_bias_two,
            grad_gain_three,
            grad_bias_three,
        ],
        axis=0,
    )
    norm_total = lax.psum(norm_grad, ("dp", "seq"))
    norm_reduced = lax.dynamic_slice_in_dim(
        norm_total, (depth * group + place) * owned, owned, axis=1
    )
    local_squares = (
        jnp.sum(attn_reduced * attn_reduced)
        + jnp.sum(cross_reduced * cross_reduced)
        + jnp.sum(norm_reduced * norm_reduced)
        + jnp.sum(ff_reduced * ff_reduced)
    )
    grad_norm = jnp.sqrt(lax.psum(local_squares, ("dp", "seq")))
    factor = jnp.minimum(1.0, clip_limit / grad_norm)
    attn_new, attn_first_new, attn_second_new = adam_step(
        attn_weight, attn_first, attn_second, attn_reduced * factor, matrix_rate, matrix_decay
    )
    cross_new, cross_first_new, cross_second_new = adam_step(
        cross_weight, cross_first, cross_second, cross_reduced * factor, matrix_rate, matrix_decay
    )
    norm_new, norm_first_new, norm_second_new = adam_step(
        norm_param, norm_first, norm_second, norm_reduced * factor, gain_rate, 0.0
    )
    ff_new, ff_first_new, ff_second_new = adam_step(
        ff_weight, ff_first, ff_second, ff_reduced * factor, matrix_rate, matrix_decay
    )
    return (
        layer_out,
        frames_grad,
        grad_norm,
        attn_new,
        cross_new,
        norm_new,
        ff_new,
        attn_first_new,
        cross_first_new,
        norm_first_new,
        ff_first_new,
        attn_second_new,
        cross_second_new,
        norm_second_new,
        ff_second_new,
    )


def solution(mesh):
    return jax.shard_map(
        plane_device if plane_fits(mesh) else per_device,
        mesh=mesh,
        in_specs=(
            P("dp", "seq", None),
            P("dp", None),
            P("dp", None),
            P("dp", None),
            P("dp"),
            P("seq", None),
            P("dp", "seq", None),
            P(("dp", "seq"), None),
            P(("dp", "seq"), None),
            P(None, ("dp", "seq")),
            P(("dp", "seq"), None),
            P(("dp", "seq"), None),
            P(("dp", "seq"), None),
            P(("dp", "seq"), None),
            P(("dp", "seq"), None),
            P(None, ("dp", "seq")),
            P(None, ("dp", "seq")),
            P(("dp", "seq"), None),
            P(("dp", "seq"), None),
        ),
        out_specs=(
            P("dp", "seq", None),
            P("dp", "seq", None),
            P(),
            P(("dp", "seq"), None),
            P(("dp", "seq"), None),
            P(None, ("dp", "seq")),
            P(("dp", "seq"), None),
            P(("dp", "seq"), None),
            P(("dp", "seq"), None),
            P(None, ("dp", "seq")),
            P(("dp", "seq"), None),
            P(("dp", "seq"), None),
            P(("dp", "seq"), None),
            P(None, ("dp", "seq")),
            P(("dp", "seq"), None),
        ),
        check_vma=False,
    )
```

```python
import functools

import jax
import jax.numpy as jnp
from jax import lax
from jax.experimental import pallas as pl
from jax.experimental.pallas import tpu as pltpu
from jax.sharding import PartitionSpec as P

HEADS = 24
HDIM = 64
FF = 6144
UPDATE_STEP = 10


norm_eps = 1e-05
beta_first = 0.5
beta_second = 0.5
adam_eps = 1e-08
matrix_decay = 0.01
matrix_rate = 0.03
gain_rate = 0.25
clip_limit = 1.0
masked_score = -1e30


def layer_norm(values, gain_row, bias_row):
    center = values - jnp.mean(values, axis=-1, keepdims=True)
    spread = jnp.mean(center * center, axis=-1, keepdims=True)
    return center * lax.rsqrt(spread + norm_eps) * gain_row + bias_row


def rotary_tables(positions, head_size):
    half_size = head_size // 2
    frequency = 10000.0 ** (-jnp.arange(half_size, dtype=jnp.float32) / half_size)
    angles = positions.astype(jnp.float32)[:, None] * frequency[None, :]
    return (jnp.cos(angles)[:, None, :], jnp.sin(angles)[:, None, :])


def rotate(values, cosine_table, sine_table):
    half_size = values.shape[-1] // 2
    first_half = values[..., :half_size]
    second_half = values[..., half_size:]
    return jnp.concatenate(
        [
            first_half * cosine_table - second_half * sine_table,
            second_half * cosine_table + first_half * sine_table,
        ],
        axis=-1,
    )


def outer_sum(left_mat, right_mat):
    return lax.dot_general(
        left_mat, right_mat, (((0,), (0,)), ((), ())), preferred_element_type=jnp.float32
    )


def times_transposed(left_mat, right_mat):
    return lax.dot_general(
        left_mat, right_mat, (((1,), (1,)), ((), ())), preferred_element_type=jnp.float32
    )


def split_parts(values):
    upper = values.astype(jnp.bfloat16)
    lower = (values - upper.astype(jnp.float32)).astype(jnp.bfloat16)
    return (upper, lower)


def split_outer(left_low, right_full):
    upper, lower = split_parts(right_full)
    return outer_sum(left_low, upper) + outer_sum(left_low, lower)


def split_times_transposed(left_full, right_low):
    upper, lower = split_parts(left_full)
    return times_transposed(upper, right_low) + times_transposed(lower, right_low)


def self_scores(queries, keys, stamp_key, keep):
    score_scale = HDIM ** (-0.5)
    frame_part = (
        jnp.einsum("cqhd,ckhd->chqk", queries, keys, preferred_element_type=jnp.float32)
        * score_scale
    )
    frame_part = jnp.where(keep[:, None, None, :], frame_part, masked_score)
    stamp_part = (
        jnp.einsum("cqhd,chd->chq", queries, stamp_key, preferred_element_type=jnp.float32)
        * score_scale
    )
    return (frame_part, stamp_part)


def self_forward(queries, keys, values, stamp_key, stamp_value, keep):
    frame_scores, stamp_scores = self_scores(queries, keys, stamp_key, keep)
    top_score = jnp.maximum(jnp.max(frame_scores, axis=-1), stamp_scores)
    frame_expo = jnp.exp(frame_scores - top_score[..., None])
    stamp_expo = jnp.exp(stamp_scores - top_score)
    denom = jnp.sum(frame_expo, axis=-1) + stamp_expo
    self_lse = top_score + jnp.log(denom)
    frame_prob = (frame_expo / denom[..., None]).astype(jnp.bfloat16)
    stamp_prob = (stamp_expo / denom).astype(jnp.bfloat16)
    mixed = jnp.einsum(
        "chqk,ckhd->cqhd", frame_prob, values, preferred_element_type=jnp.float32
    ) + jnp.einsum("chq,chd->cqhd", stamp_prob, stamp_value, preferred_element_type=jnp.float32)
    return (mixed, self_lse)


def self_backward(queries, keys, values, stamp_key, stamp_value, keep, self_lse, grad_mixed):
    score_scale = HDIM ** (-0.5)
    frame_scores, stamp_scores = self_scores(queries, keys, stamp_key, keep)
    frame_prob = jnp.exp(frame_scores - self_lse[..., None])
    stamp_prob = jnp.exp(stamp_scores - self_lse)
    grad_frame_prob = jnp.einsum(
        "cqhd,ckhd->chqk", grad_mixed, values, preferred_element_type=jnp.float32
    )
    grad_stamp_prob = jnp.einsum(
        "cqhd,chd->chq", grad_mixed, stamp_value, preferred_element_type=jnp.float32
    )
    delta = jnp.sum(frame_prob * grad_frame_prob, axis=-1) + stamp_prob * grad_stamp_prob
    grad_frame_scores = (frame_prob * (grad_frame_prob - delta[..., None])).astype(jnp.bfloat16)
    grad_stamp_scores = (stamp_prob * (grad_stamp_prob - delta)).astype(jnp.bfloat16)
    grad_queries = (
        jnp.einsum("chqk,ckhd->cqhd", grad_frame_scores, keys, preferred_element_type=jnp.float32)
        + jnp.einsum(
            "chq,chd->cqhd", grad_stamp_scores, stamp_key, preferred_element_type=jnp.float32
        )
    ) * score_scale
    key_part = (
        jnp.einsum(
            "chqk,cqhd->ckhd", grad_frame_scores, queries, preferred_element_type=jnp.float32
        )
        * score_scale
    )
    value_part = jnp.einsum(
        "chqk,cqhd->ckhd",
        frame_prob.astype(jnp.bfloat16),
        grad_mixed,
        preferred_element_type=jnp.float32,
    )
    grad_stamp_key = (
        jnp.einsum("chq,cqhd->chd", grad_stamp_scores, queries, preferred_element_type=jnp.float32)
        * score_scale
    )
    grad_stamp_value = jnp.einsum(
        "chq,cqhd->chd",
        stamp_prob.astype(jnp.bfloat16),
        grad_mixed,
        preferred_element_type=jnp.float32,
    )
    return (grad_queries, key_part, value_part, grad_stamp_key, grad_stamp_value)


def cross_scores(query, keys, keep):
    score_scale = HDIM ** (-0.5)
    scores = (
        jnp.einsum("cqhd,ckhd->chqk", query, keys, preferred_element_type=jnp.float32) * score_scale
    )
    return jnp.where(keep[:, None, None, :], scores, masked_score)


def cross_forward(query, keys, values, keep):
    scores = cross_scores(query, keys, keep)
    top_score = jnp.max(scores, axis=-1)
    expo = jnp.exp(scores - top_score[..., None])
    denom = jnp.sum(expo, axis=-1)
    cross_lse = top_score + jnp.log(denom)
    prob = (expo / denom[..., None]).astype(jnp.bfloat16)
    mixed = jnp.einsum("chqk,ckhd->cqhd", prob, values, preferred_element_type=jnp.float32)
    return (mixed, cross_lse)


def cross_backward(query, keys, values, keep, cross_lse, grad_mixed):
    score_scale = HDIM ** (-0.5)
    prob = jnp.exp(cross_scores(query, keys, keep) - cross_lse[..., None])
    grad_prob = jnp.einsum(
        "cqhd,ckhd->chqk", grad_mixed, values, preferred_element_type=jnp.float32
    )
    delta = jnp.sum(prob * grad_prob, axis=-1)
    grad_scores = (prob * (grad_prob - delta[..., None])).astype(jnp.bfloat16)
    grad_query = (
        jnp.einsum("chqk,ckhd->cqhd", grad_scores, keys, preferred_element_type=jnp.float32)
        * score_scale
    )
    grad_keys = (
        jnp.einsum("chqk,cqhd->ckhd", grad_scores, query, preferred_element_type=jnp.float32)
        * score_scale
    )
    grad_values = jnp.einsum(
        "chqk,cqhd->ckhd", prob.astype(jnp.bfloat16), grad_mixed, preferred_element_type=jnp.float32
    )
    return (grad_query, grad_keys, grad_values)


def adam_step(weight, first, second, gradient, step_rate, decay_rate):
    first_new = beta_first * first + (1.0 - beta_first) * gradient
    second_new = beta_second * second + (1.0 - beta_second) * gradient * gradient
    fix_first = 1.0 - beta_first**UPDATE_STEP
    fix_second = 1.0 - beta_second**UPDATE_STEP
    normed_step = first_new / fix_first / (jnp.sqrt(second_new / fix_second) + adam_eps)
    return (weight - step_rate * (normed_step + decay_rate * weight), first_new, second_new)


def per_device(
    frames,
    time_token,
    cond_ids,
    cond_mask,
    lengths,
    cond_table,
    cotangent,
    attn_weight,
    cross_weight,
    norm_param,
    ff_weight,
    attn_first,
    attn_second,
    cross_first,
    cross_second,
    norm_first,
    norm_second,
    ff_first,
    ff_second,
):
    clip_count, frame_rows, wide = frames.shape
    hidden_width = FF
    token_count = clip_count * frame_rows
    seq_count = lax.axis_size("seq")
    seq_frames = frame_rows * seq_count
    seq_place = lax.axis_index("seq")
    vocab_rows = cond_table.shape[0]
    relative = cond_ids - seq_place * vocab_rows
    inside = (relative >= 0) & (relative < vocab_rows)
    picked = jnp.take(cond_table, jnp.clip(relative, 0, vocab_rows - 1), axis=0).astype(jnp.float32)
    picked = jnp.where(inside[..., None], picked, 0.0)
    cond = lax.psum(picked.astype(jnp.bfloat16), "seq")
    cond_count = cond.shape[1]
    cond_flat = cond.reshape(clip_count * cond_count, cond.shape[2])
    cond_width = cond.shape[2]
    cond_keep = cond_mask > 0
    attn_low = attn_weight.astype(jnp.bfloat16)
    cross_low = cross_weight.astype(jnp.bfloat16)
    norm_low = norm_param.astype(jnp.bfloat16)
    ff_low = ff_weight.astype(jnp.bfloat16)
    stream = frames.astype(jnp.float32).reshape(token_count, wide)
    stamps = time_token.astype(jnp.float32)
    positions = seq_place * frame_rows + jnp.arange(frame_rows)
    key_keep = jnp.arange(seq_frames)[None, :] < lengths[:, None]
    frame_valid = (positions[None, :] < lengths[:, None]).reshape(token_count)
    grad_out = cotangent.astype(jnp.float32).reshape(token_count, wide) * frame_valid[
        :, None
    ].astype(jnp.float32)
    grad_out_low = grad_out.astype(jnp.bfloat16)
    piece_heads = HEADS // seq_count
    piece_wide = wide // seq_count
    piece_ff = hidden_width // seq_count
    group_rows = clip_count * seq_frames

    def pieces():
        norm_copies = jnp.tile(norm_low[None], (1, 1, seq_count))
        moved_attn, moved_cross, moved_ff, moved_norm = (
            lax.all_to_all(
                attn_low.reshape(-1, 6, wide), "seq", split_axis=2, concat_axis=0, tiled=True
            ),
            lax.all_to_all(
                cross_low.reshape(-1, 2, wide), "seq", split_axis=2, concat_axis=0, tiled=True
            ),
            lax.all_to_all(
                ff_low.reshape(-1, 3, hidden_width), "seq", split_axis=2, concat_axis=0, tiled=True
            ),
            lax.all_to_all(norm_copies, "seq", split_axis=2, concat_axis=0, tiled=True),
        )
        attn_cols, cross_cols, ff_cols, norm_blocks = (
            lax.all_gather(moved_attn, "dp", axis=0, tiled=True),
            lax.all_gather(moved_cross, "dp", axis=0, tiled=True),
            lax.all_gather(moved_ff, "dp", axis=0, tiled=True),
            lax.all_gather(moved_norm, "dp", axis=0, tiled=True),
        )
        gains = norm_blocks.transpose(1, 0, 2).reshape(6, wide).astype(jnp.float32)
        return (attn_cols, cross_cols, ff_cols, gains)

    def collect(rows):
        whole = lax.all_gather(
            rows.reshape(clip_count, frame_rows, wide), "seq", axis=1, tiled=True
        )
        return whole.reshape(group_rows, wide)

    def spread(partial_value):
        mine = lax.psum_scatter(
            partial_value.reshape(clip_count, seq_frames, wide).astype(jnp.bfloat16),
            "seq",
            scatter_dimension=1,
            tiled=True,
        ).astype(jnp.float32)
        return mine.reshape(token_count, wide)

    attn_cols, cross_cols, ff_cols, gain_rows = pieces()
    group_shape = (clip_count, seq_frames, piece_heads, HDIM)
    cosine_table, sine_table = rotary_tables(jnp.arange(seq_frames), HDIM)
    normed_one = layer_norm(stream, gain_rows[0], gain_rows[1]).astype(jnp.bfloat16)
    group_one = collect(normed_one)
    projected = jnp.dot(
        group_one,
        attn_cols[:, :3].reshape(wide, 3 * piece_wide),
        preferred_element_type=jnp.float32,
    )
    queries = rotate(
        projected[:, :piece_wide].reshape(group_shape), cosine_table, sine_table
    ).astype(jnp.bfloat16)
    all_keys = rotate(
        projected[:, piece_wide : 2 * piece_wide].reshape(group_shape), cosine_table, sine_table
    ).astype(jnp.bfloat16)
    all_values = projected[:, 2 * piece_wide :].astype(jnp.bfloat16).reshape(group_shape)
    stamp_normed = layer_norm(stamps, gain_rows[0], gain_rows[1]).astype(jnp.bfloat16)
    stamp_pair = jnp.dot(
        stamp_normed,
        attn_cols[:, 1:3].reshape(wide, 2 * piece_wide),
        preferred_element_type=jnp.float32,
    )
    stamp_key = (
        stamp_pair[:, :piece_wide].astype(jnp.bfloat16).reshape(clip_count, piece_heads, HDIM)
    )
    stamp_value = (
        stamp_pair[:, piece_wide:].astype(jnp.bfloat16).reshape(clip_count, piece_heads, HDIM)
    )
    self_mixed, self_lse = self_forward(
        queries, all_keys, all_values, stamp_key, stamp_value, key_keep
    )
    self_low = self_mixed.astype(jnp.bfloat16).reshape(group_rows, piece_wide)
    resid_one = stream + spread(times_transposed(self_low, attn_cols[:, 3]))
    normed_two = layer_norm(resid_one, gain_rows[2], gain_rows[3]).astype(jnp.bfloat16)
    group_two = collect(normed_two)
    cross_query = jnp.dot(group_two, attn_cols[:, 4], preferred_element_type=jnp.float32)
    cross_query = cross_query.astype(jnp.bfloat16).reshape(group_shape)
    cond_pair = jnp.dot(
        cond_flat,
        cross_cols.reshape(cond_width, 2 * piece_wide),
        preferred_element_type=jnp.float32,
    )
    cond_shape = (clip_count, cond_count, piece_heads, HDIM)
    cross_keys = cond_pair[:, :piece_wide].astype(jnp.bfloat16).reshape(cond_shape)
    cross_values = cond_pair[:, piece_wide:].astype(jnp.bfloat16).reshape(cond_shape)
    cross_mixed, cross_lse = cross_forward(cross_query, cross_keys, cross_values, cond_keep)
    cross_low_out = cross_mixed.astype(jnp.bfloat16).reshape(group_rows, piece_wide)
    resid_two = resid_one + spread(times_transposed(cross_low_out, attn_cols[:, 5]))
    normed_three = layer_norm(resid_two, gain_rows[4], gain_rows[5]).astype(jnp.bfloat16)
    group_three = collect(normed_three)
    gate_up = jnp.dot(
        group_three, ff_cols[:, :2].reshape(wide, 2 * piece_ff), preferred_element_type=jnp.float32
    )
    gate_val = gate_up[:, :piece_ff]
    up_val = gate_up[:, piece_ff:]
    hidden = (jax.nn.silu(gate_val) * up_val).astype(jnp.bfloat16)
    branch = spread(times_transposed(hidden, ff_cols[:, 2]))
    layer_out = (resid_two + branch).astype(jnp.bfloat16).reshape(clip_count, frame_rows, wide)
    attn_cols, cross_cols, ff_cols, gain_rows = pieces()
    group_grad_out = collect(grad_out_low)
    grad_hidden = jnp.dot(group_grad_out, ff_cols[:, 2], preferred_element_type=jnp.float32)
    sigmoid_gate = jax.nn.sigmoid(gate_val)
    grad_gate = grad_hidden * up_val * sigmoid_gate * (1.0 + gate_val * (1.0 - sigmoid_gate))
    grad_up = grad_hidden * gate_val * sigmoid_gate
    grad_gate_up = jnp.concatenate([grad_gate, grad_up], axis=1).astype(jnp.bfloat16)
    grad_normed_three = spread(
        times_transposed(grad_gate_up, ff_cols[:, :2].reshape(wide, 2 * piece_ff))
    )
    _, norm_three_back = jax.vjp(layer_norm, resid_two, gain_rows[4], gain_rows[5])
    grad_two_part, grad_gain_three, grad_bias_three = norm_three_back(grad_normed_three)
    grad_two = grad_out + grad_two_part
    grad_cross_branch = grad_two.astype(jnp.bfloat16)
    group_cross_branch = collect(grad_cross_branch)
    grad_cross_mixed = jnp.dot(
        group_cross_branch, attn_cols[:, 5], preferred_element_type=jnp.float32
    )
    grad_cross_mixed = grad_cross_mixed.astype(jnp.bfloat16).reshape(group_shape)
    grad_cross_query, grad_cross_keys, grad_cross_values = cross_backward(
        cross_query, cross_keys, cross_values, cond_keep, cross_lse, grad_cross_mixed
    )
    grad_cross_query = grad_cross_query.astype(jnp.bfloat16).reshape(group_rows, piece_wide)
    grad_normed_two = spread(times_transposed(grad_cross_query, attn_cols[:, 4]))
    _, norm_two_back = jax.vjp(layer_norm, resid_one, gain_rows[2], gain_rows[3])
    grad_one_part, grad_gain_two, grad_bias_two = norm_two_back(grad_normed_two)
    grad_one = grad_two + grad_one_part
    grad_self_branch = grad_one.astype(jnp.bfloat16)
    group_self_branch = collect(grad_self_branch)
    grad_self_mixed = jnp.dot(
        group_self_branch, attn_cols[:, 3], preferred_element_type=jnp.float32
    )
    grad_self_mixed = grad_self_mixed.astype(jnp.bfloat16).reshape(group_shape)
    grad_queries, key_part, value_part, grad_stamp_key, grad_stamp_value = self_backward(
        queries, all_keys, all_values, stamp_key, stamp_value, key_keep, self_lse, grad_self_mixed
    )
    grad_query_raw = (
        rotate(grad_queries, cosine_table, -sine_table)
        .astype(jnp.bfloat16)
        .reshape(group_rows, piece_wide)
    )
    grad_key_raw = (
        rotate(key_part, cosine_table, -sine_table)
        .astype(jnp.bfloat16)
        .reshape(group_rows, piece_wide)
    )
    grad_value = value_part.astype(jnp.bfloat16).reshape(group_rows, piece_wide)
    grad_project = jnp.concatenate([grad_query_raw, grad_key_raw, grad_value], axis=1)
    grad_normed_one = spread(
        times_transposed(grad_project, attn_cols[:, :3].reshape(wide, 3 * piece_wide))
    )
    stamp_grad = jnp.concatenate(
        [
            grad_stamp_key.reshape(clip_count, piece_wide),
            grad_stamp_value.reshape(clip_count, piece_wide),
        ],
        axis=1,
    )
    grad_stamp_normed = split_times_transposed(
        stamp_grad, attn_cols[:, 1:3].reshape(wide, 2 * piece_wide)
    )
    _, norm_one_back = jax.vjp(layer_norm, stream, gain_rows[0], gain_rows[1])
    grad_zero_part, grad_gain_one, grad_bias_one = norm_one_back(grad_normed_one)
    _, norm_stamp_back = jax.vjp(layer_norm, stamps, gain_rows[0], gain_rows[1])
    _, grad_gain_stamp, grad_bias_stamp = norm_stamp_back(grad_stamp_normed)
    frames_grad = (grad_one + grad_zero_part).reshape(clip_count, frame_rows, wide)
    project_grad = outer_sum(group_one, grad_project)
    stamp_weight_grad = split_outer(stamp_normed, stamp_grad)
    attn_piece = jnp.stack(
        [
            project_grad[:, :piece_wide],
            project_grad[:, piece_wide : 2 * piece_wide] + stamp_weight_grad[:, :piece_wide],
            project_grad[:, 2 * piece_wide :] + stamp_weight_grad[:, piece_wide:],
            outer_sum(group_self_branch, self_low),
            outer_sum(group_two, grad_cross_query),
            outer_sum(group_cross_branch, cross_low_out),
        ],
        axis=1,
    )
    cond_grad = jnp.concatenate(
        [
            grad_cross_keys.reshape(clip_count * cond_count, piece_wide),
            grad_cross_values.reshape(clip_count * cond_count, piece_wide),
        ],
        axis=1,
    )
    cross_piece = split_outer(cond_flat, cond_grad).reshape(cond_width, 2, piece_wide)
    ff_piece = jnp.stack(
        [
            outer_sum(group_three, grad_gate_up[:, :piece_ff]),
            outer_sum(group_three, grad_gate_up[:, piece_ff:]),
            outer_sum(group_grad_out, hidden),
        ],
        axis=1,
    )
    norm_grad = jnp.stack(
        [
            grad_gain_one + grad_gain_stamp,
            grad_bias_one + grad_bias_stamp,
            grad_gain_two,
            grad_bias_two,
            grad_gain_three,
            grad_bias_three,
        ],
        axis=0,
    )
    norm_column = norm_grad.T[:, :, None]
    summed_attn, summed_cross, summed_ff, summed_norm = (
        lax.psum_scatter(
            attn_piece.astype(jnp.bfloat16), "dp", scatter_dimension=0, tiled=True
        ).astype(jnp.float32),
        lax.psum_scatter(
            cross_piece.astype(jnp.bfloat16), "dp", scatter_dimension=0, tiled=True
        ).astype(jnp.float32),
        lax.psum_scatter(
            ff_piece.astype(jnp.bfloat16), "dp", scatter_dimension=0, tiled=True
        ).astype(jnp.float32),
        lax.psum_scatter(
            norm_column.astype(jnp.bfloat16), "dp", scatter_dimension=0, tiled=True
        ).astype(jnp.float32),
    )
    owned_attn, owned_cross, owned_ff, owned_norm = (
        lax.all_to_all(
            summed_attn.astype(jnp.bfloat16), "seq", split_axis=0, concat_axis=2, tiled=True
        ).astype(summed_attn.dtype),
        lax.all_to_all(
            summed_cross.astype(jnp.bfloat16), "seq", split_axis=0, concat_axis=2, tiled=True
        ).astype(summed_cross.dtype),
        lax.all_to_all(
            summed_ff.astype(jnp.bfloat16), "seq", split_axis=0, concat_axis=2, tiled=True
        ).astype(summed_ff.dtype),
        lax.all_to_all(
            summed_norm.astype(jnp.bfloat16), "seq", split_axis=0, concat_axis=2, tiled=True
        ).astype(summed_norm.dtype),
    )
    attn_reduced = owned_attn.reshape(owned_attn.shape[0], 6 * wide)
    cross_reduced = owned_cross.reshape(owned_cross.shape[0], 2 * wide)
    ff_reduced = owned_ff.reshape(owned_ff.shape[0], 3 * hidden_width)
    norm_reduced = jnp.sum(owned_norm, axis=2).T
    local_squares = (
        jnp.sum(attn_reduced * attn_reduced)
        + jnp.sum(cross_reduced * cross_reduced)
        + jnp.sum(norm_reduced * norm_reduced)
        + jnp.sum(ff_reduced * ff_reduced)
    )
    total_squares = lax.psum(local_squares, ("dp", "seq"))
    grad_norm = jnp.sqrt(total_squares)
    factor = jnp.minimum(1.0, clip_limit / grad_norm)
    attn_new, attn_first_new, attn_second_new = adam_step(
        attn_weight, attn_first, attn_second, attn_reduced * factor, matrix_rate, matrix_decay
    )
    cross_new, cross_first_new, cross_second_new = adam_step(
        cross_weight, cross_first, cross_second, cross_reduced * factor, matrix_rate, matrix_decay
    )
    norm_new, norm_first_new, norm_second_new = adam_step(
        norm_param, norm_first, norm_second, norm_reduced * factor, gain_rate, 0.0
    )
    ff_new, ff_first_new, ff_second_new = adam_step(
        ff_weight, ff_first, ff_second, ff_reduced * factor, matrix_rate, matrix_decay
    )
    return (
        layer_out,
        frames_grad,
        grad_norm,
        attn_new,
        cross_new,
        norm_new,
        ff_new,
        attn_first_new,
        cross_first_new,
        norm_first_new,
        ff_first_new,
        attn_second_new,
        cross_second_new,
        norm_second_new,
        ff_second_new,
    )


MESH = pl.DeviceIdType.MESH
DMA = pltpu.SemaphoreType.DMA
VMEM_LIMIT = 60 * 2**20


def plane_fits(mesh):
    return mesh.shape["dp"] == 8 and mesh.shape["dp"] % mesh.shape["seq"] == 0


def plane_places():
    place = lax.axis_index("dp")
    return (place, lax.axis_index("seq"), lambda mask: jnp.bitwise_xor(place, mask))


def greet(partners):
    barrier = pltpu.get_barrier_semaphore()
    for partner in partners:
        pl.semaphore_signal(barrier, inc=1, device_id=partner, device_id_type=MESH)
    pl.semaphore_wait(barrier, len(partners))


def remote(source, goal, send_sem, recv_sem, device):
    return pltpu.make_async_remote_copy(
        src_ref=source,
        dst_ref=goal,
        send_sem=send_sem,
        recv_sem=recv_sem,
        device_id=device,
        device_id_type=MESH,
    )


def communicating(collective_id):
    return pltpu.CompilerParams(
        has_side_effects=True, collective_id=collective_id, vmem_limit_bytes=VMEM_LIMIT
    )


def any_spec():
    return pl.BlockSpec(memory_space=pl.ANY)


def gather_body(clips, rows, sub, beside, own_ref, *refs):
    if beside:
        pick_ref, all_ref, cond_ref, send_sem, recv_sem, local_sem, *extra = refs
        greet_cross(*beside)
        cond = cond_steps(*beside, pick_ref, cond_ref, *extra)
        next(cond)
    else:
        all_ref, send_sem, recv_sem, local_sem = refs
    place, depth, flip = plane_places()
    core, beside_x, beside_y, across = flip(1), flip(2), flip(4), flip(6)
    if not beside:
        greet([(core, depth), (beside_x, depth), (beside_y, depth)])
    chunks = [(clip, part) for clip in range(clips) for part in range(rows // sub)]
    count = len(chunks)
    half = count // 2
    sends = []

    def view(slot, index):
        clip, part = chunks[index]
        return all_ref.at[clip, slot, pl.ds(part * sub, sub)]

    def own(index):
        clip, part = chunks[index]
        return own_ref.at[clip, pl.ds(part * sub, sub)]

    def send(source, slot, index, device):
        copy = remote(
            source,
            view(slot, index),
            send_sem.at[len(sends)],
            recv_sem.at[slot, index],
            (device, depth),
        )
        copy.start()
        sends.append(copy)

    def arrived(slot, index):
        block = view(slot, index)
        remote(
            block, block, send_sem.at[0], recv_sem.at[slot, index], (core, depth)
        ).wait_recv()

    x_order = list(range(count))
    y_order = list(range(half, count)) + list(range(half))
    for step in range(count):
        send(own(x_order[step]), place, x_order[step], beside_x)
        send(own(y_order[step]), place, y_order[step], beside_y)
    stays = []
    for clip in range(clips):
        copy = pltpu.make_async_copy(
            own_ref.at[clip], all_ref.at[clip, place], local_sem.at[clip]
        )
        copy.start()
        stays.append(copy)
    for index in range(count):
        send(own(index), place, index, core)
    if beside:
        next(cond)
    for step in range(count):
        x_index, y_index = x_order[step], y_order[step]
        arrived(beside_x, x_index)
        if x_index < half:
            send(view(beside_x, x_index), beside_x, x_index, beside_y)
        send(view(beside_x, x_index), beside_x, x_index, core)
        arrived(beside_y, y_index)
        if y_index >= half:
            send(view(beside_y, y_index), beside_y, y_index, beside_x)
        send(view(beside_y, y_index), beside_y, y_index, core)
    for step in range(half):
        for index in (x_order[step], y_order[step]):
            arrived(across, index)
            send(view(across, index), across, index, core)
    for slot in (core, flip(3), flip(5), flip(7)):
        for index in range(count):
            arrived(slot, index)
    if beside:
        next(cond)
    for copy in stays:
        copy.wait()
    for copy in sends:
        copy.wait_send()


def plane_gather(own_rows, collective_id, picked=None, sub=64):
    clips, rows, wide = own_rows.shape
    count = clips * (rows // sub)
    whole = jax.ShapeDtypeStruct((clips, 8, rows, wide), own_rows.dtype)
    scratch = [DMA((7 * count,)), DMA((8, count)), DMA((clips,))]
    if picked is None:
        return pl.pallas_call(
            functools.partial(gather_body, clips, rows, sub, None),
            out_shape=whole,
            in_specs=[any_spec()],
            out_specs=any_spec(),
            scratch_shapes=scratch,
            compiler_params=communicating(collective_id),
        )(own_rows)
    planes, per, tokens, cond_wide = picked.shape
    group = planes * per
    inside = pl.BlockSpec(memory_space=pltpu.VMEM)
    return pl.pallas_call(
        functools.partial(gather_body, clips, rows, sub, (group, planes)),
        out_shape=[
            whole,
            jax.ShapeDtypeStruct((group, per, tokens, cond_wide), picked.dtype),
        ],
        in_specs=[any_spec(), inside],
        out_specs=[any_spec(), inside],
        scratch_shapes=scratch
        + [
            pltpu.VMEM(picked.shape, picked.dtype),
            pltpu.VMEM(picked.shape[1:], picked.dtype),
            DMA((planes,)),
            DMA((planes,)),
            DMA((group,)),
            DMA((group,)),
        ],
        compiler_params=communicating(collective_id),
    )(own_rows, picked)


def reduce_body(
    clips, rows, sub, beside, part_ref, *refs
):
    if beside:
        kept_ref, sum_ref, own_ref, mid, *refs = refs
    else:
        sum_ref, *refs = refs
    pair, held, turn, from_x, from_y, send_sem, core_sem, turn_sem, x_sem, y_sem, *sems = refs
    place, depth, flip = plane_places()
    core, beside_x, beside_y = flip(1), flip(2), flip(4)
    if beside:
        greet_cross(*beside)
        going = outward_steps(*beside, kept_ref, own_ref, mid, *sems)
        next(going)
    else:
        greet([(core, depth), (beside_x, depth), (beside_y, depth)])
    chunks = [(clip, part) for clip in range(clips) for part in range(rows // sub)]
    count = len(chunks)
    half = count // 2
    sends = []

    def send(source, goal, recv_sem, device):
        copy = remote(source, goal, send_sem.at[len(sends)], recv_sem, (device, depth))
        copy.start()
        sends.append(copy)

    def arrived(block, recv_sem):
        remote(block, block, send_sem.at[0], recv_sem, (core, depth)).wait_recv()

    def term(slot, index):
        clip, part = chunks[index]
        return part_ref.at[clip, slot, pl.ds(part * sub, sub)]

    for chip in (3, 1, 2, 0):
        for index in range(count):
            send(
                term(flip((2 * chip) ^ 1), index),
                pair.at[index, chip],
                core_sem.at[index, chip],
                core,
            )

    def total(*blocks):
        return sum(block[...].astype(jnp.float32) for block in blocks)

    def combine(chip, index):
        arrived(pair.at[index, chip], core_sem.at[index, chip])
        held[index, chip] = total(term(flip(2 * chip), index), pair.at[index, chip]).astype(
            held.dtype
        )

    for low in range(half):
        high = half + low
        combine(3, low)
        send(held.at[low, 3], turn.at[low], turn_sem.at[low], beside_x)
        combine(3, high)
        send(held.at[high, 3], turn.at[high], turn_sem.at[high], beside_y)
    for low in range(half):
        high = half + low
        combine(1, low)
        send(held.at[low, 1], from_x.at[low], x_sem.at[low], beside_x)
        combine(2, high)
        send(held.at[high, 2], from_y.at[high], y_sem.at[high], beside_y)
    if beside:
        next(going)
    for low in range(half):
        high = half + low
        combine(2, low)
        arrived(turn.at[low], turn_sem.at[low])
        held[low, 2] = total(held.at[low, 2], turn.at[low]).astype(held.dtype)
        send(held.at[low, 2], from_y.at[low], y_sem.at[low], beside_y)
        combine(1, high)
        arrived(turn.at[high], turn_sem.at[high])
        held[high, 1] = total(held.at[high, 1], turn.at[high]).astype(held.dtype)
        send(held.at[high, 1], from_x.at[high], x_sem.at[high], beside_x)
    for index in range(count):
        clip, part = chunks[index]
        arrived(pair.at[index, 0], core_sem.at[index, 0])
        arrived(from_x.at[index], x_sem.at[index])
        arrived(from_y.at[index], y_sem.at[index])
        sum_ref[clip, pl.ds(part * sub, sub)] = total(
            term(place, index), pair.at[index, 0], from_x.at[index], from_y.at[index]
        )
    if beside:
        next(going)
    for copy in sends:
        copy.wait_send()


def plane_reduce(terms, collective_id, kept_rows=None, sub=64):
    clips, _, rows, wide = terms.shape
    count = clips * (rows // sub)
    kind = terms.dtype
    sums = jax.ShapeDtypeStruct((clips, rows, wide), jnp.float32)
    whole = pl.BlockSpec(memory_space=pltpu.VMEM)
    scratch = [
        pltpu.VMEM((count, 4, sub, wide), kind),
        pltpu.VMEM((count, 4, sub, wide), kind),
        pltpu.VMEM((count, sub, wide), kind),
        pltpu.VMEM((count, sub, wide), kind),
        pltpu.VMEM((count, sub, wide), kind),
        DMA((7 * count,)),
        DMA((count, 4)),
        DMA((count,)),
        DMA((count,)),
        DMA((count,)),
    ]
    if kept_rows is None:
        return pl.pallas_call(
            functools.partial(reduce_body, clips, rows, sub, None),
            out_shape=sums,
            in_specs=[whole],
            out_specs=whole,
            scratch_shapes=scratch,
            compiler_params=communicating(collective_id),
        )(terms)
    per, planes, piece, _ = kept_rows.shape
    group = per * planes
    moved = jax.ShapeDtypeStruct((group, piece, wide), kept_rows.dtype)
    total, own, _ = pl.pallas_call(
        functools.partial(reduce_body, clips, rows, sub, (group, planes)),
        out_shape=[sums, moved, moved],
        in_specs=[whole, any_spec()],
        out_specs=[whole, any_spec(), any_spec()],
        scratch_shapes=scratch + outward_scratch(group, planes),
        compiler_params=communicating(collective_id),
    )(terms, kept_rows)
    return total, own


def greet_cross(group, planes):
    place, depth, flip = plane_places()
    greet(
        [(flip(mask), depth) for mask in range(1, group)]
        + [(place, lax.rem(depth + step, planes)) for step in range(1, planes)]
    )


def outward_steps(group, planes, kept_ref, own_ref, mid, *sems):
    far_send, far_recv, near_send, near_recv, local_sem = sems
    place, depth, flip = plane_places()
    per = group // planes
    first = []
    for step in range(1, planes):
        origin = lax.rem(depth + step, planes)
        for slot in range(per):
            clip = per * depth + slot
            copy = remote(
                kept_ref.at[slot, origin],
                mid.at[clip],
                far_send.at[slot, step],
                far_recv.at[clip],
                (place, origin),
            )
            copy.start()
            first.append(copy)
    second = []

    def hand_over(block, clip):
        index = len(second)
        away = remote(
            block, own_ref.at[place], near_send.at[index], near_recv.at[place], (clip, depth)
        )
        stay = pltpu.make_async_copy(block, own_ref.at[place], local_sem.at[index])
        pl.when(clip != place)(away.start)
        pl.when(clip == place)(stay.start)
        second.append((clip, away, stay))

    for slot in range(per):
        hand_over(kept_ref.at[slot, depth], per * depth + slot)
    yield
    for step in range(1, planes):
        source = lax.rem(depth + step, planes)
        for slot in range(per):
            clip = per * source + slot
            block = mid.at[clip]
            remote(
                block, block, far_send.at[0, 0], far_recv.at[clip], (place, source)
            ).wait_recv()
            hand_over(block, clip)
    yield
    for mask in range(1, group):
        other = flip(mask)
        block = own_ref.at[other]
        remote(block, block, near_send.at[0], near_recv.at[other], (other, depth)).wait_recv()
    for clip, away, stay in second:
        pl.when(clip != place)(away.wait_send)
        pl.when(clip == place)(stay.wait)
    for copy in first:
        copy.wait_send()
    yield


def outward_scratch(group, planes):
    return [
        DMA((group // planes, planes)),
        DMA((group,)),
        DMA((group,)),
        DMA((group,)),
        DMA((group,)),
    ]


def swap_steps(own_ref, kept_ref, send_sem, recv_sem, local_sem):
    place, depth, flip = plane_places()
    copies = []
    for mask in (6, 7, 2, 3, 4, 5, 1):
        other = flip(mask)
        copy = remote(
            own_ref.at[other],
            kept_ref.at[place],
            send_sem.at[mask],
            recv_sem.at[mask],
            (other, depth),
        )
        copy.start()
        copies.append(copy)
    stay = pltpu.make_async_copy(own_ref.at[place], kept_ref.at[place], local_sem)
    stay.start()
    yield
    stay.wait()
    for copy in copies:
        copy.wait()
    yield


def swap_scratch():
    return [DMA((8,)), DMA((8,)), DMA(())]


def leave_body(
    group, planes, kept_ref, cut_ref, parts_ref, own_ref, mine_ref, norm_ref, mid, terms, *sems
):
    part_send, part_recv = sems[:2]
    place, depth, flip = plane_places()
    devices = [(flip(mask), lax.rem(depth + step, planes)) for mask, step in everyone(planes)]
    greet(devices)
    here = place * planes + depth
    rows = outward_steps(group, planes, kept_ref, own_ref, mid, *sems[2:7])
    next(rows)
    copies = []
    for index, (other, plane) in enumerate(devices):
        copy = remote(
            parts_ref.at[other * planes + plane],
            terms.at[here],
            part_send.at[index],
            part_recv.at[here],
            (other, plane),
        )
        copy.start()
        copies.append(copy)
    terms[here] = parts_ref[here]
    columns = swap_steps(cut_ref, mine_ref, *sems[7:])
    next(columns)
    next(rows)
    for other, plane in devices:
        source = other * planes + plane
        one = terms.at[source]
        remote(one, one, part_send.at[0], part_recv.at[source], (other, plane)).wait_recv()
    norm_ref[...] = jnp.sum(terms[...], axis=0)
    next(columns)
    next(rows)
    for copy in copies:
        copy.wait_send()


def leave(kept_rows, cut, norm_parts, collective_id):
    per, planes, rows, wide = kept_rows.shape
    group = per * planes
    count = group * planes
    whole = pl.BlockSpec(memory_space=pltpu.VMEM)
    like = lambda shape, array: jax.ShapeDtypeStruct(shape, array.dtype)
    own, mine, norm_sum, _ = pl.pallas_call(
        functools.partial(leave_body, group, planes),
        out_shape=[
            like((group, rows, wide), kept_rows),
            like(cut.shape, cut),
            like(norm_parts.shape[1:], norm_parts),
            like((group, rows, wide), kept_rows),
        ],
        in_specs=[any_spec(), any_spec(), whole],
        out_specs=[any_spec(), any_spec(), whole, any_spec()],
        scratch_shapes=[pltpu.VMEM(norm_parts.shape, jnp.float32), DMA((count,)), DMA((count,))]
        + outward_scratch(group, planes)
        + swap_scratch(),
        compiler_params=communicating(collective_id),
    )(kept_rows, cut, norm_parts)
    return own, mine, norm_sum


def everyone(planes):
    return [(mask, step) for mask in range(8) for step in range(planes) if mask or step]


def enter_body(
    group,
    planes,
    own_ref,
    norm_ref,
    pack_ref,
    cut_ref,
    kept_ref,
    norms_ref,
    packs_ref,
    mine_ref,
    mid,
    *sems,
):
    (
        near_send,
        near_recv,
        far_send,
        far_recv,
        local_sem,
        norm_send,
        norm_recv,
        pack_send,
        pack_recv,
        cut_send,
        cut_recv,
        stay_sem,
    ) = sems
    place, depth, flip = plane_places()
    per = group // planes
    others = everyone(planes)
    greet([(flip(mask), lax.rem(depth + step, planes)) for mask, step in others])
    here = place * planes + depth
    first = []
    for mask in (6, 7, 2, 3, 4, 5, 1):
        other = flip(mask)
        copy = remote(
            own_ref.at[other],
            mid.at[place],
            near_send.at[mask],
            near_recv.at[mask],
            (other, depth),
        )
        copy.start()
        first.append((mask, copy))
    small = []
    for index, (mask, step) in enumerate(others):
        copy = remote(
            norm_ref,
            norms_ref.at[here],
            norm_send.at[index],
            norm_recv.at[here],
            (flip(mask), lax.rem(depth + step, planes)),
        )
        copy.start()
        small.append(copy)
    for mask in range(1, group):
        copy = remote(
            pack_ref,
            packs_ref.at[place],
            pack_send.at[mask],
            pack_recv.at[mask],
            (flip(mask), depth),
        )
        copy.start()
        small.append(copy)
    stays = [
        pltpu.make_async_copy(norm_ref, norms_ref.at[here], stay_sem.at[0]),
        pltpu.make_async_copy(pack_ref, packs_ref.at[place], stay_sem.at[1]),
        pltpu.make_async_copy(cut_ref.at[place], mine_ref.at[place], stay_sem.at[2]),
    ]
    for stay in stays:
        stay.start()
    cuts = []
    for mask in (6, 7, 2, 3, 4, 5, 1):
        other = flip(mask)
        copy = remote(
            cut_ref.at[other],
            mine_ref.at[place],
            cut_send.at[mask],
            cut_recv.at[mask],
            (other, depth),
        )
        copy.start()
        cuts.append(copy)
    second = []
    arrivals = dict(first)
    for mask in (0, 1, 2, 3, 4, 5, 6, 7):
        source = flip(mask)
        goal, slot = lax.div(source, per), lax.rem(source, per)
        block = own_ref.at[place]
        if mask:
            arrivals[mask].wait_recv()
            block = mid.at[source]
        away = remote(
            block,
            kept_ref.at[slot, depth],
            far_send.at[mask],
            far_recv.at[slot, depth],
            (place, goal),
        )
        stay = pltpu.make_async_copy(block, kept_ref.at[slot, depth], local_sem.at[mask])
        pl.when(goal != depth)(away.start)
        pl.when(goal == depth)(stay.start)
        second.append((goal, away, stay))
    for slot in range(per):
        for origin in range(planes):
            block = kept_ref.at[slot, origin]
            pl.when(origin != depth)(
                remote(
                    block,
                    block,
                    far_send.at[0],
                    far_recv.at[slot, origin],
                    (place, lax.rem(depth + 1, planes)),
                ).wait_recv
            )
    for mask, step in others:
        source = flip(mask) * planes + lax.rem(depth + step, planes)
        block = norms_ref.at[source]
        remote(
            block,
            block,
            norm_send.at[0],
            norm_recv.at[source],
            (flip(mask), lax.rem(depth + step, planes)),
        ).wait_recv()
    for copy in small:
        copy.wait_send()
    for mask in range(1, group):
        block = packs_ref.at[flip(mask)]
        remote(
            block, block, pack_send.at[0], pack_recv.at[mask], (flip(mask), depth)
        ).wait_recv()
    for copy in cuts:
        copy.wait()
    for goal, away, stay in second:
        pl.when(goal != depth)(away.wait_send)
        pl.when(goal == depth)(stay.wait)
    for mask, copy in first:
        copy.wait_send()
    for stay in stays:
        stay.wait()


def enter(rows_of_clip, norm_block, pack, cut, planes, collective_id):
    group, rows, wide = rows_of_clip.shape
    count = group * planes
    like = lambda shape, array: jax.ShapeDtypeStruct(shape, array.dtype)
    kept, norms, packs, mine, _ = pl.pallas_call(
        functools.partial(enter_body, group, planes),
        out_shape=[
            like((group // planes, planes, rows, wide), rows_of_clip),
            like((count,) + norm_block.shape, norm_block),
            like((group,) + pack.shape, pack),
            like(cut.shape, cut),
            like((group, rows, wide), rows_of_clip),
        ],
        in_specs=[any_spec()] * 4,
        out_specs=[any_spec()] * 5,
        scratch_shapes=[
            DMA((group,)),
            DMA((group,)),
            DMA((group,)),
            DMA((group // planes, planes)),
            DMA((group,)),
            DMA((count,)),
            DMA((count,)),
            DMA((group,)),
            DMA((group,)),
            DMA((group,)),
            DMA((group,)),
            DMA((3,)),
        ],
        compiler_params=communicating(collective_id),
    )(rows_of_clip, norm_block, pack, cut)
    return kept, norms, packs, mine


def cond_steps(group, planes, pick_ref, cond_ref, parts, summed, *sems):
    part_send, part_recv, cond_send, cond_recv = sems
    place, depth, flip = plane_places()
    pushes = []
    for step in range(1, planes):
        goal = lax.rem(depth + step, planes)
        copy = remote(
            pick_ref.at[goal],
            parts.at[depth],
            part_send.at[step],
            part_recv.at[depth],
            (place, goal),
        )
        copy.start()
        pushes.append(copy)
    yield
    total = pick_ref[depth].astype(jnp.float32)
    for step in range(1, planes):
        source = lax.rem(depth + step, planes)
        block = parts.at[source]
        remote(
            block, block, part_send.at[0], part_recv.at[source], (place, source)
        ).wait_recv()
        total = total + parts[source].astype(jnp.float32)
    summed[...] = total.astype(summed.dtype)
    cond_ref[place] = total.astype(summed.dtype)
    for mask in range(1, group):
        copy = remote(
            summed,
            cond_ref.at[place],
            cond_send.at[mask],
            cond_recv.at[mask],
            (flip(mask), depth),
        )
        copy.start()
        pushes.append(copy)
    yield
    for mask in range(1, group):
        block = cond_ref.at[flip(mask)]
        remote(
            block, block, cond_send.at[0], cond_recv.at[mask], (flip(mask), depth)
        ).wait_recv()
    for copy in pushes:
        copy.wait_send()
    yield


def inward_beside(group, planes, own_ref, kept_ref, mid, *sems):
    near_send, near_recv, far_send, far_recv, local_sem = sems
    place, depth, flip = plane_places()
    per = group // planes

    def near(mask):
        other = flip(mask)
        return remote(
            own_ref.at[other],
            mid.at[place],
            near_send.at[mask],
            near_recv.at[mask],
            (other, depth),
        )

    def begin():
        for mask in range(1, group):
            near(mask).start()

    def second(mask):
        source = flip(mask)
        goal, slot = lax.div(source, per), lax.rem(source, per)
        block = mid.at[source] if mask else own_ref.at[place]
        away = remote(
            block,
            kept_ref.at[slot, depth],
            far_send.at[mask],
            far_recv.at[slot, depth],
            (place, goal),
        )
        stay = pltpu.make_async_copy(block, kept_ref.at[slot, depth], local_sem.at[mask])
        return goal != depth, away, stay

    def middle():
        for mask in range(group):
            if mask:
                near(mask).wait_recv()
            leaves, away, stay = second(mask)
            pl.when(leaves)(away.start)
            pl.when(jnp.logical_not(leaves))(stay.start)

    def end():
        for slot in range(per):
            for origin in range(planes):
                block = kept_ref.at[slot, origin]
                pl.when(origin != depth)(
                    remote(
                        block,
                        block,
                        far_send.at[0],
                        far_recv.at[slot, origin],
                        (place, lax.rem(depth + 1, planes)),
                    ).wait_recv
                )
        for mask in range(group):
            leaves, away, stay = second(mask)
            pl.when(leaves)(away.wait_send)
            pl.when(jnp.logical_not(leaves))(stay.wait)
            if mask:
                near(mask).wait_send()

    return begin, middle, end


def inward_scratch(group, planes):
    return [
        DMA((group,)),
        DMA((group,)),
        DMA((group,)),
        DMA((group // planes, planes)),
        DMA((group,)),
    ]


def finish_body(planes, squares_ref, total_ref, blocks, block_send, block_recv):
    place, depth, flip = plane_places()
    devices = [(flip(mask), lax.rem(depth + step, planes)) for mask, step in everyone(planes)]
    greet(devices)
    here = place * planes + depth
    copies = []
    blocks[here] = squares_ref[...]
    for index, (other, plane) in enumerate(devices):
        copy = remote(
            squares_ref,
            blocks.at[here],
            block_send.at[index],
            block_recv.at[here],
            (other, plane),
        )
        copy.start()
        copies.append(copy)
    for other, plane in devices:
        source = other * planes + plane
        one = blocks.at[source]
        remote(one, one, block_send.at[0], block_recv.at[source], (other, plane)).wait_recv()
    total_ref[...] = jnp.sum(blocks[...], axis=0)
    for copy in copies:
        copy.wait_send()


def finish(squares, planes, collective_id):
    count = 8 * planes
    whole = pl.BlockSpec(memory_space=pltpu.VMEM)
    return pl.pallas_call(
        functools.partial(finish_body, planes),
        out_shape=jax.ShapeDtypeStruct(squares.shape, jnp.float32),
        in_specs=[whole],
        out_specs=whole,
        scratch_shapes=[
            pltpu.VMEM((count,) + squares.shape, jnp.float32),
            DMA((count,)),
            DMA((count,)),
        ],
        compiler_params=communicating(collective_id),
    )(squares)


def rotary_lanes(places):
    cosine, sine = rotary_tables(places, HDIM)
    cosine, sine = cosine[:, 0], sine[:, 0]
    return jnp.stack(
        [
            jnp.concatenate([cosine] * 4, axis=1),
            jnp.concatenate([-sine, sine, -sine, sine], axis=1),
        ]
    )


def turn_heads(values, cosine, sine):
    lane = lax.broadcasted_iota(jnp.int32, values.shape, 1)
    half = HDIM // 2
    ahead = pltpu.roll(values, 2 * HDIM - half, 1)
    behind = pltpu.roll(values, half, 1)
    other = jnp.where(lax.rem(lane, HDIM) < half, ahead, behind)
    return values * cosine + other * sine


def swap_beside(cut_ref, mine_ref, *sems):
    place, depth, flip = plane_places()

    def each(act):
        for mask in (6, 7, 2, 3, 4, 5, 1):
            other = flip(mask)
            act(
                remote(
                    cut_ref.at[other],
                    mine_ref.at[place],
                    sems[0].at[mask],
                    sems[1].at[mask],
                    (other, depth),
                )
            )

    stay = pltpu.make_async_copy(cut_ref.at[place], mine_ref.at[place], sems[2])

    def begin():
        each(lambda copy: copy.start())
        stay.start()

    def end():
        each(lambda copy: copy.wait())
        stay.wait()

    return begin, end


def flash_forward_body(
    heads,
    tile,
    raw_ref,
    stamp_ref,
    bias_ref,
    rotary_ref,
    cut_ref,
    own_ref,
    turned_ref,
    out_ref,
    lse_ref,
    mine_ref,
    kept_ref,
    mid,
    *sems,
):
    group, planes = cut_ref.shape[0], kept_ref.shape[1]
    step, last = pl.program_id(0), pl.num_programs(0) - 1
    start_swap, end_swap = swap_beside(cut_ref, mine_ref, *sems[:3])
    start_rows, pass_rows, end_rows = inward_beside(
        group, planes, own_ref, kept_ref, mid, *sems[3:]
    )

    @pl.when(step == 0)
    def _():
        greet_cross(group, planes)
        start_rows()
        start_swap()

    @pl.when(step == last)
    def _():
        pass_rows()

    wide = heads * HDIM
    for pair in range(2 * wide // 128):
        lanes = slice(pair * 128, pair * 128 + 128)
        turned_ref[:, lanes] = turn_heads(
            raw_ref[:, lanes], rotary_ref[0], rotary_ref[1]
        ).astype(turned_ref.dtype)
    turned_ref[:, 2 * wide :] = raw_ref[:, 2 * wide :].astype(turned_ref.dtype)
    rows = raw_ref.shape[0]
    bias = bias_ref[0]
    scale = HDIM**-0.5
    for head in range(heads):
        lanes = slice(head * HDIM, head * HDIM + HDIM)
        keys = turned_ref[:, wide + head * HDIM : wide + head * HDIM + HDIM]
        values = turned_ref[:, 2 * wide + head * HDIM : 2 * wide + head * HDIM + HDIM]
        stamp_key = stamp_ref[0, :, lanes].astype(jnp.float32)
        stamp_value = stamp_ref[
            0, :, wide + head * HDIM : wide + head * HDIM + HDIM
        ].astype(jnp.float32)

        def one(step, carry):
            place = pl.ds(pl.multiple_of(step * tile, tile), tile)
            query = turned_ref[place, lanes] * jnp.asarray(scale, turned_ref.dtype)
            scores = times_transposed(query, keys) + bias
            stamp_score = jnp.sum(query.astype(jnp.float32) * stamp_key, axis=1, keepdims=True)
            top = jnp.maximum(jnp.max(scores, axis=1, keepdims=True), stamp_score)
            expo = jnp.exp(scores - top)
            stamp_expo = jnp.exp(stamp_score - top)
            denom = jnp.sum(expo, axis=1, keepdims=True) + stamp_expo
            share = 1.0 / denom
            prob = (expo * share).astype(values.dtype)
            stamp_prob = (stamp_expo * share).astype(values.dtype).astype(jnp.float32)
            mixed = jnp.dot(prob, values, preferred_element_type=jnp.float32)
            out_ref[place, lanes] = (mixed + stamp_prob * stamp_value).astype(out_ref.dtype)
            lse_ref[place, head : head + 1] = top + jnp.log(denom)
            return carry

        lax.fori_loop(0, rows // tile, one, 0)

    @pl.when(step == last)
    def _():
        end_swap()
        end_rows()


def flash_forward(raw, stamps, bias, rotary, heads, cut, rows_of_clip, collective_id):
    clips, rows = bias.shape
    wide = heads * HDIM
    group, piece, features = rows_of_clip.shape
    planes = group // clips
    like = lambda shape: jax.ShapeDtypeStruct(shape, rows_of_clip.dtype)
    blocked = lambda lanes: pl.BlockSpec((rows, lanes), lambda clip: (clip, 0))
    *results, _ = pl.pallas_call(
        functools.partial(flash_forward_body, heads, rows // 4),
        grid=(clips,),
        out_shape=[
            jax.ShapeDtypeStruct((clips * rows, 3 * wide), jnp.bfloat16),
            jax.ShapeDtypeStruct((clips * rows, wide), jnp.bfloat16),
            jax.ShapeDtypeStruct((clips * rows, 128), jnp.float32),
            like(cut.shape),
            like((clips, planes, piece, features)),
            like(rows_of_clip.shape),
        ],
        in_specs=[
            blocked(3 * wide),
            pl.BlockSpec((1, 1, 2 * wide), lambda clip: (clip, 0, 0)),
            pl.BlockSpec((1, 1, rows), lambda clip: (clip, 0, 0)),
            pl.BlockSpec((2, rows, 128), lambda clip: (0, 0, 0)),
            any_spec(),
            any_spec(),
        ],
        out_specs=[blocked(3 * wide), blocked(wide), blocked(128)] + [any_spec()] * 3,
        scratch_shapes=swap_scratch() + inward_scratch(group, planes),
        compiler_params=communicating(collective_id),
    )(raw, stamps[:, None], bias[:, None], rotary, cut, rows_of_clip)
    return results


def flash_backward_body(
    heads,
    tile,
    turned_ref,
    grad_ref,
    lse_ref,
    stamp_ref,
    bias_ref,
    rotary_ref,
    cut_ref,
    out_ref,
    stamp_out_ref,
    mine_ref,
    query_grad,
    key_grad,
    value_grad,
    *sems,
):
    place, depth, flip = plane_places()
    start_swap, end_swap = swap_beside(cut_ref, mine_ref, *sems)

    @pl.when(pl.program_id(0) == 0)
    def _():
        greet([(flip(mask), depth) for mask in range(1, 8)])
        start_swap()

    wide = heads * HDIM
    rows = turned_ref.shape[0]
    scale = HDIM**-0.5
    low = turned_ref.dtype
    f32 = jnp.float32
    lse_rows = lse_ref[...].T
    first_row = lax.broadcasted_iota(jnp.int32, (8, tile), 0) == 0
    for head in range(heads):
        lanes = slice(head * HDIM, head * HDIM + HDIM)
        later = slice(wide + head * HDIM, wide + head * HDIM + HDIM)
        keys = turned_ref[:, later]
        values = turned_ref[:, 2 * wide + head * HDIM : 2 * wide + head * HDIM + HDIM]
        keys_across = keys.astype(f32).T.astype(low)
        stamp_key = jnp.broadcast_to(stamp_ref[0, :, lanes], (8, HDIM))
        stamp_value = jnp.broadcast_to(stamp_ref[0, :, later], (8, HDIM))
        stamp_column = stamp_ref[0, :, lanes].astype(f32).T
        bias = bias_ref[0]
        key_total = jnp.zeros((rows, HDIM), f32)
        value_total = jnp.zeros((rows, HDIM), f32)
        stamp_key_total = jnp.zeros((8, HDIM), f32)
        stamp_value_total = jnp.zeros((8, HDIM), f32)
        for step in range(rows // tile):
            place = slice(step * tile, step * tile + tile)
            query = turned_ref[place, lanes] * jnp.asarray(scale, low)
            grad = grad_ref[place, lanes]
            lse = lse_rows[head : head + 1, place]
            prob = jnp.exp(times_transposed(keys, query) + bias - lse)
            stamp_prob = jnp.exp(times_transposed(stamp_key, query) - lse)
            grad_prob = times_transposed(values, grad)
            stamp_grad_prob = times_transposed(stamp_value, grad)
            delta = jnp.sum(prob * grad_prob, axis=0, keepdims=True)
            delta = delta + (stamp_prob * stamp_grad_prob)[:1]
            scores = (prob * (grad_prob - delta)).astype(low)
            stamp_scores = (stamp_prob * (stamp_grad_prob - delta)).astype(low)
            stamp_scores = jnp.where(first_row, stamp_scores.astype(f32), 0.0)
            value_total += jnp.dot(prob.astype(low), grad, preferred_element_type=f32)
            key_total += jnp.dot(scores, query, preferred_element_type=f32)
            across = jnp.dot(keys_across, scores, preferred_element_type=f32)
            across = across + stamp_column * stamp_scores[:1]
            query_grad[place, lanes] = across.T * scale
            stamp_key_total += jnp.dot(
                stamp_scores.astype(low), query, preferred_element_type=f32
            )
            stamp_value_total += jnp.dot(
                jnp.where(first_row, stamp_prob, 0.0).astype(low), grad, preferred_element_type=f32
            )
        key_grad[:, lanes] = key_total
        value_grad[:, lanes] = value_total
        stamp_out_ref[0, :, lanes] = stamp_key_total[:1]
        stamp_out_ref[0, :, later] = stamp_value_total[:1]
    both = jnp.concatenate([query_grad[...], key_grad[...]], axis=1)
    for pair in range(2 * wide // 128):
        lanes = slice(pair * 128, pair * 128 + 128)
        out_ref[:, lanes] = turn_heads(both[:, lanes], rotary_ref[0], -rotary_ref[1]).astype(low)
    out_ref[:, 2 * wide :] = value_grad[...].astype(low)
    pl.when(pl.program_id(0) == pl.num_programs(0) - 1)(end_swap)


def flash_backward(turned, grad, lse, stamps, bias, rotary, heads, cut, collective_id):
    clips, rows = bias.shape
    wide = heads * HDIM
    blocked = lambda lanes: pl.BlockSpec((rows, lanes), lambda clip: (clip, 0))
    grads, stamp_grads, mine = pl.pallas_call(
        functools.partial(flash_backward_body, heads, rows // 4),
        grid=(clips,),
        out_shape=[
            jax.ShapeDtypeStruct((clips * rows, 3 * wide), jnp.bfloat16),
            jax.ShapeDtypeStruct((clips, 1, 2 * wide), jnp.float32),
            jax.ShapeDtypeStruct(cut.shape, cut.dtype),
        ],
        in_specs=[
            blocked(3 * wide),
            blocked(wide),
            blocked(128),
            pl.BlockSpec((1, 1, 2 * wide), lambda clip: (clip, 0, 0)),
            pl.BlockSpec((1, rows, 1), lambda clip: (clip, 0, 0)),
            pl.BlockSpec((2, rows, 128), lambda clip: (0, 0, 0)),
            any_spec(),
        ],
        out_specs=[
            blocked(3 * wide),
            pl.BlockSpec((1, 1, 2 * wide), lambda clip: (clip, 0, 0)),
            any_spec(),
        ],
        scratch_shapes=[pltpu.VMEM((rows, wide), jnp.float32)] * 3 + swap_scratch(),
        compiler_params=communicating(collective_id),
    )(turned, grad, lse, stamps[:, None], bias[:, :, None], rotary, cut)
    return grads, stamp_grads[:, 0], mine


def ff_outer_body(normed_ref, gates_ref, grads_ref, hidden_ref, out_ref):
    last = pl.program_id(0) == pl.num_programs(0) - 1

    @pl.when(jnp.logical_not(last))
    def _():
        out_ref[...] = outer_sum(normed_ref[...], gates_ref[...]).astype(out_ref.dtype)

    @pl.when(last)
    def _():
        out_ref[...] = outer_sum(grads_ref[...], hidden_ref[...]).astype(out_ref.dtype)


def ff_outer(normed, gates, grads, hidden):
    rows, wide = normed.shape
    width = hidden.shape[1]
    tile = wide // 3
    ends = gates.shape[1] // width
    return pl.pallas_call(
        ff_outer_body,
        grid=(ends + 1, wide // tile),
        out_shape=jax.ShapeDtypeStruct((wide, (ends + 1) * width), jnp.bfloat16),
        in_specs=[
            pl.BlockSpec(
                (rows, tile), lambda n, m: (0, jnp.where(n < ends, m, wide // tile - 1))
            ),
            pl.BlockSpec((rows, width), lambda n, m: (0, jnp.minimum(n, ends - 1))),
            pl.BlockSpec((rows, tile), lambda n, m: (0, jnp.where(n < ends, 0, m))),
            pl.BlockSpec((rows, width), lambda n, m: (0, 0)),
        ],
        out_specs=pl.BlockSpec((tile, width), lambda n, m: (m, n)),
        compiler_params=pltpu.CompilerParams(vmem_limit_bytes=VMEM_LIMIT),
    )(normed, gates, grads, hidden)


def adam_body(split, factor_ref, weight_ref, first_ref, second_ref, grad_ref, *outs):
    parts, _, held = grad_ref.shape
    width = held // split
    choices = [
        jnp.concatenate(
            [grad_ref[part, :, side * width : (side + 1) * width] for part in range(parts)], axis=1
        ).astype(jnp.float32)
        for side in range(split)
    ]
    gradient = choices[0]
    for side in range(1, split):
        gradient = jnp.where(lax.rem(pl.program_id(0), split) == side, choices[side], gradient)
    results = adam_step(
        weight_ref[...],
        first_ref[...],
        second_ref[...],
        gradient * factor_ref[0, 0],
        matrix_rate,
        matrix_decay,
    )
    for out, result in zip(outs, results):
        out[...] = result


def adam_matrix(factor, weight, first, second, owned, width, split, parts):
    rows, columns = weight.shape
    group = owned.shape[0]
    blocks = columns // (group * width)
    steps = group // parts
    piece = pl.BlockSpec((rows, parts * width), lambda block, step: (0, block * steps + step))
    grads = pl.BlockSpec(
        (parts, rows, split * width), lambda block, step: (step, 0, block // split)
    )
    return pl.pallas_call(
        functools.partial(adam_body, split),
        grid=(blocks, steps),
        out_shape=[jax.ShapeDtypeStruct(weight.shape, jnp.float32)] * 3,
        in_specs=[pl.BlockSpec(memory_space=pltpu.SMEM), piece, piece, piece, grads],
        out_specs=[piece] * 3,
        compiler_params=pltpu.CompilerParams(vmem_limit_bytes=VMEM_LIMIT),
    )(factor, weight, first, second, owned)


def plane_device(
    frames,
    time_token,
    cond_ids,
    cond_mask,
    lengths,
    cond_table,
    cotangent,
    attn_weight,
    cross_weight,
    norm_param,
    ff_weight,
    attn_first,
    attn_second,
    cross_first,
    cross_second,
    norm_first,
    norm_second,
    ff_first,
    ff_second,
):
    group, planes = lax.axis_size("dp"), lax.axis_size("seq")
    place, depth = lax.axis_index("dp"), lax.axis_index("seq")
    clips = group // planes
    _, frame_rows, wide = frames.shape
    piece = frame_rows // group
    seq_frames = frame_rows * planes
    own_rows = planes * piece
    heads = HEADS // group
    head_wide = heads * HDIM
    ff_wide = FF // group
    owned = wide // (group * planes)
    cond_count, cond_wide = cond_ids.shape[1], cond_table.shape[1]
    cond_owned = cross_weight.shape[0]

    order = jnp.arange(wide).reshape(group, planes, owned).swapaxes(0, 1).reshape(wide)
    order_mat = (jnp.arange(wide)[:, None] == order[None, :]).astype(jnp.bfloat16)

    def to_plane_order(values):
        return jnp.dot(values, order_mat, preferred_element_type=jnp.float32).astype(jnp.bfloat16)

    def to_whole_order(values):
        return times_transposed(values, order_mat)

    attn_low = attn_weight.astype(jnp.bfloat16).reshape(owned, 6, group, head_wide)
    attn_cut = attn_low.transpose(2, 0, 1, 3).reshape(group, owned, 6 * head_wide)
    cross_low = cross_weight.astype(jnp.bfloat16).reshape(cond_owned, 2, group, head_wide)
    cross_cut = cross_low.transpose(2, 0, 1, 3).reshape(group, owned, -1)
    norm_block = norm_param.astype(jnp.bfloat16).astype(jnp.float32)
    norm_block = jnp.pad(norm_block, ((0, 2), (0, 128 - owned)))
    pack = jnp.concatenate(
        [
            time_token.astype(jnp.float32),
            jnp.pad(cond_ids.astype(jnp.float32), ((0, 0), (0, wide - cond_count))),
            jnp.pad(cond_mask.astype(jnp.float32), ((0, 0), (0, wide - cond_count))),
            jnp.broadcast_to(lengths.astype(jnp.float32)[:, None], (1, wide)),
            jnp.zeros((4, wide), jnp.float32),
        ],
        axis=0,
    )
    stream, norm_all, packs, attn_mine = enter(
        to_plane_order(frames[0]).reshape(group, piece, wide),
        norm_block,
        pack,
        jnp.concatenate([attn_cut, cross_cut], axis=2),
        planes,
        1,
    )
    stream = stream.reshape(clips, own_rows, wide).astype(jnp.float32)
    ff_low = ff_weight.astype(jnp.bfloat16).reshape(owned, 3, group, ff_wide)
    ff_cut = ff_low.transpose(2, 0, 1, 3).reshape(group, owned, 3 * ff_wide)

    def over_planes(block):
        return lax.all_gather(block.reshape(group * owned, -1), "seq", axis=0, tiled=True)

    w_qkv = over_planes(attn_mine[:, :, : 3 * head_wide])
    w_rest = over_planes(attn_mine[:, :, 3 * head_wide :])
    w_self_out = w_rest[:, :head_wide]
    w_cross_query = w_rest[:, head_wide : 2 * head_wide]
    w_cross_out = w_rest[:, 2 * head_wide : 3 * head_wide]
    w_cond = w_rest[:, 3 * head_wide :].reshape(planes, group, cond_owned, -1)
    w_cond = jnp.swapaxes(w_cond, 0, 1).reshape(cond_wide, 2 * head_wide)
    norm_all = norm_all.reshape(group, planes, 8, 128)[:, :, :6, :owned].transpose(2, 1, 0, 3)
    gain_rows = norm_all.reshape(6, wide)

    plane_packs = lax.dynamic_slice_in_dim(packs, depth * clips, clips, axis=0)
    stamps = to_plane_order(plane_packs[:, 0].astype(jnp.bfloat16)).astype(jnp.float32)
    cond_keep = plane_packs[:, 2, :cond_count] > 0
    clip_lengths = plane_packs[:, 3, 0].astype(jnp.int32)
    share = cond_count // group
    all_ids = packs[:, 1, :cond_count].astype(jnp.int32)
    own_ids = lax.dynamic_slice_in_dim(all_ids, place * share, share, axis=1)
    vocab_rows = cond_table.shape[0]
    relative = own_ids - depth * vocab_rows
    inside = (relative >= 0) & (relative < vocab_rows)
    picked = jnp.take(cond_table, jnp.clip(relative, 0, vocab_rows - 1), axis=0)
    picked = jnp.where(inside[..., None], picked, jnp.zeros((), picked.dtype))
    picked = picked.reshape(planes, clips, share, cond_wide)
    positions = depth * frame_rows + jnp.arange(frame_rows)
    frame_valid = (positions[None, :] < lengths[:, None]).astype(cotangent.dtype)
    masked = to_plane_order((cotangent * frame_valid[..., None])[0])

    group_rows = clips * seq_frames
    row_place = jnp.arange(seq_frames)
    row_owner, row_rest = row_place // own_rows, row_place % own_rows
    true_place = (row_rest // piece) * frame_rows + row_owner * piece + row_rest % piece
    key_keep = true_place[None, :] < clip_lengths[:, None]
    group_shape = (clips, seq_frames, heads, HDIM)

    def collect(rows, collective_id):
        return plane_gather(rows, collective_id).reshape(group_rows, wide)

    def spread(partial_value, collective_id):
        terms = partial_value.astype(jnp.bfloat16).reshape(clips, group, own_rows, wide)
        return plane_reduce(terms, collective_id)

    normed_one = layer_norm(stream, gain_rows[0], gain_rows[1]).astype(jnp.bfloat16)
    group_one, cond = plane_gather(normed_one, 5, picked)
    group_one = group_one.reshape(group_rows, wide)
    cond_flat = cond.swapaxes(0, 1).reshape(clips * cond_count, cond_wide)
    projected = jnp.dot(group_one, w_qkv, preferred_element_type=jnp.float32)
    stamp_normed = layer_norm(stamps, gain_rows[0], gain_rows[1]).astype(jnp.bfloat16)
    stamp_pair = jnp.dot(stamp_normed, w_qkv[:, head_wide:], preferred_element_type=jnp.float32)
    stamp_pair = stamp_pair.astype(jnp.bfloat16)
    rotary = rotary_lanes(true_place)
    key_bias = jnp.where(key_keep, 0.0, masked_score)
    rotated, self_low, self_lse, ff_mine, grad_out_low = flash_forward(
        projected,
        stamp_pair,
        key_bias,
        rotary,
        heads,
        ff_cut,
        masked.reshape(group, piece, wide),
        2,
    )
    grad_out_low = grad_out_low.reshape(clips, own_rows, wide)
    grad_out = grad_out_low.astype(jnp.float32)
    w_gate_up = over_planes(ff_mine[:, :, : 2 * ff_wide])
    w_down = over_planes(ff_mine[:, :, 2 * ff_wide :])
    resid_one = stream + spread(times_transposed(self_low, w_self_out), 6)
    normed_two = layer_norm(resid_one, gain_rows[2], gain_rows[3]).astype(jnp.bfloat16)
    group_two = collect(normed_two, 7)
    cross_query = jnp.dot(group_two, w_cross_query, preferred_element_type=jnp.float32)
    cross_query = cross_query.astype(jnp.bfloat16).reshape(group_shape)
    cond_pair = jnp.dot(cond_flat, w_cond, preferred_element_type=jnp.float32)
    cond_pair = cond_pair.astype(jnp.bfloat16)
    cond_shape = (clips, cond_count, heads, HDIM)
    cross_keys = cond_pair[:, :head_wide].reshape(cond_shape)
    cross_values = cond_pair[:, head_wide:].reshape(cond_shape)
    cross_mixed, cross_lse = cross_forward(cross_query, cross_keys, cross_values, cond_keep)
    cross_out = cross_mixed.astype(jnp.bfloat16).reshape(group_rows, head_wide)
    resid_two = resid_one + spread(times_transposed(cross_out, w_cross_out), 8)
    normed_three = layer_norm(resid_two, gain_rows[4], gain_rows[5]).astype(jnp.bfloat16)
    group_three = collect(normed_three, 9)
    gate_up = jnp.dot(group_three, w_gate_up, preferred_element_type=jnp.float32)
    gate_up, grad_out_low = lax.optimization_barrier((gate_up, grad_out_low))
    group_grad_out = collect(grad_out_low, 10)
    gate_val, up_val = gate_up[:, :ff_wide], gate_up[:, ff_wide:]
    hidden = (jax.nn.silu(gate_val) * up_val).astype(jnp.bfloat16)
    branch = lax.psum_scatter(
        times_transposed(hidden, w_down)
        .astype(jnp.bfloat16)
        .reshape(clips, group, own_rows, wide),
        "dp",
        scatter_dimension=1,
        tiled=False,
    )
    layer_rows = (resid_two + branch.astype(jnp.float32)).astype(jnp.bfloat16)

    grad_hidden = jnp.dot(group_grad_out, w_down, preferred_element_type=jnp.float32)
    sigmoid_gate = jax.nn.sigmoid(gate_val)
    grad_gate = grad_hidden * up_val * sigmoid_gate * (1.0 + gate_val * (1.0 - sigmoid_gate))
    grad_up = grad_hidden * gate_val * sigmoid_gate
    grad_gate_up = jnp.concatenate([grad_gate, grad_up], axis=1).astype(jnp.bfloat16)

    def over_rows(block):
        return lax.psum_scatter(
            block.astype(jnp.bfloat16), "seq", scatter_dimension=0, tiled=True
        ).reshape(group, owned, -1)

    ff_piece = ff_outer(group_three, grad_gate_up, group_grad_out, hidden)
    grad_gate_up, ff_piece = lax.optimization_barrier((grad_gate_up, ff_piece))
    ff_rows = over_rows(ff_piece)
    grad_normed_three = spread(times_transposed(grad_gate_up, w_gate_up), 13)

    _, norm_three_back = jax.vjp(layer_norm, resid_two, gain_rows[4], gain_rows[5])
    grad_two_part, grad_gain_three, grad_bias_three = norm_three_back(grad_normed_three)
    grad_two = grad_out + grad_two_part
    group_cross_branch = collect(grad_two.astype(jnp.bfloat16), 15)
    grad_cross_mixed = jnp.dot(group_cross_branch, w_cross_out, preferred_element_type=jnp.float32)
    grad_cross_mixed = grad_cross_mixed.astype(jnp.bfloat16).reshape(group_shape)
    grad_cross_query, grad_cross_keys, grad_cross_values = cross_backward(
        cross_query, cross_keys, cross_values, cond_keep, cross_lse, grad_cross_mixed
    )
    grad_cross_query = grad_cross_query.astype(jnp.bfloat16).reshape(group_rows, head_wide)
    terms_two = times_transposed(grad_cross_query, w_cross_query).astype(jnp.bfloat16)
    grad_normed_two, layer_out = plane_reduce(
        terms_two.reshape(clips, group, own_rows, wide),
        16,
        layer_rows.reshape(clips, planes, piece, wide),
    )
    layer_out = to_whole_order(layer_out.reshape(frame_rows, wide)).astype(jnp.bfloat16)
    layer_out = layer_out.reshape(frames.shape)
    _, norm_two_back = jax.vjp(layer_norm, resid_one, gain_rows[2], gain_rows[3])
    grad_one_part, grad_gain_two, grad_bias_two = norm_two_back(grad_normed_two)
    grad_one = grad_two + grad_one_part
    group_self_branch = collect(grad_one.astype(jnp.bfloat16), 17)
    grad_self_mixed = jnp.dot(group_self_branch, w_self_out, preferred_element_type=jnp.float32)
    grad_self_mixed = grad_self_mixed.astype(jnp.bfloat16)
    cond_grad = jnp.concatenate(
        [
            grad_cross_keys.reshape(clips * cond_count, head_wide),
            grad_cross_values.reshape(clips * cond_count, head_wide),
        ],
        axis=1,
    )
    cross_piece = split_outer(cond_flat, cond_grad)
    cross_piece = cross_piece.reshape(group, planes, cond_owned, 2 * head_wide)
    cross_piece = jnp.swapaxes(cross_piece, 0, 1).reshape(wide, head_wide)
    rest_piece = jnp.concatenate(
        [
            outer_sum(group_self_branch, self_low),
            outer_sum(group_two, grad_cross_query),
            outer_sum(group_cross_branch, cross_out),
            cross_piece,
        ],
        axis=1,
    )
    rest_piece = rest_piece.astype(jnp.bfloat16)
    grad_self_mixed, rest_piece = lax.optimization_barrier((grad_self_mixed, rest_piece))
    rest_piece, ff_rows = lax.optimization_barrier((rest_piece, ff_rows))
    rest_rows = over_rows(rest_piece)
    grad_project, stamp_grad, ff_owned = flash_backward(
        rotated, grad_self_mixed, self_lse, stamp_pair, key_bias, rotary, heads, ff_rows, 3
    )
    grad_stamp_normed = split_times_transposed(stamp_grad, w_qkv[:, head_wide:])
    qkv_piece = outer_sum(group_one, grad_project)
    stamp_weight_grad = split_outer(stamp_normed, stamp_grad)
    qkv_piece = jnp.concatenate(
        [qkv_piece[:, :head_wide], qkv_piece[:, head_wide:] + stamp_weight_grad], axis=1
    )
    qkv_piece = qkv_piece.astype(jnp.bfloat16)
    grad_project, qkv_piece = lax.optimization_barrier((grad_project, qkv_piece))
    qkv_rows = over_rows(qkv_piece)
    grad_project, rest_rows = lax.optimization_barrier((grad_project, rest_rows))
    grad_normed_one = spread(times_transposed(grad_project, w_qkv), 18)
    _, norm_one_back = jax.vjp(layer_norm, stream, gain_rows[0], gain_rows[1])
    grad_zero_part, grad_gain_one, grad_bias_one = norm_one_back(grad_normed_one)
    _, norm_stamp_back = jax.vjp(layer_norm, stamps, gain_rows[0], gain_rows[1])
    _, grad_gain_stamp, grad_bias_stamp = norm_stamp_back(grad_stamp_normed)
    frames_grad = (grad_one + grad_zero_part).astype(jnp.bfloat16)
    norm_grad = jnp.stack(
        [
            grad_gain_one + grad_gain_stamp,
            grad_bias_one + grad_bias_stamp,
            grad_gain_two,
            grad_bias_two,
            grad_gain_three,
            grad_bias_three,
        ],
        axis=0,
    )
    norm_parts = norm_grad.reshape(6, planes, group, owned).transpose(2, 1, 0, 3)
    norm_parts = norm_parts.reshape(group * planes, 6, owned)
    norm_parts = jnp.pad(norm_parts, ((0, 0), (0, 2), (0, 128 - owned)))
    frames_grad, attn_owned, norm_sum = leave(
        frames_grad.reshape(clips, planes, piece, wide),
        jnp.concatenate([qkv_rows, rest_rows], axis=2),
        norm_parts,
        20,
    )
    frames_grad = to_whole_order(frames_grad.reshape(frame_rows, wide)).reshape(frames.shape)
    cross_reduced = attn_owned[:, :, 6 * head_wide :].reshape(group, cond_owned, 2, head_wide)
    cross_reduced = cross_reduced.transpose(1, 2, 0, 3).reshape(cross_weight.shape)
    cross_reduced = cross_reduced.astype(jnp.float32)
    squares = jnp.sum(jnp.square(attn_owned.astype(jnp.float32)))
    squares = squares + jnp.sum(jnp.square(ff_owned.astype(jnp.float32)))
    squares = squares + jnp.sum(jnp.square(norm_sum))
    total = finish(jnp.broadcast_to(squares, (8, 128)), planes, 21)
    norm_reduced = norm_sum[:6, :owned]
    grad_norm = jnp.sqrt(total[0, 0])
    factor = jnp.minimum(1.0, clip_limit / grad_norm)
    factor_block = factor.reshape(1, 1)
    attn_new, attn_first_new, attn_second_new = adam_matrix(
        factor_block, attn_weight, attn_first, attn_second, attn_owned, head_wide, 2, group
    )
    cross_new, cross_first_new, cross_second_new = adam_step(
        cross_weight, cross_first, cross_second, cross_reduced * factor, matrix_rate, matrix_decay
    )
    norm_new, norm_first_new, norm_second_new = adam_step(
        norm_param, norm_first, norm_second, norm_reduced * factor, gain_rate, 0.0
    )
    ff_new, ff_first_new, ff_second_new = adam_matrix(
        factor_block, ff_weight, ff_first, ff_second, ff_owned, ff_wide, 1, group // 2
    )
    return (
        layer_out,
        frames_grad,
        grad_norm,
        attn_new,
        cross_new,
        norm_new,
        ff_new,
        attn_first_new,
        cross_first_new,
        norm_first_new,
        ff_first_new,
        attn_second_new,
        cross_second_new,
        norm_second_new,
        ff_second_new,
    )


def solution(mesh):
    return jax.shard_map(
        plane_device if plane_fits(mesh) else per_device,
        mesh=mesh,
        in_specs=(
            P("dp", "seq", None),
            P("dp", None),
            P("dp", None),
            P("dp", None),
            P("dp"),
            P("seq", None),
            P("dp", "seq", None),
            P(("dp", "seq"), None),
            P(("dp", "seq"), None),
            P(None, ("dp", "seq")),
            P(("dp", "seq"), None),
            P(("dp", "seq"), None),
            P(("dp", "seq"), None),
            P(("dp", "seq"), None),
            P(("dp", "seq"), None),
            P(None, ("dp", "seq")),
            P(None, ("dp", "seq")),
            P(("dp", "seq"), None),
            P(("dp", "seq"), None),
        ),
        out_specs=(
            P("dp", "seq", None),
            P("dp", "seq", None),
            P(),
            P(("dp", "seq"), None),
            P(("dp", "seq"), None),
            P(None, ("dp", "seq")),
            P(("dp", "seq"), None),
            P(("dp", "seq"), None),
            P(("dp", "seq"), None),
            P(None, ("dp", "seq")),
            P(("dp", "seq"), None),
            P(("dp", "seq"), None),
            P(("dp", "seq"), None),
            P(None, ("dp", "seq")),
            P(("dp", "seq"), None),
        ),
        check_vma=False,
    )
```

```python
import functools

import jax
import jax.numpy as jnp
from jax import lax
from jax.experimental import pallas as pl
from jax.experimental.pallas import tpu as pltpu
from jax.sharding import PartitionSpec as P

HEADS = 24
HDIM = 64
FF = 6144
UPDATE_STEP = 10


norm_eps = 1e-05
beta_first = 0.5
beta_second = 0.5
adam_eps = 1e-08
matrix_decay = 0.01
matrix_rate = 0.03
gain_rate = 0.25
clip_limit = 1.0
masked_score = -1e30


def layer_norm(values, gain_row, bias_row):
    center = values - jnp.mean(values, axis=-1, keepdims=True)
    spread = jnp.mean(center * center, axis=-1, keepdims=True)
    return center * lax.rsqrt(spread + norm_eps) * gain_row + bias_row


def rotary_tables(positions, head_size):
    half_size = head_size // 2
    frequency = 10000.0 ** (-jnp.arange(half_size, dtype=jnp.float32) / half_size)
    angles = positions.astype(jnp.float32)[:, None] * frequency[None, :]
    return (jnp.cos(angles)[:, None, :], jnp.sin(angles)[:, None, :])


def rotate(values, cosine_table, sine_table):
    half_size = values.shape[-1] // 2
    first_half = values[..., :half_size]
    second_half = values[..., half_size:]
    return jnp.concatenate(
        [
            first_half * cosine_table - second_half * sine_table,
            second_half * cosine_table + first_half * sine_table,
        ],
        axis=-1,
    )


def outer_sum(left_mat, right_mat):
    return lax.dot_general(
        left_mat, right_mat, (((0,), (0,)), ((), ())), preferred_element_type=jnp.float32
    )


def times_transposed(left_mat, right_mat):
    return lax.dot_general(
        left_mat, right_mat, (((1,), (1,)), ((), ())), preferred_element_type=jnp.float32
    )


def split_parts(values):
    upper = values.astype(jnp.bfloat16)
    lower = (values - upper.astype(jnp.float32)).astype(jnp.bfloat16)
    return (upper, lower)


def split_outer(left_low, right_full):
    upper, lower = split_parts(right_full)
    return outer_sum(left_low, upper) + outer_sum(left_low, lower)


def split_times_transposed(left_full, right_low):
    upper, lower = split_parts(left_full)
    return times_transposed(upper, right_low) + times_transposed(lower, right_low)


def self_scores(queries, keys, stamp_key, keep):
    score_scale = HDIM ** (-0.5)
    frame_part = (
        jnp.einsum("cqhd,ckhd->chqk", queries, keys, preferred_element_type=jnp.float32)
        * score_scale
    )
    frame_part = jnp.where(keep[:, None, None, :], frame_part, masked_score)
    stamp_part = (
        jnp.einsum("cqhd,chd->chq", queries, stamp_key, preferred_element_type=jnp.float32)
        * score_scale
    )
    return (frame_part, stamp_part)


def self_forward(queries, keys, values, stamp_key, stamp_value, keep):
    frame_scores, stamp_scores = self_scores(queries, keys, stamp_key, keep)
    top_score = jnp.maximum(jnp.max(frame_scores, axis=-1), stamp_scores)
    frame_expo = jnp.exp(frame_scores - top_score[..., None])
    stamp_expo = jnp.exp(stamp_scores - top_score)
    denom = jnp.sum(frame_expo, axis=-1) + stamp_expo
    self_lse = top_score + jnp.log(denom)
    frame_prob = (frame_expo / denom[..., None]).astype(jnp.bfloat16)
    stamp_prob = (stamp_expo / denom).astype(jnp.bfloat16)
    mixed = jnp.einsum(
        "chqk,ckhd->cqhd", frame_prob, values, preferred_element_type=jnp.float32
    ) + jnp.einsum("chq,chd->cqhd", stamp_prob, stamp_value, preferred_element_type=jnp.float32)
    return (mixed, self_lse)


def self_backward(queries, keys, values, stamp_key, stamp_value, keep, self_lse, grad_mixed):
    score_scale = HDIM ** (-0.5)
    frame_scores, stamp_scores = self_scores(queries, keys, stamp_key, keep)
    frame_prob = jnp.exp(frame_scores - self_lse[..., None])
    stamp_prob = jnp.exp(stamp_scores - self_lse)
    grad_frame_prob = jnp.einsum(
        "cqhd,ckhd->chqk", grad_mixed, values, preferred_element_type=jnp.float32
    )
    grad_stamp_prob = jnp.einsum(
        "cqhd,chd->chq", grad_mixed, stamp_value, preferred_element_type=jnp.float32
    )
    delta = jnp.sum(frame_prob * grad_frame_prob, axis=-1) + stamp_prob * grad_stamp_prob
    grad_frame_scores = (frame_prob * (grad_frame_prob - delta[..., None])).astype(jnp.bfloat16)
    grad_stamp_scores = (stamp_prob * (grad_stamp_prob - delta)).astype(jnp.bfloat16)
    grad_queries = (
        jnp.einsum("chqk,ckhd->cqhd", grad_frame_scores, keys, preferred_element_type=jnp.float32)
        + jnp.einsum(
            "chq,chd->cqhd", grad_stamp_scores, stamp_key, preferred_element_type=jnp.float32
        )
    ) * score_scale
    key_part = (
        jnp.einsum(
            "chqk,cqhd->ckhd", grad_frame_scores, queries, preferred_element_type=jnp.float32
        )
        * score_scale
    )
    value_part = jnp.einsum(
        "chqk,cqhd->ckhd",
        frame_prob.astype(jnp.bfloat16),
        grad_mixed,
        preferred_element_type=jnp.float32,
    )
    grad_stamp_key = (
        jnp.einsum("chq,cqhd->chd", grad_stamp_scores, queries, preferred_element_type=jnp.float32)
        * score_scale
    )
    grad_stamp_value = jnp.einsum(
        "chq,cqhd->chd",
        stamp_prob.astype(jnp.bfloat16),
        grad_mixed,
        preferred_element_type=jnp.float32,
    )
    return (grad_queries, key_part, value_part, grad_stamp_key, grad_stamp_value)


def cross_scores(query, keys, keep):
    score_scale = HDIM ** (-0.5)
    scores = (
        jnp.einsum("cqhd,ckhd->chqk", query, keys, preferred_element_type=jnp.float32) * score_scale
    )
    return jnp.where(keep[:, None, None, :], scores, masked_score)


def cross_forward(query, keys, values, keep):
    scores = cross_scores(query, keys, keep)
    top_score = jnp.max(scores, axis=-1)
    expo = jnp.exp(scores - top_score[..., None])
    denom = jnp.sum(expo, axis=-1)
    cross_lse = top_score + jnp.log(denom)
    prob = (expo / denom[..., None]).astype(jnp.bfloat16)
    mixed = jnp.einsum("chqk,ckhd->cqhd", prob, values, preferred_element_type=jnp.float32)
    return (mixed, cross_lse)


def cross_backward(query, keys, values, keep, cross_lse, grad_mixed):
    score_scale = HDIM ** (-0.5)
    prob = jnp.exp(cross_scores(query, keys, keep) - cross_lse[..., None])
    grad_prob = jnp.einsum(
        "cqhd,ckhd->chqk", grad_mixed, values, preferred_element_type=jnp.float32
    )
    delta = jnp.sum(prob * grad_prob, axis=-1)
    grad_scores = (prob * (grad_prob - delta[..., None])).astype(jnp.bfloat16)
    grad_query = (
        jnp.einsum("chqk,ckhd->cqhd", grad_scores, keys, preferred_element_type=jnp.float32)
        * score_scale
    )
    grad_keys = (
        jnp.einsum("chqk,cqhd->ckhd", grad_scores, query, preferred_element_type=jnp.float32)
        * score_scale
    )
    grad_values = jnp.einsum(
        "chqk,cqhd->ckhd", prob.astype(jnp.bfloat16), grad_mixed, preferred_element_type=jnp.float32
    )
    return (grad_query, grad_keys, grad_values)


def adam_step(weight, first, second, gradient, step_rate, decay_rate):
    first_new = beta_first * first + (1.0 - beta_first) * gradient
    second_new = beta_second * second + (1.0 - beta_second) * gradient * gradient
    fix_first = 1.0 - beta_first**UPDATE_STEP
    fix_second = 1.0 - beta_second**UPDATE_STEP
    normed_step = first_new / fix_first / (jnp.sqrt(second_new / fix_second) + adam_eps)
    return (weight - step_rate * (normed_step + decay_rate * weight), first_new, second_new)


def per_device(
    frames,
    time_token,
    cond_ids,
    cond_mask,
    lengths,
    cond_table,
    cotangent,
    attn_weight,
    cross_weight,
    norm_param,
    ff_weight,
    attn_first,
    attn_second,
    cross_first,
    cross_second,
    norm_first,
    norm_second,
    ff_first,
    ff_second,
):
    clip_count, frame_rows, wide = frames.shape
    hidden_width = FF
    token_count = clip_count * frame_rows
    seq_count = lax.axis_size("seq")
    seq_frames = frame_rows * seq_count
    seq_place = lax.axis_index("seq")
    vocab_rows = cond_table.shape[0]
    relative = cond_ids - seq_place * vocab_rows
    inside = (relative >= 0) & (relative < vocab_rows)
    picked = jnp.take(cond_table, jnp.clip(relative, 0, vocab_rows - 1), axis=0).astype(jnp.float32)
    picked = jnp.where(inside[..., None], picked, 0.0)
    cond = lax.psum(picked.astype(jnp.bfloat16), "seq")
    cond_count = cond.shape[1]
    cond_flat = cond.reshape(clip_count * cond_count, cond.shape[2])
    cond_width = cond.shape[2]
    cond_keep = cond_mask > 0
    attn_low = attn_weight.astype(jnp.bfloat16)
    cross_low = cross_weight.astype(jnp.bfloat16)
    norm_low = norm_param.astype(jnp.bfloat16)
    ff_low = ff_weight.astype(jnp.bfloat16)
    stream = frames.astype(jnp.float32).reshape(token_count, wide)
    stamps = time_token.astype(jnp.float32)
    positions = seq_place * frame_rows + jnp.arange(frame_rows)
    key_keep = jnp.arange(seq_frames)[None, :] < lengths[:, None]
    frame_valid = (positions[None, :] < lengths[:, None]).reshape(token_count)
    grad_out = cotangent.astype(jnp.float32).reshape(token_count, wide) * frame_valid[
        :, None
    ].astype(jnp.float32)
    grad_out_low = grad_out.astype(jnp.bfloat16)
    piece_heads = HEADS // seq_count
    piece_wide = wide // seq_count
    piece_ff = hidden_width // seq_count
    group_rows = clip_count * seq_frames

    def pieces():
        norm_copies = jnp.tile(norm_low[None], (1, 1, seq_count))
        moved_attn, moved_cross, moved_ff, moved_norm = (
            lax.all_to_all(
                attn_low.reshape(-1, 6, wide), "seq", split_axis=2, concat_axis=0, tiled=True
            ),
            lax.all_to_all(
                cross_low.reshape(-1, 2, wide), "seq", split_axis=2, concat_axis=0, tiled=True
            ),
            lax.all_to_all(
                ff_low.reshape(-1, 3, hidden_width), "seq", split_axis=2, concat_axis=0, tiled=True
            ),
            lax.all_to_all(norm_copies, "seq", split_axis=2, concat_axis=0, tiled=True),
        )
        attn_cols, cross_cols, ff_cols, norm_blocks = (
            lax.all_gather(moved_attn, "dp", axis=0, tiled=True),
            lax.all_gather(moved_cross, "dp", axis=0, tiled=True),
            lax.all_gather(moved_ff, "dp", axis=0, tiled=True),
            lax.all_gather(moved_norm, "dp", axis=0, tiled=True),
        )
        gains = norm_blocks.transpose(1, 0, 2).reshape(6, wide).astype(jnp.float32)
        return (attn_cols, cross_cols, ff_cols, gains)

    def collect(rows):
        whole = lax.all_gather(
            rows.reshape(clip_count, frame_rows, wide), "seq", axis=1, tiled=True
        )
        return whole.reshape(group_rows, wide)

    def spread(partial_value):
        mine = lax.psum_scatter(
            partial_value.reshape(clip_count, seq_frames, wide).astype(jnp.bfloat16),
            "seq",
            scatter_dimension=1,
            tiled=True,
        ).astype(jnp.float32)
        return mine.reshape(token_count, wide)

    attn_cols, cross_cols, ff_cols, gain_rows = pieces()
    group_shape = (clip_count, seq_frames, piece_heads, HDIM)
    cosine_table, sine_table = rotary_tables(jnp.arange(seq_frames), HDIM)
    normed_one = layer_norm(stream, gain_rows[0], gain_rows[1]).astype(jnp.bfloat16)
    group_one = collect(normed_one)
    projected = jnp.dot(
        group_one,
        attn_cols[:, :3].reshape(wide, 3 * piece_wide),
        preferred_element_type=jnp.float32,
    )
    queries = rotate(
        projected[:, :piece_wide].reshape(group_shape), cosine_table, sine_table
    ).astype(jnp.bfloat16)
    all_keys = rotate(
        projected[:, piece_wide : 2 * piece_wide].reshape(group_shape), cosine_table, sine_table
    ).astype(jnp.bfloat16)
    all_values = projected[:, 2 * piece_wide :].astype(jnp.bfloat16).reshape(group_shape)
    stamp_normed = layer_norm(stamps, gain_rows[0], gain_rows[1]).astype(jnp.bfloat16)
    stamp_pair = jnp.dot(
        stamp_normed,
        attn_cols[:, 1:3].reshape(wide, 2 * piece_wide),
        preferred_element_type=jnp.float32,
    )
    stamp_key = (
        stamp_pair[:, :piece_wide].astype(jnp.bfloat16).reshape(clip_count, piece_heads, HDIM)
    )
    stamp_value = (
        stamp_pair[:, piece_wide:].astype(jnp.bfloat16).reshape(clip_count, piece_heads, HDIM)
    )
    self_mixed, self_lse = self_forward(
        queries, all_keys, all_values, stamp_key, stamp_value, key_keep
    )
    self_low = self_mixed.astype(jnp.bfloat16).reshape(group_rows, piece_wide)
    resid_one = stream + spread(times_transposed(self_low, attn_cols[:, 3]))
    normed_two = layer_norm(resid_one, gain_rows[2], gain_rows[3]).astype(jnp.bfloat16)
    group_two = collect(normed_two)
    cross_query = jnp.dot(group_two, attn_cols[:, 4], preferred_element_type=jnp.float32)
    cross_query = cross_query.astype(jnp.bfloat16).reshape(group_shape)
    cond_pair = jnp.dot(
        cond_flat,
        cross_cols.reshape(cond_width, 2 * piece_wide),
        preferred_element_type=jnp.float32,
    )
    cond_shape = (clip_count, cond_count, piece_heads, HDIM)
    cross_keys = cond_pair[:, :piece_wide].astype(jnp.bfloat16).reshape(cond_shape)
    cross_values = cond_pair[:, piece_wide:].astype(jnp.bfloat16).reshape(cond_shape)
    cross_mixed, cross_lse = cross_forward(cross_query, cross_keys, cross_values, cond_keep)
    cross_low_out = cross_mixed.astype(jnp.bfloat16).reshape(group_rows, piece_wide)
    resid_two = resid_one + spread(times_transposed(cross_low_out, attn_cols[:, 5]))
    normed_three = layer_norm(resid_two, gain_rows[4], gain_rows[5]).astype(jnp.bfloat16)
    group_three = collect(normed_three)
    gate_up = jnp.dot(
        group_three, ff_cols[:, :2].reshape(wide, 2 * piece_ff), preferred_element_type=jnp.float32
    )
    gate_val = gate_up[:, :piece_ff]
    up_val = gate_up[:, piece_ff:]
    hidden = (jax.nn.silu(gate_val) * up_val).astype(jnp.bfloat16)
    branch = spread(times_transposed(hidden, ff_cols[:, 2]))
    layer_out = (resid_two + branch).astype(jnp.bfloat16).reshape(clip_count, frame_rows, wide)
    attn_cols, cross_cols, ff_cols, gain_rows = pieces()
    group_grad_out = collect(grad_out_low)
    grad_hidden = jnp.dot(group_grad_out, ff_cols[:, 2], preferred_element_type=jnp.float32)
    sigmoid_gate = jax.nn.sigmoid(gate_val)
    grad_gate = grad_hidden * up_val * sigmoid_gate * (1.0 + gate_val * (1.0 - sigmoid_gate))
    grad_up = grad_hidden * gate_val * sigmoid_gate
    grad_gate_up = jnp.concatenate([grad_gate, grad_up], axis=1).astype(jnp.bfloat16)
    grad_normed_three = spread(
        times_transposed(grad_gate_up, ff_cols[:, :2].reshape(wide, 2 * piece_ff))
    )
    _, norm_three_back = jax.vjp(layer_norm, resid_two, gain_rows[4], gain_rows[5])
    grad_two_part, grad_gain_three, grad_bias_three = norm_three_back(grad_normed_three)
    grad_two = grad_out + grad_two_part
    grad_cross_branch = grad_two.astype(jnp.bfloat16)
    group_cross_branch = collect(grad_cross_branch)
    grad_cross_mixed = jnp.dot(
        group_cross_branch, attn_cols[:, 5], preferred_element_type=jnp.float32
    )
    grad_cross_mixed = grad_cross_mixed.astype(jnp.bfloat16).reshape(group_shape)
    grad_cross_query, grad_cross_keys, grad_cross_values = cross_backward(
        cross_query, cross_keys, cross_values, cond_keep, cross_lse, grad_cross_mixed
    )
    grad_cross_query = grad_cross_query.astype(jnp.bfloat16).reshape(group_rows, piece_wide)
    grad_normed_two = spread(times_transposed(grad_cross_query, attn_cols[:, 4]))
    _, norm_two_back = jax.vjp(layer_norm, resid_one, gain_rows[2], gain_rows[3])
    grad_one_part, grad_gain_two, grad_bias_two = norm_two_back(grad_normed_two)
    grad_one = grad_two + grad_one_part
    grad_self_branch = grad_one.astype(jnp.bfloat16)
    group_self_branch = collect(grad_self_branch)
    grad_self_mixed = jnp.dot(
        group_self_branch, attn_cols[:, 3], preferred_element_type=jnp.float32
    )
    grad_self_mixed = grad_self_mixed.astype(jnp.bfloat16).reshape(group_shape)
    grad_queries, key_part, value_part, grad_stamp_key, grad_stamp_value = self_backward(
        queries, all_keys, all_values, stamp_key, stamp_value, key_keep, self_lse, grad_self_mixed
    )
    grad_query_raw = (
        rotate(grad_queries, cosine_table, -sine_table)
        .astype(jnp.bfloat16)
        .reshape(group_rows, piece_wide)
    )
    grad_key_raw = (
        rotate(key_part, cosine_table, -sine_table)
        .astype(jnp.bfloat16)
        .reshape(group_rows, piece_wide)
    )
    grad_value = value_part.astype(jnp.bfloat16).reshape(group_rows, piece_wide)
    grad_project = jnp.concatenate([grad_query_raw, grad_key_raw, grad_value], axis=1)
    grad_normed_one = spread(
        times_transposed(grad_project, attn_cols[:, :3].reshape(wide, 3 * piece_wide))
    )
    stamp_grad = jnp.concatenate(
        [
            grad_stamp_key.reshape(clip_count, piece_wide),
            grad_stamp_value.reshape(clip_count, piece_wide),
        ],
        axis=1,
    )
    grad_stamp_normed = split_times_transposed(
        stamp_grad, attn_cols[:, 1:3].reshape(wide, 2 * piece_wide)
    )
    _, norm_one_back = jax.vjp(layer_norm, stream, gain_rows[0], gain_rows[1])
    grad_zero_part, grad_gain_one, grad_bias_one = norm_one_back(grad_normed_one)
    _, norm_stamp_back = jax.vjp(layer_norm, stamps, gain_rows[0], gain_rows[1])
    _, grad_gain_stamp, grad_bias_stamp = norm_stamp_back(grad_stamp_normed)
    frames_grad = (grad_one + grad_zero_part).reshape(clip_count, frame_rows, wide)
    project_grad = outer_sum(group_one, grad_project)
    stamp_weight_grad = split_outer(stamp_normed, stamp_grad)
    attn_piece = jnp.stack(
        [
            project_grad[:, :piece_wide],
            project_grad[:, piece_wide : 2 * piece_wide] + stamp_weight_grad[:, :piece_wide],
            project_grad[:, 2 * piece_wide :] + stamp_weight_grad[:, piece_wide:],
            outer_sum(group_self_branch, self_low),
            outer_sum(group_two, grad_cross_query),
            outer_sum(group_cross_branch, cross_low_out),
        ],
        axis=1,
    )
    cond_grad = jnp.concatenate(
        [
            grad_cross_keys.reshape(clip_count * cond_count, piece_wide),
            grad_cross_values.reshape(clip_count * cond_count, piece_wide),
        ],
        axis=1,
    )
    cross_piece = split_outer(cond_flat, cond_grad).reshape(cond_width, 2, piece_wide)
    ff_piece = jnp.stack(
        [
            outer_sum(group_three, grad_gate_up[:, :piece_ff]),
            outer_sum(group_three, grad_gate_up[:, piece_ff:]),
            outer_sum(group_grad_out, hidden),
        ],
        axis=1,
    )
    norm_grad = jnp.stack(
        [
            grad_gain_one + grad_gain_stamp,
            grad_bias_one + grad_bias_stamp,
            grad_gain_two,
            grad_bias_two,
            grad_gain_three,
            grad_bias_three,
        ],
        axis=0,
    )
    norm_column = norm_grad.T[:, :, None]
    summed_attn, summed_cross, summed_ff, summed_norm = (
        lax.psum_scatter(
            attn_piece.astype(jnp.bfloat16), "dp", scatter_dimension=0, tiled=True
        ).astype(jnp.float32),
        lax.psum_scatter(
            cross_piece.astype(jnp.bfloat16), "dp", scatter_dimension=0, tiled=True
        ).astype(jnp.float32),
        lax.psum_scatter(
            ff_piece.astype(jnp.bfloat16), "dp", scatter_dimension=0, tiled=True
        ).astype(jnp.float32),
        lax.psum_scatter(
            norm_column.astype(jnp.bfloat16), "dp", scatter_dimension=0, tiled=True
        ).astype(jnp.float32),
    )
    owned_attn, owned_cross, owned_ff, owned_norm = (
        lax.all_to_all(
            summed_attn.astype(jnp.bfloat16), "seq", split_axis=0, concat_axis=2, tiled=True
        ).astype(summed_attn.dtype),
        lax.all_to_all(
            summed_cross.astype(jnp.bfloat16), "seq", split_axis=0, concat_axis=2, tiled=True
        ).astype(summed_cross.dtype),
        lax.all_to_all(
            summed_ff.astype(jnp.bfloat16), "seq", split_axis=0, concat_axis=2, tiled=True
        ).astype(summed_ff.dtype),
        lax.all_to_all(
            summed_norm.astype(jnp.bfloat16), "seq", split_axis=0, concat_axis=2, tiled=True
        ).astype(summed_norm.dtype),
    )
    attn_reduced = owned_attn.reshape(owned_attn.shape[0], 6 * wide)
    cross_reduced = owned_cross.reshape(owned_cross.shape[0], 2 * wide)
    ff_reduced = owned_ff.reshape(owned_ff.shape[0], 3 * hidden_width)
    norm_reduced = jnp.sum(owned_norm, axis=2).T
    local_squares = (
        jnp.sum(attn_reduced * attn_reduced)
        + jnp.sum(cross_reduced * cross_reduced)
        + jnp.sum(norm_reduced * norm_reduced)
        + jnp.sum(ff_reduced * ff_reduced)
    )
    total_squares = lax.psum(local_squares, ("dp", "seq"))
    grad_norm = jnp.sqrt(total_squares)
    factor = jnp.minimum(1.0, clip_limit / grad_norm)
    attn_new, attn_first_new, attn_second_new = adam_step(
        attn_weight, attn_first, attn_second, attn_reduced * factor, matrix_rate, matrix_decay
    )
    cross_new, cross_first_new, cross_second_new = adam_step(
        cross_weight, cross_first, cross_second, cross_reduced * factor, matrix_rate, matrix_decay
    )
    norm_new, norm_first_new, norm_second_new = adam_step(
        norm_param, norm_first, norm_second, norm_reduced * factor, gain_rate, 0.0
    )
    ff_new, ff_first_new, ff_second_new = adam_step(
        ff_weight, ff_first, ff_second, ff_reduced * factor, matrix_rate, matrix_decay
    )
    return (
        layer_out,
        frames_grad,
        grad_norm,
        attn_new,
        cross_new,
        norm_new,
        ff_new,
        attn_first_new,
        cross_first_new,
        norm_first_new,
        ff_first_new,
        attn_second_new,
        cross_second_new,
        norm_second_new,
        ff_second_new,
    )


MESH = pl.DeviceIdType.MESH
DMA = pltpu.SemaphoreType.DMA
VMEM_LIMIT = 60 * 2**20


def plane_fits(mesh):
    return mesh.shape["dp"] == 8 and mesh.shape["dp"] % mesh.shape["seq"] == 0


def plane_places():
    place = lax.axis_index("dp")
    return (place, lax.axis_index("seq"), lambda mask: jnp.bitwise_xor(place, mask))


def greet(partners):
    barrier = pltpu.get_barrier_semaphore()
    for partner in partners:
        pl.semaphore_signal(barrier, inc=1, device_id=partner, device_id_type=MESH)
    pl.semaphore_wait(barrier, len(partners))


def remote(source, goal, send_sem, recv_sem, device):
    return pltpu.make_async_remote_copy(
        src_ref=source,
        dst_ref=goal,
        send_sem=send_sem,
        recv_sem=recv_sem,
        device_id=device,
        device_id_type=MESH,
    )


def communicating(collective_id):
    return pltpu.CompilerParams(
        has_side_effects=True, collective_id=collective_id, vmem_limit_bytes=VMEM_LIMIT
    )


def any_spec():
    return pl.BlockSpec(memory_space=pl.ANY)


def greet_cross(group, planes):
    place, depth, flip = plane_places()
    greet(
        [(flip(mask), depth) for mask in range(1, group)]
        + [(place, lax.rem(depth + step, planes)) for step in range(1, planes)]
    )


def outward_steps(group, planes, kept_ref, own_ref, mid, *sems):
    far_send, far_recv, near_send, near_recv, local_sem = sems
    place, depth, flip = plane_places()
    per = group // planes
    first = []
    for step in range(1, planes):
        origin = lax.rem(depth + step, planes)
        for slot in range(per):
            clip = per * depth + slot
            copy = remote(
                kept_ref.at[slot, origin],
                mid.at[clip],
                far_send.at[slot, step],
                far_recv.at[clip],
                (place, origin),
            )
            copy.start()
            first.append(copy)
    second = []

    def hand_over(block, clip):
        index = len(second)
        away = remote(
            block, own_ref.at[place], near_send.at[index], near_recv.at[place], (clip, depth)
        )
        stay = pltpu.make_async_copy(block, own_ref.at[place], local_sem.at[index])
        pl.when(clip != place)(away.start)
        pl.when(clip == place)(stay.start)
        second.append((clip, away, stay))

    for slot in range(per):
        hand_over(kept_ref.at[slot, depth], per * depth + slot)
    yield
    for step in range(1, planes):
        source = lax.rem(depth + step, planes)
        for slot in range(per):
            clip = per * source + slot
            block = mid.at[clip]
            remote(
                block, block, far_send.at[0, 0], far_recv.at[clip], (place, source)
            ).wait_recv()
            hand_over(block, clip)
    yield
    for mask in range(1, group):
        other = flip(mask)
        block = own_ref.at[other]
        remote(block, block, near_send.at[0], near_recv.at[other], (other, depth)).wait_recv()
    for clip, away, stay in second:
        pl.when(clip != place)(away.wait_send)
        pl.when(clip == place)(stay.wait)
    for copy in first:
        copy.wait_send()
    yield


def outward_scratch(group, planes):
    return [
        DMA((group // planes, planes)),
        DMA((group,)),
        DMA((group,)),
        DMA((group,)),
        DMA((group,)),
    ]


def swap_steps(own_ref, kept_ref, send_sem, recv_sem, local_sem):
    place, depth, flip = plane_places()
    copies = []
    for mask in (6, 7, 2, 3, 4, 5, 1):
        other = flip(mask)
        copy = remote(
            own_ref.at[other],
            kept_ref.at[place],
            send_sem.at[mask],
            recv_sem.at[mask],
            (other, depth),
        )
        copy.start()
        copies.append(copy)
    stay = pltpu.make_async_copy(own_ref.at[place], kept_ref.at[place], local_sem)
    stay.start()
    yield
    stay.wait()
    for copy in copies:
        copy.wait()
    yield


def swap_scratch():
    return [DMA((8,)), DMA((8,)), DMA(())]


def leave_body(
    group, planes, kept_ref, cut_ref, parts_ref, own_ref, mine_ref, norm_ref, mid, terms, *sems
):
    part_send, part_recv = sems[:2]
    place, depth, flip = plane_places()
    devices = [(flip(mask), lax.rem(depth + step, planes)) for mask, step in everyone(planes)]
    greet(devices)
    here = place * planes + depth
    rows = outward_steps(group, planes, kept_ref, own_ref, mid, *sems[2:7])
    next(rows)
    copies = []
    for index, (other, plane) in enumerate(devices):
        copy = remote(
            parts_ref.at[other * planes + plane],
            terms.at[here],
            part_send.at[index],
            part_recv.at[here],
            (other, plane),
        )
        copy.start()
        copies.append(copy)
    terms[here] = parts_ref[here]
    columns = swap_steps(cut_ref, mine_ref, *sems[7:])
    next(columns)
    next(rows)
    for other, plane in devices:
        source = other * planes + plane
        one = terms.at[source]
        remote(one, one, part_send.at[0], part_recv.at[source], (other, plane)).wait_recv()
    norm_ref[...] = jnp.sum(terms[...], axis=0)
    next(columns)
    next(rows)
    for copy in copies:
        copy.wait_send()


def leave(kept_rows, cut, norm_parts, collective_id):
    per, planes, rows, wide = kept_rows.shape
    group = per * planes
    count = group * planes
    whole = pl.BlockSpec(memory_space=pltpu.VMEM)
    like = lambda shape, array: jax.ShapeDtypeStruct(shape, array.dtype)
    own, mine, norm_sum, _ = pl.pallas_call(
        functools.partial(leave_body, group, planes),
        out_shape=[
            like((group, rows, wide), kept_rows),
            like(cut.shape, cut),
            like(norm_parts.shape[1:], norm_parts),
            like((group, rows, wide), kept_rows),
        ],
        in_specs=[any_spec(), any_spec(), whole],
        out_specs=[any_spec(), any_spec(), whole, any_spec()],
        scratch_shapes=[pltpu.VMEM(norm_parts.shape, jnp.float32), DMA((count,)), DMA((count,))]
        + outward_scratch(group, planes)
        + swap_scratch(),
        compiler_params=communicating(collective_id),
    )(kept_rows, cut, norm_parts)
    return own, mine, norm_sum


def everyone(planes):
    return [(mask, step) for mask in range(8) for step in range(planes) if mask or step]


def enter_body(
    group,
    planes,
    own_ref,
    norm_ref,
    pack_ref,
    first_cut_ref,
    rest_cut_ref,
    kept_ref,
    gains_ref,
    packs_ref,
    first_mine_ref,
    rest_mine_ref,
    mid,
    norms_ref,
    *sems,
):
    (
        near_send,
        near_recv,
        far_send,
        far_recv,
        local_sem,
        norm_send,
        norm_recv,
        pack_send,
        pack_recv,
        cut_send,
        cut_recv,
        stay_sem,
    ) = sems
    place, depth, flip = plane_places()
    per = group // planes
    others = everyone(planes)
    greet([(flip(mask), lax.rem(depth + step, planes)) for mask, step in others])
    here = place * planes + depth
    first = []
    for mask in (6, 7, 2, 3, 4, 5, 1):
        other = flip(mask)
        copy = remote(
            own_ref.at[other],
            mid.at[place],
            near_send.at[mask],
            near_recv.at[mask],
            (other, depth),
        )
        copy.start()
        first.append((mask, copy))
    small = []
    for index, (mask, step) in enumerate(others):
        copy = remote(
            norm_ref,
            norms_ref.at[here],
            norm_send.at[index],
            norm_recv.at[here],
            (flip(mask), lax.rem(depth + step, planes)),
        )
        copy.start()
        small.append(copy)
    for mask in range(1, group):
        copy = remote(
            pack_ref,
            packs_ref.at[place],
            pack_send.at[mask],
            pack_recv.at[mask],
            (flip(mask), depth),
        )
        copy.start()
        small.append(copy)
    stays = [
        pltpu.make_async_copy(norm_ref, norms_ref.at[here], stay_sem.at[0]),
        pltpu.make_async_copy(pack_ref, packs_ref.at[place], stay_sem.at[1]),
        pltpu.make_async_copy(
            first_cut_ref.at[place], first_mine_ref.at[place], stay_sem.at[2]
        ),
        pltpu.make_async_copy(rest_cut_ref.at[place], rest_mine_ref.at[place], stay_sem.at[3]),
    ]
    for stay in stays:
        stay.start()
    cuts = []
    for which, (cut_ref, mine_ref) in enumerate(
        ((first_cut_ref, first_mine_ref), (rest_cut_ref, rest_mine_ref))
    ):
        for mask in (6, 7, 2, 3, 4, 5, 1):
            other = flip(mask)
            copy = remote(
                cut_ref.at[other],
                mine_ref.at[place],
                cut_send.at[which, mask],
                cut_recv.at[which, mask],
                (other, depth),
            )
            copy.start()
            cuts.append(copy)
    second = []
    arrivals = dict(first)
    for mask in (0, 1, 2, 3, 4, 5, 6, 7):
        source = flip(mask)
        goal, slot = lax.div(source, per), lax.rem(source, per)
        block = own_ref.at[place]
        if mask:
            arrivals[mask].wait_recv()
            block = mid.at[source]
        away = remote(
            block,
            kept_ref.at[slot, depth],
            far_send.at[mask],
            far_recv.at[slot, depth],
            (place, goal),
        )
        stay = pltpu.make_async_copy(block, kept_ref.at[slot, depth], local_sem.at[mask])
        pl.when(goal != depth)(away.start)
        pl.when(goal == depth)(stay.start)
        second.append((goal, away, stay))
    for slot in range(per):
        for origin in range(planes):
            block = kept_ref.at[slot, origin]
            pl.when(origin != depth)(
                remote(
                    block,
                    block,
                    far_send.at[0],
                    far_recv.at[slot, origin],
                    (place, lax.rem(depth + 1, planes)),
                ).wait_recv
            )
    for mask, step in others:
        source = flip(mask) * planes + lax.rem(depth + step, planes)
        block = norms_ref.at[source]
        remote(
            block,
            block,
            norm_send.at[0],
            norm_recv.at[source],
            (flip(mask), lax.rem(depth + step, planes)),
        ).wait_recv()
    for copy in small:
        copy.wait_send()
    stays[0].wait()
    width = gains_ref.shape[1] // (group * planes)
    gains_ref[...] = jnp.concatenate(
        [
            norms_ref[owner * planes + plane, :, :width]
            for plane in range(planes)
            for owner in range(group)
        ],
        axis=1,
    )
    for mask in range(1, group):
        block = packs_ref.at[flip(mask)]
        remote(
            block, block, pack_send.at[0], pack_recv.at[mask], (flip(mask), depth)
        ).wait_recv()
    for copy in cuts:
        copy.wait()
    for goal, away, stay in second:
        pl.when(goal != depth)(away.wait_send)
        pl.when(goal == depth)(stay.wait)
    for mask, copy in first:
        copy.wait_send()
    for stay in stays[1:]:
        stay.wait()


def enter(rows_of_clip, norm_block, pack, first_cut, rest_cut, planes, collective_id):
    group, rows, wide = rows_of_clip.shape
    count = group * planes
    like = lambda shape, array: jax.ShapeDtypeStruct(shape, array.dtype)
    inside = pl.BlockSpec(memory_space=pltpu.VMEM)
    *results, _ = pl.pallas_call(
        functools.partial(enter_body, group, planes),
        out_shape=[
            like((group // planes, planes, rows, wide), rows_of_clip),
            like((norm_block.shape[0], wide), norm_block),
            like((group,) + pack.shape, pack),
            like(first_cut.shape, first_cut),
            like(rest_cut.shape, rest_cut),
            like((group, rows, wide), rows_of_clip),
        ],
        in_specs=[any_spec(), inside, any_spec(), any_spec(), any_spec()],
        out_specs=[any_spec(), inside] + [any_spec()] * 4,
        scratch_shapes=[
            pltpu.VMEM((count,) + norm_block.shape, norm_block.dtype),
            DMA((group,)),
            DMA((group,)),
            DMA((group,)),
            DMA((group // planes, planes)),
            DMA((group,)),
            DMA((count,)),
            DMA((count,)),
            DMA((group,)),
            DMA((group,)),
            DMA((2, group)),
            DMA((2, group)),
            DMA((4,)),
        ],
        compiler_params=communicating(collective_id),
    )(rows_of_clip, norm_block, pack, first_cut, rest_cut)
    return results


def cond_steps(group, planes, pick_ref, cond_ref, parts, summed, *sems):
    part_send, part_recv, cond_send, cond_recv = sems
    place, depth, flip = plane_places()
    pushes = []
    for step in range(1, planes):
        goal = lax.rem(depth + step, planes)
        copy = remote(
            pick_ref.at[goal],
            parts.at[depth],
            part_send.at[step],
            part_recv.at[depth],
            (place, goal),
        )
        copy.start()
        pushes.append(copy)
    yield
    total = pick_ref[depth].astype(jnp.float32)
    for step in range(1, planes):
        source = lax.rem(depth + step, planes)
        block = parts.at[source]
        remote(
            block, block, part_send.at[0], part_recv.at[source], (place, source)
        ).wait_recv()
        total = total + parts[source].astype(jnp.float32)
    summed[...] = total.astype(summed.dtype)
    cond_ref[place] = total.astype(summed.dtype)
    for mask in range(1, group):
        copy = remote(
            summed,
            cond_ref.at[place],
            cond_send.at[mask],
            cond_recv.at[mask],
            (flip(mask), depth),
        )
        copy.start()
        pushes.append(copy)
    yield
    for mask in range(1, group):
        block = cond_ref.at[flip(mask)]
        remote(
            block, block, cond_send.at[0], cond_recv.at[mask], (flip(mask), depth)
        ).wait_recv()
    for copy in pushes:
        copy.wait_send()
    yield


def inward_beside(group, planes, own_ref, kept_ref, mid, *sems):
    near_send, near_recv, far_send, far_recv, local_sem = sems
    place, depth, flip = plane_places()
    per = group // planes

    def near(mask):
        other = flip(mask)
        return remote(
            own_ref.at[other],
            mid.at[place],
            near_send.at[mask],
            near_recv.at[mask],
            (other, depth),
        )

    def begin():
        for mask in range(1, group):
            near(mask).start()

    def second(mask):
        source = flip(mask)
        goal, slot = lax.div(source, per), lax.rem(source, per)
        block = mid.at[source] if mask else own_ref.at[place]
        away = remote(
            block,
            kept_ref.at[slot, depth],
            far_send.at[mask],
            far_recv.at[slot, depth],
            (place, goal),
        )
        stay = pltpu.make_async_copy(block, kept_ref.at[slot, depth], local_sem.at[mask])
        return goal != depth, away, stay

    def middle():
        for mask in range(group):
            if mask:
                near(mask).wait_recv()
            leaves, away, stay = second(mask)
            pl.when(leaves)(away.start)
            pl.when(jnp.logical_not(leaves))(stay.start)

    def end():
        for slot in range(per):
            for origin in range(planes):
                block = kept_ref.at[slot, origin]
                pl.when(origin != depth)(
                    remote(
                        block,
                        block,
                        far_send.at[0],
                        far_recv.at[slot, origin],
                        (place, lax.rem(depth + 1, planes)),
                    ).wait_recv
                )
        for mask in range(group):
            leaves, away, stay = second(mask)
            pl.when(leaves)(away.wait_send)
            pl.when(jnp.logical_not(leaves))(stay.wait)
            if mask:
                near(mask).wait_send()

    return begin, middle, end


def inward_scratch(group, planes):
    return [
        DMA((group,)),
        DMA((group,)),
        DMA((group,)),
        DMA((group // planes, planes)),
        DMA((group,)),
    ]


def dot_tiles(left, right_ref, transposed, width):
    count = right_ref.shape[0] if transposed else right_ref.shape[1]
    for start in range(0, count, width):
        stop = min(start + width, count)
        if transposed:
            yield start, stop, times_transposed(left, right_ref[start:stop, :])
        else:
            yield start, stop, jnp.dot(
                left, right_ref[:, start:stop], preferred_element_type=jnp.float32
            )


def gather_dot_body(clips, rows, sub, normed, mode, beside, own_ref, *refs):
    refs = list(refs)
    take = lambda count: [refs.pop(0) for _ in range(count)]
    gain_ref = take(1)[0] if normed else None
    mat_ref = take(1)[0] if mode != "rows" else None
    gates_ref = take(1)[0] if mode == "gates" else None
    extra_ref = take(1)[0] if beside else None
    all_ref = take(1)[0]
    prod_refs = take({"rows": 0, "dot": 1, "gates": 2}[mode])
    extra_outs = take({"cond": 1, "outward": 2}[beside[0]]) if beside else []
    held, send_sem, recv_sem, all_sem = take(4)
    mat, mat_sem = take(2) if mode != "rows" else (None, None)
    stages = take(len(prod_refs))
    prod_sem = take(1)[0] if prod_refs else None
    gates, gates_sem = take(2) if mode == "gates" else (None, None)
    place, depth, flip = plane_places()
    core, beside_x, beside_y, across = flip(1), flip(2), flip(4), flip(6)
    if mode != "rows":
        load = pltpu.make_async_copy(mat_ref, mat, mat_sem)
        load.start()
    slots = [flip(mask) for mask in (0, 1, 2, 4, 3, 5, 6, 7)]
    gate_loads = {}
    if mode == "gates":
        for mask, slot in zip((0, 1, 2, 4, 3, 5, 6, 7), slots):
            gate_loads[mask] = [
                pltpu.make_async_copy(
                    gates_ref.at[clip, slot], gates.at[slot, clip], gates_sem.at[slot, clip]
                )
                for clip in range(clips)
            ]
            for copy in gate_loads[mask]:
                copy.start()
    if beside:
        greet_cross(*beside[1:])
        if beside[0] == "cond":
            going = cond_steps(*beside[1:], extra_ref, extra_outs[0], *refs)
        else:
            going = outward_steps(*beside[1:], extra_ref, *extra_outs, *refs)
        next(going)
    else:
        greet([(core, depth), (beside_x, depth), (beside_y, depth)])
    values = own_ref[...]
    if normed:
        values = layer_norm(values, gain_ref[0:1], gain_ref[1:2])
    held[place] = values.astype(held.dtype)
    chunks = [(clip, part) for clip in range(clips) for part in range(rows // sub)]
    count = len(chunks)
    half = count // 2
    sends = []

    def view(slot, index):
        clip, part = chunks[index]
        return held.at[slot, clip, pl.ds(part * sub, sub)]

    def send(slot, index, device):
        block = view(slot, index)
        copy = remote(
            block, block, send_sem.at[len(sends)], recv_sem.at[slot, index], (device, depth)
        )
        copy.start()
        sends.append(copy)

    def arrived(slot, index):
        block = view(slot, index)
        remote(
            block, block, send_sem.at[0], recv_sem.at[slot, index], (core, depth)
        ).wait_recv()

    x_order = list(range(count))
    y_order = list(range(half, count)) + list(range(half))
    for step in range(count):
        send(place, x_order[step], beside_x)
        send(place, y_order[step], beside_y)
    for index in range(count):
        send(place, index, core)
    outs = []

    def leave_here(source, goal, sem, major):
        for clip in range(clips):
            there = goal.at[major, clip] if goal.shape[0] == 8 else goal.at[clip, major]
            copy = pltpu.make_async_copy(source.at[major, clip], there, sem.at[major, clip])
            copy.start()
            outs.append(copy)

    def multiply(mask):
        slot = flip(mask)
        leave_here(held, all_ref, all_sem, slot)
        if mode == "rows":
            return
        left = held[slot].reshape(clips * rows, held.shape[3])
        for copy in gate_loads.get(mask, ()):
            copy.wait()
        for start, stop, product in dot_tiles(left, mat, False, 256 * (3 if mode == "dot" else 1)):
            product = product.reshape(clips, rows, stop - start)
            if mode == "dot":
                stages[0][slot, :, :, start:stop] = product.astype(stages[0].dtype)
                continue
            width = stages[1].shape[3]
            gate = gates[slot, :, :, start:stop]
            up = gates[slot, :, :, width + start : width + stop]
            sigmoid = jax.nn.sigmoid(gate)
            active = gate * sigmoid
            low = stages[0].dtype
            stages[0][slot, :, :, start:stop] = (
                product * up * sigmoid * (1.0 + gate * (1.0 - sigmoid))
            ).astype(low)
            stages[0][slot, :, :, width + start : width + stop] = (product * active).astype(low)
            stages[1][slot, :, :, start:stop] = (active * up).astype(low)
        for which, (stage, prod_ref) in enumerate(zip(stages, prod_refs)):
            leave_here(stage, prod_ref, prod_sem.at[which], slot)

    if mode != "rows":
        load.wait()
    multiply(0)
    if beside:
        next(going)
    for step in range(count):
        x_index, y_index = x_order[step], y_order[step]
        arrived(beside_x, x_index)
        if x_index < half:
            send(beside_x, x_index, beside_y)
        send(beside_x, x_index, core)
        arrived(beside_y, y_index)
        if y_index >= half:
            send(beside_y, y_index, beside_x)
        send(beside_y, y_index, core)
        if step == 0:
            for index in range(count):
                arrived(core, index)
            multiply(1)
    multiply(2)
    for step in range(half):
        for index in (x_order[step], y_order[step]):
            arrived(across, index)
            send(across, index, core)
        if step == 0:
            multiply(4)
    for mask in (3, 5):
        for index in range(count):
            arrived(flip(mask), index)
        multiply(mask)
    multiply(6)
    for index in range(count):
        arrived(flip(7), index)
    multiply(7)
    if beside:
        next(going)
    for copy in outs:
        copy.wait()
    for copy in sends:
        copy.wait_send()


def gather_dot(
    own_rows,
    matrix,
    kind,
    collective_id,
    gains=None,
    picked=None,
    kept_rows=None,
    gate_up=None,
    sub=64,
):
    clips, rows, wide = own_rows.shape
    count = clips * (rows // sub)
    low = jnp.bfloat16
    mode = "rows" if matrix is None else "dot" if gate_up is None else "gates"
    inside = pl.BlockSpec(memory_space=pltpu.VMEM)
    by_clip = lambda columns, of: jax.ShapeDtypeStruct((clips, 8, rows, columns), of)
    by_device = lambda columns, of: jax.ShapeDtypeStruct((8, clips, rows, columns), of)
    args, in_specs = [own_rows], [inside]
    if gains is not None:
        args.append(gains)
        in_specs.append(inside)
    outs = [by_device(wide, low) if mode == "gates" else by_clip(wide, low)]
    scratch = [
        pltpu.VMEM((8, clips, rows, wide), low),
        DMA((7 * count,)),
        DMA((8, count)),
        DMA((8, clips)),
    ]
    if mode != "rows":
        columns = matrix.shape[1]
        args.append(matrix)
        in_specs.append(any_spec())
        scratch += [pltpu.VMEM(matrix.shape, low), DMA(())]
    if mode == "dot":
        outs.append(by_clip(columns, kind))
        scratch += [pltpu.VMEM((8, clips, rows, columns), kind), DMA((1, 8, clips))]
    if mode == "gates":
        args.append(gate_up.reshape(clips, 8, rows, 2 * columns))
        in_specs.append(any_spec())
        outs += [by_clip(2 * columns, low), by_device(columns, low)]
        scratch += [
            pltpu.VMEM((8, clips, rows, 2 * columns), low),
            pltpu.VMEM((8, clips, rows, columns), low),
            DMA((2, 8, clips)),
            pltpu.VMEM((8, clips, rows, 2 * columns), jnp.float32),
            DMA((8, clips)),
        ]
    out_specs = [any_spec()] * len(outs)
    mains = len(outs)
    beside = None
    if picked is not None:
        planes, per, tokens, cond_wide = picked.shape
        beside = ("cond", planes * per, planes)
        args.append(picked)
        in_specs.append(inside)
        outs.append(jax.ShapeDtypeStruct((8, per, tokens, cond_wide), picked.dtype))
        out_specs.append(inside)
        scratch += [
            pltpu.VMEM(picked.shape, picked.dtype),
            pltpu.VMEM(picked.shape[1:], picked.dtype),
            DMA((planes,)),
            DMA((planes,)),
            DMA((8,)),
            DMA((8,)),
        ]
    if kept_rows is not None:
        per, planes, piece, _ = kept_rows.shape
        beside = ("outward", planes * per, planes)
        args.append(kept_rows)
        in_specs.append(any_spec())
        outs += [jax.ShapeDtypeStruct((per * planes, piece, wide), kept_rows.dtype)] * 2
        out_specs += [any_spec()] * 2
        scratch += outward_scratch(*beside[1:])
    results = pl.pallas_call(
        functools.partial(
            gather_dot_body, clips, rows, sub, gains is not None, mode, beside
        ),
        out_shape=outs,
        in_specs=in_specs,
        out_specs=out_specs,
        scratch_shapes=scratch,
        compiler_params=communicating(collective_id),
    )(*args)
    flat = [block.reshape(clips * 8 * rows, block.shape[3]) for block in results[:mains]]
    return flat + list(results[mains : mains + 1])


def dot_reduce_body(clips, rows, sub, added, beside, left_ref, mat_ref, *refs):
    refs = list(refs)
    base_ref = refs.pop(0) if added else None
    kept_ref = refs.pop(0) if beside else None
    sum_ref = refs.pop(0)
    own_ref, mid = (refs.pop(0), refs.pop(0)) if beside else (None, None)
    left, mat, terms, pair, held, turn, from_x, from_y, *sems = refs
    mat_sem, left_sem, send_sem, core_sem, turn_sem, x_sem, y_sem, *extra = sems
    place, depth, flip = plane_places()
    core, beside_x, beside_y = flip(1), flip(2), flip(4)
    order = [flip(mask) for mask in (7, 6, 3, 2, 5, 4, 1, 0)]
    load = pltpu.make_async_copy(mat_ref, mat, mat_sem)
    load.start()
    loads = {}
    for number, slot in enumerate(order):
        loads[number] = [
            pltpu.make_async_copy(
                left_ref.at[clip, slot], left.at[number, clip], left_sem.at[number, clip]
            )
            for clip in range(clips)
        ]
        for copy in loads[number]:
            copy.start()
    if beside:
        greet_cross(*beside)
        going = outward_steps(*beside, kept_ref, own_ref, mid, *extra)
        next(going)
    else:
        greet([(core, depth), (beside_x, depth), (beside_y, depth)])
    chunks = [(clip, part) for clip in range(clips) for part in range(rows // sub)]
    count = len(chunks)
    half = count // 2
    sends = []

    def send(source, goal, recv_sem, device):
        copy = remote(source, goal, send_sem.at[len(sends)], recv_sem, (device, depth))
        copy.start()
        sends.append(copy)

    def arrived(block, recv_sem):
        remote(block, block, send_sem.at[0], recv_sem, (core, depth)).wait_recv()

    def term(number, index):
        clip, part = chunks[index]
        return terms.at[number, clip, pl.ds(part * sub, sub)]

    def multiply(number):
        for copy in loads[number]:
            copy.wait()
        block = left[number].reshape(clips * rows, left.shape[3])
        for start, stop, product in dot_tiles(block, mat, True, 256 * 2):
            terms[number, :, :, start:stop] = product.astype(terms.dtype).reshape(
                clips, rows, stop - start
            )

    def give(number, chip):
        for index in range(count):
            send(term(number, index), pair.at[index, chip], core_sem.at[index, chip], core)

    def total(*blocks):
        return sum(block[...].astype(jnp.float32) for block in blocks)

    numbers = {3: 1, 1: 3, 2: 5, 0: 7}

    def combine(chip, index):
        arrived(pair.at[index, chip], core_sem.at[index, chip])
        held[index, chip] = total(term(numbers[chip], index), pair.at[index, chip]).astype(
            held.dtype
        )

    load.wait()
    multiply(0)
    give(0, 3)
    multiply(1)
    multiply(2)
    give(2, 1)
    for low in range(half):
        high = half + low
        combine(3, low)
        send(held.at[low, 3], turn.at[low], turn_sem.at[low], beside_x)
        combine(3, high)
        send(held.at[high, 3], turn.at[high], turn_sem.at[high], beside_y)
    multiply(3)
    multiply(4)
    give(4, 2)
    for low in range(half):
        combine(1, low)
        send(held.at[low, 1], from_x.at[low], x_sem.at[low], beside_x)
    multiply(5)
    for high in range(half, count):
        combine(2, high)
        send(held.at[high, 2], from_y.at[high], y_sem.at[high], beside_y)
    multiply(6)
    give(6, 0)
    if beside:
        next(going)
    for low in range(half):
        high = half + low
        combine(2, low)
        arrived(turn.at[low], turn_sem.at[low])
        held[low, 2] = total(held.at[low, 2], turn.at[low]).astype(held.dtype)
        send(held.at[low, 2], from_y.at[low], y_sem.at[low], beside_y)
        combine(1, high)
        arrived(turn.at[high], turn_sem.at[high])
        held[high, 1] = total(held.at[high, 1], turn.at[high]).astype(held.dtype)
        send(held.at[high, 1], from_x.at[high], x_sem.at[high], beside_x)
    multiply(7)
    for index in range(count):
        clip, part = chunks[index]
        span = pl.ds(part * sub, sub)
        arrived(pair.at[index, 0], core_sem.at[index, 0])
        arrived(from_x.at[index], x_sem.at[index])
        arrived(from_y.at[index], y_sem.at[index])
        result = total(term(7, index), pair.at[index, 0], from_x.at[index], from_y.at[index])
        if added:
            result = base_ref[clip, span] + result
        sum_ref[clip, span] = result
    if beside:
        next(going)
    for copy in sends:
        copy.wait_send()


def dot_reduce(left, matrix, clips, collective_id, base=None, kept_rows=None, sub=64):
    wide, inner = matrix.shape
    rows = left.shape[0] // (8 * clips)
    count = clips * (rows // sub)
    low = jnp.bfloat16
    inside = pl.BlockSpec(memory_space=pltpu.VMEM)
    args = [left.reshape(clips, 8, rows, inner), matrix]
    in_specs = [any_spec(), any_spec()]
    outs, out_specs = [jax.ShapeDtypeStruct((clips, rows, wide), jnp.float32)], [inside]
    scratch = [
        pltpu.VMEM((8, clips, rows, inner), low),
        pltpu.VMEM(matrix.shape, low),
        pltpu.VMEM((8, clips, rows, wide), low),
        pltpu.VMEM((count, 4, sub, wide), low),
        pltpu.VMEM((count, 4, sub, wide), low),
        pltpu.VMEM((count, sub, wide), low),
        pltpu.VMEM((count, sub, wide), low),
        pltpu.VMEM((count, sub, wide), low),
        DMA(()),
        DMA((8, clips)),
        DMA((7 * count,)),
        DMA((count, 4)),
        DMA((count,)),
        DMA((count,)),
        DMA((count,)),
    ]
    if base is not None:
        args.append(base)
        in_specs.append(inside)
    beside = None
    if kept_rows is not None:
        per, planes, piece, _ = kept_rows.shape
        beside = (per * planes, planes)
        args.append(kept_rows)
        in_specs.append(any_spec())
        moved = jax.ShapeDtypeStruct((per * planes, piece, wide), kept_rows.dtype)
        outs += [moved, moved]
        out_specs += [any_spec(), any_spec()]
        scratch += outward_scratch(*beside)
    results = pl.pallas_call(
        functools.partial(dot_reduce_body, clips, rows, sub, base is not None, beside),
        out_shape=outs,
        in_specs=in_specs,
        out_specs=out_specs,
        scratch_shapes=scratch,
        compiler_params=communicating(collective_id),
    )(*args)
    return results[0] if kept_rows is None else results[:2]


def finish_body(planes, squares_ref, total_ref, blocks, block_send, block_recv):
    place, depth, flip = plane_places()
    devices = [(flip(mask), lax.rem(depth + step, planes)) for mask, step in everyone(planes)]
    greet(devices)
    here = place * planes + depth
    copies = []
    blocks[here] = squares_ref[...]
    for index, (other, plane) in enumerate(devices):
        copy = remote(
            squares_ref,
            blocks.at[here],
            block_send.at[index],
            block_recv.at[here],
            (other, plane),
        )
        copy.start()
        copies.append(copy)
    for other, plane in devices:
        source = other * planes + plane
        one = blocks.at[source]
        remote(one, one, block_send.at[0], block_recv.at[source], (other, plane)).wait_recv()
    total_ref[...] = jnp.sum(blocks[...], axis=0)
    for copy in copies:
        copy.wait_send()


def finish(squares, planes, collective_id):
    count = 8 * planes
    whole = pl.BlockSpec(memory_space=pltpu.VMEM)
    return pl.pallas_call(
        functools.partial(finish_body, planes),
        out_shape=jax.ShapeDtypeStruct(squares.shape, jnp.float32),
        in_specs=[whole],
        out_specs=whole,
        scratch_shapes=[
            pltpu.VMEM((count,) + squares.shape, jnp.float32),
            DMA((count,)),
            DMA((count,)),
        ],
        compiler_params=communicating(collective_id),
    )(squares)


def rotary_lanes(places):
    cosine, sine = rotary_tables(places, HDIM)
    cosine, sine = cosine[:, 0], sine[:, 0]
    return jnp.stack(
        [
            jnp.concatenate([cosine] * 4, axis=1),
            jnp.concatenate([-sine, sine, -sine, sine], axis=1),
        ]
    )


def turn_heads(values, cosine, sine):
    lane = lax.broadcasted_iota(jnp.int32, values.shape, 1)
    half = HDIM // 2
    ahead = pltpu.roll(values, 2 * HDIM - half, 1)
    behind = pltpu.roll(values, half, 1)
    other = jnp.where(lax.rem(lane, HDIM) < half, ahead, behind)
    return values * cosine + other * sine


def swap_beside(pairs, send_sem, recv_sem, local_sem):
    place, depth, flip = plane_places()

    def each(act):
        for which, (source, goal) in enumerate(pairs):
            for mask in (6, 7, 2, 3, 4, 5, 1):
                other = flip(mask)
                act(
                    remote(
                        source(other),
                        goal(place),
                        send_sem.at[which, mask],
                        recv_sem.at[which, mask],
                        (other, depth),
                    )
                )

    stays = [
        pltpu.make_async_copy(source(place), goal(place), local_sem.at[which])
        for which, (source, goal) in enumerate(pairs)
    ]

    def begin():
        each(lambda copy: copy.start())
        for stay in stays:
            stay.start()

    def end():
        each(lambda copy: copy.wait())
        for stay in stays:
            stay.wait()

    return begin, end


def swap_beside_scratch(count):
    return [DMA((count, 8)), DMA((count, 8)), DMA((count,))]


def flash_forward_body(
    heads,
    tile,
    normed_ref,
    mat_ref,
    stamp_ref,
    bias_ref,
    rotary_ref,
    ff_ref,
    own_ref,
    turned_ref,
    out_ref,
    lse_ref,
    gate_up_ref,
    down_ref,
    kept_ref,
    mid,
    raw_ref,
    *sems,
):
    group, planes = gate_up_ref.shape[0], kept_ref.shape[1]
    hidden = down_ref.shape[2]
    step, last = pl.program_id(0), pl.num_programs(0) - 1

    def columns(block):
        return lambda other: ff_ref.at[
            :, pl.ds(pl.multiple_of((block * group + other) * hidden, 128), hidden)
        ]

    start_swap, end_swap = swap_beside(
        [
            (columns(0), lambda other: gate_up_ref.at[other, :, pl.ds(0, hidden)]),
            (columns(1), lambda other: gate_up_ref.at[other, :, pl.ds(hidden, hidden)]),
            (columns(2), lambda other: down_ref.at[other]),
        ],
        *sems[:3],
    )
    start_rows, pass_rows, end_rows = inward_beside(
        group, planes, own_ref, kept_ref, mid, *sems[3:]
    )

    @pl.when(step == 0)
    def _():
        greet_cross(group, planes)
        start_rows()
        start_swap()

    @pl.when(step == last)
    def _():
        pass_rows()

    def project(index, carry):
        place = pl.ds(pl.multiple_of(index * tile, tile), tile)
        raw_ref[place, :] = jnp.dot(
            normed_ref[place, :], mat_ref[...], preferred_element_type=jnp.float32
        )
        return carry

    lax.fori_loop(0, raw_ref.shape[0] // tile, project, 0)
    wide = heads * HDIM
    for pair in range(2 * wide // 128):
        lanes = slice(pair * 128, pair * 128 + 128)
        turned_ref[:, lanes] = turn_heads(
            raw_ref[:, lanes], rotary_ref[0], rotary_ref[1]
        ).astype(turned_ref.dtype)
    turned_ref[:, 2 * wide :] = raw_ref[:, 2 * wide :].astype(turned_ref.dtype)
    rows = raw_ref.shape[0]
    bias = bias_ref[0]
    scale = HDIM**-0.5
    for head in range(heads):
        lanes = slice(head * HDIM, head * HDIM + HDIM)
        keys = turned_ref[:, wide + head * HDIM : wide + head * HDIM + HDIM]
        values = turned_ref[:, 2 * wide + head * HDIM : 2 * wide + head * HDIM + HDIM]
        stamp_key = stamp_ref[0, :, lanes].astype(jnp.float32)
        stamp_value = stamp_ref[
            0, :, wide + head * HDIM : wide + head * HDIM + HDIM
        ].astype(jnp.float32)

        def one(step, carry):
            place = pl.ds(pl.multiple_of(step * tile, tile), tile)
            query = turned_ref[place, lanes] * jnp.asarray(scale, turned_ref.dtype)
            scores = times_transposed(query, keys) + bias
            stamp_score = jnp.sum(query.astype(jnp.float32) * stamp_key, axis=1, keepdims=True)
            top = jnp.maximum(jnp.max(scores, axis=1, keepdims=True), stamp_score)
            expo = jnp.exp(scores - top)
            stamp_expo = jnp.exp(stamp_score - top)
            denom = jnp.sum(expo, axis=1, keepdims=True) + stamp_expo
            share = 1.0 / denom
            prob = (expo * share).astype(values.dtype)
            stamp_prob = (stamp_expo * share).astype(values.dtype).astype(jnp.float32)
            mixed = jnp.dot(prob, values, preferred_element_type=jnp.float32)
            out_ref[place, lanes] = (mixed + stamp_prob * stamp_value).astype(out_ref.dtype)
            lse_ref[place, head : head + 1] = top + jnp.log(denom)
            return carry

        lax.fori_loop(0, rows // tile, one, 0)

    @pl.when(step == last)
    def _():
        end_swap()
        end_rows()


def flash_forward(normed, matrix, stamps, bias, rotary, heads, ff_low, rows_of_clip, collective_id):
    clips, rows = bias.shape
    wide = heads * HDIM
    group, piece, features = rows_of_clip.shape
    planes = group // clips
    owned, columns = ff_low.shape
    hidden = columns // (3 * group)
    like = lambda *shape: jax.ShapeDtypeStruct(shape, rows_of_clip.dtype)
    blocked = lambda lanes: pl.BlockSpec((rows, lanes), lambda clip: (clip, 0))
    *results, _ = pl.pallas_call(
        functools.partial(flash_forward_body, heads, rows // 4),
        grid=(clips,),
        out_shape=[
            like(clips * rows, 3 * wide),
            like(clips * rows, wide),
            jax.ShapeDtypeStruct((clips * rows, 128), jnp.float32),
            like(group, owned, 2 * hidden),
            like(group, owned, hidden),
            like(clips, planes, piece, features),
            like(group, piece, features),
        ],
        in_specs=[
            blocked(features),
            pl.BlockSpec(matrix.shape, lambda clip: (0, 0)),
            pl.BlockSpec((1, 1, 2 * wide), lambda clip: (clip, 0, 0)),
            pl.BlockSpec((1, 1, rows), lambda clip: (clip, 0, 0)),
            pl.BlockSpec((2, rows, 128), lambda clip: (0, 0, 0)),
            any_spec(),
            any_spec(),
        ],
        out_specs=[blocked(3 * wide), blocked(wide), blocked(128)] + [any_spec()] * 4,
        scratch_shapes=[pltpu.VMEM((rows, 3 * wide), jnp.float32)]
        + swap_beside_scratch(3)
        + inward_scratch(group, planes),
        compiler_params=communicating(collective_id),
    )(normed, matrix, stamps[:, None], bias[:, None], rotary, ff_low, rows_of_clip)
    return results


def flash_backward_body(
    heads,
    tile,
    turned_ref,
    grad_ref,
    lse_ref,
    stamp_ref,
    bias_ref,
    rotary_ref,
    cut_ref,
    out_ref,
    stamp_out_ref,
    mine_ref,
    query_grad,
    key_grad,
    value_grad,
    *sems,
):
    place, depth, flip = plane_places()
    start_swap, end_swap = swap_beside(
        [(lambda other: cut_ref.at[other], lambda other: mine_ref.at[other])], *sems
    )

    @pl.when(pl.program_id(0) == 0)
    def _():
        greet([(flip(mask), depth) for mask in range(1, 8)])
        start_swap()

    wide = heads * HDIM
    rows = turned_ref.shape[0]
    scale = HDIM**-0.5
    low = turned_ref.dtype
    f32 = jnp.float32
    lse_rows = lse_ref[...].T
    first_row = lax.broadcasted_iota(jnp.int32, (8, tile), 0) == 0
    for head in range(heads):
        lanes = slice(head * HDIM, head * HDIM + HDIM)
        later = slice(wide + head * HDIM, wide + head * HDIM + HDIM)
        keys = turned_ref[:, later]
        values = turned_ref[:, 2 * wide + head * HDIM : 2 * wide + head * HDIM + HDIM]
        keys_across = keys.astype(f32).T.astype(low)
        stamp_key = jnp.broadcast_to(stamp_ref[0, :, lanes], (8, HDIM))
        stamp_value = jnp.broadcast_to(stamp_ref[0, :, later], (8, HDIM))
        stamp_column = stamp_ref[0, :, lanes].astype(f32).T
        bias = bias_ref[0]
        key_total = jnp.zeros((rows, HDIM), f32)
        value_total = jnp.zeros((rows, HDIM), f32)
        stamp_key_total = jnp.zeros((8, HDIM), f32)
        stamp_value_total = jnp.zeros((8, HDIM), f32)
        for step in range(rows // tile):
            place = slice(step * tile, step * tile + tile)
            query = turned_ref[place, lanes] * jnp.asarray(scale, low)
            grad = grad_ref[place, lanes]
            lse = lse_rows[head : head + 1, place]
            prob = jnp.exp(times_transposed(keys, query) + bias - lse)
            stamp_prob = jnp.exp(times_transposed(stamp_key, query) - lse)
            grad_prob = times_transposed(values, grad)
            stamp_grad_prob = times_transposed(stamp_value, grad)
            delta = jnp.sum(prob * grad_prob, axis=0, keepdims=True)
            delta = delta + (stamp_prob * stamp_grad_prob)[:1]
            scores = (prob * (grad_prob - delta)).astype(low)
            stamp_scores = (stamp_prob * (stamp_grad_prob - delta)).astype(low)
            stamp_scores = jnp.where(first_row, stamp_scores.astype(f32), 0.0)
            value_total += jnp.dot(prob.astype(low), grad, preferred_element_type=f32)
            key_total += jnp.dot(scores, query, preferred_element_type=f32)
            across = jnp.dot(keys_across, scores, preferred_element_type=f32)
            across = across + stamp_column * stamp_scores[:1]
            query_grad[place, lanes] = across.T * scale
            stamp_key_total += jnp.dot(
                stamp_scores.astype(low), query, preferred_element_type=f32
            )
            stamp_value_total += jnp.dot(
                jnp.where(first_row, stamp_prob, 0.0).astype(low), grad, preferred_element_type=f32
            )
        key_grad[:, lanes] = key_total
        value_grad[:, lanes] = value_total
        stamp_out_ref[0, :, lanes] = stamp_key_total[:1]
        stamp_out_ref[0, :, later] = stamp_value_total[:1]
    both = jnp.concatenate([query_grad[...], key_grad[...]], axis=1)
    for pair in range(2 * wide // 128):
        lanes = slice(pair * 128, pair * 128 + 128)
        out_ref[:, lanes] = turn_heads(both[:, lanes], rotary_ref[0], -rotary_ref[1]).astype(low)
    out_ref[:, 2 * wide :] = value_grad[...].astype(low)
    pl.when(pl.program_id(0) == pl.num_programs(0) - 1)(end_swap)


def flash_backward(turned, grad, lse, stamps, bias, rotary, heads, cut, collective_id):
    clips, rows = bias.shape
    wide = heads * HDIM
    blocked = lambda lanes: pl.BlockSpec((rows, lanes), lambda clip: (clip, 0))
    grads, stamp_grads, mine = pl.pallas_call(
        functools.partial(flash_backward_body, heads, rows // 4),
        grid=(clips,),
        out_shape=[
            jax.ShapeDtypeStruct((clips * rows, 3 * wide), jnp.bfloat16),
            jax.ShapeDtypeStruct((clips, 1, 2 * wide), jnp.float32),
            jax.ShapeDtypeStruct(cut.shape, cut.dtype),
        ],
        in_specs=[
            blocked(3 * wide),
            blocked(wide),
            blocked(128),
            pl.BlockSpec((1, 1, 2 * wide), lambda clip: (clip, 0, 0)),
            pl.BlockSpec((1, rows, 1), lambda clip: (clip, 0, 0)),
            pl.BlockSpec((2, rows, 128), lambda clip: (0, 0, 0)),
            any_spec(),
        ],
        out_specs=[
            blocked(3 * wide),
            pl.BlockSpec((1, 1, 2 * wide), lambda clip: (clip, 0, 0)),
            any_spec(),
        ],
        scratch_shapes=[pltpu.VMEM((rows, wide), jnp.float32)] * 3 + swap_beside_scratch(1),
        compiler_params=communicating(collective_id),
    )(turned, grad, lse, stamps[:, None], bias[:, :, None], rotary, cut)
    return grads, stamp_grads[:, 0], mine


def ff_outer_body(normed_ref, gates_ref, grads_ref, hidden_ref, out_ref):
    last = pl.program_id(0) == pl.num_programs(0) - 1

    @pl.when(jnp.logical_not(last))
    def _():
        out_ref[...] = outer_sum(normed_ref[...], gates_ref[...]).astype(out_ref.dtype)

    @pl.when(last)
    def _():
        out_ref[...] = outer_sum(grads_ref[...], hidden_ref[...]).astype(out_ref.dtype)


def ff_outer(normed, gates, grads, hidden):
    rows, wide = normed.shape
    width = hidden.shape[1]
    tile = wide // 3
    ends = gates.shape[1] // width
    return pl.pallas_call(
        ff_outer_body,
        grid=(ends + 1, wide // tile),
        out_shape=jax.ShapeDtypeStruct((wide, (ends + 1) * width), jnp.bfloat16),
        in_specs=[
            pl.BlockSpec(
                (rows, tile), lambda n, m: (0, jnp.where(n < ends, m, wide // tile - 1))
            ),
            pl.BlockSpec((rows, width), lambda n, m: (0, jnp.minimum(n, ends - 1))),
            pl.BlockSpec((rows, tile), lambda n, m: (0, jnp.where(n < ends, 0, m))),
            pl.BlockSpec((rows, width), lambda n, m: (0, 0)),
        ],
        out_specs=pl.BlockSpec((tile, width), lambda n, m: (m, n)),
        compiler_params=pltpu.CompilerParams(vmem_limit_bytes=VMEM_LIMIT),
    )(normed, gates, grads, hidden)


def adam_body(split, factor_ref, weight_ref, first_ref, second_ref, grad_ref, *outs):
    parts, _, held = grad_ref.shape
    width = held // split
    choices = [
        jnp.concatenate(
            [grad_ref[part, :, side * width : (side + 1) * width] for part in range(parts)], axis=1
        ).astype(jnp.float32)
        for side in range(split)
    ]
    gradient = choices[0]
    for side in range(1, split):
        gradient = jnp.where(lax.rem(pl.program_id(0), split) == side, choices[side], gradient)
    results = adam_step(
        weight_ref[...],
        first_ref[...],
        second_ref[...],
        gradient * factor_ref[0, 0],
        matrix_rate,
        matrix_decay,
    )
    for out, result in zip(outs, results):
        out[...] = result


def adam_matrix(factor, weight, first, second, owned, width, split, parts):
    rows, columns = weight.shape
    group = owned.shape[0]
    blocks = columns // (group * width)
    steps = group // parts
    piece = pl.BlockSpec((rows, parts * width), lambda block, step: (0, block * steps + step))
    grads = pl.BlockSpec(
        (parts, rows, split * width), lambda block, step: (step, 0, block // split)
    )
    return pl.pallas_call(
        functools.partial(adam_body, split),
        grid=(blocks, steps),
        out_shape=[jax.ShapeDtypeStruct(weight.shape, jnp.float32)] * 3,
        in_specs=[pl.BlockSpec(memory_space=pltpu.SMEM), piece, piece, piece, grads],
        out_specs=[piece] * 3,
        compiler_params=pltpu.CompilerParams(vmem_limit_bytes=VMEM_LIMIT),
    )(factor, weight, first, second, owned)


def plane_device(
    frames,
    time_token,
    cond_ids,
    cond_mask,
    lengths,
    cond_table,
    cotangent,
    attn_weight,
    cross_weight,
    norm_param,
    ff_weight,
    attn_first,
    attn_second,
    cross_first,
    cross_second,
    norm_first,
    norm_second,
    ff_first,
    ff_second,
):
    group, planes = lax.axis_size("dp"), lax.axis_size("seq")
    place, depth = lax.axis_index("dp"), lax.axis_index("seq")
    clips = group // planes
    _, frame_rows, wide = frames.shape
    piece = frame_rows // group
    seq_frames = frame_rows * planes
    own_rows = planes * piece
    heads = HEADS // group
    head_wide = heads * HDIM
    ff_wide = FF // group
    owned = wide // (group * planes)
    cond_count, cond_wide = cond_ids.shape[1], cond_table.shape[1]
    cond_owned = cross_weight.shape[0]

    order = jnp.arange(wide).reshape(group, planes, owned).swapaxes(0, 1).reshape(wide)
    order_mat = (jnp.arange(wide)[:, None] == order[None, :]).astype(jnp.bfloat16)

    def to_plane_order(values):
        return jnp.dot(values, order_mat, preferred_element_type=jnp.float32).astype(jnp.bfloat16)

    def to_whole_order(values):
        return times_transposed(values, order_mat)

    attn_low = attn_weight.astype(jnp.bfloat16).reshape(owned, 6, group, head_wide)
    attn_cut = attn_low.transpose(2, 0, 1, 3).reshape(group, owned, 6 * head_wide)
    cross_low = cross_weight.astype(jnp.bfloat16).reshape(cond_owned, 2, group, head_wide)
    cross_cut = cross_low.transpose(2, 0, 1, 3).reshape(group, owned, -1)
    norm_block = norm_param.astype(jnp.bfloat16).astype(jnp.float32)
    norm_block = jnp.pad(norm_block, ((0, 2), (0, 128 - owned)))
    pack = jnp.concatenate(
        [
            time_token.astype(jnp.float32),
            jnp.pad(cond_ids.astype(jnp.float32), ((0, 0), (0, wide - cond_count))),
            jnp.pad(cond_mask.astype(jnp.float32), ((0, 0), (0, wide - cond_count))),
            jnp.broadcast_to(lengths.astype(jnp.float32)[:, None], (1, wide)),
            jnp.zeros((4, wide), jnp.float32),
        ],
        axis=0,
    )
    stream, gain_rows, packs, qkv_mine, rest_mine = enter(
        to_plane_order(frames[0]).reshape(group, piece, wide),
        norm_block,
        pack,
        attn_cut[:, :, : 3 * head_wide],
        jnp.concatenate([attn_cut[:, :, 3 * head_wide :], cross_cut], axis=2),
        planes,
        1,
    )
    stream = stream.reshape(clips, own_rows, wide).astype(jnp.float32)
    ff_low = ff_weight.astype(jnp.bfloat16)

    def over_planes(block):
        return lax.all_gather(block.reshape(group * owned, -1), "seq", axis=0, tiled=True)

    w_qkv = over_planes(qkv_mine)
    w_rest = over_planes(rest_mine)
    w_self_out = w_rest[:, :head_wide]
    w_cross_query = w_rest[:, head_wide : 2 * head_wide]
    w_cross_out = w_rest[:, 2 * head_wide : 3 * head_wide]
    w_cond = w_rest[:, 3 * head_wide :].reshape(planes, group, cond_owned, -1)
    w_cond = jnp.swapaxes(w_cond, 0, 1).reshape(cond_wide, 2 * head_wide)
    plane_packs = lax.dynamic_slice_in_dim(packs, depth * clips, clips, axis=0)
    stamps = to_plane_order(plane_packs[:, 0].astype(jnp.bfloat16)).astype(jnp.float32)
    cond_keep = plane_packs[:, 2, :cond_count] > 0
    clip_lengths = plane_packs[:, 3, 0].astype(jnp.int32)
    share = cond_count // group
    all_ids = packs[:, 1, :cond_count].astype(jnp.int32)
    own_ids = lax.dynamic_slice_in_dim(all_ids, place * share, share, axis=1)
    vocab_rows = cond_table.shape[0]
    relative = own_ids - depth * vocab_rows
    inside = (relative >= 0) & (relative < vocab_rows)
    picked = jnp.take(cond_table, jnp.clip(relative, 0, vocab_rows - 1), axis=0)
    picked = jnp.where(inside[..., None], picked, jnp.zeros((), picked.dtype))
    picked = picked.reshape(planes, clips, share, cond_wide)
    positions = depth * frame_rows + jnp.arange(frame_rows)
    frame_valid = (positions[None, :] < lengths[:, None]).astype(cotangent.dtype)
    masked = to_plane_order((cotangent * frame_valid[..., None])[0])

    group_rows = clips * seq_frames
    row_place = jnp.arange(seq_frames)
    row_owner, row_rest = row_place // own_rows, row_place % own_rows
    true_place = (row_rest // piece) * frame_rows + row_owner * piece + row_rest % piece
    key_keep = true_place[None, :] < clip_lengths[:, None]
    group_shape = (clips, seq_frames, heads, HDIM)

    group_one, cond = gather_dot(stream, None, None, 5, gain_rows[0:2], picked)
    cond_flat = cond.swapaxes(0, 1).reshape(clips * cond_count, cond_wide)
    stamp_normed = layer_norm(stamps, gain_rows[0], gain_rows[1]).astype(jnp.bfloat16)
    stamp_pair = jnp.dot(stamp_normed, w_qkv[:, head_wide:], preferred_element_type=jnp.float32)
    stamp_pair = stamp_pair.astype(jnp.bfloat16)
    rotary = rotary_lanes(true_place)
    key_bias = jnp.where(key_keep, 0.0, masked_score)
    rotated, self_low, self_lse, gate_up_mine, down_mine, grad_out_low = flash_forward(
        group_one,
        w_qkv,
        stamp_pair,
        key_bias,
        rotary,
        heads,
        ff_low,
        masked.reshape(group, piece, wide),
        2,
    )
    grad_out_low = grad_out_low.reshape(clips, own_rows, wide)
    grad_out = grad_out_low.astype(jnp.float32)
    w_gate_up = over_planes(gate_up_mine)
    w_down = over_planes(down_mine)
    resid_one = dot_reduce(self_low, w_self_out, clips, 6, stream)
    group_two, cross_query = gather_dot(
        resid_one, w_cross_query, jnp.bfloat16, 7, gain_rows[2:4]
    )
    cross_query = cross_query.reshape(group_shape)
    cond_pair = jnp.dot(cond_flat, w_cond, preferred_element_type=jnp.float32)
    cond_pair = cond_pair.astype(jnp.bfloat16)
    cond_shape = (clips, cond_count, heads, HDIM)
    cross_keys = cond_pair[:, :head_wide].reshape(cond_shape)
    cross_values = cond_pair[:, head_wide:].reshape(cond_shape)
    cross_mixed, cross_lse = cross_forward(cross_query, cross_keys, cross_values, cond_keep)
    cross_out = cross_mixed.astype(jnp.bfloat16).reshape(group_rows, head_wide)
    resid_two = dot_reduce(cross_out, w_cross_out, clips, 8, resid_one)
    group_three, gate_up = gather_dot(resid_two, w_gate_up, jnp.float32, 9, gain_rows[4:6])
    gate_up, grad_out_low = lax.optimization_barrier((gate_up, grad_out_low))
    group_grad_out, grad_gate_up, hidden = gather_dot(
        grad_out_low, w_down, None, 10, gate_up=gate_up
    )
    branch = lax.psum_scatter(
        times_transposed(hidden, w_down)
        .astype(jnp.bfloat16)
        .reshape(group, clips, own_rows, wide),
        "dp",
        scatter_dimension=0,
        tiled=False,
    )
    layer_rows = (resid_two + branch.astype(jnp.float32)).astype(jnp.bfloat16)

    def over_rows(block):
        return lax.psum_scatter(
            block.astype(jnp.bfloat16), "seq", scatter_dimension=0, tiled=True
        ).reshape(group, owned, -1)

    ff_piece = ff_outer(group_three, grad_gate_up, group_grad_out, hidden)
    grad_gate_up, ff_piece = lax.optimization_barrier((grad_gate_up, ff_piece))
    ff_rows = over_rows(ff_piece)
    grad_normed_three = dot_reduce(grad_gate_up, w_gate_up, clips, 13)

    _, norm_three_back = jax.vjp(layer_norm, resid_two, gain_rows[4], gain_rows[5])
    grad_two_part, grad_gain_three, grad_bias_three = norm_three_back(grad_normed_three)
    grad_two = grad_out + grad_two_part
    group_cross_branch, grad_cross_mixed = gather_dot(
        grad_two.astype(jnp.bfloat16), w_cross_out, jnp.bfloat16, 15
    )
    grad_cross_mixed = grad_cross_mixed.reshape(group_shape)
    grad_cross_query, grad_cross_keys, grad_cross_values = cross_backward(
        cross_query, cross_keys, cross_values, cond_keep, cross_lse, grad_cross_mixed
    )
    grad_cross_query = grad_cross_query.astype(jnp.bfloat16).reshape(group_rows, head_wide)
    grad_normed_two = dot_reduce(grad_cross_query, w_cross_query, clips, 16)
    _, norm_two_back = jax.vjp(layer_norm, resid_one, gain_rows[2], gain_rows[3])
    grad_one_part, grad_gain_two, grad_bias_two = norm_two_back(grad_normed_two)
    grad_one = grad_two + grad_one_part
    group_self_branch, grad_self_mixed, layer_out = gather_dot(
        grad_one.astype(jnp.bfloat16),
        w_self_out,
        jnp.bfloat16,
        17,
        kept_rows=layer_rows.reshape(clips, planes, piece, wide),
    )
    layer_out = to_whole_order(layer_out.reshape(frame_rows, wide)).astype(jnp.bfloat16)
    layer_out = layer_out.reshape(frames.shape)
    cond_grad = jnp.concatenate(
        [
            grad_cross_keys.reshape(clips * cond_count, head_wide),
            grad_cross_values.reshape(clips * cond_count, head_wide),
        ],
        axis=1,
    )
    cross_piece = split_outer(cond_flat, cond_grad)
    cross_piece = cross_piece.reshape(group, planes, cond_owned, 2 * head_wide)
    cross_piece = jnp.swapaxes(cross_piece, 0, 1).reshape(wide, head_wide)
    rest_piece = jnp.concatenate(
        [
            outer_sum(group_self_branch, self_low),
            outer_sum(group_two, grad_cross_query),
            outer_sum(group_cross_branch, cross_out),
            cross_piece,
        ],
        axis=1,
    )
    rest_piece = rest_piece.astype(jnp.bfloat16)
    grad_self_mixed, rest_piece = lax.optimization_barrier((grad_self_mixed, rest_piece))
    rest_piece, ff_rows = lax.optimization_barrier((rest_piece, ff_rows))
    rest_rows = over_rows(rest_piece)
    grad_project, stamp_grad, ff_owned = flash_backward(
        rotated, grad_self_mixed, self_lse, stamp_pair, key_bias, rotary, heads, ff_rows, 3
    )
    grad_stamp_normed = split_times_transposed(stamp_grad, w_qkv[:, head_wide:])
    qkv_piece = outer_sum(group_one, grad_project)
    stamp_weight_grad = split_outer(stamp_normed, stamp_grad)
    qkv_piece = jnp.concatenate(
        [qkv_piece[:, :head_wide], qkv_piece[:, head_wide:] + stamp_weight_grad], axis=1
    )
    qkv_piece = qkv_piece.astype(jnp.bfloat16)
    grad_project, qkv_piece = lax.optimization_barrier((grad_project, qkv_piece))
    qkv_rows = over_rows(qkv_piece)
    grad_project, rest_rows = lax.optimization_barrier((grad_project, rest_rows))
    grad_normed_one = dot_reduce(grad_project, w_qkv, clips, 18)
    _, norm_one_back = jax.vjp(layer_norm, stream, gain_rows[0], gain_rows[1])
    grad_zero_part, grad_gain_one, grad_bias_one = norm_one_back(grad_normed_one)
    _, norm_stamp_back = jax.vjp(layer_norm, stamps, gain_rows[0], gain_rows[1])
    _, grad_gain_stamp, grad_bias_stamp = norm_stamp_back(grad_stamp_normed)
    frames_grad = (grad_one + grad_zero_part).astype(jnp.bfloat16)
    norm_grad = jnp.stack(
        [
            grad_gain_one + grad_gain_stamp,
            grad_bias_one + grad_bias_stamp,
            grad_gain_two,
            grad_bias_two,
            grad_gain_three,
            grad_bias_three,
        ],
        axis=0,
    )
    norm_parts = norm_grad.reshape(6, planes, group, owned).transpose(2, 1, 0, 3)
    norm_parts = norm_parts.reshape(group * planes, 6, owned)
    norm_parts = jnp.pad(norm_parts, ((0, 0), (0, 2), (0, 128 - owned)))
    frames_grad, attn_owned, norm_sum = leave(
        frames_grad.reshape(clips, planes, piece, wide),
        jnp.concatenate([qkv_rows, rest_rows], axis=2),
        norm_parts,
        20,
    )
    frames_grad = to_whole_order(frames_grad.reshape(frame_rows, wide)).reshape(frames.shape)
    cross_reduced = attn_owned[:, :, 6 * head_wide :].reshape(group, cond_owned, 2, head_wide)
    cross_reduced = cross_reduced.transpose(1, 2, 0, 3).reshape(cross_weight.shape)
    cross_reduced = cross_reduced.astype(jnp.float32)
    squares = jnp.sum(jnp.square(attn_owned.astype(jnp.float32)))
    squares = squares + jnp.sum(jnp.square(ff_owned.astype(jnp.float32)))
    squares = squares + jnp.sum(jnp.square(norm_sum))
    total = finish(jnp.broadcast_to(squares, (8, 128)), planes, 21)
    norm_reduced = norm_sum[:6, :owned]
    grad_norm = jnp.sqrt(total[0, 0])
    factor = jnp.minimum(1.0, clip_limit / grad_norm)
    factor_block = factor.reshape(1, 1)
    attn_new, attn_first_new, attn_second_new = adam_matrix(
        factor_block, attn_weight, attn_first, attn_second, attn_owned, head_wide, 2, group
    )
    cross_new, cross_first_new, cross_second_new = adam_step(
        cross_weight, cross_first, cross_second, cross_reduced * factor, matrix_rate, matrix_decay
    )
    norm_new, norm_first_new, norm_second_new = adam_step(
        norm_param, norm_first, norm_second, norm_reduced * factor, gain_rate, 0.0
    )
    ff_new, ff_first_new, ff_second_new = adam_matrix(
        factor_block, ff_weight, ff_first, ff_second, ff_owned, ff_wide, 1, group // 2
    )
    return (
        layer_out,
        frames_grad,
        grad_norm,
        attn_new,
        cross_new,
        norm_new,
        ff_new,
        attn_first_new,
        cross_first_new,
        norm_first_new,
        ff_first_new,
        attn_second_new,
        cross_second_new,
        norm_second_new,
        ff_second_new,
    )


def solution(mesh):
    return jax.shard_map(
        plane_device if plane_fits(mesh) else per_device,
        mesh=mesh,
        in_specs=(
            P("dp", "seq", None),
            P("dp", None),
            P("dp", None),
            P("dp", None),
            P("dp"),
            P("seq", None),
            P("dp", "seq", None),
            P(("dp", "seq"), None),
            P(("dp", "seq"), None),
            P(None, ("dp", "seq")),
            P(("dp", "seq"), None),
            P(("dp", "seq"), None),
            P(("dp", "seq"), None),
            P(("dp", "seq"), None),
            P(("dp", "seq"), None),
            P(None, ("dp", "seq")),
            P(None, ("dp", "seq")),
            P(("dp", "seq"), None),
            P(("dp", "seq"), None),
        ),
        out_specs=(
            P("dp", "seq", None),
            P("dp", "seq", None),
            P(),
            P(("dp", "seq"), None),
            P(("dp", "seq"), None),
            P(None, ("dp", "seq")),
            P(("dp", "seq"), None),
            P(("dp", "seq"), None),
            P(("dp", "seq"), None),
            P(None, ("dp", "seq")),
            P(("dp", "seq"), None),
            P(("dp", "seq"), None),
            P(("dp", "seq"), None),
            P(None, ("dp", "seq")),
            P(("dp", "seq"), None),
        ),
        check_vma=False,
    )
```

```python
import functools

import jax
import jax.numpy as jnp
import numpy as np
from jax import lax
from jax.experimental import pallas as pl
from jax.experimental.pallas import tpu as pltpu
from jax.sharding import PartitionSpec as P

HEADS = 24
HDIM = 64
FF = 6144
UPDATE_STEP = 10


norm_eps = 1e-05
beta_first = 0.5
beta_second = 0.5
adam_eps = 1e-08
matrix_decay = 0.01
matrix_rate = 0.03
gain_rate = 0.25
clip_limit = 1.0
masked_score = -1e30


def layer_norm(values, gain_row, bias_row):
    center = values - jnp.mean(values, axis=-1, keepdims=True)
    spread = jnp.mean(center * center, axis=-1, keepdims=True)
    return center * lax.rsqrt(spread + norm_eps) * gain_row + bias_row


def rotary_tables(positions, head_size):
    half_size = head_size // 2
    frequency = 10000.0 ** (-jnp.arange(half_size, dtype=jnp.float32) / half_size)
    angles = positions.astype(jnp.float32)[:, None] * frequency[None, :]
    return (jnp.cos(angles)[:, None, :], jnp.sin(angles)[:, None, :])


def rotate(values, cosine_table, sine_table):
    half_size = values.shape[-1] // 2
    first_half = values[..., :half_size]
    second_half = values[..., half_size:]
    return jnp.concatenate(
        [
            first_half * cosine_table - second_half * sine_table,
            second_half * cosine_table + first_half * sine_table,
        ],
        axis=-1,
    )


def outer_sum(left_mat, right_mat):
    return lax.dot_general(
        left_mat, right_mat, (((0,), (0,)), ((), ())), preferred_element_type=jnp.float32
    )


def times_transposed(left_mat, right_mat):
    return lax.dot_general(
        left_mat, right_mat, (((1,), (1,)), ((), ())), preferred_element_type=jnp.float32
    )


def split_parts(values):
    upper = values.astype(jnp.bfloat16)
    lower = (values - upper.astype(jnp.float32)).astype(jnp.bfloat16)
    return (upper, lower)


def split_outer(left_low, right_full):
    upper, lower = split_parts(right_full)
    return outer_sum(left_low, upper) + outer_sum(left_low, lower)


def split_times_transposed(left_full, right_low):
    upper, lower = split_parts(left_full)
    return times_transposed(upper, right_low) + times_transposed(lower, right_low)


def self_scores(queries, keys, stamp_key, keep):
    score_scale = HDIM ** (-0.5)
    frame_part = (
        jnp.einsum("cqhd,ckhd->chqk", queries, keys, preferred_element_type=jnp.float32)
        * score_scale
    )
    frame_part = jnp.where(keep[:, None, None, :], frame_part, masked_score)
    stamp_part = (
        jnp.einsum("cqhd,chd->chq", queries, stamp_key, preferred_element_type=jnp.float32)
        * score_scale
    )
    return (frame_part, stamp_part)


def self_forward(queries, keys, values, stamp_key, stamp_value, keep):
    frame_scores, stamp_scores = self_scores(queries, keys, stamp_key, keep)
    top_score = jnp.maximum(jnp.max(frame_scores, axis=-1), stamp_scores)
    frame_expo = jnp.exp(frame_scores - top_score[..., None])
    stamp_expo = jnp.exp(stamp_scores - top_score)
    denom = jnp.sum(frame_expo, axis=-1) + stamp_expo
    self_lse = top_score + jnp.log(denom)
    frame_prob = (frame_expo / denom[..., None]).astype(jnp.bfloat16)
    stamp_prob = (stamp_expo / denom).astype(jnp.bfloat16)
    mixed = jnp.einsum(
        "chqk,ckhd->cqhd", frame_prob, values, preferred_element_type=jnp.float32
    ) + jnp.einsum("chq,chd->cqhd", stamp_prob, stamp_value, preferred_element_type=jnp.float32)
    return (mixed, self_lse)


def self_backward(queries, keys, values, stamp_key, stamp_value, keep, self_lse, grad_mixed):
    score_scale = HDIM ** (-0.5)
    frame_scores, stamp_scores = self_scores(queries, keys, stamp_key, keep)
    frame_prob = jnp.exp(frame_scores - self_lse[..., None])
    stamp_prob = jnp.exp(stamp_scores - self_lse)
    grad_frame_prob = jnp.einsum(
        "cqhd,ckhd->chqk", grad_mixed, values, preferred_element_type=jnp.float32
    )
    grad_stamp_prob = jnp.einsum(
        "cqhd,chd->chq", grad_mixed, stamp_value, preferred_element_type=jnp.float32
    )
    delta = jnp.sum(frame_prob * grad_frame_prob, axis=-1) + stamp_prob * grad_stamp_prob
    grad_frame_scores = (frame_prob * (grad_frame_prob - delta[..., None])).astype(jnp.bfloat16)
    grad_stamp_scores = (stamp_prob * (grad_stamp_prob - delta)).astype(jnp.bfloat16)
    grad_queries = (
        jnp.einsum("chqk,ckhd->cqhd", grad_frame_scores, keys, preferred_element_type=jnp.float32)
        + jnp.einsum(
            "chq,chd->cqhd", grad_stamp_scores, stamp_key, preferred_element_type=jnp.float32
        )
    ) * score_scale
    key_part = (
        jnp.einsum(
            "chqk,cqhd->ckhd", grad_frame_scores, queries, preferred_element_type=jnp.float32
        )
        * score_scale
    )
    value_part = jnp.einsum(
        "chqk,cqhd->ckhd",
        frame_prob.astype(jnp.bfloat16),
        grad_mixed,
        preferred_element_type=jnp.float32,
    )
    grad_stamp_key = (
        jnp.einsum("chq,cqhd->chd", grad_stamp_scores, queries, preferred_element_type=jnp.float32)
        * score_scale
    )
    grad_stamp_value = jnp.einsum(
        "chq,cqhd->chd",
        stamp_prob.astype(jnp.bfloat16),
        grad_mixed,
        preferred_element_type=jnp.float32,
    )
    return (grad_queries, key_part, value_part, grad_stamp_key, grad_stamp_value)


def cross_scores(query, keys, keep):
    score_scale = HDIM ** (-0.5)
    scores = (
        jnp.einsum("cqhd,ckhd->chqk", query, keys, preferred_element_type=jnp.float32) * score_scale
    )
    return jnp.where(keep[:, None, None, :], scores, masked_score)


def cross_forward(query, keys, values, keep):
    scores = cross_scores(query, keys, keep)
    top_score = jnp.max(scores, axis=-1)
    expo = jnp.exp(scores - top_score[..., None])
    denom = jnp.sum(expo, axis=-1)
    cross_lse = top_score + jnp.log(denom)
    prob = (expo / denom[..., None]).astype(jnp.bfloat16)
    mixed = jnp.einsum("chqk,ckhd->cqhd", prob, values, preferred_element_type=jnp.float32)
    return (mixed, cross_lse)


def cross_backward(query, keys, values, keep, cross_lse, grad_mixed):
    score_scale = HDIM ** (-0.5)
    prob = jnp.exp(cross_scores(query, keys, keep) - cross_lse[..., None])
    grad_prob = jnp.einsum(
        "cqhd,ckhd->chqk", grad_mixed, values, preferred_element_type=jnp.float32
    )
    delta = jnp.sum(prob * grad_prob, axis=-1)
    grad_scores = (prob * (grad_prob - delta[..., None])).astype(jnp.bfloat16)
    grad_query = (
        jnp.einsum("chqk,ckhd->cqhd", grad_scores, keys, preferred_element_type=jnp.float32)
        * score_scale
    )
    grad_keys = (
        jnp.einsum("chqk,cqhd->ckhd", grad_scores, query, preferred_element_type=jnp.float32)
        * score_scale
    )
    grad_values = jnp.einsum(
        "chqk,cqhd->ckhd", prob.astype(jnp.bfloat16), grad_mixed, preferred_element_type=jnp.float32
    )
    return (grad_query, grad_keys, grad_values)


def adam_step(weight, first, second, gradient, step_rate, decay_rate):
    first_new = beta_first * first + (1.0 - beta_first) * gradient
    second_new = beta_second * second + (1.0 - beta_second) * gradient * gradient
    fix_first = 1.0 - beta_first**UPDATE_STEP
    fix_second = 1.0 - beta_second**UPDATE_STEP
    normed_step = first_new / fix_first / (jnp.sqrt(second_new / fix_second) + adam_eps)
    return (weight - step_rate * (normed_step + decay_rate * weight), first_new, second_new)


def per_device(
    frames,
    time_token,
    cond_ids,
    cond_mask,
    lengths,
    cond_table,
    cotangent,
    attn_weight,
    cross_weight,
    norm_param,
    ff_weight,
    attn_first,
    attn_second,
    cross_first,
    cross_second,
    norm_first,
    norm_second,
    ff_first,
    ff_second,
):
    clip_count, frame_rows, wide = frames.shape
    hidden_width = FF
    token_count = clip_count * frame_rows
    seq_count = lax.axis_size("seq")
    seq_frames = frame_rows * seq_count
    seq_place = lax.axis_index("seq")
    vocab_rows = cond_table.shape[0]
    relative = cond_ids - seq_place * vocab_rows
    inside = (relative >= 0) & (relative < vocab_rows)
    picked = jnp.take(cond_table, jnp.clip(relative, 0, vocab_rows - 1), axis=0).astype(jnp.float32)
    picked = jnp.where(inside[..., None], picked, 0.0)
    cond = lax.psum(picked.astype(jnp.bfloat16), "seq")
    cond_count = cond.shape[1]
    cond_flat = cond.reshape(clip_count * cond_count, cond.shape[2])
    cond_width = cond.shape[2]
    cond_keep = cond_mask > 0
    attn_low = attn_weight.astype(jnp.bfloat16)
    cross_low = cross_weight.astype(jnp.bfloat16)
    norm_low = norm_param.astype(jnp.bfloat16)
    ff_low = ff_weight.astype(jnp.bfloat16)
    stream = frames.astype(jnp.float32).reshape(token_count, wide)
    stamps = time_token.astype(jnp.float32)
    positions = seq_place * frame_rows + jnp.arange(frame_rows)
    key_keep = jnp.arange(seq_frames)[None, :] < lengths[:, None]
    frame_valid = (positions[None, :] < lengths[:, None]).reshape(token_count)
    grad_out = cotangent.astype(jnp.float32).reshape(token_count, wide) * frame_valid[
        :, None
    ].astype(jnp.float32)
    grad_out_low = grad_out.astype(jnp.bfloat16)
    piece_heads = HEADS // seq_count
    piece_wide = wide // seq_count
    piece_ff = hidden_width // seq_count
    group_rows = clip_count * seq_frames

    def pieces():
        norm_copies = jnp.tile(norm_low[None], (1, 1, seq_count))
        moved_attn, moved_cross, moved_ff, moved_norm = (
            lax.all_to_all(
                attn_low.reshape(-1, 6, wide), "seq", split_axis=2, concat_axis=0, tiled=True
            ),
            lax.all_to_all(
                cross_low.reshape(-1, 2, wide), "seq", split_axis=2, concat_axis=0, tiled=True
            ),
            lax.all_to_all(
                ff_low.reshape(-1, 3, hidden_width), "seq", split_axis=2, concat_axis=0, tiled=True
            ),
            lax.all_to_all(norm_copies, "seq", split_axis=2, concat_axis=0, tiled=True),
        )
        attn_cols, cross_cols, ff_cols, norm_blocks = (
            lax.all_gather(moved_attn, "dp", axis=0, tiled=True),
            lax.all_gather(moved_cross, "dp", axis=0, tiled=True),
            lax.all_gather(moved_ff, "dp", axis=0, tiled=True),
            lax.all_gather(moved_norm, "dp", axis=0, tiled=True),
        )
        gains = norm_blocks.transpose(1, 0, 2).reshape(6, wide).astype(jnp.float32)
        return (attn_cols, cross_cols, ff_cols, gains)

    def collect(rows):
        whole = lax.all_gather(
            rows.reshape(clip_count, frame_rows, wide), "seq", axis=1, tiled=True
        )
        return whole.reshape(group_rows, wide)

    def spread(partial_value):
        mine = lax.psum_scatter(
            partial_value.reshape(clip_count, seq_frames, wide).astype(jnp.bfloat16),
            "seq",
            scatter_dimension=1,
            tiled=True,
        ).astype(jnp.float32)
        return mine.reshape(token_count, wide)

    attn_cols, cross_cols, ff_cols, gain_rows = pieces()
    group_shape = (clip_count, seq_frames, piece_heads, HDIM)
    cosine_table, sine_table = rotary_tables(jnp.arange(seq_frames), HDIM)
    normed_one = layer_norm(stream, gain_rows[0], gain_rows[1]).astype(jnp.bfloat16)
    group_one = collect(normed_one)
    projected = jnp.dot(
        group_one,
        attn_cols[:, :3].reshape(wide, 3 * piece_wide),
        preferred_element_type=jnp.float32,
    )
    queries = rotate(
        projected[:, :piece_wide].reshape(group_shape), cosine_table, sine_table
    ).astype(jnp.bfloat16)
    all_keys = rotate(
        projected[:, piece_wide : 2 * piece_wide].reshape(group_shape), cosine_table, sine_table
    ).astype(jnp.bfloat16)
    all_values = projected[:, 2 * piece_wide :].astype(jnp.bfloat16).reshape(group_shape)
    stamp_normed = layer_norm(stamps, gain_rows[0], gain_rows[1]).astype(jnp.bfloat16)
    stamp_pair = jnp.dot(
        stamp_normed,
        attn_cols[:, 1:3].reshape(wide, 2 * piece_wide),
        preferred_element_type=jnp.float32,
    )
    stamp_key = (
        stamp_pair[:, :piece_wide].astype(jnp.bfloat16).reshape(clip_count, piece_heads, HDIM)
    )
    stamp_value = (
        stamp_pair[:, piece_wide:].astype(jnp.bfloat16).reshape(clip_count, piece_heads, HDIM)
    )
    self_mixed, self_lse = self_forward(
        queries, all_keys, all_values, stamp_key, stamp_value, key_keep
    )
    self_low = self_mixed.astype(jnp.bfloat16).reshape(group_rows, piece_wide)
    resid_one = stream + spread(times_transposed(self_low, attn_cols[:, 3]))
    normed_two = layer_norm(resid_one, gain_rows[2], gain_rows[3]).astype(jnp.bfloat16)
    group_two = collect(normed_two)
    cross_query = jnp.dot(group_two, attn_cols[:, 4], preferred_element_type=jnp.float32)
    cross_query = cross_query.astype(jnp.bfloat16).reshape(group_shape)
    cond_pair = jnp.dot(
        cond_flat,
        cross_cols.reshape(cond_width, 2 * piece_wide),
        preferred_element_type=jnp.float32,
    )
    cond_shape = (clip_count, cond_count, piece_heads, HDIM)
    cross_keys = cond_pair[:, :piece_wide].astype(jnp.bfloat16).reshape(cond_shape)
    cross_values = cond_pair[:, piece_wide:].astype(jnp.bfloat16).reshape(cond_shape)
    cross_mixed, cross_lse = cross_forward(cross_query, cross_keys, cross_values, cond_keep)
    cross_low_out = cross_mixed.astype(jnp.bfloat16).reshape(group_rows, piece_wide)
    resid_two = resid_one + spread(times_transposed(cross_low_out, attn_cols[:, 5]))
    normed_three = layer_norm(resid_two, gain_rows[4], gain_rows[5]).astype(jnp.bfloat16)
    group_three = collect(normed_three)
    gate_up = jnp.dot(
        group_three, ff_cols[:, :2].reshape(wide, 2 * piece_ff), preferred_element_type=jnp.float32
    )
    gate_val = gate_up[:, :piece_ff]
    up_val = gate_up[:, piece_ff:]
    hidden = (jax.nn.silu(gate_val) * up_val).astype(jnp.bfloat16)
    branch = spread(times_transposed(hidden, ff_cols[:, 2]))
    layer_out = (resid_two + branch).astype(jnp.bfloat16).reshape(clip_count, frame_rows, wide)
    attn_cols, cross_cols, ff_cols, gain_rows = pieces()
    group_grad_out = collect(grad_out_low)
    grad_hidden = jnp.dot(group_grad_out, ff_cols[:, 2], preferred_element_type=jnp.float32)
    sigmoid_gate = jax.nn.sigmoid(gate_val)
    grad_gate = grad_hidden * up_val * sigmoid_gate * (1.0 + gate_val * (1.0 - sigmoid_gate))
    grad_up = grad_hidden * gate_val * sigmoid_gate
    grad_gate_up = jnp.concatenate([grad_gate, grad_up], axis=1).astype(jnp.bfloat16)
    grad_normed_three = spread(
        times_transposed(grad_gate_up, ff_cols[:, :2].reshape(wide, 2 * piece_ff))
    )
    _, norm_three_back = jax.vjp(layer_norm, resid_two, gain_rows[4], gain_rows[5])
    grad_two_part, grad_gain_three, grad_bias_three = norm_three_back(grad_normed_three)
    grad_two = grad_out + grad_two_part
    grad_cross_branch = grad_two.astype(jnp.bfloat16)
    group_cross_branch = collect(grad_cross_branch)
    grad_cross_mixed = jnp.dot(
        group_cross_branch, attn_cols[:, 5], preferred_element_type=jnp.float32
    )
    grad_cross_mixed = grad_cross_mixed.astype(jnp.bfloat16).reshape(group_shape)
    grad_cross_query, grad_cross_keys, grad_cross_values = cross_backward(
        cross_query, cross_keys, cross_values, cond_keep, cross_lse, grad_cross_mixed
    )
    grad_cross_query = grad_cross_query.astype(jnp.bfloat16).reshape(group_rows, piece_wide)
    grad_normed_two = spread(times_transposed(grad_cross_query, attn_cols[:, 4]))
    _, norm_two_back = jax.vjp(layer_norm, resid_one, gain_rows[2], gain_rows[3])
    grad_one_part, grad_gain_two, grad_bias_two = norm_two_back(grad_normed_two)
    grad_one = grad_two + grad_one_part
    grad_self_branch = grad_one.astype(jnp.bfloat16)
    group_self_branch = collect(grad_self_branch)
    grad_self_mixed = jnp.dot(
        group_self_branch, attn_cols[:, 3], preferred_element_type=jnp.float32
    )
    grad_self_mixed = grad_self_mixed.astype(jnp.bfloat16).reshape(group_shape)
    grad_queries, key_part, value_part, grad_stamp_key, grad_stamp_value = self_backward(
        queries, all_keys, all_values, stamp_key, stamp_value, key_keep, self_lse, grad_self_mixed
    )
    grad_query_raw = (
        rotate(grad_queries, cosine_table, -sine_table)
        .astype(jnp.bfloat16)
        .reshape(group_rows, piece_wide)
    )
    grad_key_raw = (
        rotate(key_part, cosine_table, -sine_table)
        .astype(jnp.bfloat16)
        .reshape(group_rows, piece_wide)
    )
    grad_value = value_part.astype(jnp.bfloat16).reshape(group_rows, piece_wide)
    grad_project = jnp.concatenate([grad_query_raw, grad_key_raw, grad_value], axis=1)
    grad_normed_one = spread(
        times_transposed(grad_project, attn_cols[:, :3].reshape(wide, 3 * piece_wide))
    )
    stamp_grad = jnp.concatenate(
        [
            grad_stamp_key.reshape(clip_count, piece_wide),
            grad_stamp_value.reshape(clip_count, piece_wide),
        ],
        axis=1,
    )
    grad_stamp_normed = split_times_transposed(
        stamp_grad, attn_cols[:, 1:3].reshape(wide, 2 * piece_wide)
    )
    _, norm_one_back = jax.vjp(layer_norm, stream, gain_rows[0], gain_rows[1])
    grad_zero_part, grad_gain_one, grad_bias_one = norm_one_back(grad_normed_one)
    _, norm_stamp_back = jax.vjp(layer_norm, stamps, gain_rows[0], gain_rows[1])
    _, grad_gain_stamp, grad_bias_stamp = norm_stamp_back(grad_stamp_normed)
    frames_grad = (grad_one + grad_zero_part).reshape(clip_count, frame_rows, wide)
    project_grad = outer_sum(group_one, grad_project)
    stamp_weight_grad = split_outer(stamp_normed, stamp_grad)
    attn_piece = jnp.stack(
        [
            project_grad[:, :piece_wide],
            project_grad[:, piece_wide : 2 * piece_wide] + stamp_weight_grad[:, :piece_wide],
            project_grad[:, 2 * piece_wide :] + stamp_weight_grad[:, piece_wide:],
            outer_sum(group_self_branch, self_low),
            outer_sum(group_two, grad_cross_query),
            outer_sum(group_cross_branch, cross_low_out),
        ],
        axis=1,
    )
    cond_grad = jnp.concatenate(
        [
            grad_cross_keys.reshape(clip_count * cond_count, piece_wide),
            grad_cross_values.reshape(clip_count * cond_count, piece_wide),
        ],
        axis=1,
    )
    cross_piece = split_outer(cond_flat, cond_grad).reshape(cond_width, 2, piece_wide)
    ff_piece = jnp.stack(
        [
            outer_sum(group_three, grad_gate_up[:, :piece_ff]),
            outer_sum(group_three, grad_gate_up[:, piece_ff:]),
            outer_sum(group_grad_out, hidden),
        ],
        axis=1,
    )
    norm_grad = jnp.stack(
        [
            grad_gain_one + grad_gain_stamp,
            grad_bias_one + grad_bias_stamp,
            grad_gain_two,
            grad_bias_two,
            grad_gain_three,
            grad_bias_three,
        ],
        axis=0,
    )
    norm_column = norm_grad.T[:, :, None]
    summed_attn, summed_cross, summed_ff, summed_norm = (
        lax.psum_scatter(
            attn_piece.astype(jnp.bfloat16), "dp", scatter_dimension=0, tiled=True
        ).astype(jnp.float32),
        lax.psum_scatter(
            cross_piece.astype(jnp.bfloat16), "dp", scatter_dimension=0, tiled=True
        ).astype(jnp.float32),
        lax.psum_scatter(
            ff_piece.astype(jnp.bfloat16), "dp", scatter_dimension=0, tiled=True
        ).astype(jnp.float32),
        lax.psum_scatter(
            norm_column.astype(jnp.bfloat16), "dp", scatter_dimension=0, tiled=True
        ).astype(jnp.float32),
    )
    owned_attn, owned_cross, owned_ff, owned_norm = (
        lax.all_to_all(
            summed_attn.astype(jnp.bfloat16), "seq", split_axis=0, concat_axis=2, tiled=True
        ).astype(summed_attn.dtype),
        lax.all_to_all(
            summed_cross.astype(jnp.bfloat16), "seq", split_axis=0, concat_axis=2, tiled=True
        ).astype(summed_cross.dtype),
        lax.all_to_all(
            summed_ff.astype(jnp.bfloat16), "seq", split_axis=0, concat_axis=2, tiled=True
        ).astype(summed_ff.dtype),
        lax.all_to_all(
            summed_norm.astype(jnp.bfloat16), "seq", split_axis=0, concat_axis=2, tiled=True
        ).astype(summed_norm.dtype),
    )
    attn_reduced = owned_attn.reshape(owned_attn.shape[0], 6 * wide)
    cross_reduced = owned_cross.reshape(owned_cross.shape[0], 2 * wide)
    ff_reduced = owned_ff.reshape(owned_ff.shape[0], 3 * hidden_width)
    norm_reduced = jnp.sum(owned_norm, axis=2).T
    local_squares = (
        jnp.sum(attn_reduced * attn_reduced)
        + jnp.sum(cross_reduced * cross_reduced)
        + jnp.sum(norm_reduced * norm_reduced)
        + jnp.sum(ff_reduced * ff_reduced)
    )
    total_squares = lax.psum(local_squares, ("dp", "seq"))
    grad_norm = jnp.sqrt(total_squares)
    factor = jnp.minimum(1.0, clip_limit / grad_norm)
    attn_new, attn_first_new, attn_second_new = adam_step(
        attn_weight, attn_first, attn_second, attn_reduced * factor, matrix_rate, matrix_decay
    )
    cross_new, cross_first_new, cross_second_new = adam_step(
        cross_weight, cross_first, cross_second, cross_reduced * factor, matrix_rate, matrix_decay
    )
    norm_new, norm_first_new, norm_second_new = adam_step(
        norm_param, norm_first, norm_second, norm_reduced * factor, gain_rate, 0.0
    )
    ff_new, ff_first_new, ff_second_new = adam_step(
        ff_weight, ff_first, ff_second, ff_reduced * factor, matrix_rate, matrix_decay
    )
    return (
        layer_out,
        frames_grad,
        grad_norm,
        attn_new,
        cross_new,
        norm_new,
        ff_new,
        attn_first_new,
        cross_first_new,
        norm_first_new,
        ff_first_new,
        attn_second_new,
        cross_second_new,
        norm_second_new,
        ff_second_new,
    )


MESH = pl.DeviceIdType.MESH
DMA = pltpu.SemaphoreType.DMA
VMEM_LIMIT = 60 * 2**20


def plane_fits(mesh):
    return mesh.shape["dp"] == 8 and mesh.shape["dp"] % mesh.shape["seq"] == 0


def plane_places():
    place = lax.axis_index("dp")
    return (place, lax.axis_index("seq"), lambda mask: jnp.bitwise_xor(place, mask))


def greet(partners):
    barrier = pltpu.get_barrier_semaphore()
    for partner in partners:
        pl.semaphore_signal(barrier, inc=1, device_id=partner, device_id_type=MESH)
    pl.semaphore_wait(barrier, len(partners))


def remote(source, goal, send_sem, recv_sem, device):
    return pltpu.make_async_remote_copy(
        src_ref=source,
        dst_ref=goal,
        send_sem=send_sem,
        recv_sem=recv_sem,
        device_id=device,
        device_id_type=MESH,
    )


def communicating(collective_id):
    return pltpu.CompilerParams(
        has_side_effects=True, collective_id=collective_id, vmem_limit_bytes=VMEM_LIMIT
    )


def any_spec():
    return pl.BlockSpec(memory_space=pl.ANY)


def greet_cross(group, planes):
    place, depth, flip = plane_places()
    greet(
        [(flip(mask), depth) for mask in range(1, group)]
        + [(place, lax.rem(depth + step, planes)) for step in range(1, planes)]
    )


def outward_steps(group, planes, kept_ref, own_ref, mid, *sems):
    far_send, far_recv, near_send, near_recv, local_sem = sems
    place, depth, flip = plane_places()
    per = group // planes
    first = []
    for step in range(1, planes):
        origin = lax.rem(depth + step, planes)
        for slot in range(per):
            clip = per * depth + slot
            copy = remote(
                kept_ref.at[slot, origin],
                mid.at[clip],
                far_send.at[slot, step],
                far_recv.at[clip],
                (place, origin),
            )
            copy.start()
            first.append(copy)
    second = []

    def hand_over(block, clip):
        index = len(second)
        away = remote(
            block, own_ref.at[place], near_send.at[index], near_recv.at[place], (clip, depth)
        )
        stay = pltpu.make_async_copy(block, own_ref.at[place], local_sem.at[index])
        pl.when(clip != place)(away.start)
        pl.when(clip == place)(stay.start)
        second.append((clip, away, stay))

    for slot in range(per):
        hand_over(kept_ref.at[slot, depth], per * depth + slot)
    yield
    for step in range(1, planes):
        source = lax.rem(depth + step, planes)
        for slot in range(per):
            clip = per * source + slot
            block = mid.at[clip]
            remote(
                block, block, far_send.at[0, 0], far_recv.at[clip], (place, source)
            ).wait_recv()
            hand_over(block, clip)
    yield
    for mask in range(1, group):
        other = flip(mask)
        block = own_ref.at[other]
        remote(block, block, near_send.at[0], near_recv.at[other], (other, depth)).wait_recv()
    for clip, away, stay in second:
        pl.when(clip != place)(away.wait_send)
        pl.when(clip == place)(stay.wait)
    for copy in first:
        copy.wait_send()
    yield


def outward_scratch(group, planes):
    return [
        DMA((group // planes, planes)),
        DMA((group,)),
        DMA((group,)),
        DMA((group,)),
        DMA((group,)),
    ]


def leave_body(
    group,
    planes,
    kept_ref,
    first_cut_ref,
    rest_cut_ref,
    parts_ref,
    squares_ref,
    own_ref,
    first_mine_ref,
    rest_mine_ref,
    norm_ref,
    total_ref,
    mid,
    terms,
    block,
    blocks,
    *sems,
):
    part_send, part_recv, block_send, block_recv = sems[:4]
    place, depth, flip = plane_places()
    devices = [(flip(mask), lax.rem(depth + step, planes)) for mask, step in everyone(planes)]
    greet(devices)
    here = place * planes + depth
    rows = outward_steps(group, planes, kept_ref, own_ref, mid, *sems[4:9])
    next(rows)
    copies = []
    for index, (other, plane) in enumerate(devices):
        copy = remote(
            parts_ref.at[other * planes + plane],
            terms.at[here],
            part_send.at[index],
            part_recv.at[here],
            (other, plane),
        )
        copy.start()
        copies.append(copy)
    terms[here] = parts_ref[here]
    start_swap, end_swap = swap_beside(
        [
            (lambda other: first_cut_ref.at[other], lambda other: first_mine_ref.at[other]),
            (lambda other: rest_cut_ref.at[other], lambda other: rest_mine_ref.at[other]),
        ],
        *sems[9:],
    )
    start_swap()
    next(rows)
    for other, plane in devices:
        source = other * planes + plane
        one = terms.at[source]
        remote(one, one, part_send.at[0], part_recv.at[source], (other, plane)).wait_recv()
    norm_sum = jnp.sum(terms[...], axis=0)
    norm_ref[...] = norm_sum
    end_swap()
    squares = squares_ref[0, 0] + jnp.sum(norm_sum * norm_sum)
    for mine_ref in (first_mine_ref, rest_mine_ref):
        for piece in range(group):
            values = mine_ref[piece].astype(jnp.float32)
            squares = squares + jnp.sum(values * values)
    block[...] = jnp.full(block.shape, squares)
    blocks[here] = block[...]
    for index, (other, plane) in enumerate(devices):
        copy = remote(
            block, blocks.at[here], block_send.at[index], block_recv.at[here], (other, plane)
        )
        copy.start()
        copies.append(copy)
    next(rows)
    for other, plane in devices:
        source = other * planes + plane
        one = blocks.at[source]
        remote(one, one, block_send.at[0], block_recv.at[source], (other, plane)).wait_recv()
    total_ref[...] = jnp.sum(blocks[...], axis=0)
    for copy in copies:
        copy.wait_send()


def leave(kept_rows, first_cut, rest_cut, norm_parts, squares, collective_id):
    per, planes, rows, wide = kept_rows.shape
    group = per * planes
    count = group * planes
    inside = pl.BlockSpec(memory_space=pltpu.VMEM)
    like = lambda shape, array: jax.ShapeDtypeStruct(shape, array.dtype)
    *results, _ = pl.pallas_call(
        functools.partial(leave_body, group, planes),
        out_shape=[
            like((group, rows, wide), kept_rows),
            like(first_cut.shape, first_cut),
            like(rest_cut.shape, rest_cut),
            like(norm_parts.shape[1:], norm_parts),
            like((8, 128), norm_parts),
            like((group, rows, wide), kept_rows),
        ],
        in_specs=[any_spec()] * 3 + [inside, pl.BlockSpec(memory_space=pltpu.SMEM)],
        out_specs=[any_spec()] + [inside] * 4 + [any_spec()],
        scratch_shapes=[
            pltpu.VMEM(norm_parts.shape, jnp.float32),
            pltpu.VMEM((8, 128), jnp.float32),
            pltpu.VMEM((count, 8, 128), jnp.float32),
            DMA((count,)),
            DMA((count,)),
            DMA((count,)),
            DMA((count,)),
        ]
        + outward_scratch(group, planes)
        + swap_beside_scratch(2),
        compiler_params=communicating(collective_id),
    )(kept_rows, first_cut, rest_cut, norm_parts, squares)
    return results


def everyone(planes):
    return [(mask, step) for mask in range(8) for step in range(planes) if mask or step]


def enter_body(
    group,
    planes,
    own_ref,
    norm_ref,
    pack_ref,
    first_cut_ref,
    rest_cut_ref,
    kept_ref,
    gains_ref,
    packs_ref,
    first_mine_ref,
    rest_mine_ref,
    mid,
    norms_ref,
    *sems,
):
    (
        near_send,
        near_recv,
        far_send,
        far_recv,
        local_sem,
        norm_send,
        norm_recv,
        pack_send,
        pack_recv,
        cut_send,
        cut_recv,
        stay_sem,
    ) = sems
    place, depth, flip = plane_places()
    per = group // planes
    others = everyone(planes)
    greet([(flip(mask), lax.rem(depth + step, planes)) for mask, step in others])
    here = place * planes + depth
    first = []
    for mask in (6, 7, 2, 3, 4, 5, 1):
        other = flip(mask)
        copy = remote(
            own_ref.at[other],
            mid.at[place],
            near_send.at[mask],
            near_recv.at[mask],
            (other, depth),
        )
        copy.start()
        first.append((mask, copy))
    small = []
    for index, (mask, step) in enumerate(others):
        copy = remote(
            norm_ref,
            norms_ref.at[here],
            norm_send.at[index],
            norm_recv.at[here],
            (flip(mask), lax.rem(depth + step, planes)),
        )
        copy.start()
        small.append(copy)
    for mask in range(1, group):
        copy = remote(
            pack_ref,
            packs_ref.at[place],
            pack_send.at[mask],
            pack_recv.at[mask],
            (flip(mask), depth),
        )
        copy.start()
        small.append(copy)
    stays = [
        pltpu.make_async_copy(norm_ref, norms_ref.at[here], stay_sem.at[0]),
        pltpu.make_async_copy(pack_ref, packs_ref.at[place], stay_sem.at[1]),
        pltpu.make_async_copy(
            first_cut_ref.at[place], first_mine_ref.at[place], stay_sem.at[2]
        ),
        pltpu.make_async_copy(rest_cut_ref.at[place], rest_mine_ref.at[place], stay_sem.at[3]),
    ]
    for stay in stays:
        stay.start()
    cuts = []
    for which, (cut_ref, mine_ref) in enumerate(
        ((first_cut_ref, first_mine_ref), (rest_cut_ref, rest_mine_ref))
    ):
        for mask in (6, 7, 2, 3, 4, 5, 1):
            other = flip(mask)
            copy = remote(
                cut_ref.at[other],
                mine_ref.at[place],
                cut_send.at[which, mask],
                cut_recv.at[which, mask],
                (other, depth),
            )
            copy.start()
            cuts.append(copy)
    second = []
    arrivals = dict(first)
    for mask in (0, 1, 2, 3, 4, 5, 6, 7):
        source = flip(mask)
        goal, slot = lax.div(source, per), lax.rem(source, per)
        block = own_ref.at[place]
        if mask:
            arrivals[mask].wait_recv()
            block = mid.at[source]
        away = remote(
            block,
            kept_ref.at[slot, depth],
            far_send.at[mask],
            far_recv.at[slot, depth],
            (place, goal),
        )
        stay = pltpu.make_async_copy(block, kept_ref.at[slot, depth], local_sem.at[mask])
        pl.when(goal != depth)(away.start)
        pl.when(goal == depth)(stay.start)
        second.append((goal, away, stay))
    for slot in range(per):
        for origin in range(planes):
            block = kept_ref.at[slot, origin]
            pl.when(origin != depth)(
                remote(
                    block,
                    block,
                    far_send.at[0],
                    far_recv.at[slot, origin],
                    (place, lax.rem(depth + 1, planes)),
                ).wait_recv
            )
    for mask, step in others:
        source = flip(mask) * planes + lax.rem(depth + step, planes)
        block = norms_ref.at[source]
        remote(
            block,
            block,
            norm_send.at[0],
            norm_recv.at[source],
            (flip(mask), lax.rem(depth + step, planes)),
        ).wait_recv()
    for copy in small:
        copy.wait_send()
    stays[0].wait()
    width = gains_ref.shape[1] // (group * planes)
    gains_ref[...] = jnp.concatenate(
        [
            norms_ref[owner * planes + plane, :, :width]
            for plane in range(planes)
            for owner in range(group)
        ],
        axis=1,
    )
    for mask in range(1, group):
        block = packs_ref.at[flip(mask)]
        remote(
            block, block, pack_send.at[0], pack_recv.at[mask], (flip(mask), depth)
        ).wait_recv()
    for copy in cuts:
        copy.wait()
    for goal, away, stay in second:
        pl.when(goal != depth)(away.wait_send)
        pl.when(goal == depth)(stay.wait)
    for mask, copy in first:
        copy.wait_send()
    for stay in stays[1:]:
        stay.wait()


def enter(rows_of_clip, norm_block, pack, first_cut, rest_cut, planes, collective_id):
    group, rows, wide = rows_of_clip.shape
    count = group * planes
    like = lambda shape, array: jax.ShapeDtypeStruct(shape, array.dtype)
    inside = pl.BlockSpec(memory_space=pltpu.VMEM)
    *results, _ = pl.pallas_call(
        functools.partial(enter_body, group, planes),
        out_shape=[
            like((group // planes, planes, rows, wide), rows_of_clip),
            like((norm_block.shape[0], wide), norm_block),
            like((group,) + pack.shape, pack),
            like(first_cut.shape, first_cut),
            like(rest_cut.shape, rest_cut),
            like((group, rows, wide), rows_of_clip),
        ],
        in_specs=[any_spec(), inside, any_spec(), any_spec(), any_spec()],
        out_specs=[any_spec(), inside] + [any_spec()] * 4,
        scratch_shapes=[
            pltpu.VMEM((count,) + norm_block.shape, norm_block.dtype),
            DMA((group,)),
            DMA((group,)),
            DMA((group,)),
            DMA((group // planes, planes)),
            DMA((group,)),
            DMA((count,)),
            DMA((count,)),
            DMA((group,)),
            DMA((group,)),
            DMA((2, group)),
            DMA((2, group)),
            DMA((4,)),
        ],
        compiler_params=communicating(collective_id),
    )(rows_of_clip, norm_block, pack, first_cut, rest_cut)
    return results


def cond_steps(group, planes, pick_ref, cond_ref, parts, summed, *sems):
    part_send, part_recv, cond_send, cond_recv = sems
    place, depth, flip = plane_places()
    pushes = []
    for step in range(1, planes):
        goal = lax.rem(depth + step, planes)
        copy = remote(
            pick_ref.at[goal],
            parts.at[depth],
            part_send.at[step],
            part_recv.at[depth],
            (place, goal),
        )
        copy.start()
        pushes.append(copy)
    yield
    total = pick_ref[depth].astype(jnp.float32)
    for step in range(1, planes):
        source = lax.rem(depth + step, planes)
        block = parts.at[source]
        remote(
            block, block, part_send.at[0], part_recv.at[source], (place, source)
        ).wait_recv()
        total = total + parts[source].astype(jnp.float32)
    summed[...] = total.astype(summed.dtype)
    cond_ref[place] = total.astype(summed.dtype)
    for mask in range(1, group):
        copy = remote(
            summed,
            cond_ref.at[place],
            cond_send.at[mask],
            cond_recv.at[mask],
            (flip(mask), depth),
        )
        copy.start()
        pushes.append(copy)
    yield
    for mask in range(1, group):
        block = cond_ref.at[flip(mask)]
        remote(
            block, block, cond_send.at[0], cond_recv.at[mask], (flip(mask), depth)
        ).wait_recv()
    for copy in pushes:
        copy.wait_send()
    yield


def inward_beside(group, planes, own_ref, kept_ref, mid, *sems):
    near_send, near_recv, far_send, far_recv, local_sem = sems
    place, depth, flip = plane_places()
    per = group // planes

    def near(mask):
        other = flip(mask)
        return remote(
            own_ref.at[other],
            mid.at[place],
            near_send.at[mask],
            near_recv.at[mask],
            (other, depth),
        )

    def begin():
        for mask in range(1, group):
            near(mask).start()

    def second(mask):
        source = flip(mask)
        goal, slot = lax.div(source, per), lax.rem(source, per)
        block = mid.at[source] if mask else own_ref.at[place]
        away = remote(
            block,
            kept_ref.at[slot, depth],
            far_send.at[mask],
            far_recv.at[slot, depth],
            (place, goal),
        )
        stay = pltpu.make_async_copy(block, kept_ref.at[slot, depth], local_sem.at[mask])
        return goal != depth, away, stay

    def middle():
        for mask in range(group):
            if mask:
                near(mask).wait_recv()
            leaves, away, stay = second(mask)
            pl.when(leaves)(away.start)
            pl.when(jnp.logical_not(leaves))(stay.start)

    def end():
        for slot in range(per):
            for origin in range(planes):
                block = kept_ref.at[slot, origin]
                pl.when(origin != depth)(
                    remote(
                        block,
                        block,
                        far_send.at[0],
                        far_recv.at[slot, origin],
                        (place, lax.rem(depth + 1, planes)),
                    ).wait_recv
                )
        for mask in range(group):
            leaves, away, stay = second(mask)
            pl.when(leaves)(away.wait_send)
            pl.when(jnp.logical_not(leaves))(stay.wait)
            if mask:
                near(mask).wait_send()

    return begin, middle, end


def inward_scratch(group, planes):
    return [
        DMA((group,)),
        DMA((group,)),
        DMA((group,)),
        DMA((group // planes, planes)),
        DMA((group,)),
    ]


def dot_tiles(left, right_ref, span, transposed, width):
    first, last = span
    count = right_ref.shape[0] if transposed else last - first
    for start in range(0, count, width):
        stop = min(start + width, count)
        if transposed:
            yield start, stop, times_transposed(left, right_ref[start:stop, first:last])
        else:
            yield start, stop, jnp.dot(
                left, right_ref[:, first + start : first + stop], preferred_element_type=jnp.float32
            )


def window_of(matrix, span):
    first, last = span or (0, matrix.shape[1])
    start = first // 128 * 128
    while (matrix.shape[1] - start) * 2 > matrix.shape[1] and start and start % 384:
        start -= 128
    stop = min(-(-last // 128) * 128, matrix.shape[1])
    return (start, stop - start), (first - start, last - start)


def cross_shares(queries, pair_ref, bias_ref):
    wide = queries[0].shape[1]
    keys = [
        (clip, start, pair_ref[clip, :, start : start + HDIM])
        for clip in range(len(queries))
        for start in range(0, wide, HDIM)
    ]
    scores = [
        times_transposed(queries[clip][:, start : start + HDIM], key) * HDIM ** (-0.5)
        + bias_ref[clip]
        for clip, start, key in keys
    ]
    tops = [jnp.max(score, axis=1, keepdims=True) for score in scores]
    expos = [jnp.exp(score - top) for score, top in zip(scores, tops)]
    sums = [jnp.sum(expo, axis=1, keepdims=True) for expo in expos]
    return keys, [expo / total for expo, total in zip(expos, sums)]


def by_clip_of(results, clips, low):
    heads = len(results) // clips
    return [
        jnp.concatenate(results[clip * heads : (clip + 1) * heads], axis=1).astype(low)
        for clip in range(clips)
    ]


def cross_rows(queries, pair_ref, bias_ref):
    low, wide = queries[0].dtype, queries[0].shape[1]
    keys, shares = cross_shares(queries, pair_ref, bias_ref)
    mixed = [
        jnp.dot(
            share.astype(low),
            pair_ref[clip, :, wide + start : wide + start + HDIM],
            preferred_element_type=jnp.float32,
        )
        for (clip, start, _), share in zip(keys, shares)
    ]
    return by_clip_of(mixed, len(queries), low)


def cross_rows_back(queries, grads, pair_ref, bias_ref, pair_grad_ref):
    low, wide = queries[0].dtype, queries[0].shape[1]
    scale = HDIM ** (-0.5)
    keys, shares = cross_shares(queries, pair_ref, bias_ref)
    own_grads = [grads[clip][:, start : start + HDIM] for clip, start, _ in keys]
    grad_shares = [
        times_transposed(grad, pair_ref[clip, :, wide + start : wide + start + HDIM])
        for (clip, start, _), grad in zip(keys, own_grads)
    ]
    deltas = [
        jnp.sum(share * grad_share, axis=1, keepdims=True)
        for share, grad_share in zip(shares, grad_shares)
    ]
    scores = [
        (share * (grad_share - delta)).astype(low)
        for share, grad_share, delta in zip(shares, grad_shares, deltas)
    ]
    results = [
        jnp.dot(score, key, preferred_element_type=jnp.float32) * scale
        for score, (_, _, key) in zip(scores, keys)
    ]
    key_grads = [
        outer_sum(score, queries[clip][:, start : start + HDIM]) * scale
        for score, (clip, start, _) in zip(scores, keys)
    ]
    value_grads = [
        outer_sum(share.astype(low), grad) for share, grad in zip(shares, own_grads)
    ]
    heads = len(keys) // len(queries)
    for clip in range(len(queries)):
        mine = slice(clip * heads, (clip + 1) * heads)
        pair_grad_ref[clip] += jnp.concatenate(key_grads[mine] + value_grads[mine], axis=1)
    return by_clip_of(results, len(queries), low)


def gather_dot_body(clips, rows, sub, normed, mode, window, span, beside, own_ref, *refs):
    refs = list(refs)
    take = lambda count: [refs.pop(0) for _ in range(count)]
    gain_ref = take(1)[0] if normed else None
    mat_ref = take(1)[0] if mode != "rows" else None
    gates_ref = take(1)[0] if mode == "gates" else None
    pair_ref, bias_ref = take(2) if mode in ("cross", "cross_back") else (None, None)
    query_ref = take(1)[0] if mode == "cross_back" else None
    extra_ref = take(1)[0] if beside else None
    all_ref = take(1)[0]
    prod_refs = take({"rows": 0, "dot": 1, "gates": 2, "cross": 2, "cross_back": 1}[mode])
    pair_grad_ref = take(1)[0] if mode == "cross_back" else None
    extra_outs = take({"cond": 1, "outward": 2}[beside[0]]) if beside else []
    held, send_sem, recv_sem, all_sem = take(4)
    mat, mat_sem = take(2) if mode != "rows" else (None, None)
    stages = take(len(prod_refs))
    prod_sem = take(1)[0] if prod_refs else None
    gates, gates_sem = take(2) if mode == "gates" else (None, None)
    queries, query_sem = take(2) if mode == "cross_back" else (None, None)
    place, depth, flip = plane_places()
    core, beside_x, beside_y, across = flip(1), flip(2), flip(4), flip(6)
    if mode != "rows":
        load = pltpu.make_async_copy(mat_ref.at[:, pl.ds(*window)], mat, mat_sem)
        load.start()
    if mode == "cross_back":
        query_load = pltpu.make_async_copy(query_ref, queries, query_sem)
        query_load.start()
        pair_grad_ref[...] = jnp.zeros_like(pair_grad_ref)
    slots = [flip(mask) for mask in (0, 1, 2, 4, 3, 5, 6, 7)]
    gate_loads = {}
    if mode == "gates":
        for mask, slot in zip((0, 1, 2, 4, 3, 5, 6, 7), slots):
            gate_loads[mask] = [
                pltpu.make_async_copy(
                    gates_ref.at[clip, slot], gates.at[slot, clip], gates_sem.at[slot, clip]
                )
                for clip in range(clips)
            ]
            for copy in gate_loads[mask]:
                copy.start()
    if beside:
        greet_cross(*beside[1:])
        if beside[0] == "cond":
            going = cond_steps(*beside[1:], extra_ref, extra_outs[0], *refs)
        else:
            going = outward_steps(*beside[1:], extra_ref, *extra_outs, *refs)
        next(going)
    else:
        greet([(core, depth), (beside_x, depth), (beside_y, depth)])
    values = own_ref[...]
    if normed:
        values = layer_norm(values, gain_ref[0:1], gain_ref[1:2])
    held[place] = values.astype(held.dtype)
    chunks = [(clip, part) for clip in range(clips) for part in range(rows // sub)]
    count = len(chunks)
    half = count // 2
    sends = []

    def view(slot, index):
        clip, part = chunks[index]
        return held.at[slot, clip, pl.ds(part * sub, sub)]

    def send(slot, index, device):
        block = view(slot, index)
        copy = remote(
            block, block, send_sem.at[len(sends)], recv_sem.at[slot, index], (device, depth)
        )
        copy.start()
        sends.append(copy)

    def arrived(slot, index):
        block = view(slot, index)
        remote(
            block, block, send_sem.at[0], recv_sem.at[slot, index], (core, depth)
        ).wait_recv()

    x_order = list(range(count))
    y_order = list(range(half, count)) + list(range(half))
    for step in range(count):
        send(place, x_order[step], beside_x)
        send(place, y_order[step], beside_y)
    for index in range(count):
        send(place, index, core)
    outs = []

    def leave_here(source, goal, sem, major):
        for clip in range(clips):
            there = goal.at[major, clip] if goal.shape[0] == 8 else goal.at[clip, major]
            copy = pltpu.make_async_copy(source.at[major, clip], there, sem.at[major, clip])
            copy.start()
            outs.append(copy)

    def multiply(mask):
        slot = flip(mask)
        leave_here(held, all_ref, all_sem, slot)
        if mode == "rows":
            return
        left = held[slot].reshape(clips * rows, held.shape[3])
        for copy in gate_loads.get(mask, ()):
            copy.wait()
        for start, stop, product in dot_tiles(
            left, mat, span, False, 256 * (1 if mode == "gates" else 3)
        ):
            product = product.reshape(clips, rows, stop - start)
            if mode == "cross":
                query = product.astype(stages[0].dtype)
                stages[0][slot] = query
                mixed = cross_rows([query[clip] for clip in range(clips)], pair_ref, bias_ref)
                for clip in range(clips):
                    stages[1][slot, clip] = mixed[clip]
                continue
            if mode == "cross_back":
                grad = product.astype(stages[0].dtype)
                results = cross_rows_back(
                    [queries[clip, slot] for clip in range(clips)],
                    [grad[clip] for clip in range(clips)],
                    pair_ref,
                    bias_ref,
                    pair_grad_ref,
                )
                for clip in range(clips):
                    stages[0][slot, clip] = results[clip]
                continue
            if mode == "dot":
                stages[0][slot, :, :, start:stop] = product.astype(stages[0].dtype)
                continue
            width = stages[1].shape[3]
            gate = gates[slot, :, :, start:stop]
            up = gates[slot, :, :, width + start : width + stop]
            sigmoid = jax.nn.sigmoid(gate)
            active = gate * sigmoid
            low = stages[0].dtype
            stages[0][slot, :, :, start:stop] = (
                product * up * sigmoid * (1.0 + gate * (1.0 - sigmoid))
            ).astype(low)
            stages[0][slot, :, :, width + start : width + stop] = (product * active).astype(low)
            stages[1][slot, :, :, start:stop] = (active * up).astype(low)
        for which, (stage, prod_ref) in enumerate(zip(stages, prod_refs)):
            leave_here(stage, prod_ref, prod_sem.at[which], slot)

    if mode != "rows":
        load.wait()
    if mode == "cross_back":
        query_load.wait()
    multiply(0)
    if beside:
        next(going)
    for step in range(count):
        x_index, y_index = x_order[step], y_order[step]
        arrived(beside_x, x_index)
        if x_index < half:
            send(beside_x, x_index, beside_y)
        send(beside_x, x_index, core)
        arrived(beside_y, y_index)
        if y_index >= half:
            send(beside_y, y_index, beside_x)
        send(beside_y, y_index, core)
        if step == 0:
            for index in range(count):
                arrived(core, index)
            multiply(1)
    multiply(2)
    for step in range(half):
        for index in (x_order[step], y_order[step]):
            arrived(across, index)
            send(across, index, core)
        if step == 0:
            multiply(4)
    for mask in (3, 5):
        for index in range(count):
            arrived(flip(mask), index)
        multiply(mask)
    multiply(6)
    for index in range(count):
        arrived(flip(7), index)
    multiply(7)
    if beside:
        next(going)
    for copy in outs:
        copy.wait()
    for copy in sends:
        copy.wait_send()


def gather_dot(
    own_rows,
    matrix,
    kind,
    collective_id,
    gains=None,
    picked=None,
    kept_rows=None,
    gate_up=None,
    span=None,
    pair=None,
    bias=None,
    query=None,
    sub=64,
):
    clips, rows, wide = own_rows.shape
    count = clips * (rows // sub)
    low = jnp.bfloat16
    mode = "rows" if matrix is None else "dot"
    if gate_up is not None:
        mode = "gates"
    if pair is not None:
        mode = "cross" if query is None else "cross_back"
    window = inner = None
    inside = pl.BlockSpec(memory_space=pltpu.VMEM)
    by_clip = lambda columns, of: jax.ShapeDtypeStruct((clips, 8, rows, columns), of)
    by_device = lambda columns, of: jax.ShapeDtypeStruct((8, clips, rows, columns), of)
    args, in_specs = [own_rows], [inside]
    if gains is not None:
        args.append(gains)
        in_specs.append(inside)
    outs = [by_device(wide, low) if mode == "gates" else by_clip(wide, low)]
    scratch = [
        pltpu.VMEM((8, clips, rows, wide), low),
        DMA((7 * count,)),
        DMA((8, count)),
        DMA((8, clips)),
    ]
    if mode != "rows":
        window, inner = window_of(matrix, span)
        columns = inner[1] - inner[0]
        args.append(matrix)
        in_specs.append(any_spec())
        scratch += [pltpu.VMEM((wide, window[1]), low), DMA(())]
    if mode == "dot":
        outs.append(by_clip(columns, kind))
        scratch += [pltpu.VMEM((8, clips, rows, columns), kind), DMA((1, 8, clips))]
    if mode == "gates":
        args.append(gate_up.reshape(clips, 8, rows, 2 * columns))
        in_specs.append(any_spec())
        outs += [by_clip(2 * columns, low), by_device(columns, low)]
        scratch += [
            pltpu.VMEM((8, clips, rows, 2 * columns), low),
            pltpu.VMEM((8, clips, rows, columns), low),
            DMA((2, 8, clips)),
            pltpu.VMEM((8, clips, rows, 2 * columns), jnp.float32),
            DMA((8, clips)),
        ]
    if mode == "cross":
        args += [pair, bias]
        in_specs += [inside] * 2
        outs += [by_clip(columns, low)] * 2
        scratch += [pltpu.VMEM((8, clips, rows, columns), low)] * 2 + [DMA((2, 8, clips))]
    out_specs = [any_spec()] * len(outs)
    if mode == "cross_back":
        args += [pair, bias, query.reshape(clips, 8, rows, columns)]
        in_specs += [inside, inside, any_spec()]
        outs += [by_clip(columns, low), jax.ShapeDtypeStruct(pair.shape, jnp.float32)]
        out_specs += [any_spec(), inside]
        scratch += [
            pltpu.VMEM((8, clips, rows, columns), low),
            DMA((1, 8, clips)),
            pltpu.VMEM((clips, 8, rows, columns), low),
            DMA(()),
        ]
    mains = len(outs)
    beside = None
    if picked is not None:
        planes, per, tokens, cond_wide = picked.shape
        beside = ("cond", planes * per, planes)
        args.append(picked)
        in_specs.append(inside)
        outs.append(jax.ShapeDtypeStruct((8, per, tokens, cond_wide), picked.dtype))
        out_specs.append(inside)
        scratch += [
            pltpu.VMEM(picked.shape, picked.dtype),
            pltpu.VMEM(picked.shape[1:], picked.dtype),
            DMA((planes,)),
            DMA((planes,)),
            DMA((8,)),
            DMA((8,)),
        ]
    if kept_rows is not None:
        per, planes, piece, _ = kept_rows.shape
        beside = ("outward", planes * per, planes)
        args.append(kept_rows)
        in_specs.append(any_spec())
        outs += [jax.ShapeDtypeStruct((per * planes, piece, wide), kept_rows.dtype)] * 2
        out_specs += [any_spec()] * 2
        scratch += outward_scratch(*beside[1:])
    results = pl.pallas_call(
        functools.partial(
            gather_dot_body, clips, rows, sub, gains is not None, mode, window, inner, beside
        ),
        out_shape=outs,
        in_specs=in_specs,
        out_specs=out_specs,
        scratch_shapes=scratch,
        compiler_params=communicating(collective_id),
    )(*args)
    flat = [
        block.reshape(clips * 8 * rows, block.shape[3]) if len(block.shape) == 4 else block
        for block in results[:mains]
    ]
    return flat + list(results[mains : mains + 1])


def reduce_steps(clips, rows, sub, multiply, final, terms, pair, turn, from_x, from_y, *sems):
    send_sem, core_sem, turn_sem, x_sem, y_sem = sems
    place, depth, flip = plane_places()
    core, beside_x, beside_y = flip(1), flip(2), flip(4)
    chunks = [(clip, part) for clip in range(clips) for part in range(rows // sub)]
    count = len(chunks)
    half = count // 2
    sends = []

    def send(source, goal, recv_sem, device):
        copy = remote(source, goal, send_sem.at[len(sends)], recv_sem, (device, depth))
        copy.start()
        sends.append(copy)

    def arrived(block, recv_sem):
        remote(block, block, send_sem.at[0], recv_sem, (core, depth)).wait_recv()

    def term(number, index):
        clip, part = chunks[index]
        return terms.at[number, clip, pl.ds(part * sub, sub)]

    def give(number, chip):
        for index in range(count):
            send(term(number, index), pair.at[index, chip], core_sem.at[index, chip], core)

    def total(*blocks):
        return sum(block[...].astype(jnp.float32) for block in blocks)

    def add(block, other):
        block[...] = total(block, other).astype(terms.dtype)

    numbers = {3: 1, 1: 3, 2: 5, 0: 7}

    def combine(chip, index):
        arrived(pair.at[index, chip], core_sem.at[index, chip])
        block = term(numbers[chip], index)
        add(block, pair.at[index, chip])
        return block

    multiply(0)
    give(0, 3)
    multiply(1)
    multiply(2)
    give(2, 1)
    for low in range(half):
        high = half + low
        send(combine(3, low), turn.at[low], turn_sem.at[low], beside_x)
        send(combine(3, high), turn.at[high], turn_sem.at[high], beside_y)
    multiply(3)
    multiply(4)
    give(4, 2)
    for low in range(half):
        send(combine(1, low), from_x.at[low], x_sem.at[low], beside_x)
    multiply(5)
    for high in range(half, count):
        send(combine(2, high), from_y.at[high], y_sem.at[high], beside_y)
    multiply(6)
    give(6, 0)
    multiply(7)
    yield
    for low in range(half):
        high = half + low
        block = combine(2, low)
        arrived(turn.at[low], turn_sem.at[low])
        add(block, turn.at[low])
        send(block, from_y.at[low], y_sem.at[low], beside_y)
        block = combine(1, high)
        arrived(turn.at[high], turn_sem.at[high])
        add(block, turn.at[high])
        send(block, from_x.at[high], x_sem.at[high], beside_x)
    yield
    for index in range(count):
        clip, part = chunks[index]
        arrived(pair.at[index, 0], core_sem.at[index, 0])
        arrived(from_x.at[index], x_sem.at[index])
        arrived(from_y.at[index], y_sem.at[index])
        result = total(term(7, index), pair.at[index, 0], from_x.at[index], from_y.at[index])
        final(index, clip, pl.ds(part * sub, sub), result)
    yield
    for copy in sends:
        copy.wait_send()
    yield


def plane_order():
    place, depth, flip = plane_places()
    return [flip(mask) for mask in (7, 6, 3, 2, 5, 4, 1, 0)]


def reduce_scratch(clips, rows, sub, wide):
    count = clips * (rows // sub)
    low = jnp.bfloat16
    return [
        pltpu.VMEM((8, clips, rows, wide), low),
        pltpu.VMEM((count, 4, sub, wide), low),
        pltpu.VMEM((count, sub, wide), low),
        pltpu.VMEM((count, sub, wide), low),
        pltpu.VMEM((count, sub, wide), low),
        DMA((7 * count,)),
        DMA((count, 4)),
        DMA((count,)),
        DMA((count,)),
        DMA((count,)),
    ]


def norm_back(values, gain, grad):
    center = values - jnp.mean(values, axis=1, keepdims=True)
    inverse = lax.rsqrt(jnp.mean(center * center, axis=1, keepdims=True) + norm_eps)
    unit = center * inverse
    stats = [
        jnp.sum(grad * unit, axis=0, keepdims=True),
        jnp.sum(grad, axis=0, keepdims=True),
    ]
    scaled = grad * gain
    result = inverse * (
        scaled
        - jnp.mean(scaled, axis=1, keepdims=True)
        - unit * jnp.mean(scaled * unit, axis=1, keepdims=True)
    )
    return result, stats


def final_back(values_ref, gain_ref, base_ref, sum_ref, stats_ref):
    def final(index, clip, span, result):
        if values_ref is not None:
            result, stats = norm_back(values_ref[clip, span], gain_ref[...], result)
            for which, row in enumerate(stats):
                row = row + stats_ref[which : which + 1] if index else row
                stats_ref[which : which + 1] = row
        result = base_ref[clip, span].astype(jnp.float32) + result
        sum_ref[clip, span] = result.astype(sum_ref.dtype)

    return final


def terms_of(clips, rows, blocks, mat, span, terms):
    def multiply(number):
        block = blocks(number)
        block = block.reshape(clips * rows, block.shape[-1])
        for start, stop, product in dot_tiles(block, mat, span, True, 256 * 2):
            terms[number, :, :, start:stop] = product.astype(terms.dtype).reshape(
                clips, rows, stop - start
            )

    return multiply


def dot_reduce_body(clips, rows, sub, window, span, back, left_ref, mat_ref, base_ref, *refs):
    refs = list(refs)
    take = lambda count: [refs.pop(0) for _ in range(count)]
    values_ref, gain_ref = take(2) if back else (None, None)
    sum_ref = take(1)[0]
    stats_ref = take(1)[0] if back else None
    left, mat, mat_sem, left_sem = take(4)
    terms = refs[0]
    place, depth, flip = plane_places()
    load = pltpu.make_async_copy(mat_ref.at[:, pl.ds(*window)], mat, mat_sem)
    load.start()
    loads = {}
    for number, slot in enumerate(plane_order()):
        loads[number] = [
            pltpu.make_async_copy(
                left_ref.at[clip, slot], left.at[number, clip], left_sem.at[number, clip]
            )
            for clip in range(clips)
        ]
        for copy in loads[number]:
            copy.start()
    greet([(flip(1), depth), (flip(2), depth), (flip(4), depth)])
    load.wait()

    def blocks(number):
        for copy in loads[number]:
            copy.wait()
        return left[number]

    steps = reduce_steps(
        clips,
        rows,
        sub,
        terms_of(clips, rows, blocks, mat, span, terms),
        final_back(values_ref, gain_ref, base_ref, sum_ref, stats_ref),
        *refs,
    )
    for _ in steps:
        pass


def dot_reduce(left, matrix, clips, collective_id, base, span=None, back=None, kind=jnp.float32, sub=64):
    wide = matrix.shape[0]
    rows, inner = left.shape[0] // (8 * clips), left.shape[1]
    low = jnp.bfloat16
    window, span = window_of(matrix, span)
    inside = pl.BlockSpec(memory_space=pltpu.VMEM)
    args = [left.reshape(clips, 8, rows, inner), matrix, base]
    in_specs = [any_spec(), any_spec(), inside]
    outs, out_specs = [jax.ShapeDtypeStruct((clips, rows, wide), kind)], [inside]
    if back is not None:
        args += list(back)
        in_specs += [inside] * 2
        outs.append(jax.ShapeDtypeStruct((2, wide), jnp.float32))
        out_specs.append(inside)
    return pl.pallas_call(
        functools.partial(dot_reduce_body, clips, rows, sub, window, span, back is not None),
        out_shape=outs,
        in_specs=in_specs,
        out_specs=out_specs,
        scratch_shapes=[
            pltpu.VMEM((8, clips, rows, inner), low),
            pltpu.VMEM((wide, window[1]), low),
            DMA(()),
            DMA((8, clips)),
        ]
        + reduce_scratch(clips, rows, sub, wide),
        compiler_params=communicating(collective_id),
    )(*args)


def ff_back_body(
    group,
    planes,
    clips,
    rows,
    sub,
    gates_ref,
    gate_mat_ref,
    hidden_ref,
    down_ref,
    normed_ref,
    grads_ref,
    base_ref,
    values_ref,
    gain_ref,
    sum_ref,
    stats_ref,
    outer_ref,
    own_ref,
    mid,
    gates,
    gate_mat,
    hidden,
    down,
    normed,
    grads,
    stage,
    kept,
    load_sem,
    gates_sem,
    tile_sem,
    stage_sem,
    *refs,
):
    refs = list(refs)
    first_refs, second_refs, sems = refs[:10], refs[10:20], refs[20:]
    place, depth, flip = plane_places()
    order = plane_order()
    loads = [
        pltpu.make_async_copy(down_ref, down, load_sem.at[0]),
        pltpu.make_async_copy(hidden_ref, hidden, load_sem.at[1]),
        pltpu.make_async_copy(gate_mat_ref, gate_mat, load_sem.at[2]),
    ]
    for copy in loads:
        copy.start()
    gate_loads = {}
    for number, slot in enumerate(order):
        gate_loads[number] = [
            pltpu.make_async_copy(
                gates_ref.at[clip, slot], gates.at[clip, slot], gates_sem.at[number, clip]
            )
            for clip in range(clips)
        ]
        for copy in gate_loads[number]:
            copy.start()
    tile = stage.shape[1]
    tiles = normed_ref.shape[3] // tile
    total_rows = 8 * clips * rows
    inner = gates.shape[3]

    def fetch(index):
        lanes = pl.ds(pl.multiple_of(index * tile, tile), tile)
        spot = lax.rem(index, 2)
        return [
            pltpu.make_async_copy(
                source.at[:, :, :, lanes], goal.at[spot], tile_sem.at[which, spot]
            )
            for which, (source, goal) in enumerate(((normed_ref, normed), (grads_ref, grads)))
        ]

    def stored(index):
        there = outer_ref.at[pl.ds(pl.multiple_of(index * tile, tile), tile)]
        spot = lax.rem(index, 2)
        return pltpu.make_async_copy(stage.at[spot], there, stage_sem.at[spot])

    def outer_tiles(first, last):
        def one(index, carry):
            spot = lax.rem(index, 2)

            @pl.when(index >= 2)
            def _():
                stored(index - 2).wait()

            for copy in fetch(index):
                copy.wait()
            stage[spot, :, :inner] = outer_sum(
                normed[spot].reshape(total_rows, tile), gates[...].reshape(total_rows, inner)
            ).astype(stage.dtype)
            stage[spot, :, inner:] = outer_sum(
                grads[spot].reshape(total_rows, tile),
                hidden[...].reshape(total_rows, hidden.shape[3]),
            ).astype(stage.dtype)
            stored(index).start()

            @pl.when(index + 2 < tiles)
            def _():
                for copy in fetch(index + 2):
                    copy.start()

            return carry

        lax.fori_loop(first, last, one, 0)

    for index in range(2):
        for copy in fetch(index):
            copy.start()
    greet_cross(group, planes)
    loads[0].wait()
    loads[1].wait()
    piece = kept.shape[2]

    def layer_rows(index, clip, span, result):
        result = (values_ref[clip, span] + result).astype(kept.dtype)
        start = index % (rows // sub) * sub
        for part in range(sub // piece):
            kept[clip, start // piece + part] = result[part * piece : part * piece + piece]

    first = reduce_steps(
        clips,
        rows,
        sub,
        terms_of(
            clips, rows, lambda number: hidden[order[number]], down, (0, down.shape[1]), first_refs[0]
        ),
        layer_rows,
        *first_refs,
    )

    def gate_rows(number):
        for copy in gate_loads[number]:
            copy.wait()
        return gates[:, order[number]]

    second = reduce_steps(
        clips,
        rows,
        sub,
        terms_of(clips, rows, gate_rows, gate_mat, (0, inner), second_refs[0]),
        final_back(values_ref, gain_ref, base_ref, sum_ref, stats_ref),
        *second_refs,
    )
    next(first)
    loads[2].wait()
    next(second)
    next(first)
    outer_tiles(0, 2)
    next(first)
    going = outward_steps(group, planes, kept, own_ref, mid, *sems)
    next(going)
    next(second)
    outer_tiles(2, tiles)
    next(going)
    next(second)
    next(going)
    for index in range(max(tiles - 2, 0), tiles):
        stored(index).wait()
    next(first)
    next(second)


def ff_back(gates, gate_mat, hidden, down, normed, grads, base, values, gain, planes, collective_id, sub=64):
    clips, rows, wide = base.shape
    group = 8
    piece = rows // planes
    low = jnp.bfloat16
    inner, columns = gates.shape[1], gates.shape[1] + hidden.shape[1]
    tile = 256
    inside = pl.BlockSpec(memory_space=pltpu.VMEM)
    moved = jax.ShapeDtypeStruct((group, piece, wide), low)
    *results, _ = pl.pallas_call(
        functools.partial(ff_back_body, group, planes, clips, rows, sub),
        out_shape=[
            jax.ShapeDtypeStruct((clips, rows, wide), jnp.float32),
            jax.ShapeDtypeStruct((2, wide), jnp.float32),
            jax.ShapeDtypeStruct((wide, columns), low),
            moved,
            moved,
        ],
        in_specs=[any_spec()] * 6 + [inside] * 3,
        out_specs=[inside] * 2 + [any_spec()] * 3,
        scratch_shapes=[
            pltpu.VMEM((clips, 8, rows, inner), low),
            pltpu.VMEM(gate_mat.shape, low),
            pltpu.VMEM((8, clips, rows, hidden.shape[1]), low),
            pltpu.VMEM(down.shape, low),
            pltpu.VMEM((2, clips, 8, rows, tile), low),
            pltpu.VMEM((2, 8, clips, rows, tile), low),
            pltpu.VMEM((2, tile, columns), low),
            pltpu.VMEM((clips, planes, piece, wide), low),
            DMA((3,)),
            DMA((8, clips)),
            DMA((2, 2)),
            DMA((2,)),
        ]
        + reduce_scratch(clips, rows, sub, wide) * 2
        + outward_scratch(group, planes),
        compiler_params=communicating(collective_id),
    )(
        gates.reshape(clips, 8, rows, inner),
        gate_mat,
        hidden.reshape(8, clips, rows, hidden.shape[1]),
        down,
        normed.reshape(clips, 8, rows, wide),
        grads.reshape(8, clips, rows, wide),
        base,
        values,
        gain,
    )
    return results


def rotary_lanes(places):
    half = HDIM // 2
    frequency = 10000.0 ** (-np.arange(half, dtype=np.float32) / np.float32(half))
    angles = places.astype(np.float32)[:, None] * frequency.astype(np.float32)[None, :]
    cosine, sine = np.cos(angles), np.sin(angles)
    both = [
        np.concatenate([cosine] * 4, axis=1),
        np.concatenate([-sine, sine, -sine, sine], axis=1),
    ]
    return jnp.asarray(np.stack(both).astype(np.float32))


def turn_heads(values, cosine, sine):
    lane = lax.broadcasted_iota(jnp.int32, values.shape, 1)
    half = HDIM // 2
    ahead = pltpu.roll(values, 2 * HDIM - half, 1)
    behind = pltpu.roll(values, half, 1)
    other = jnp.where(lax.rem(lane, HDIM) < half, ahead, behind)
    return values * cosine + other * sine


def swap_beside(pairs, send_sem, recv_sem, local_sem):
    place, depth, flip = plane_places()

    def each(act):
        for which, (source, goal) in enumerate(pairs):
            for mask in (6, 7, 2, 3, 4, 5, 1):
                other = flip(mask)
                act(
                    remote(
                        source(other),
                        goal(place),
                        send_sem.at[which, mask],
                        recv_sem.at[which, mask],
                        (other, depth),
                    )
                )

    stays = [
        pltpu.make_async_copy(source(place), goal(place), local_sem.at[which])
        for which, (source, goal) in enumerate(pairs)
    ]

    def begin():
        each(lambda copy: copy.start())
        for stay in stays:
            stay.start()

    def end():
        each(lambda copy: copy.wait())
        for stay in stays:
            stay.wait()

    return begin, end


def swap_beside_scratch(count):
    return [DMA((count, 8)), DMA((count, 8)), DMA((count,))]


def flash_forward_body(
    heads,
    tile,
    normed_ref,
    mat_ref,
    stamp_ref,
    bias_ref,
    rotary_ref,
    ff_ref,
    own_ref,
    turned_ref,
    out_ref,
    lse_ref,
    gate_up_ref,
    down_ref,
    kept_ref,
    mid,
    raw_ref,
    *sems,
):
    group, planes = gate_up_ref.shape[0], kept_ref.shape[1]
    hidden = down_ref.shape[2]
    step, last = pl.program_id(0), pl.num_programs(0) - 1

    def columns(block):
        return lambda other: ff_ref.at[
            :, pl.ds(pl.multiple_of((block * group + other) * hidden, 128), hidden)
        ]

    start_swap, end_swap = swap_beside(
        [
            (columns(0), lambda other: gate_up_ref.at[other, :, pl.ds(0, hidden)]),
            (columns(1), lambda other: gate_up_ref.at[other, :, pl.ds(hidden, hidden)]),
            (columns(2), lambda other: down_ref.at[other]),
        ],
        *sems[:3],
    )
    start_rows, pass_rows, end_rows = inward_beside(
        group, planes, own_ref, kept_ref, mid, *sems[3:]
    )

    @pl.when(step == 0)
    def _():
        greet_cross(group, planes)
        start_rows()
        start_swap()

    @pl.when(step == last)
    def _():
        pass_rows()

    def project(index, carry):
        place = pl.ds(pl.multiple_of(index * tile, tile), tile)
        raw_ref[place, :] = jnp.dot(
            normed_ref[place, :], mat_ref[...], preferred_element_type=jnp.float32
        )
        return carry

    lax.fori_loop(0, raw_ref.shape[0] // tile, project, 0)
    wide = heads * HDIM
    for pair in range(2 * wide // 128):
        lanes = slice(pair * 128, pair * 128 + 128)
        turned_ref[:, lanes] = turn_heads(
            raw_ref[:, lanes], rotary_ref[0], rotary_ref[1]
        ).astype(turned_ref.dtype)
    turned_ref[:, 2 * wide :] = raw_ref[:, 2 * wide :].astype(turned_ref.dtype)
    rows = raw_ref.shape[0]
    bias = bias_ref[0]
    scale = HDIM**-0.5
    for head in range(heads):
        lanes = slice(head * HDIM, head * HDIM + HDIM)
        keys = turned_ref[:, wide + head * HDIM : wide + head * HDIM + HDIM]
        values = turned_ref[:, 2 * wide + head * HDIM : 2 * wide + head * HDIM + HDIM]
        stamp_key = stamp_ref[0, :, lanes].astype(jnp.float32)
        stamp_value = stamp_ref[
            0, :, wide + head * HDIM : wide + head * HDIM + HDIM
        ].astype(jnp.float32)

        def one(step, carry):
            place = pl.ds(pl.multiple_of(step * tile, tile), tile)
            query = turned_ref[place, lanes] * jnp.asarray(scale, turned_ref.dtype)
            scores = times_transposed(query, keys) + bias
            stamp_score = jnp.sum(query.astype(jnp.float32) * stamp_key, axis=1, keepdims=True)
            top = jnp.maximum(jnp.max(scores, axis=1, keepdims=True), stamp_score)
            expo = jnp.exp(scores - top)
            stamp_expo = jnp.exp(stamp_score - top)
            denom = jnp.sum(expo, axis=1, keepdims=True) + stamp_expo
            share = 1.0 / denom
            prob = (expo * share).astype(values.dtype)
            stamp_prob = (stamp_expo * share).astype(values.dtype).astype(jnp.float32)
            mixed = jnp.dot(prob, values, preferred_element_type=jnp.float32)
            out_ref[place, lanes] = (mixed + stamp_prob * stamp_value).astype(out_ref.dtype)
            lse_ref[place, head : head + 1] = top + jnp.log(denom)
            return carry

        lax.fori_loop(0, rows // tile, one, 0)

    @pl.when(step == last)
    def _():
        end_swap()
        end_rows()


def flash_forward(normed, matrix, stamps, bias, rotary, heads, ff_low, rows_of_clip, collective_id):
    clips, rows = bias.shape
    wide = heads * HDIM
    group, piece, features = rows_of_clip.shape
    planes = group // clips
    owned, columns = ff_low.shape
    hidden = columns // (3 * group)
    like = lambda *shape: jax.ShapeDtypeStruct(shape, rows_of_clip.dtype)
    blocked = lambda lanes: pl.BlockSpec((rows, lanes), lambda clip: (clip, 0))
    *results, _ = pl.pallas_call(
        functools.partial(flash_forward_body, heads, rows // 4),
        grid=(clips,),
        out_shape=[
            like(clips * rows, 3 * wide),
            like(clips * rows, wide),
            jax.ShapeDtypeStruct((clips * rows, 128), jnp.float32),
            like(group, owned, 2 * hidden),
            like(group, owned, hidden),
            like(clips, planes, piece, features),
            like(group, piece, features),
        ],
        in_specs=[
            blocked(features),
            pl.BlockSpec(matrix.shape, lambda clip: (0, 0)),
            pl.BlockSpec((1, 1, 2 * wide), lambda clip: (clip, 0, 0)),
            pl.BlockSpec((1, 1, rows), lambda clip: (clip, 0, 0)),
            pl.BlockSpec((2, rows, 128), lambda clip: (0, 0, 0)),
            any_spec(),
            any_spec(),
        ],
        out_specs=[blocked(3 * wide), blocked(wide), blocked(128)] + [any_spec()] * 4,
        scratch_shapes=[pltpu.VMEM((rows, 3 * wide), jnp.float32)]
        + swap_beside_scratch(3)
        + inward_scratch(group, planes),
        compiler_params=communicating(collective_id),
    )(normed, matrix, stamps[:, None], bias[:, None], rotary, ff_low, rows_of_clip)
    return results


def flash_backward_body(
    heads,
    tile,
    turned_ref,
    grad_ref,
    lse_ref,
    stamp_ref,
    bias_ref,
    rotary_ref,
    cut_ref,
    out_ref,
    stamp_out_ref,
    mine_ref,
    query_grad,
    key_grad,
    value_grad,
    *sems,
):
    place, depth, flip = plane_places()
    start_swap, end_swap = swap_beside(
        [(lambda other: cut_ref.at[other], lambda other: mine_ref.at[other])], *sems
    )

    @pl.when(pl.program_id(0) == 0)
    def _():
        greet([(flip(mask), depth) for mask in range(1, 8)])
        start_swap()

    wide = heads * HDIM
    rows = turned_ref.shape[0]
    scale = HDIM**-0.5
    low = turned_ref.dtype
    f32 = jnp.float32
    lse_rows = lse_ref[...].T
    first_row = lax.broadcasted_iota(jnp.int32, (8, tile), 0) == 0
    for head in range(heads):
        lanes = slice(head * HDIM, head * HDIM + HDIM)
        later = slice(wide + head * HDIM, wide + head * HDIM + HDIM)
        keys = turned_ref[:, later]
        values = turned_ref[:, 2 * wide + head * HDIM : 2 * wide + head * HDIM + HDIM]
        keys_across = keys.astype(f32).T.astype(low)
        stamp_key = jnp.broadcast_to(stamp_ref[0, :, lanes], (8, HDIM))
        stamp_value = jnp.broadcast_to(stamp_ref[0, :, later], (8, HDIM))
        stamp_column = stamp_ref[0, :, lanes].astype(f32).T
        bias = bias_ref[0]
        key_total = jnp.zeros((rows, HDIM), f32)
        value_total = jnp.zeros((rows, HDIM), f32)
        stamp_key_total = jnp.zeros((8, HDIM), f32)
        stamp_value_total = jnp.zeros((8, HDIM), f32)
        for step in range(rows // tile):
            place = slice(step * tile, step * tile + tile)
            query = turned_ref[place, lanes] * jnp.asarray(scale, low)
            grad = grad_ref[place, lanes]
            lse = lse_rows[head : head + 1, place]
            prob = jnp.exp(times_transposed(keys, query) + bias - lse)
            stamp_prob = jnp.exp(times_transposed(stamp_key, query) - lse)
            grad_prob = times_transposed(values, grad)
            stamp_grad_prob = times_transposed(stamp_value, grad)
            delta = jnp.sum(prob * grad_prob, axis=0, keepdims=True)
            delta = delta + (stamp_prob * stamp_grad_prob)[:1]
            scores = (prob * (grad_prob - delta)).astype(low)
            stamp_scores = (stamp_prob * (stamp_grad_prob - delta)).astype(low)
            stamp_scores = jnp.where(first_row, stamp_scores.astype(f32), 0.0)
            value_total += jnp.dot(prob.astype(low), grad, preferred_element_type=f32)
            key_total += jnp.dot(scores, query, preferred_element_type=f32)
            across = jnp.dot(keys_across, scores, preferred_element_type=f32)
            across = across + stamp_column * stamp_scores[:1]
            query_grad[place, lanes] = across.T * scale
            stamp_key_total += jnp.dot(
                stamp_scores.astype(low), query, preferred_element_type=f32
            )
            stamp_value_total += jnp.dot(
                jnp.where(first_row, stamp_prob, 0.0).astype(low), grad, preferred_element_type=f32
            )
        key_grad[:, lanes] = key_total
        value_grad[:, lanes] = value_total
        stamp_out_ref[0, :, lanes] = stamp_key_total[:1]
        stamp_out_ref[0, :, later] = stamp_value_total[:1]
    both = jnp.concatenate([query_grad[...], key_grad[...]], axis=1)
    for pair in range(2 * wide // 128):
        lanes = slice(pair * 128, pair * 128 + 128)
        out_ref[:, lanes] = turn_heads(both[:, lanes], rotary_ref[0], -rotary_ref[1]).astype(low)
    out_ref[:, 2 * wide :] = value_grad[...].astype(low)
    pl.when(pl.program_id(0) == pl.num_programs(0) - 1)(end_swap)


def flash_backward(turned, grad, lse, stamps, bias, rotary, heads, cut, collective_id):
    clips, rows = bias.shape
    wide = heads * HDIM
    blocked = lambda lanes: pl.BlockSpec((rows, lanes), lambda clip: (clip, 0))
    grads, stamp_grads, mine = pl.pallas_call(
        functools.partial(flash_backward_body, heads, rows // 4),
        grid=(clips,),
        out_shape=[
            jax.ShapeDtypeStruct((clips * rows, 3 * wide), jnp.bfloat16),
            jax.ShapeDtypeStruct((clips, 1, 2 * wide), jnp.float32),
            jax.ShapeDtypeStruct(cut.shape, cut.dtype),
        ],
        in_specs=[
            blocked(3 * wide),
            blocked(wide),
            blocked(128),
            pl.BlockSpec((1, 1, 2 * wide), lambda clip: (clip, 0, 0)),
            pl.BlockSpec((1, rows, 1), lambda clip: (clip, 0, 0)),
            pl.BlockSpec((2, rows, 128), lambda clip: (0, 0, 0)),
            any_spec(),
        ],
        out_specs=[
            blocked(3 * wide),
            pl.BlockSpec((1, 1, 2 * wide), lambda clip: (clip, 0, 0)),
            any_spec(),
        ],
        scratch_shapes=[pltpu.VMEM((rows, wide), jnp.float32)] * 3 + swap_beside_scratch(1),
        compiler_params=communicating(collective_id),
    )(turned, grad, lse, stamps[:, None], bias[:, :, None], rotary, cut)
    return grads, stamp_grads[:, 0], mine


def adam_body(factor_ref, weight_ref, first_ref, second_ref, grad_ref, *outs):
    gradient = jnp.concatenate(
        [grad_ref[part] for part in range(grad_ref.shape[0])], axis=1
    ).astype(jnp.float32)
    results = adam_step(
        weight_ref[...],
        first_ref[...],
        second_ref[...],
        gradient * factor_ref[0, 0],
        matrix_rate,
        matrix_decay,
    )
    for out, result in zip(outs, results):
        out[...] = result


def adam_blocks_body(places, factor_ref, weight_ref, first_ref, second_ref, *refs):
    *owned_refs, weight_out, first_out, second_out = refs
    for block, (which, start, stop) in enumerate(places):

        @pl.when(pl.program_id(0) == block)
        def _(owned_ref=owned_refs[which], start=start, stop=stop):
            gradient = jnp.concatenate(
                [owned_ref[part, :, start:stop] for part in range(owned_ref.shape[0])], axis=1
            ).astype(jnp.float32)
            results = adam_step(
                weight_ref[...],
                first_ref[...],
                second_ref[...],
                gradient * factor_ref[0, 0],
                matrix_rate,
                matrix_decay,
            )
            weight_out[...], first_out[...], second_out[...] = results


def adam_blocks(factor, weight, first, second, owned, width):
    rows, columns = weight.shape
    group = owned[0].shape[0]
    blocks = columns // (group * width)
    places = [
        (which, start, start + width)
        for which, pieces in enumerate(owned)
        for start in range(0, pieces.shape[2], width)
    ][:blocks]
    piece = pl.BlockSpec((rows, group * width), lambda block: (0, block))
    whole = [pl.BlockSpec(pieces.shape, lambda block: (0, 0, 0)) for pieces in owned]
    return pl.pallas_call(
        functools.partial(adam_blocks_body, places),
        grid=(blocks,),
        out_shape=[jax.ShapeDtypeStruct(weight.shape, jnp.float32)] * 3,
        in_specs=[pl.BlockSpec(memory_space=pltpu.SMEM), piece, piece, piece] + whole,
        out_specs=[piece] * 3,
        compiler_params=pltpu.CompilerParams(vmem_limit_bytes=VMEM_LIMIT),
    )(factor, weight, first, second, *owned)


def adam_matrix(factor, weight, first, second, owned, width, parts):
    rows, columns = weight.shape
    group = owned.shape[0]
    steps = group // parts
    piece = pl.BlockSpec((rows, parts * width), lambda block, step: (0, block * steps + step))
    grads = pl.BlockSpec((parts, rows, width), lambda block, step: (step, 0, block))
    return pl.pallas_call(
        adam_body,
        grid=(columns // (group * width), steps),
        out_shape=[jax.ShapeDtypeStruct(weight.shape, jnp.float32)] * 3,
        in_specs=[pl.BlockSpec(memory_space=pltpu.SMEM), piece, piece, piece, grads],
        out_specs=[piece] * 3,
        compiler_params=pltpu.CompilerParams(vmem_limit_bytes=VMEM_LIMIT),
    )(factor, weight, first, second, owned)


def plane_device(
    frames,
    time_token,
    cond_ids,
    cond_mask,
    lengths,
    cond_table,
    cotangent,
    attn_weight,
    cross_weight,
    norm_param,
    ff_weight,
    attn_first,
    attn_second,
    cross_first,
    cross_second,
    norm_first,
    norm_second,
    ff_first,
    ff_second,
):
    group, planes = lax.axis_size("dp"), lax.axis_size("seq")
    place, depth = lax.axis_index("dp"), lax.axis_index("seq")
    clips = group // planes
    _, frame_rows, wide = frames.shape
    piece = frame_rows // group
    seq_frames = frame_rows * planes
    own_rows = planes * piece
    heads = HEADS // group
    head_wide = heads * HDIM
    ff_wide = FF // group
    owned = wide // (group * planes)
    cond_count, cond_wide = cond_ids.shape[1], cond_table.shape[1]
    cond_owned = cross_weight.shape[0]

    order = jnp.arange(wide).reshape(group, planes, owned).swapaxes(0, 1).reshape(wide)
    order_mat = (jnp.arange(wide)[:, None] == order[None, :]).astype(jnp.bfloat16)

    def to_plane_order(values):
        return jnp.dot(values, order_mat, preferred_element_type=jnp.float32).astype(jnp.bfloat16)

    def to_whole_order(values):
        return times_transposed(values, order_mat)

    attn_low = attn_weight.astype(jnp.bfloat16).reshape(owned, 6, group, head_wide)
    attn_cut = attn_low.transpose(2, 0, 1, 3).reshape(group, owned, 6 * head_wide)
    cross_low = cross_weight.astype(jnp.bfloat16).reshape(cond_owned, 2, group, head_wide)
    cross_cut = cross_low.transpose(2, 0, 1, 3).reshape(group, owned, -1)
    norm_block = norm_param.astype(jnp.bfloat16).astype(jnp.float32)
    norm_block = jnp.pad(norm_block, ((0, 2), (0, 128 - owned)))
    pack = jnp.concatenate(
        [
            time_token.astype(jnp.float32),
            jnp.pad(cond_ids.astype(jnp.float32), ((0, 0), (0, wide - cond_count))),
            jnp.pad(cond_mask.astype(jnp.float32), ((0, 0), (0, wide - cond_count))),
            jnp.broadcast_to(lengths.astype(jnp.float32)[:, None], (1, wide)),
            jnp.zeros((4, wide), jnp.float32),
        ],
        axis=0,
    )
    stream, gain_rows, packs, qkv_mine, rest_mine = enter(
        to_plane_order(frames[0]).reshape(group, piece, wide),
        norm_block,
        pack,
        attn_cut[:, :, : 3 * head_wide],
        jnp.concatenate([attn_cut[:, :, 3 * head_wide :], cross_cut], axis=2),
        planes,
        1,
    )
    stream = stream.reshape(clips, own_rows, wide).astype(jnp.float32)
    ff_low = ff_weight.astype(jnp.bfloat16)

    def over_planes(block):
        return lax.all_gather(block.reshape(group * owned, -1), "seq", axis=0, tiled=True)

    w_qkv = over_planes(qkv_mine)
    w_rest = over_planes(rest_mine)
    of_self_out = (0, head_wide)
    of_cross_query = (head_wide, 2 * head_wide)
    of_cross_out = (2 * head_wide, 3 * head_wide)
    w_cond = w_rest[:, 3 * head_wide :].reshape(planes, group, cond_owned, -1)
    w_cond = jnp.swapaxes(w_cond, 0, 1).reshape(cond_wide, 2 * head_wide)
    plane_packs = lax.dynamic_slice_in_dim(packs, depth * clips, clips, axis=0)
    stamps = to_plane_order(plane_packs[:, 0].astype(jnp.bfloat16)).astype(jnp.float32)
    cond_keep = plane_packs[:, 2, :cond_count] > 0
    clip_lengths = plane_packs[:, 3, 0].astype(jnp.int32)
    share = cond_count // group
    all_ids = packs[:, 1, :cond_count].astype(jnp.int32)
    own_ids = lax.dynamic_slice_in_dim(all_ids, place * share, share, axis=1)
    vocab_rows = cond_table.shape[0]
    relative = own_ids - depth * vocab_rows
    inside = (relative >= 0) & (relative < vocab_rows)
    picked = jnp.take(cond_table, jnp.clip(relative, 0, vocab_rows - 1), axis=0)
    picked = jnp.where(inside[..., None], picked, jnp.zeros((), picked.dtype))
    picked = picked.reshape(planes, clips, share, cond_wide)
    positions = depth * frame_rows + jnp.arange(frame_rows)
    frame_valid = (positions[None, :] < lengths[:, None]).astype(cotangent.dtype)
    masked = to_plane_order((cotangent * frame_valid[..., None])[0])

    group_rows = clips * seq_frames
    row_place = np.arange(seq_frames)
    row_owner, row_rest = row_place // own_rows, row_place % own_rows
    true_place = (row_rest // piece) * frame_rows + row_owner * piece + row_rest % piece
    key_keep = true_place[None, :] < clip_lengths[:, None]
    group_shape = (clips, seq_frames, heads, HDIM)

    group_one, cond = gather_dot(stream, None, None, 5, gain_rows[0:2], picked)
    cond_flat = cond.swapaxes(0, 1).reshape(clips * cond_count, cond_wide)
    stamp_normed = layer_norm(stamps, gain_rows[0], gain_rows[1]).astype(jnp.bfloat16)
    stamp_pair = jnp.dot(stamp_normed, w_qkv[:, head_wide:], preferred_element_type=jnp.float32)
    stamp_pair = stamp_pair.astype(jnp.bfloat16)
    rotary = rotary_lanes(true_place)
    key_bias = jnp.where(key_keep, 0.0, masked_score)
    rotated, self_low, self_lse, gate_up_mine, down_mine, grad_out_low = flash_forward(
        group_one,
        w_qkv,
        stamp_pair,
        key_bias,
        rotary,
        heads,
        ff_low,
        masked.reshape(group, piece, wide),
        2,
    )
    grad_out_low = grad_out_low.reshape(clips, own_rows, wide)
    grad_out = grad_out_low.astype(jnp.float32)
    w_gate_up = over_planes(gate_up_mine)
    w_down = over_planes(down_mine)
    cond_pair = jnp.dot(cond_flat, w_cond, preferred_element_type=jnp.float32)
    cond_pair = cond_pair.astype(jnp.bfloat16).reshape(clips, cond_count, 2 * head_wide)
    cond_bias = jnp.where(cond_keep, 0.0, masked_score)[:, None]
    (resid_one,) = dot_reduce(self_low, w_rest, clips, 6, stream, of_self_out)
    group_two, cross_query, cross_out = gather_dot(
        resid_one,
        w_rest,
        None,
        7,
        gain_rows[2:4],
        span=of_cross_query,
        pair=cond_pair,
        bias=cond_bias,
    )
    (resid_two,) = dot_reduce(cross_out, w_rest, clips, 8, resid_one, of_cross_out)
    group_three, gate_up = gather_dot(resid_two, w_gate_up, jnp.float32, 9, gain_rows[4:6])
    gate_up, grad_out_low = lax.optimization_barrier((gate_up, grad_out_low))
    group_grad_out, grad_gate_up, hidden = gather_dot(
        grad_out_low, w_down, None, 10, gate_up=gate_up
    )
    def over_rows(block):
        return lax.psum_scatter(
            block.astype(jnp.bfloat16), "seq", scatter_dimension=0, tiled=True
        ).reshape(group, owned, -1)

    grad_two, stats_three, ff_piece, layer_out = ff_back(
        grad_gate_up,
        w_gate_up,
        hidden,
        w_down,
        group_three,
        group_grad_out,
        grad_out_low,
        resid_two,
        gain_rows[4:5],
        planes,
        13,
    )
    layer_out = to_whole_order(layer_out.reshape(frame_rows, wide)).astype(jnp.bfloat16)
    layer_out = layer_out.reshape(frames.shape)
    ff_rows = over_rows(ff_piece)
    group_cross_branch, grad_cross_query, cond_grad = gather_dot(
        grad_two,
        w_rest,
        None,
        15,
        span=of_cross_out,
        pair=cond_pair,
        bias=cond_bias,
        query=cross_query,
    )
    grad_one, stats_two = dot_reduce(
        grad_cross_query,
        w_rest,
        clips,
        16,
        grad_two,
        of_cross_query,
        back=(resid_one, gain_rows[2:3]),
    )
    group_self_branch, grad_self_mixed = gather_dot(
        grad_one, w_rest, jnp.bfloat16, 17, span=of_self_out
    )
    cond_grad = cond_grad.reshape(clips * cond_count, 2 * head_wide)
    cross_piece = split_outer(cond_flat, cond_grad)
    cross_piece = cross_piece.reshape(group, planes, cond_owned, 2 * head_wide)
    cross_piece = jnp.swapaxes(cross_piece, 0, 1).reshape(wide, head_wide)
    rest_piece = jnp.concatenate(
        [
            outer_sum(group_self_branch, self_low),
            outer_sum(group_two, grad_cross_query),
            outer_sum(group_cross_branch, cross_out),
            cross_piece,
        ],
        axis=1,
    )
    rest_piece = rest_piece.astype(jnp.bfloat16)
    grad_self_mixed, rest_piece = lax.optimization_barrier((grad_self_mixed, rest_piece))
    rest_piece, ff_rows = lax.optimization_barrier((rest_piece, ff_rows))
    rest_rows = over_rows(rest_piece)
    grad_project, stamp_grad, ff_owned = flash_backward(
        rotated, grad_self_mixed, self_lse, stamp_pair, key_bias, rotary, heads, ff_rows, 3
    )
    grad_stamp_normed = split_times_transposed(stamp_grad, w_qkv[:, head_wide:])
    qkv_piece = outer_sum(group_one, grad_project)
    stamp_weight_grad = split_outer(stamp_normed, stamp_grad)
    qkv_piece = jnp.concatenate(
        [qkv_piece[:, :head_wide], qkv_piece[:, head_wide:] + stamp_weight_grad], axis=1
    )
    qkv_piece = qkv_piece.astype(jnp.bfloat16)
    grad_project, qkv_piece = lax.optimization_barrier((grad_project, qkv_piece))
    qkv_rows = over_rows(qkv_piece)
    grad_project, rest_rows = lax.optimization_barrier((grad_project, rest_rows))
    frames_grad, stats_one = dot_reduce(
        grad_project,
        w_qkv,
        clips,
        18,
        grad_one,
        back=(stream, gain_rows[0:1]),
        kind=jnp.bfloat16,
    )
    _, norm_stamp_back = jax.vjp(layer_norm, stamps, gain_rows[0], gain_rows[1])
    _, grad_gain_stamp, grad_bias_stamp = norm_stamp_back(grad_stamp_normed)
    stamp_stats = jnp.stack([grad_gain_stamp, grad_bias_stamp])
    norm_grad = jnp.concatenate([stats_one + stamp_stats, stats_two, stats_three], axis=0)
    norm_parts = norm_grad.reshape(6, planes, group, owned).transpose(2, 1, 0, 3)
    norm_parts = norm_parts.reshape(group * planes, 6, owned)
    norm_parts = jnp.pad(norm_parts, ((0, 0), (0, 2), (0, 128 - owned)))
    ff_squares = jnp.sum(jnp.square(ff_owned.astype(jnp.float32)))
    frames_grad, qkv_owned, rest_owned, norm_sum, total = leave(
        frames_grad.reshape(clips, planes, piece, wide),
        qkv_rows,
        rest_rows,
        norm_parts,
        ff_squares.reshape(1, 1),
        20,
    )
    frames_grad = to_whole_order(frames_grad.reshape(frame_rows, wide)).reshape(frames.shape)
    cross_reduced = rest_owned[:, :, 3 * head_wide :].reshape(group, cond_owned, 2, head_wide)
    cross_reduced = cross_reduced.transpose(1, 2, 0, 3).reshape(cross_weight.shape)
    cross_reduced = cross_reduced.astype(jnp.float32)
    norm_reduced = norm_sum[:6, :owned]
    grad_norm = jnp.sqrt(total[0, 0])
    factor = jnp.minimum(1.0, clip_limit / grad_norm)
    factor_block = factor.reshape(1, 1)
    attn_new, attn_first_new, attn_second_new = adam_blocks(
        factor_block, attn_weight, attn_first, attn_second, [qkv_owned, rest_owned], head_wide
    )
    cross_new, cross_first_new, cross_second_new = adam_step(
        cross_weight, cross_first, cross_second, cross_reduced * factor, matrix_rate, matrix_decay
    )
    norm_new, norm_first_new, norm_second_new = adam_step(
        norm_param, norm_first, norm_second, norm_reduced * factor, gain_rate, 0.0
    )
    ff_new, ff_first_new, ff_second_new = adam_matrix(
        factor_block, ff_weight, ff_first, ff_second, ff_owned, ff_wide, group // 2
    )
    return (
        layer_out,
        frames_grad,
        grad_norm,
        attn_new,
        cross_new,
        norm_new,
        ff_new,
        attn_first_new,
        cross_first_new,
        norm_first_new,
        ff_first_new,
        attn_second_new,
        cross_second_new,
        norm_second_new,
        ff_second_new,
    )


def solution(mesh):
    return jax.shard_map(
        plane_device if plane_fits(mesh) else per_device,
        mesh=mesh,
        in_specs=(
            P("dp", "seq", None),
            P("dp", None),
            P("dp", None),
            P("dp", None),
            P("dp"),
            P("seq", None),
            P("dp", "seq", None),
            P(("dp", "seq"), None),
            P(("dp", "seq"), None),
            P(None, ("dp", "seq")),
            P(("dp", "seq"), None),
            P(("dp", "seq"), None),
            P(("dp", "seq"), None),
            P(("dp", "seq"), None),
            P(("dp", "seq"), None),
            P(None, ("dp", "seq")),
            P(None, ("dp", "seq")),
            P(("dp", "seq"), None),
            P(("dp", "seq"), None),
        ),
        out_specs=(
            P("dp", "seq", None),
            P("dp", "seq", None),
            P(),
            P(("dp", "seq"), None),
            P(("dp", "seq"), None),
            P(None, ("dp", "seq")),
            P(("dp", "seq"), None),
            P(("dp", "seq"), None),
            P(("dp", "seq"), None),
            P(None, ("dp", "seq")),
            P(("dp", "seq"), None),
            P(("dp", "seq"), None),
            P(("dp", "seq"), None),
            P(None, ("dp", "seq")),
            P(("dp", "seq"), None),
        ),
        check_vma=False,
    )
```

```python
import functools

import jax
import jax.numpy as jnp
import numpy as np
from jax import lax
from jax.experimental import pallas as pl
from jax.experimental.pallas import tpu as pltpu
from jax.sharding import PartitionSpec as P

HEADS = 24
HDIM = 64
FF = 6144
UPDATE_STEP = 10


norm_eps = 1e-05
beta_first = 0.5
beta_second = 0.5
adam_eps = 1e-08
matrix_decay = 0.01
matrix_rate = 0.03
gain_rate = 0.25
clip_limit = 1.0
masked_score = -1e30


def layer_norm(values, gain_row, bias_row):
    center = values - jnp.mean(values, axis=-1, keepdims=True)
    spread = jnp.mean(center * center, axis=-1, keepdims=True)
    return center * lax.rsqrt(spread + norm_eps) * gain_row + bias_row


def rotary_tables(positions, head_size):
    half_size = head_size // 2
    frequency = 10000.0 ** (-jnp.arange(half_size, dtype=jnp.float32) / half_size)
    angles = positions.astype(jnp.float32)[:, None] * frequency[None, :]
    return (jnp.cos(angles)[:, None, :], jnp.sin(angles)[:, None, :])


def rotate(values, cosine_table, sine_table):
    half_size = values.shape[-1] // 2
    first_half = values[..., :half_size]
    second_half = values[..., half_size:]
    return jnp.concatenate(
        [
            first_half * cosine_table - second_half * sine_table,
            second_half * cosine_table + first_half * sine_table,
        ],
        axis=-1,
    )


def outer_sum(left_mat, right_mat):
    return lax.dot_general(
        left_mat, right_mat, (((0,), (0,)), ((), ())), preferred_element_type=jnp.float32
    )


def times_transposed(left_mat, right_mat):
    return lax.dot_general(
        left_mat, right_mat, (((1,), (1,)), ((), ())), preferred_element_type=jnp.float32
    )


def split_parts(values):
    upper = values.astype(jnp.bfloat16)
    lower = (values - upper.astype(jnp.float32)).astype(jnp.bfloat16)
    return (upper, lower)


def split_outer(left_low, right_full):
    upper, lower = split_parts(right_full)
    return outer_sum(left_low, upper) + outer_sum(left_low, lower)


def split_times_transposed(left_full, right_low):
    upper, lower = split_parts(left_full)
    return times_transposed(upper, right_low) + times_transposed(lower, right_low)


def self_scores(queries, keys, stamp_key, keep):
    score_scale = HDIM ** (-0.5)
    frame_part = (
        jnp.einsum("cqhd,ckhd->chqk", queries, keys, preferred_element_type=jnp.float32)
        * score_scale
    )
    frame_part = jnp.where(keep[:, None, None, :], frame_part, masked_score)
    stamp_part = (
        jnp.einsum("cqhd,chd->chq", queries, stamp_key, preferred_element_type=jnp.float32)
        * score_scale
    )
    return (frame_part, stamp_part)


def self_forward(queries, keys, values, stamp_key, stamp_value, keep):
    frame_scores, stamp_scores = self_scores(queries, keys, stamp_key, keep)
    top_score = jnp.maximum(jnp.max(frame_scores, axis=-1), stamp_scores)
    frame_expo = jnp.exp(frame_scores - top_score[..., None])
    stamp_expo = jnp.exp(stamp_scores - top_score)
    denom = jnp.sum(frame_expo, axis=-1) + stamp_expo
    self_lse = top_score + jnp.log(denom)
    frame_prob = (frame_expo / denom[..., None]).astype(jnp.bfloat16)
    stamp_prob = (stamp_expo / denom).astype(jnp.bfloat16)
    mixed = jnp.einsum(
        "chqk,ckhd->cqhd", frame_prob, values, preferred_element_type=jnp.float32
    ) + jnp.einsum("chq,chd->cqhd", stamp_prob, stamp_value, preferred_element_type=jnp.float32)
    return (mixed, self_lse)


def self_backward(queries, keys, values, stamp_key, stamp_value, keep, self_lse, grad_mixed):
    score_scale = HDIM ** (-0.5)
    frame_scores, stamp_scores = self_scores(queries, keys, stamp_key, keep)
    frame_prob = jnp.exp(frame_scores - self_lse[..., None])
    stamp_prob = jnp.exp(stamp_scores - self_lse)
    grad_frame_prob = jnp.einsum(
        "cqhd,ckhd->chqk", grad_mixed, values, preferred_element_type=jnp.float32
    )
    grad_stamp_prob = jnp.einsum(
        "cqhd,chd->chq", grad_mixed, stamp_value, preferred_element_type=jnp.float32
    )
    delta = jnp.sum(frame_prob * grad_frame_prob, axis=-1) + stamp_prob * grad_stamp_prob
    grad_frame_scores = (frame_prob * (grad_frame_prob - delta[..., None])).astype(jnp.bfloat16)
    grad_stamp_scores = (stamp_prob * (grad_stamp_prob - delta)).astype(jnp.bfloat16)
    grad_queries = (
        jnp.einsum("chqk,ckhd->cqhd", grad_frame_scores, keys, preferred_element_type=jnp.float32)
        + jnp.einsum(
            "chq,chd->cqhd", grad_stamp_scores, stamp_key, preferred_element_type=jnp.float32
        )
    ) * score_scale
    key_part = (
        jnp.einsum(
            "chqk,cqhd->ckhd", grad_frame_scores, queries, preferred_element_type=jnp.float32
        )
        * score_scale
    )
    value_part = jnp.einsum(
        "chqk,cqhd->ckhd",
        frame_prob.astype(jnp.bfloat16),
        grad_mixed,
        preferred_element_type=jnp.float32,
    )
    grad_stamp_key = (
        jnp.einsum("chq,cqhd->chd", grad_stamp_scores, queries, preferred_element_type=jnp.float32)
        * score_scale
    )
    grad_stamp_value = jnp.einsum(
        "chq,cqhd->chd",
        stamp_prob.astype(jnp.bfloat16),
        grad_mixed,
        preferred_element_type=jnp.float32,
    )
    return (grad_queries, key_part, value_part, grad_stamp_key, grad_stamp_value)


def cross_scores(query, keys, keep):
    score_scale = HDIM ** (-0.5)
    scores = (
        jnp.einsum("cqhd,ckhd->chqk", query, keys, preferred_element_type=jnp.float32) * score_scale
    )
    return jnp.where(keep[:, None, None, :], scores, masked_score)


def cross_forward(query, keys, values, keep):
    scores = cross_scores(query, keys, keep)
    top_score = jnp.max(scores, axis=-1)
    expo = jnp.exp(scores - top_score[..., None])
    denom = jnp.sum(expo, axis=-1)
    cross_lse = top_score + jnp.log(denom)
    prob = (expo / denom[..., None]).astype(jnp.bfloat16)
    mixed = jnp.einsum("chqk,ckhd->cqhd", prob, values, preferred_element_type=jnp.float32)
    return (mixed, cross_lse)


def cross_backward(query, keys, values, keep, cross_lse, grad_mixed):
    score_scale = HDIM ** (-0.5)
    prob = jnp.exp(cross_scores(query, keys, keep) - cross_lse[..., None])
    grad_prob = jnp.einsum(
        "cqhd,ckhd->chqk", grad_mixed, values, preferred_element_type=jnp.float32
    )
    delta = jnp.sum(prob * grad_prob, axis=-1)
    grad_scores = (prob * (grad_prob - delta[..., None])).astype(jnp.bfloat16)
    grad_query = (
        jnp.einsum("chqk,ckhd->cqhd", grad_scores, keys, preferred_element_type=jnp.float32)
        * score_scale
    )
    grad_keys = (
        jnp.einsum("chqk,cqhd->ckhd", grad_scores, query, preferred_element_type=jnp.float32)
        * score_scale
    )
    grad_values = jnp.einsum(
        "chqk,cqhd->ckhd", prob.astype(jnp.bfloat16), grad_mixed, preferred_element_type=jnp.float32
    )
    return (grad_query, grad_keys, grad_values)


def adam_step(weight, first, second, gradient, step_rate, decay_rate):
    first_new = beta_first * first + (1.0 - beta_first) * gradient
    second_new = beta_second * second + (1.0 - beta_second) * gradient * gradient
    fix_first = 1.0 - beta_first**UPDATE_STEP
    fix_second = 1.0 - beta_second**UPDATE_STEP
    normed_step = first_new / fix_first / (jnp.sqrt(second_new / fix_second) + adam_eps)
    return (weight - step_rate * (normed_step + decay_rate * weight), first_new, second_new)


def per_device(
    frames,
    time_token,
    cond_ids,
    cond_mask,
    lengths,
    cond_table,
    cotangent,
    attn_weight,
    cross_weight,
    norm_param,
    ff_weight,
    attn_first,
    attn_second,
    cross_first,
    cross_second,
    norm_first,
    norm_second,
    ff_first,
    ff_second,
):
    clip_count, frame_rows, wide = frames.shape
    hidden_width = FF
    token_count = clip_count * frame_rows
    seq_count = lax.axis_size("seq")
    seq_frames = frame_rows * seq_count
    seq_place = lax.axis_index("seq")
    vocab_rows = cond_table.shape[0]
    relative = cond_ids - seq_place * vocab_rows
    inside = (relative >= 0) & (relative < vocab_rows)
    picked = jnp.take(cond_table, jnp.clip(relative, 0, vocab_rows - 1), axis=0).astype(jnp.float32)
    picked = jnp.where(inside[..., None], picked, 0.0)
    cond = lax.psum(picked.astype(jnp.bfloat16), "seq")
    cond_count = cond.shape[1]
    cond_flat = cond.reshape(clip_count * cond_count, cond.shape[2])
    cond_width = cond.shape[2]
    cond_keep = cond_mask > 0
    attn_low = attn_weight.astype(jnp.bfloat16)
    cross_low = cross_weight.astype(jnp.bfloat16)
    norm_low = norm_param.astype(jnp.bfloat16)
    ff_low = ff_weight.astype(jnp.bfloat16)
    stream = frames.astype(jnp.float32).reshape(token_count, wide)
    stamps = time_token.astype(jnp.float32)
    positions = seq_place * frame_rows + jnp.arange(frame_rows)
    key_keep = jnp.arange(seq_frames)[None, :] < lengths[:, None]
    frame_valid = (positions[None, :] < lengths[:, None]).reshape(token_count)
    grad_out = cotangent.astype(jnp.float32).reshape(token_count, wide) * frame_valid[
        :, None
    ].astype(jnp.float32)
    grad_out_low = grad_out.astype(jnp.bfloat16)
    piece_heads = HEADS // seq_count
    piece_wide = wide // seq_count
    piece_ff = hidden_width // seq_count
    group_rows = clip_count * seq_frames

    def pieces():
        norm_copies = jnp.tile(norm_low[None], (1, 1, seq_count))
        moved_attn, moved_cross, moved_ff, moved_norm = (
            lax.all_to_all(
                attn_low.reshape(-1, 6, wide), "seq", split_axis=2, concat_axis=0, tiled=True
            ),
            lax.all_to_all(
                cross_low.reshape(-1, 2, wide), "seq", split_axis=2, concat_axis=0, tiled=True
            ),
            lax.all_to_all(
                ff_low.reshape(-1, 3, hidden_width), "seq", split_axis=2, concat_axis=0, tiled=True
            ),
            lax.all_to_all(norm_copies, "seq", split_axis=2, concat_axis=0, tiled=True),
        )
        attn_cols, cross_cols, ff_cols, norm_blocks = (
            lax.all_gather(moved_attn, "dp", axis=0, tiled=True),
            lax.all_gather(moved_cross, "dp", axis=0, tiled=True),
            lax.all_gather(moved_ff, "dp", axis=0, tiled=True),
            lax.all_gather(moved_norm, "dp", axis=0, tiled=True),
        )
        gains = norm_blocks.transpose(1, 0, 2).reshape(6, wide).astype(jnp.float32)
        return (attn_cols, cross_cols, ff_cols, gains)

    def collect(rows):
        whole = lax.all_gather(
            rows.reshape(clip_count, frame_rows, wide), "seq", axis=1, tiled=True
        )
        return whole.reshape(group_rows, wide)

    def spread(partial_value):
        mine = lax.psum_scatter(
            partial_value.reshape(clip_count, seq_frames, wide).astype(jnp.bfloat16),
            "seq",
            scatter_dimension=1,
            tiled=True,
        ).astype(jnp.float32)
        return mine.reshape(token_count, wide)

    attn_cols, cross_cols, ff_cols, gain_rows = pieces()
    group_shape = (clip_count, seq_frames, piece_heads, HDIM)
    cosine_table, sine_table = rotary_tables(jnp.arange(seq_frames), HDIM)
    normed_one = layer_norm(stream, gain_rows[0], gain_rows[1]).astype(jnp.bfloat16)
    group_one = collect(normed_one)
    projected = jnp.dot(
        group_one,
        attn_cols[:, :3].reshape(wide, 3 * piece_wide),
        preferred_element_type=jnp.float32,
    )
    queries = rotate(
        projected[:, :piece_wide].reshape(group_shape), cosine_table, sine_table
    ).astype(jnp.bfloat16)
    all_keys = rotate(
        projected[:, piece_wide : 2 * piece_wide].reshape(group_shape), cosine_table, sine_table
    ).astype(jnp.bfloat16)
    all_values = projected[:, 2 * piece_wide :].astype(jnp.bfloat16).reshape(group_shape)
    stamp_normed = layer_norm(stamps, gain_rows[0], gain_rows[1]).astype(jnp.bfloat16)
    stamp_pair = jnp.dot(
        stamp_normed,
        attn_cols[:, 1:3].reshape(wide, 2 * piece_wide),
        preferred_element_type=jnp.float32,
    )
    stamp_key = (
        stamp_pair[:, :piece_wide].astype(jnp.bfloat16).reshape(clip_count, piece_heads, HDIM)
    )
    stamp_value = (
        stamp_pair[:, piece_wide:].astype(jnp.bfloat16).reshape(clip_count, piece_heads, HDIM)
    )
    self_mixed, self_lse = self_forward(
        queries, all_keys, all_values, stamp_key, stamp_value, key_keep
    )
    self_low = self_mixed.astype(jnp.bfloat16).reshape(group_rows, piece_wide)
    resid_one = stream + spread(times_transposed(self_low, attn_cols[:, 3]))
    normed_two = layer_norm(resid_one, gain_rows[2], gain_rows[3]).astype(jnp.bfloat16)
    group_two = collect(normed_two)
    cross_query = jnp.dot(group_two, attn_cols[:, 4], preferred_element_type=jnp.float32)
    cross_query = cross_query.astype(jnp.bfloat16).reshape(group_shape)
    cond_pair = jnp.dot(
        cond_flat,
        cross_cols.reshape(cond_width, 2 * piece_wide),
        preferred_element_type=jnp.float32,
    )
    cond_shape = (clip_count, cond_count, piece_heads, HDIM)
    cross_keys = cond_pair[:, :piece_wide].astype(jnp.bfloat16).reshape(cond_shape)
    cross_values = cond_pair[:, piece_wide:].astype(jnp.bfloat16).reshape(cond_shape)
    cross_mixed, cross_lse = cross_forward(cross_query, cross_keys, cross_values, cond_keep)
    cross_low_out = cross_mixed.astype(jnp.bfloat16).reshape(group_rows, piece_wide)
    resid_two = resid_one + spread(times_transposed(cross_low_out, attn_cols[:, 5]))
    normed_three = layer_norm(resid_two, gain_rows[4], gain_rows[5]).astype(jnp.bfloat16)
    group_three = collect(normed_three)
    gate_up = jnp.dot(
        group_three, ff_cols[:, :2].reshape(wide, 2 * piece_ff), preferred_element_type=jnp.float32
    )
    gate_val = gate_up[:, :piece_ff]
    up_val = gate_up[:, piece_ff:]
    hidden = (jax.nn.silu(gate_val) * up_val).astype(jnp.bfloat16)
    branch = spread(times_transposed(hidden, ff_cols[:, 2]))
    layer_out = (resid_two + branch).astype(jnp.bfloat16).reshape(clip_count, frame_rows, wide)
    attn_cols, cross_cols, ff_cols, gain_rows = pieces()
    group_grad_out = collect(grad_out_low)
    grad_hidden = jnp.dot(group_grad_out, ff_cols[:, 2], preferred_element_type=jnp.float32)
    sigmoid_gate = jax.nn.sigmoid(gate_val)
    grad_gate = grad_hidden * up_val * sigmoid_gate * (1.0 + gate_val * (1.0 - sigmoid_gate))
    grad_up = grad_hidden * gate_val * sigmoid_gate
    grad_gate_up = jnp.concatenate([grad_gate, grad_up], axis=1).astype(jnp.bfloat16)
    grad_normed_three = spread(
        times_transposed(grad_gate_up, ff_cols[:, :2].reshape(wide, 2 * piece_ff))
    )
    _, norm_three_back = jax.vjp(layer_norm, resid_two, gain_rows[4], gain_rows[5])
    grad_two_part, grad_gain_three, grad_bias_three = norm_three_back(grad_normed_three)
    grad_two = grad_out + grad_two_part
    grad_cross_branch = grad_two.astype(jnp.bfloat16)
    group_cross_branch = collect(grad_cross_branch)
    grad_cross_mixed = jnp.dot(
        group_cross_branch, attn_cols[:, 5], preferred_element_type=jnp.float32
    )
    grad_cross_mixed = grad_cross_mixed.astype(jnp.bfloat16).reshape(group_shape)
    grad_cross_query, grad_cross_keys, grad_cross_values = cross_backward(
        cross_query, cross_keys, cross_values, cond_keep, cross_lse, grad_cross_mixed
    )
    grad_cross_query = grad_cross_query.astype(jnp.bfloat16).reshape(group_rows, piece_wide)
    grad_normed_two = spread(times_transposed(grad_cross_query, attn_cols[:, 4]))
    _, norm_two_back = jax.vjp(layer_norm, resid_one, gain_rows[2], gain_rows[3])
    grad_one_part, grad_gain_two, grad_bias_two = norm_two_back(grad_normed_two)
    grad_one = grad_two + grad_one_part
    grad_self_branch = grad_one.astype(jnp.bfloat16)
    group_self_branch = collect(grad_self_branch)
    grad_self_mixed = jnp.dot(
        group_self_branch, attn_cols[:, 3], preferred_element_type=jnp.float32
    )
    grad_self_mixed = grad_self_mixed.astype(jnp.bfloat16).reshape(group_shape)
    grad_queries, key_part, value_part, grad_stamp_key, grad_stamp_value = self_backward(
        queries, all_keys, all_values, stamp_key, stamp_value, key_keep, self_lse, grad_self_mixed
    )
    grad_query_raw = (
        rotate(grad_queries, cosine_table, -sine_table)
        .astype(jnp.bfloat16)
        .reshape(group_rows, piece_wide)
    )
    grad_key_raw = (
        rotate(key_part, cosine_table, -sine_table)
        .astype(jnp.bfloat16)
        .reshape(group_rows, piece_wide)
    )
    grad_value = value_part.astype(jnp.bfloat16).reshape(group_rows, piece_wide)
    grad_project = jnp.concatenate([grad_query_raw, grad_key_raw, grad_value], axis=1)
    grad_normed_one = spread(
        times_transposed(grad_project, attn_cols[:, :3].reshape(wide, 3 * piece_wide))
    )
    stamp_grad = jnp.concatenate(
        [
            grad_stamp_key.reshape(clip_count, piece_wide),
            grad_stamp_value.reshape(clip_count, piece_wide),
        ],
        axis=1,
    )
    grad_stamp_normed = split_times_transposed(
        stamp_grad, attn_cols[:, 1:3].reshape(wide, 2 * piece_wide)
    )
    _, norm_one_back = jax.vjp(layer_norm, stream, gain_rows[0], gain_rows[1])
    grad_zero_part, grad_gain_one, grad_bias_one = norm_one_back(grad_normed_one)
    _, norm_stamp_back = jax.vjp(layer_norm, stamps, gain_rows[0], gain_rows[1])
    _, grad_gain_stamp, grad_bias_stamp = norm_stamp_back(grad_stamp_normed)
    frames_grad = (grad_one + grad_zero_part).reshape(clip_count, frame_rows, wide)
    project_grad = outer_sum(group_one, grad_project)
    stamp_weight_grad = split_outer(stamp_normed, stamp_grad)
    attn_piece = jnp.stack(
        [
            project_grad[:, :piece_wide],
            project_grad[:, piece_wide : 2 * piece_wide] + stamp_weight_grad[:, :piece_wide],
            project_grad[:, 2 * piece_wide :] + stamp_weight_grad[:, piece_wide:],
            outer_sum(group_self_branch, self_low),
            outer_sum(group_two, grad_cross_query),
            outer_sum(group_cross_branch, cross_low_out),
        ],
        axis=1,
    )
    cond_grad = jnp.concatenate(
        [
            grad_cross_keys.reshape(clip_count * cond_count, piece_wide),
            grad_cross_values.reshape(clip_count * cond_count, piece_wide),
        ],
        axis=1,
    )
    cross_piece = split_outer(cond_flat, cond_grad).reshape(cond_width, 2, piece_wide)
    ff_piece = jnp.stack(
        [
            outer_sum(group_three, grad_gate_up[:, :piece_ff]),
            outer_sum(group_three, grad_gate_up[:, piece_ff:]),
            outer_sum(group_grad_out, hidden),
        ],
        axis=1,
    )
    norm_grad = jnp.stack(
        [
            grad_gain_one + grad_gain_stamp,
            grad_bias_one + grad_bias_stamp,
            grad_gain_two,
            grad_bias_two,
            grad_gain_three,
            grad_bias_three,
        ],
        axis=0,
    )
    norm_column = norm_grad.T[:, :, None]
    summed_attn, summed_cross, summed_ff, summed_norm = (
        lax.psum_scatter(
            attn_piece.astype(jnp.bfloat16), "dp", scatter_dimension=0, tiled=True
        ).astype(jnp.float32),
        lax.psum_scatter(
            cross_piece.astype(jnp.bfloat16), "dp", scatter_dimension=0, tiled=True
        ).astype(jnp.float32),
        lax.psum_scatter(
            ff_piece.astype(jnp.bfloat16), "dp", scatter_dimension=0, tiled=True
        ).astype(jnp.float32),
        lax.psum_scatter(
            norm_column.astype(jnp.bfloat16), "dp", scatter_dimension=0, tiled=True
        ).astype(jnp.float32),
    )
    owned_attn, owned_cross, owned_ff, owned_norm = (
        lax.all_to_all(
            summed_attn.astype(jnp.bfloat16), "seq", split_axis=0, concat_axis=2, tiled=True
        ).astype(summed_attn.dtype),
        lax.all_to_all(
            summed_cross.astype(jnp.bfloat16), "seq", split_axis=0, concat_axis=2, tiled=True
        ).astype(summed_cross.dtype),
        lax.all_to_all(
            summed_ff.astype(jnp.bfloat16), "seq", split_axis=0, concat_axis=2, tiled=True
        ).astype(summed_ff.dtype),
        lax.all_to_all(
            summed_norm.astype(jnp.bfloat16), "seq", split_axis=0, concat_axis=2, tiled=True
        ).astype(summed_norm.dtype),
    )
    attn_reduced = owned_attn.reshape(owned_attn.shape[0], 6 * wide)
    cross_reduced = owned_cross.reshape(owned_cross.shape[0], 2 * wide)
    ff_reduced = owned_ff.reshape(owned_ff.shape[0], 3 * hidden_width)
    norm_reduced = jnp.sum(owned_norm, axis=2).T
    local_squares = (
        jnp.sum(attn_reduced * attn_reduced)
        + jnp.sum(cross_reduced * cross_reduced)
        + jnp.sum(norm_reduced * norm_reduced)
        + jnp.sum(ff_reduced * ff_reduced)
    )
    total_squares = lax.psum(local_squares, ("dp", "seq"))
    grad_norm = jnp.sqrt(total_squares)
    factor = jnp.minimum(1.0, clip_limit / grad_norm)
    attn_new, attn_first_new, attn_second_new = adam_step(
        attn_weight, attn_first, attn_second, attn_reduced * factor, matrix_rate, matrix_decay
    )
    cross_new, cross_first_new, cross_second_new = adam_step(
        cross_weight, cross_first, cross_second, cross_reduced * factor, matrix_rate, matrix_decay
    )
    norm_new, norm_first_new, norm_second_new = adam_step(
        norm_param, norm_first, norm_second, norm_reduced * factor, gain_rate, 0.0
    )
    ff_new, ff_first_new, ff_second_new = adam_step(
        ff_weight, ff_first, ff_second, ff_reduced * factor, matrix_rate, matrix_decay
    )
    return (
        layer_out,
        frames_grad,
        grad_norm,
        attn_new,
        cross_new,
        norm_new,
        ff_new,
        attn_first_new,
        cross_first_new,
        norm_first_new,
        ff_first_new,
        attn_second_new,
        cross_second_new,
        norm_second_new,
        ff_second_new,
    )


MESH = pl.DeviceIdType.MESH
DMA = pltpu.SemaphoreType.DMA
VMEM_LIMIT = 60 * 2**20


def plane_fits(mesh):
    return mesh.shape["dp"] == 8 and mesh.shape["dp"] % mesh.shape["seq"] == 0


def plane_places():
    place = lax.axis_index("dp")
    return (place, lax.axis_index("seq"), lambda mask: jnp.bitwise_xor(place, mask))


def greet(partners):
    barrier = pltpu.get_barrier_semaphore()
    for partner in partners:
        pl.semaphore_signal(barrier, inc=1, device_id=partner, device_id_type=MESH)
    pl.semaphore_wait(barrier, len(partners))


def remote(source, goal, send_sem, recv_sem, device):
    return pltpu.make_async_remote_copy(
        src_ref=source,
        dst_ref=goal,
        send_sem=send_sem,
        recv_sem=recv_sem,
        device_id=device,
        device_id_type=MESH,
    )


def communicating(collective_id):
    return pltpu.CompilerParams(
        has_side_effects=True, collective_id=collective_id, vmem_limit_bytes=VMEM_LIMIT
    )


def any_spec():
    return pl.BlockSpec(memory_space=pl.ANY)


def greet_cross(group, planes):
    place, depth, flip = plane_places()
    greet(
        [(flip(mask), depth) for mask in range(1, group)]
        + [(place, lax.rem(depth + step, planes)) for step in range(1, planes)]
    )


def outward_steps(group, planes, kept_ref, own_ref, mid, *sems):
    far_send, far_recv, near_send, near_recv, local_sem = sems
    place, depth, flip = plane_places()
    per = group // planes
    first = []
    for step in range(1, planes):
        origin = lax.rem(depth + step, planes)
        for slot in range(per):
            clip = per * depth + slot
            copy = remote(
                kept_ref.at[slot, origin],
                mid.at[clip],
                far_send.at[slot, step],
                far_recv.at[clip],
                (place, origin),
            )
            copy.start()
            first.append(copy)
    second = []

    def hand_over(block, clip):
        index = len(second)
        away = remote(
            block, own_ref.at[place], near_send.at[index], near_recv.at[place], (clip, depth)
        )
        stay = pltpu.make_async_copy(block, own_ref.at[place], local_sem.at[index])
        pl.when(clip != place)(away.start)
        pl.when(clip == place)(stay.start)
        second.append((clip, away, stay))

    for slot in range(per):
        hand_over(kept_ref.at[slot, depth], per * depth + slot)
    yield
    for step in range(1, planes):
        source = lax.rem(depth + step, planes)
        for slot in range(per):
            clip = per * source + slot
            block = mid.at[clip]
            remote(
                block, block, far_send.at[0, 0], far_recv.at[clip], (place, source)
            ).wait_recv()
            hand_over(block, clip)
    yield
    for mask in range(1, group):
        other = flip(mask)
        block = own_ref.at[other]
        remote(block, block, near_send.at[0], near_recv.at[other], (other, depth)).wait_recv()
    for clip, away, stay in second:
        pl.when(clip != place)(away.wait_send)
        pl.when(clip == place)(stay.wait)
    for copy in first:
        copy.wait_send()
    yield


def outward_scratch(group, planes):
    return [
        DMA((group // planes, planes)),
        DMA((group,)),
        DMA((group,)),
        DMA((group,)),
        DMA((group,)),
    ]


def leave_body(group, planes, cuts, kept_ref, *refs):
    cut_refs, refs = refs[:cuts], refs[cuts:]
    parts_ref, squares_ref, own_ref, *refs = refs
    mine_refs, refs = refs[:cuts], refs[cuts:]
    norm_ref, total_ref, mid, terms, block, blocks, *sems = refs
    part_send, part_recv, block_send, block_recv = sems[:4]
    place, depth, flip = plane_places()
    devices = [(flip(mask), lax.rem(depth + step, planes)) for mask, step in everyone(planes)]
    greet(devices)
    here = place * planes + depth
    rows = outward_steps(group, planes, kept_ref, own_ref, mid, *sems[4:9])
    next(rows)
    copies = []
    for index, (other, plane) in enumerate(devices):
        copy = remote(
            parts_ref.at[other * planes + plane],
            terms.at[here],
            part_send.at[index],
            part_recv.at[here],
            (other, plane),
        )
        copy.start()
        copies.append(copy)
    terms[here] = parts_ref[here]
    start_swap, end_swap = swap_beside(
        [
            (
                lambda other, cut_ref=cut_ref: cut_ref.at[other],
                lambda other, mine_ref=mine_ref: mine_ref.at[other],
            )
            for cut_ref, mine_ref in zip(cut_refs, mine_refs)
        ],
        *sems[9:],
    )
    start_swap()
    next(rows)
    for other, plane in devices:
        source = other * planes + plane
        one = terms.at[source]
        remote(one, one, part_send.at[0], part_recv.at[source], (other, plane)).wait_recv()
    norm_sum = jnp.sum(terms[...], axis=0)
    norm_ref[...] = norm_sum
    end_swap()
    squares = squares_ref[0, 0] + jnp.sum(norm_sum * norm_sum)
    for mine_ref in mine_refs:
        for piece in range(group):
            values = mine_ref[piece].astype(jnp.float32)
            squares = squares + jnp.sum(values * values)
    block[...] = jnp.full(block.shape, squares)
    blocks[here] = block[...]
    for index, (other, plane) in enumerate(devices):
        copy = remote(
            block, blocks.at[here], block_send.at[index], block_recv.at[here], (other, plane)
        )
        copy.start()
        copies.append(copy)
    next(rows)
    for other, plane in devices:
        source = other * planes + plane
        one = blocks.at[source]
        remote(one, one, block_send.at[0], block_recv.at[source], (other, plane)).wait_recv()
    total_ref[...] = jnp.sum(blocks[...], axis=0)
    for copy in copies:
        copy.wait_send()


def leave(kept_rows, cuts, norm_parts, squares, collective_id):
    per, planes, rows, wide = kept_rows.shape
    group = per * planes
    count = group * planes
    inside = pl.BlockSpec(memory_space=pltpu.VMEM)
    like = lambda shape, array: jax.ShapeDtypeStruct(shape, array.dtype)
    own, *results, norm_sum, total, _ = pl.pallas_call(
        functools.partial(leave_body, group, planes, len(cuts)),
        out_shape=[like((group, rows, wide), kept_rows)]
        + [like(cut.shape, cut) for cut in cuts]
        + [
            like(norm_parts.shape[1:], norm_parts),
            like((8, 128), norm_parts),
            like((group, rows, wide), kept_rows),
        ],
        in_specs=[any_spec()] * (1 + len(cuts)) + [inside, pl.BlockSpec(memory_space=pltpu.SMEM)],
        out_specs=[any_spec()] + [inside] * (len(cuts) + 2) + [any_spec()],
        scratch_shapes=[
            pltpu.VMEM(norm_parts.shape, jnp.float32),
            pltpu.VMEM((8, 128), jnp.float32),
            pltpu.VMEM((count, 8, 128), jnp.float32),
            DMA((count,)),
            DMA((count,)),
            DMA((count,)),
            DMA((count,)),
        ]
        + outward_scratch(group, planes)
        + swap_beside_scratch(len(cuts)),
        compiler_params=communicating(collective_id),
    )(kept_rows, *cuts, norm_parts, squares)
    return own, results, norm_sum, total


def everyone(planes):
    return [(mask, step) for mask in range(8) for step in range(planes) if mask or step]


def enter_body(
    group,
    planes,
    own_ref,
    norm_ref,
    pack_ref,
    first_cut_ref,
    rest_cut_ref,
    ff_ref,
    kept_ref,
    gains_ref,
    packs_ref,
    first_mine_ref,
    rest_mine_ref,
    ff_low_ref,
    mid,
    norms_ref,
    ff_full,
    ff_low,
    ff_sem,
    *sems,
):
    (
        near_send,
        near_recv,
        far_send,
        far_recv,
        local_sem,
        norm_send,
        norm_recv,
        pack_send,
        pack_recv,
        cut_send,
        cut_recv,
        stay_sem,
    ) = sems
    place, depth, flip = plane_places()
    per = group // planes
    others = everyone(planes)
    ff_load = pltpu.make_async_copy(ff_ref, ff_full, ff_sem.at[0])
    ff_load.start()
    greet([(flip(mask), lax.rem(depth + step, planes)) for mask, step in others])
    here = place * planes + depth
    first = []
    for mask in (6, 7, 2, 3, 4, 5, 1):
        other = flip(mask)
        copy = remote(
            own_ref.at[other],
            mid.at[place],
            near_send.at[mask],
            near_recv.at[mask],
            (other, depth),
        )
        copy.start()
        first.append((mask, copy))
    small = []
    for index, (mask, step) in enumerate(others):
        copy = remote(
            norm_ref,
            norms_ref.at[here],
            norm_send.at[index],
            norm_recv.at[here],
            (flip(mask), lax.rem(depth + step, planes)),
        )
        copy.start()
        small.append(copy)
    for mask in range(1, group):
        copy = remote(
            pack_ref,
            packs_ref.at[place],
            pack_send.at[mask],
            pack_recv.at[mask],
            (flip(mask), depth),
        )
        copy.start()
        small.append(copy)
    stays = [
        pltpu.make_async_copy(norm_ref, norms_ref.at[here], stay_sem.at[0]),
        pltpu.make_async_copy(pack_ref, packs_ref.at[place], stay_sem.at[1]),
        pltpu.make_async_copy(
            first_cut_ref.at[place], first_mine_ref.at[place], stay_sem.at[2]
        ),
        pltpu.make_async_copy(rest_cut_ref.at[place], rest_mine_ref.at[place], stay_sem.at[3]),
    ]
    for stay in stays:
        stay.start()
    cuts = []
    for which, (cut_ref, mine_ref) in enumerate(
        ((first_cut_ref, first_mine_ref), (rest_cut_ref, rest_mine_ref))
    ):
        for mask in (6, 7, 2, 3, 4, 5, 1):
            other = flip(mask)
            copy = remote(
                cut_ref.at[other],
                mine_ref.at[place],
                cut_send.at[which, mask],
                cut_recv.at[which, mask],
                (other, depth),
            )
            copy.start()
            cuts.append(copy)
    ff_load.wait()
    tile = ff_full.shape[1] // 24

    def round_tile(index, carry):
        lanes = pl.ds(pl.multiple_of(index * tile, 128), tile)
        ff_low[:, lanes] = ff_full[:, lanes].astype(ff_low.dtype)
        return carry

    second = []
    arrivals = dict(first)
    for mask in (0, 1, 2, 3, 4, 5, 6, 7):
        source = flip(mask)
        goal, slot = lax.div(source, per), lax.rem(source, per)
        block = own_ref.at[place]
        if mask:
            arrivals[mask].wait_recv()
            block = mid.at[source]
        away = remote(
            block,
            kept_ref.at[slot, depth],
            far_send.at[mask],
            far_recv.at[slot, depth],
            (place, goal),
        )
        stay = pltpu.make_async_copy(block, kept_ref.at[slot, depth], local_sem.at[mask])
        pl.when(goal != depth)(away.start)
        pl.when(goal == depth)(stay.start)
        second.append((goal, away, stay))
    lax.fori_loop(0, 24, round_tile, 0)
    ff_store = pltpu.make_async_copy(ff_low, ff_low_ref, ff_sem.at[1])
    ff_store.start()
    for slot in range(per):
        for origin in range(planes):
            block = kept_ref.at[slot, origin]
            pl.when(origin != depth)(
                remote(
                    block,
                    block,
                    far_send.at[0],
                    far_recv.at[slot, origin],
                    (place, lax.rem(depth + 1, planes)),
                ).wait_recv
            )
    ff_store.wait()
    for mask, step in others:
        source = flip(mask) * planes + lax.rem(depth + step, planes)
        block = norms_ref.at[source]
        remote(
            block,
            block,
            norm_send.at[0],
            norm_recv.at[source],
            (flip(mask), lax.rem(depth + step, planes)),
        ).wait_recv()
    for copy in small:
        copy.wait_send()
    stays[0].wait()
    width = gains_ref.shape[1] // (group * planes)
    gains_ref[...] = jnp.concatenate(
        [
            norms_ref[owner * planes + plane, :, :width]
            for plane in range(planes)
            for owner in range(group)
        ],
        axis=1,
    )
    for mask in range(1, group):
        block = packs_ref.at[flip(mask)]
        remote(
            block, block, pack_send.at[0], pack_recv.at[mask], (flip(mask), depth)
        ).wait_recv()
    for copy in cuts:
        copy.wait()
    for goal, away, stay in second:
        pl.when(goal != depth)(away.wait_send)
        pl.when(goal == depth)(stay.wait)
    for mask, copy in first:
        copy.wait_send()
    for stay in stays[1:]:
        stay.wait()


def enter(rows_of_clip, norm_block, pack, first_cut, rest_cut, ff_weight, planes, collective_id):
    group, rows, wide = rows_of_clip.shape
    count = group * planes
    like = lambda shape, array: jax.ShapeDtypeStruct(shape, array.dtype)
    inside = pl.BlockSpec(memory_space=pltpu.VMEM)
    *results, _ = pl.pallas_call(
        functools.partial(enter_body, group, planes),
        out_shape=[
            like((group // planes, planes, rows, wide), rows_of_clip),
            like((norm_block.shape[0], wide), norm_block),
            like((group,) + pack.shape, pack),
            like(first_cut.shape, first_cut),
            like(rest_cut.shape, rest_cut),
            like(ff_weight.shape, rest_cut),
            like((group, rows, wide), rows_of_clip),
        ],
        in_specs=[any_spec(), inside] + [any_spec()] * 4,
        out_specs=[any_spec(), inside] + [any_spec()] * 5,
        scratch_shapes=[
            pltpu.VMEM((count,) + norm_block.shape, norm_block.dtype),
            pltpu.VMEM(ff_weight.shape, ff_weight.dtype),
            pltpu.VMEM(ff_weight.shape, rest_cut.dtype),
            DMA((2,)),
            DMA((group,)),
            DMA((group,)),
            DMA((group,)),
            DMA((group // planes, planes)),
            DMA((group,)),
            DMA((count,)),
            DMA((count,)),
            DMA((group,)),
            DMA((group,)),
            DMA((2, group)),
            DMA((2, group)),
            DMA((4,)),
        ],
        compiler_params=communicating(collective_id),
    )(rows_of_clip, norm_block, pack, first_cut, rest_cut, ff_weight)
    return results


def cond_steps(group, planes, pick_ref, cond_ref, parts, summed, *sems):
    part_send, part_recv, cond_send, cond_recv = sems
    place, depth, flip = plane_places()
    pushes = []
    for step in range(1, planes):
        goal = lax.rem(depth + step, planes)
        copy = remote(
            pick_ref.at[goal],
            parts.at[depth],
            part_send.at[step],
            part_recv.at[depth],
            (place, goal),
        )
        copy.start()
        pushes.append(copy)
    yield
    total = pick_ref[depth].astype(jnp.float32)
    for step in range(1, planes):
        source = lax.rem(depth + step, planes)
        block = parts.at[source]
        remote(
            block, block, part_send.at[0], part_recv.at[source], (place, source)
        ).wait_recv()
        total = total + parts[source].astype(jnp.float32)
    summed[...] = total.astype(summed.dtype)
    cond_ref[place] = total.astype(summed.dtype)
    for mask in range(1, group):
        copy = remote(
            summed,
            cond_ref.at[place],
            cond_send.at[mask],
            cond_recv.at[mask],
            (flip(mask), depth),
        )
        copy.start()
        pushes.append(copy)
    yield
    for mask in range(1, group):
        block = cond_ref.at[flip(mask)]
        remote(
            block, block, cond_send.at[0], cond_recv.at[mask], (flip(mask), depth)
        ).wait_recv()
    for copy in pushes:
        copy.wait_send()
    yield


def inward_over(group, planes, mid_ref, kept_ref, send_sem, recv_sem, local_sem):
    place, depth, flip = plane_places()
    per = group // planes

    def piece(source):
        goal, slot = lax.div(source, per), lax.rem(source, per)
        block = mid_ref.at[source]
        away = remote(
            block,
            kept_ref.at[slot, depth],
            send_sem.at[source],
            recv_sem.at[slot, depth],
            (place, goal),
        )
        stay = pltpu.make_async_copy(block, kept_ref.at[slot, depth], local_sem.at[source])
        return goal != depth, away, stay

    def begin():
        for source in range(group):
            leaves, away, stay = piece(source)
            pl.when(leaves)(away.start)
            pl.when(jnp.logical_not(leaves))(stay.start)

    def end():
        for slot in range(per):
            for origin in range(planes):
                block = kept_ref.at[slot, origin]
                pl.when(origin != depth)(
                    remote(
                        block,
                        block,
                        send_sem.at[0],
                        recv_sem.at[slot, origin],
                        (place, lax.rem(depth + 1, planes)),
                    ).wait_recv
                )
        for source in range(group):
            leaves, away, stay = piece(source)
            pl.when(leaves)(away.wait_send)
            pl.when(jnp.logical_not(leaves))(stay.wait)

    return begin, end


def dot_tiles(left, right_ref, span, transposed, width):
    first, last = span
    count = right_ref.shape[0] if transposed else last - first
    for start in range(0, count, width):
        stop = min(start + width, count)
        if transposed:
            yield start, stop, times_transposed(left, right_ref[start:stop, first:last])
        else:
            yield start, stop, jnp.dot(
                left, right_ref[:, first + start : first + stop], preferred_element_type=jnp.float32
            )


def window_of(matrix, span):
    first, last = span or (0, matrix.shape[1])
    start = first // 128 * 128
    while (matrix.shape[1] - start) * 2 > matrix.shape[1] and start and start % 384:
        start -= 128
    stop = min(-(-last // 128) * 128, matrix.shape[1])
    return (start, stop - start), (first - start, last - start)


def cross_shares(queries, pair_ref, bias_ref):
    wide = queries[0].shape[1]
    keys = [
        (clip, start, pair_ref[clip, :, start : start + HDIM])
        for clip in range(len(queries))
        for start in range(0, wide, HDIM)
    ]
    scores = [
        times_transposed(queries[clip][:, start : start + HDIM], key) * HDIM ** (-0.5)
        + bias_ref[clip]
        for clip, start, key in keys
    ]
    tops = [jnp.max(score, axis=1, keepdims=True) for score in scores]
    expos = [jnp.exp(score - top) for score, top in zip(scores, tops)]
    sums = [jnp.sum(expo, axis=1, keepdims=True) for expo in expos]
    return keys, [expo / total for expo, total in zip(expos, sums)]


def by_clip_of(results, clips, low):
    heads = len(results) // clips
    return [
        jnp.concatenate(results[clip * heads : (clip + 1) * heads], axis=1).astype(low)
        for clip in range(clips)
    ]


def cross_rows(queries, pair_ref, bias_ref):
    low, wide = queries[0].dtype, queries[0].shape[1]
    keys, shares = cross_shares(queries, pair_ref, bias_ref)
    mixed = [
        jnp.dot(
            share.astype(low),
            pair_ref[clip, :, wide + start : wide + start + HDIM],
            preferred_element_type=jnp.float32,
        )
        for (clip, start, _), share in zip(keys, shares)
    ]
    return by_clip_of(mixed, len(queries), low)


def cross_rows_back(queries, grads, pair_ref, bias_ref, pair_grad_ref):
    low, wide = queries[0].dtype, queries[0].shape[1]
    scale = HDIM ** (-0.5)
    keys, shares = cross_shares(queries, pair_ref, bias_ref)
    own_grads = [grads[clip][:, start : start + HDIM] for clip, start, _ in keys]
    grad_shares = [
        times_transposed(grad, pair_ref[clip, :, wide + start : wide + start + HDIM])
        for (clip, start, _), grad in zip(keys, own_grads)
    ]
    deltas = [
        jnp.sum(share * grad_share, axis=1, keepdims=True)
        for share, grad_share in zip(shares, grad_shares)
    ]
    scores = [
        (share * (grad_share - delta)).astype(low)
        for share, grad_share, delta in zip(shares, grad_shares, deltas)
    ]
    results = [
        jnp.dot(score, key, preferred_element_type=jnp.float32) * scale
        for score, (_, _, key) in zip(scores, keys)
    ]
    key_grads = [
        outer_sum(score, queries[clip][:, start : start + HDIM]) * scale
        for score, (clip, start, _) in zip(scores, keys)
    ]
    value_grads = [
        outer_sum(share.astype(low), grad) for share, grad in zip(shares, own_grads)
    ]
    heads = len(keys) // len(queries)
    for clip in range(len(queries)):
        mine = slice(clip * heads, (clip + 1) * heads)
        pair_grad_ref[clip] += jnp.concatenate(key_grads[mine] + value_grads[mine], axis=1)
    return by_clip_of(results, len(queries), low)


def outer_columns(out_ref, start, small, big):
    width = small.shape[-1]
    product = outer_sum(small.reshape(-1, width), big.reshape(-1, big.shape[-1]))
    out_ref[:, start : start + width] = product.T.astype(out_ref.dtype)


def by_slot_loads(source, goal, sem):
    clips = source.shape[0]
    return [
        pltpu.make_async_copy(source.at[clip, slot], goal.at[slot, clip], sem.at[slot, clip])
        for slot in range(8)
        for clip in range(clips)
    ]


def gather_parts(clips, rows, sub, mode, window, span, ins, outs_refs, scratch):
    ins, outs_refs, scratch = list(ins), list(outs_refs), list(scratch)
    mat_ref = ins.pop(0) if mode != "rows" else None
    gates_ref = ins.pop(0) if mode == "gates" else None
    pair_ref, bias_ref = (ins.pop(0), ins.pop(0)) if mode in ("cross", "cross_back") else (None, None)
    query_ref = ins.pop(0) if mode == "cross_back" else None
    all_ref = outs_refs.pop(0)
    pair_grad_ref = outs_refs.pop() if mode == "cross_back" else None
    prod_refs = outs_refs
    take = lambda count: [scratch.pop(0) for _ in range(count)]
    held, send_sem, recv_sem, all_sem = take(4)
    mat, mat_sem = take(2) if mode != "rows" else (None, None)
    stages = take(len(prod_refs))
    prod_sem = take(1)[0] if prod_refs else None
    gates, gates_sem = take(2) if mode == "gates" else (None, None)
    queries, query_sem = take(2) if mode == "cross_back" else (None, None)
    place, depth, flip = plane_places()
    core, beside_x, beside_y, across = flip(1), flip(2), flip(4), flip(6)
    loads = []
    gate_loads = {}
    if mode != "rows":
        loads.append(pltpu.make_async_copy(mat_ref.at[:, pl.ds(*window)], mat, mat_sem))
    if mode == "cross_back":
        loads.append(pltpu.make_async_copy(query_ref, queries, query_sem))
    if mode == "gates":
        for mask in (0, 1, 2, 4, 3, 5, 6, 7):
            slot = flip(mask)
            gate_loads[mask] = [
                pltpu.make_async_copy(
                    gates_ref.at[clip, slot], gates.at[slot, clip], gates_sem.at[slot, clip]
                )
                for clip in range(clips)
            ]

    def load():
        if mode == "cross_back":
            pair_grad_ref[...] = jnp.zeros_like(pair_grad_ref)
        for copy in loads + [copy for copies in gate_loads.values() for copy in copies]:
            copy.start()

    chunks = [(clip, part) for clip in range(clips) for part in range(rows // sub)]
    count = len(chunks)
    half = count // 2
    sends = []

    def view(slot, index):
        clip, part = chunks[index]
        return held.at[slot, clip, pl.ds(part * sub, sub)]

    def send(slot, index, device):
        block = view(slot, index)
        copy = remote(
            block, block, send_sem.at[len(sends)], recv_sem.at[slot, index], (device, depth)
        )
        copy.start()
        sends.append(copy)

    def arrived(slot, index):
        block = view(slot, index)
        remote(
            block, block, send_sem.at[0], recv_sem.at[slot, index], (core, depth)
        ).wait_recv()

    x_order = list(range(count))
    y_order = list(range(half, count)) + list(range(half))

    def put(index, values):
        clip, part = chunks[index]
        held[place, clip, pl.ds(part * sub, sub)] = values.astype(held.dtype)
        if index < half:
            send(place, index, beside_x)
        else:
            send(place, index, beside_y)
        send(place, index, core)
        if index == count - 1:
            for low in range(half):
                send(place, half + low, beside_x)
                send(place, low, beside_y)

    outs = []

    def leave_here(source, goal, sem, major):
        for clip in range(clips):
            there = goal.at[major, clip] if goal.shape[0] == 8 else goal.at[clip, major]
            copy = pltpu.make_async_copy(source.at[major, clip], there, sem.at[major, clip])
            copy.start()
            outs.append(copy)

    def multiply(mask):
        slot = flip(mask)
        leave_here(held, all_ref, all_sem, slot)
        if mode == "rows":
            return
        left = held[slot].reshape(clips * rows, held.shape[3])
        for copy in gate_loads.get(mask, ()):
            copy.wait()
        for start, stop, product in dot_tiles(
            left, mat, span, False, 256 * (1 if mode == "gates" else 3)
        ):
            product = product.reshape(clips, rows, stop - start)
            if mode == "cross":
                query = product.astype(stages[0].dtype)
                stages[0][slot] = query
                mixed = cross_rows([query[clip] for clip in range(clips)], pair_ref, bias_ref)
                for clip in range(clips):
                    stages[1][slot, clip] = mixed[clip]
                continue
            if mode == "cross_back":
                grad = product.astype(stages[0].dtype)
                results = cross_rows_back(
                    [queries[clip, slot] for clip in range(clips)],
                    [grad[clip] for clip in range(clips)],
                    pair_ref,
                    bias_ref,
                    pair_grad_ref,
                )
                for clip in range(clips):
                    stages[0][slot, clip] = results[clip]
                continue
            if mode == "dot":
                stages[0][slot, :, :, start:stop] = product.astype(stages[0].dtype)
                continue
            width = stages[1].shape[3]
            gate = gates[slot, :, :, start:stop]
            up = gates[slot, :, :, width + start : width + stop]
            sigmoid = jax.nn.sigmoid(gate)
            active = gate * sigmoid
            low = stages[0].dtype
            stages[0][slot, :, :, start:stop] = (
                product * up * sigmoid * (1.0 + gate * (1.0 - sigmoid))
            ).astype(low)
            stages[0][slot, :, :, width + start : width + stop] = (product * active).astype(low)
            stages[1][slot, :, :, start:stop] = (active * up).astype(low)
        for which, (stage, prod_ref) in enumerate(zip(stages, prod_refs)):
            leave_here(stage, prod_ref, prod_sem.at[which], slot)

    def run(late=lambda: None):
        for copy in loads:
            copy.wait()
        multiply(0)
        for step in range(count):
            x_index, y_index = x_order[step], y_order[step]
            arrived(beside_x, x_index)
            if x_index < half:
                send(beside_x, x_index, beside_y)
            send(beside_x, x_index, core)
            arrived(beside_y, y_index)
            if y_index >= half:
                send(beside_y, y_index, beside_x)
            send(beside_y, y_index, core)
            if step == 0:
                for index in range(count):
                    arrived(core, index)
                multiply(1)
        late()
        multiply(2)
        for step in range(half):
            for index in (x_order[step], y_order[step]):
                arrived(across, index)
                send(across, index, core)
            if step == 0:
                multiply(4)
        for mask in (3, 5):
            for index in range(count):
                arrived(flip(mask), index)
            multiply(mask)
        multiply(6)
        for index in range(count):
            arrived(flip(7), index)
        multiply(7)
        for copy in outs:
            copy.wait()
        for copy in sends:
            copy.wait_send()

    return load, put, run


def chunk_order(clips, rows, sub):
    half = clips * (rows // sub) // 2
    return [index for low in range(half) for index in (low, half + low)]


def gather_plan(clips, rows, wide, sub, matrix, kind, gate_up, span, pair, bias, query):
    count = clips * (rows // sub)
    low = jnp.bfloat16
    inside = pl.BlockSpec(memory_space=pltpu.VMEM)
    by_clip = lambda columns, of: jax.ShapeDtypeStruct((clips, 8, rows, columns), of)
    by_device = lambda columns, of: jax.ShapeDtypeStruct((8, clips, rows, columns), of)
    mode = "rows" if matrix is None else "dot"
    if gate_up is not None:
        mode = "gates"
    if pair is not None:
        mode = "cross" if query is None else "cross_back"
    window = inner = None
    args, in_specs = [], []
    outs = [by_device(wide, low) if mode == "gates" else by_clip(wide, low)]
    scratch = [
        pltpu.VMEM((8, clips, rows, wide), low),
        DMA((7 * count,)),
        DMA((8, count)),
        DMA((8, clips)),
    ]
    if mode != "rows":
        window, inner = window_of(matrix, span)
        columns = inner[1] - inner[0]
        args.append(matrix)
        in_specs.append(any_spec())
        scratch += [pltpu.VMEM((wide, window[1]), low), DMA(())]
    if mode == "dot":
        outs.append(by_clip(columns, kind))
        scratch += [pltpu.VMEM((8, clips, rows, columns), kind), DMA((1, 8, clips))]
    if mode == "gates":
        args.append(gate_up.reshape(clips, 8, rows, 2 * columns))
        in_specs.append(any_spec())
        outs += [by_clip(2 * columns, low), by_device(columns, low)]
        scratch += [
            pltpu.VMEM((8, clips, rows, 2 * columns), low),
            pltpu.VMEM((8, clips, rows, columns), low),
            DMA((2, 8, clips)),
            pltpu.VMEM((8, clips, rows, 2 * columns), jnp.float32),
            DMA((8, clips)),
        ]
    if mode == "cross":
        args += [pair, bias]
        in_specs += [inside] * 2
        outs += [by_clip(columns, low)] * 2
        scratch += [pltpu.VMEM((8, clips, rows, columns), low)] * 2 + [DMA((2, 8, clips))]
    out_specs = [any_spec()] * len(outs)
    if mode == "cross_back":
        args += [pair, bias, query.reshape(clips, 8, rows, columns)]
        in_specs += [inside, inside, any_spec()]
        outs += [by_clip(columns, low), jax.ShapeDtypeStruct(pair.shape, jnp.float32)]
        out_specs += [any_spec(), inside]
        scratch += [
            pltpu.VMEM((8, clips, rows, columns), low),
            DMA((1, 8, clips)),
            pltpu.VMEM((clips, 8, rows, columns), low),
            DMA(()),
        ]
    return (mode, window, inner), args, in_specs, outs, out_specs, scratch


def flat_rows(results):
    return [
        block.reshape(-1, block.shape[3]) if len(block.shape) == 4 else block for block in results
    ]


def gather_dot_body(clips, rows, sub, normed, plan, beside, outer, counts, own_ref, *refs):
    refs = list(refs)
    take = lambda count: [refs.pop(0) for _ in range(count)]
    gain_ref = take(1)[0] if normed else None
    ins = take(counts[0])
    pick_ref = take(1)[0] if beside else None
    past_ref, mixed_ref = take(2) if outer else (None, None)
    outs = take(counts[1])
    cond_ref = take(1)[0] if beside else None
    outer_ref = take(1)[0] if outer else None
    scratch = take(counts[2])
    load, put, run = gather_parts(clips, rows, sub, *plan, ins, outs, scratch)
    load()
    if outer:
        past, mixed, past_sem, mixed_sem = refs
        outer_loads = by_slot_loads(past_ref, past, past_sem)
        outer_loads += by_slot_loads(mixed_ref, mixed, mixed_sem)
        for copy in outer_loads:
            copy.start()
    place, depth, flip = plane_places()
    if beside:
        greet_cross(*beside)
        cond = cond_steps(*beside, pick_ref, cond_ref, *refs)
        next(cond)
    else:
        greet([(flip(1), depth), (flip(2), depth), (flip(4), depth)])
    for index in chunk_order(clips, rows, sub):
        clip, part = divmod(index, rows // sub)
        values = own_ref[clip, pl.ds(part * sub, sub)]
        if normed:
            values = layer_norm(values.astype(jnp.float32), gain_ref[0:1], gain_ref[1:2])
        put(index, values)
    if beside:
        run(lambda: next(cond))
        next(cond)
    else:
        run()
    if outer:
        for copy in outer_loads:
            copy.wait()
        held, queries = scratch[0], scratch[6]
        outer_columns(outer_ref, 0, queries[...], past[...])
        outer_columns(outer_ref, queries.shape[3], mixed[...], held[...])


def gather_dot(
    own_rows,
    matrix,
    kind,
    collective_id,
    gains=None,
    picked=None,
    gate_up=None,
    span=None,
    pair=None,
    bias=None,
    query=None,
    outer=None,
    sub=64,
):
    clips, rows, wide = own_rows.shape
    plan, args, in_specs, outs, out_specs, scratch = gather_plan(
        clips, rows, wide, sub, matrix, kind, gate_up, span, pair, bias, query
    )
    inside = pl.BlockSpec(memory_space=pltpu.VMEM)
    counts = (len(args), len(outs), len(scratch))
    if gains is not None:
        args, in_specs = [gains] + args, [inside] + in_specs
    args, in_specs = [own_rows] + args, [inside] + in_specs
    beside = None
    if picked is not None:
        planes, per, tokens, cond_wide = picked.shape
        beside = (planes * per, planes)
        args.append(picked)
        in_specs.append(inside)
        outs.append(jax.ShapeDtypeStruct((8, per, tokens, cond_wide), picked.dtype))
        out_specs.append(inside)
        scratch += [
            pltpu.VMEM(picked.shape, picked.dtype),
            pltpu.VMEM(picked.shape[1:], picked.dtype),
            DMA((planes,)),
            DMA((planes,)),
            DMA((8,)),
            DMA((8,)),
        ]
    if outer is not None:
        past, mixed = outer
        width = mixed.shape[1]
        args += [past.reshape(clips, 8, rows, wide), mixed.reshape(clips, 8, rows, width)]
        in_specs += [any_spec()] * 2
        outs.append(jax.ShapeDtypeStruct((wide, 2 * width), jnp.bfloat16))
        out_specs.append(inside)
        scratch += [
            pltpu.VMEM((8, clips, rows, wide), jnp.bfloat16),
            pltpu.VMEM((8, clips, rows, width), jnp.bfloat16),
            DMA((8, clips)),
            DMA((8, clips)),
        ]
    results = pl.pallas_call(
        functools.partial(
            gather_dot_body,
            clips,
            rows,
            sub,
            gains is not None,
            plan,
            beside,
            outer is not None,
            counts,
        ),
        out_shape=outs,
        in_specs=in_specs,
        out_specs=out_specs,
        scratch_shapes=scratch,
        compiler_params=communicating(collective_id),
    )(*args)
    return flat_rows(results[: counts[1]]) + list(results[counts[1] :])


def reduce_steps(clips, rows, sub, multiply, final, terms, pair, turn, from_x, from_y, *sems):
    send_sem, core_sem, turn_sem, x_sem, y_sem = sems
    place, depth, flip = plane_places()
    core, beside_x, beside_y = flip(1), flip(2), flip(4)
    chunks = [(clip, part) for clip in range(clips) for part in range(rows // sub)]
    count = len(chunks)
    half = count // 2
    sends = []

    def send(source, goal, recv_sem, device):
        copy = remote(source, goal, send_sem.at[len(sends)], recv_sem, (device, depth))
        copy.start()
        sends.append(copy)

    def arrived(block, recv_sem):
        remote(block, block, send_sem.at[0], recv_sem, (core, depth)).wait_recv()

    def term(number, index):
        clip, part = chunks[index]
        return terms.at[number, clip, pl.ds(part * sub, sub)]

    def give(number, chip):
        for index in range(count):
            send(term(number, index), pair.at[index, chip], core_sem.at[index, chip], core)

    def total(*blocks):
        return sum(block[...].astype(jnp.float32) for block in blocks)

    def add(block, other):
        block[...] = total(block, other).astype(terms.dtype)

    numbers = {3: 1, 1: 3, 2: 5, 0: 7}

    def combine(chip, index):
        arrived(pair.at[index, chip], core_sem.at[index, chip])
        block = term(numbers[chip], index)
        add(block, pair.at[index, chip])
        return block

    multiply(0)
    give(0, 3)
    multiply(1)
    multiply(2)
    give(2, 1)
    for low in range(half):
        high = half + low
        send(combine(3, low), turn.at[low], turn_sem.at[low], beside_x)
        send(combine(3, high), turn.at[high], turn_sem.at[high], beside_y)
    multiply(3)
    multiply(4)
    give(4, 2)
    for low in range(half):
        send(combine(1, low), from_x.at[low], x_sem.at[low], beside_x)
    multiply(5)
    for high in range(half, count):
        send(combine(2, high), from_y.at[high], y_sem.at[high], beside_y)
    multiply(6)
    give(6, 0)
    multiply(7)
    yield
    for low in range(half):
        high = half + low
        block = combine(2, low)
        arrived(turn.at[low], turn_sem.at[low])
        add(block, turn.at[low])
        send(block, from_y.at[low], y_sem.at[low], beside_y)
        block = combine(1, high)
        arrived(turn.at[high], turn_sem.at[high])
        add(block, turn.at[high])
        send(block, from_x.at[high], x_sem.at[high], beside_x)
    yield
    for index in chunk_order(clips, rows, sub):
        clip, part = chunks[index]
        arrived(pair.at[index, 0], core_sem.at[index, 0])
        arrived(from_x.at[index], x_sem.at[index])
        arrived(from_y.at[index], y_sem.at[index])
        result = total(term(7, index), pair.at[index, 0], from_x.at[index], from_y.at[index])
        final(index, clip, pl.ds(part * sub, sub), result)
    yield
    for copy in sends:
        copy.wait_send()
    yield


def plane_order():
    place, depth, flip = plane_places()
    return [flip(mask) for mask in (7, 6, 3, 2, 5, 4, 1, 0)]


def reduce_scratch(clips, rows, sub, wide):
    count = clips * (rows // sub)
    low = jnp.bfloat16
    return [
        pltpu.VMEM((8, clips, rows, wide), low),
        pltpu.VMEM((count, 4, sub, wide), low),
        pltpu.VMEM((count, sub, wide), low),
        pltpu.VMEM((count, sub, wide), low),
        pltpu.VMEM((count, sub, wide), low),
        DMA((7 * count,)),
        DMA((count, 4)),
        DMA((count,)),
        DMA((count,)),
        DMA((count,)),
    ]


def norm_back(values, gain, grad):
    center = values - jnp.mean(values, axis=1, keepdims=True)
    inverse = lax.rsqrt(jnp.mean(center * center, axis=1, keepdims=True) + norm_eps)
    unit = center * inverse
    stats = [
        jnp.sum(grad * unit, axis=0, keepdims=True),
        jnp.sum(grad, axis=0, keepdims=True),
    ]
    scaled = grad * gain
    result = inverse * (
        scaled
        - jnp.mean(scaled, axis=1, keepdims=True)
        - unit * jnp.mean(scaled * unit, axis=1, keepdims=True)
    )
    return result, stats


def final_back(values_ref, gain_ref, base_ref, sum_ref, stats_ref):
    def final(index, clip, span, result):
        if values_ref is not None:
            result, stats = norm_back(values_ref[clip, span], gain_ref[...], result)
            for which, row in enumerate(stats):
                row = row + stats_ref[which : which + 1] if index else row
                stats_ref[which : which + 1] = row
        result = base_ref[clip, span].astype(jnp.float32) + result
        sum_ref[clip, span] = result.astype(sum_ref.dtype)
        return result

    return final


def terms_of(clips, rows, blocks, mat, span, terms):
    def multiply(number):
        block = blocks(number)
        block = block.reshape(clips * rows, block.shape[-1])
        for start, stop, product in dot_tiles(block, mat, span, True, 256 * 2):
            terms[number, :, :, start:stop] = product.astype(terms.dtype).reshape(
                clips, rows, stop - start
            )

    return multiply


def dot_reduce_body(clips, rows, sub, window, span, back, left_ref, mat_ref, base_ref, *refs):
    refs = list(refs)
    take = lambda count: [refs.pop(0) for _ in range(count)]
    values_ref, gain_ref = take(2) if back else (None, None)
    sum_ref = take(1)[0]
    stats_ref = take(1)[0] if back else None
    left, mat, mat_sem, left_sem = take(4)
    terms = refs[0]
    place, depth, flip = plane_places()
    load = pltpu.make_async_copy(mat_ref.at[:, pl.ds(*window)], mat, mat_sem)
    load.start()
    loads = {}
    for number, slot in enumerate(plane_order()):
        loads[number] = [
            pltpu.make_async_copy(
                left_ref.at[clip, slot], left.at[number, clip], left_sem.at[number, clip]
            )
            for clip in range(clips)
        ]
        for copy in loads[number]:
            copy.start()
    greet([(flip(1), depth), (flip(2), depth), (flip(4), depth)])
    load.wait()

    def blocks(number):
        for copy in loads[number]:
            copy.wait()
        return left[number]

    steps = reduce_steps(
        clips,
        rows,
        sub,
        terms_of(clips, rows, blocks, mat, span, terms),
        final_back(values_ref, gain_ref, base_ref, sum_ref, stats_ref),
        *refs,
    )
    for _ in steps:
        pass


def dot_reduce(left, matrix, clips, collective_id, base, span=None, back=None, kind=jnp.float32, sub=64):
    wide = matrix.shape[0]
    rows, inner = left.shape[0] // (8 * clips), left.shape[1]
    low = jnp.bfloat16
    window, span = window_of(matrix, span)
    inside = pl.BlockSpec(memory_space=pltpu.VMEM)
    args = [left.reshape(clips, 8, rows, inner), matrix, base]
    in_specs = [any_spec(), any_spec(), inside]
    outs, out_specs = [jax.ShapeDtypeStruct((clips, rows, wide), kind)], [inside]
    if back is not None:
        args += list(back)
        in_specs += [inside] * 2
        outs.append(jax.ShapeDtypeStruct((2, wide), jnp.float32))
        out_specs.append(inside)
    return pl.pallas_call(
        functools.partial(dot_reduce_body, clips, rows, sub, window, span, back is not None),
        out_shape=outs,
        in_specs=in_specs,
        out_specs=out_specs,
        scratch_shapes=[
            pltpu.VMEM((8, clips, rows, inner), low),
            pltpu.VMEM((wide, window[1]), low),
            DMA(()),
            DMA((8, clips)),
        ]
        + reduce_scratch(clips, rows, sub, wide),
        compiler_params=communicating(collective_id),
    )(*args)


def add_steps(parts_ref, sum_ref, landed, send_sem, recv_sem, local_sem):
    place, depth, flip = plane_places()
    planes = parts_ref.shape[0]
    copies = []
    for step in range(1, planes):
        goal = lax.rem(depth + step, planes)
        copy = remote(
            parts_ref.at[goal],
            landed.at[depth],
            send_sem.at[step],
            recv_sem.at[depth],
            (place, goal),
        )
        copy.start()
        copies.append(copy)
    stay = pltpu.make_async_copy(parts_ref.at[depth], landed.at[depth], local_sem)
    stay.start()
    yield
    stay.wait()
    for step in range(1, planes):
        source = lax.rem(depth + step, planes)
        block = landed.at[source]
        remote(block, block, send_sem.at[0], recv_sem.at[source], (place, source)).wait_recv()
    sum_ref[...] = jnp.sum(landed[...].astype(jnp.float32), axis=0).astype(sum_ref.dtype)
    for copy in copies:
        copy.wait_send()
    yield


def reduce_gather_body(
    clips, rows, sub, spans, back, normed, plan, counts, passing, outer, leaving, adding, left_ref, mat_ref, base_ref, *refs
):
    refs = list(refs)
    take = lambda count: [refs.pop(0) for _ in range(count)]
    values_ref, back_gain_ref = take(2) if back else (None, None)
    gain_ref = take(1)[0] if normed else None
    ins = take(counts[0])
    mid_ref = take(1)[0] if passing else None
    low_ref, ending_ref = take(2) if outer else (None, None)
    leaving_ref = take(1)[0] if leaving else None
    adding_ref = take(1)[0] if adding else None
    sum_ref = take(1)[0]
    stats_ref = take(1)[0] if back else None
    outs = take(counts[1])
    kept_ref = take(1)[0] if passing else None
    outer_ref = take(1)[0] if outer else None
    own_ref, own_mid = take(2) if leaving else (None, None)
    added_ref = take(1)[0] if adding else None
    left, mat, mat_sem, left_sem = take(4)
    terms, *others = reduce_refs = take(10)
    gather_scratch = take(counts[2])
    load, put, run = gather_parts(clips, rows, sub, *plan, ins, outs, gather_scratch)
    window, span = spans
    place, depth, flip = plane_places()
    mat_load = pltpu.make_async_copy(mat_ref.at[:, pl.ds(*window)], mat, mat_sem)
    mat_load.start()
    loads = {}
    for number, slot in enumerate(plane_order()):
        loads[number] = [
            pltpu.make_async_copy(
                left_ref.at[clip, slot], left.at[number, clip], left_sem.at[number, clip]
            )
            for clip in range(clips)
        ]
        for copy in loads[number]:
            copy.start()
    load()
    if outer:
        low, low_sem = take(2)
        outer_loads = by_slot_loads(low_ref, low, low_sem)
        for copy in outer_loads:
            copy.start()
    if adding:
        adder = add_steps(adding_ref, added_ref, *take(4))
    if passing:
        greet_cross(*passing)
        pass_rows, end_rows = inward_over(*passing, mid_ref, kept_ref, *refs)
        pass_rows()
    elif leaving:
        greet_cross(*leaving)
        going = outward_steps(*leaving, leaving_ref, own_ref, own_mid, *refs)
        next(going)
    else:
        greet([(flip(1), depth), (flip(2), depth), (flip(4), depth)])
    mat_load.wait()

    def blocks(number):
        for copy in loads[number]:
            copy.wait()
        return left[number]

    keep = final_back(values_ref, back_gain_ref, base_ref, sum_ref, stats_ref)

    def final(index, clip, span_rows, result):
        result = keep(index, clip, span_rows, result)
        if normed:
            result = layer_norm(result, gain_ref[0:1], gain_ref[1:2])
        put(index, result)

    steps = reduce_steps(
        clips,
        rows,
        sub,
        terms_of(clips, rows, blocks, mat, span, terms),
        final,
        *reduce_refs,
    )

    next(steps)
    next(steps)
    next(steps)
    if adding:
        next(adder)
    run((lambda: next(going)) if leaving else (lambda: None))
    if outer:
        for copy in outer_loads:
            copy.wait()
        outer_columns(outer_ref, 0, low[...], gather_scratch[0][...])
        outer_ref[:, low.shape[3] :] = ending_ref[...]
    next(steps)
    if passing:
        end_rows()
    if leaving:
        next(going)
    if adding:
        next(adder)


def reduce_gather(
    left,
    matrix,
    clips,
    collective_id,
    base,
    second,
    kind=jnp.bfloat16,
    span=None,
    back=None,
    gains=None,
    second_span=None,
    pair=None,
    bias=None,
    passing=None,
    outer=None,
    leaving=None,
    adding=None,
    sub=64,
):
    wide = matrix.shape[0]
    rows, inner = left.shape[0] // (8 * clips), left.shape[1]
    low = jnp.bfloat16
    spans = window_of(matrix, span)
    inside = pl.BlockSpec(memory_space=pltpu.VMEM)
    plan, more, more_specs, outs, out_specs, more_scratch = gather_plan(
        clips, rows, wide, sub, second, kind, None, second_span, pair, bias, None
    )
    counts = (len(more), len(outs), len(more_scratch))
    args = [left.reshape(clips, 8, rows, inner), matrix, base]
    in_specs = [any_spec(), any_spec(), inside]
    first_outs = [jax.ShapeDtypeStruct((clips, rows, wide), jnp.float32)]
    scratch = [
        pltpu.VMEM((8, clips, rows, inner), low),
        pltpu.VMEM((wide, spans[0][1]), low),
        DMA(()),
        DMA((8, clips)),
    ] + reduce_scratch(clips, rows, sub, wide)
    if back is not None:
        args += list(back)
        in_specs += [inside] * 2
        first_outs.append(jax.ShapeDtypeStruct((2, wide), jnp.float32))
    if gains is not None:
        args.append(gains)
        in_specs.append(inside)
    args += more
    in_specs += more_specs
    scratch += more_scratch
    outs = first_outs + outs
    out_specs = [inside] * len(first_outs) + out_specs
    flat = len(outs)
    if passing is not None:
        group, piece, _ = passing.shape
        planes = group // clips
        args.append(passing)
        in_specs.append(any_spec())
        outs.append(jax.ShapeDtypeStruct((clips, planes, piece, wide), passing.dtype))
        out_specs.append(any_spec())
        scratch += [DMA((group,)), DMA((clips, planes)), DMA((group,))]
    if outer is not None:
        low_rows, ending = outer
        columns = low_rows.shape[1]
        args += [low_rows.reshape(clips, 8, rows, columns), ending]
        in_specs += [any_spec(), inside]
        outs.append(jax.ShapeDtypeStruct((wide, columns + ending.shape[1]), low))
        out_specs.append(inside)
        scratch += [pltpu.VMEM((8, clips, rows, columns), low), DMA((8, clips))]
    if leaving is not None:
        per, planes, piece, _ = leaving.shape
        group = per * planes
        args.append(leaving)
        in_specs.append(any_spec())
        outs += [jax.ShapeDtypeStruct((group, piece, wide), leaving.dtype)] * 2
        leaving_mid = len(outs) - 1
        out_specs += [any_spec()] * 2
    if adding is not None:
        args.append(adding)
        in_specs.append(any_spec())
        outs.append(jax.ShapeDtypeStruct(adding.shape[1:], adding.dtype))
        out_specs.append(inside)
        scratch += [
            pltpu.VMEM(adding.shape, adding.dtype),
            DMA((adding.shape[0],)),
            DMA((adding.shape[0],)),
            DMA(()),
        ]
    if leaving is not None:
        scratch += outward_scratch(group, planes)
    results = pl.pallas_call(
        functools.partial(
            reduce_gather_body,
            clips,
            rows,
            sub,
            spans,
            back is not None,
            gains is not None,
            plan,
            counts,
            passing is not None and (group, planes),
            outer is not None,
            leaving is not None and (group, planes),
            adding is not None,
        ),
        out_shape=outs,
        in_specs=in_specs,
        out_specs=out_specs,
        scratch_shapes=scratch,
        compiler_params=communicating(collective_id),
    )(*args)
    first = len(first_outs)
    if leaving is not None:
        results = [block for which, block in enumerate(results) if which != leaving_mid]
    return list(results[:first]) + flat_rows(results[first:flat]) + list(results[flat:])


def ff_outer_body(
    clips,
    rows,
    sub,
    gates_ref,
    hidden_ref,
    down_ref,
    normed_ref,
    grads_ref,
    values_ref,
    layer_ref,
    outer_ref,
    gates,
    hidden,
    down,
    normed,
    grads,
    stage,
    load_sem,
    tile_sem,
    stage_sem,
    *reduce_refs,
):
    place, depth, flip = plane_places()
    order = plane_order()
    loads = [
        pltpu.make_async_copy(source, goal, load_sem.at[which])
        for which, (source, goal) in enumerate(
            ((down_ref, down), (hidden_ref, hidden), (gates_ref, gates))
        )
    ]
    for copy in loads:
        copy.start()
    tile = stage.shape[1]
    tiles = normed_ref.shape[3] // tile
    total_rows = 8 * clips * rows
    inner = gates.shape[3]

    def fetch(index):
        return [
            pltpu.make_async_copy(
                source.at[:, :, :, pl.ds(index * tile, tile)],
                goal.at[index % 2],
                tile_sem.at[which, index % 2],
            )
            for which, (source, goal) in enumerate(((normed_ref, normed), (grads_ref, grads)))
        ]

    def stored(index):
        return pltpu.make_async_copy(
            stage.at[index % 2],
            outer_ref.at[pl.ds(index * tile, tile)],
            stage_sem.at[index % 2],
        )

    def outer_tile(index):
        spot = index % 2
        if index >= 2:
            stored(index - 2).wait()
        for copy in fetch(index):
            copy.wait()
        stage[spot, :, :inner] = outer_sum(
            normed[spot].reshape(total_rows, tile), gates[...].reshape(total_rows, inner)
        ).astype(stage.dtype)
        stage[spot, :, inner:] = outer_sum(
            grads[spot].reshape(total_rows, tile),
            hidden[...].reshape(total_rows, hidden.shape[3]),
        ).astype(stage.dtype)
        stored(index).start()
        if index + 2 < tiles:
            for copy in fetch(index + 2):
                copy.start()

    for index in range(2):
        for copy in fetch(index):
            copy.start()
    greet([(flip(1), depth), (flip(2), depth), (flip(4), depth)])
    loads[0].wait()
    loads[1].wait()

    def layer_rows(index, clip, span, result):
        layer_ref[clip, span] = (values_ref[clip, span] + result).astype(layer_ref.dtype)

    steps = reduce_steps(
        clips,
        rows,
        sub,
        terms_of(
            clips, rows, lambda number: hidden[order[number]], down, (0, down.shape[1]), reduce_refs[0]
        ),
        layer_rows,
        *reduce_refs,
    )
    next(steps)
    loads[2].wait()
    outer_tile(0)
    next(steps)
    for index in range(1, tiles):
        outer_tile(index)
    next(steps)
    for index in range(max(tiles - 2, 0), tiles):
        stored(index).wait()
    next(steps)


def ff_outer(gates, hidden, down, normed, grads, values, collective_id, sub=64):
    clips, rows, wide = values.shape
    low = jnp.bfloat16
    inner, columns = gates.shape[1], gates.shape[1] + hidden.shape[1]
    tile = 512
    inside = pl.BlockSpec(memory_space=pltpu.VMEM)
    return pl.pallas_call(
        functools.partial(ff_outer_body, clips, rows, sub),
        out_shape=[
            jax.ShapeDtypeStruct((clips, rows, wide), low),
            jax.ShapeDtypeStruct((wide, columns), low),
        ],
        in_specs=[any_spec()] * 5 + [inside],
        out_specs=[inside, any_spec()],
        scratch_shapes=[
            pltpu.VMEM((clips, 8, rows, inner), low),
            pltpu.VMEM((8, clips, rows, hidden.shape[1]), low),
            pltpu.VMEM(down.shape, low),
            pltpu.VMEM((2, clips, 8, rows, tile), low),
            pltpu.VMEM((2, 8, clips, rows, tile), low),
            pltpu.VMEM((2, tile, columns), low),
            DMA((3,)),
            DMA((2, 2)),
            DMA((2,)),
        ]
        + reduce_scratch(clips, rows, sub, wide),
        compiler_params=communicating(collective_id),
    )(
        gates.reshape(clips, 8, rows, inner),
        hidden.reshape(8, clips, rows, hidden.shape[1]),
        down,
        normed.reshape(clips, 8, rows, wide),
        grads.reshape(8, clips, rows, wide),
        values,
    )


def rotary_lanes(places):
    half = HDIM // 2
    frequency = 10000.0 ** (-np.arange(half, dtype=np.float32) / np.float32(half))
    angles = places.astype(np.float32)[:, None] * frequency.astype(np.float32)[None, :]
    cosine, sine = np.cos(angles), np.sin(angles)
    both = [
        np.concatenate([cosine] * 4, axis=1),
        np.concatenate([-sine, sine, -sine, sine], axis=1),
    ]
    return jnp.asarray(np.stack(both).astype(np.float32))


def turn_heads(values, cosine, sine):
    lane = lax.broadcasted_iota(jnp.int32, values.shape, 1)
    half = HDIM // 2
    ahead = pltpu.roll(values, 2 * HDIM - half, 1)
    behind = pltpu.roll(values, half, 1)
    other = jnp.where(lax.rem(lane, HDIM) < half, ahead, behind)
    return values * cosine + other * sine


def swap_beside(pairs, send_sem, recv_sem, local_sem):
    place, depth, flip = plane_places()

    def each(act):
        for which, (source, goal) in enumerate(pairs):
            for mask in (6, 7, 2, 3, 4, 5, 1):
                other = flip(mask)
                act(
                    remote(
                        source(other),
                        goal(place),
                        send_sem.at[which, mask],
                        recv_sem.at[which, mask],
                        (other, depth),
                    )
                )

    stays = [
        pltpu.make_async_copy(source(place), goal(place), local_sem.at[which])
        for which, (source, goal) in enumerate(pairs)
    ]

    def begin():
        each(lambda copy: copy.start())
        for stay in stays:
            stay.start()

    def end():
        each(lambda copy: copy.wait())
        for stay in stays:
            stay.wait()

    return begin, end


def swap_beside_scratch(count):
    return [DMA((count, 8)), DMA((count, 8)), DMA((count,))]


def flash_forward_body(
    heads,
    tile,
    normed_ref,
    mat_ref,
    stamp_ref,
    bias_ref,
    rotary_ref,
    ff_ref,
    own_ref,
    turned_ref,
    out_ref,
    lse_ref,
    gate_up_ref,
    down_ref,
    mid_ref,
    raw_ref,
    *sems,
):
    group = gate_up_ref.shape[0]
    hidden = down_ref.shape[2]
    step, last = pl.program_id(0), pl.num_programs(0) - 1

    def columns(block):
        return lambda other: ff_ref.at[
            :, pl.ds(pl.multiple_of((block * group + other) * hidden, 128), hidden)
        ]

    start_swap, end_swap = swap_beside(
        [
            (lambda other: own_ref.at[other], lambda other: mid_ref.at[other]),
            (columns(0), lambda other: gate_up_ref.at[other, :, pl.ds(0, hidden)]),
            (columns(1), lambda other: gate_up_ref.at[other, :, pl.ds(hidden, hidden)]),
            (columns(2), lambda other: down_ref.at[other]),
        ],
        *sems,
    )
    place, depth, flip = plane_places()

    @pl.when(step == 0)
    def _():
        greet([(flip(mask), depth) for mask in range(1, group)])
        start_swap()

    def project(index, carry):
        place = pl.ds(pl.multiple_of(index * tile, tile), tile)
        raw_ref[place, :] = jnp.dot(
            normed_ref[place, :], mat_ref[...], preferred_element_type=jnp.float32
        )
        return carry

    lax.fori_loop(0, raw_ref.shape[0] // tile, project, 0)
    wide = heads * HDIM
    for pair in range(2 * wide // 128):
        lanes = slice(pair * 128, pair * 128 + 128)
        turned_ref[:, lanes] = turn_heads(
            raw_ref[:, lanes], rotary_ref[0], rotary_ref[1]
        ).astype(turned_ref.dtype)
    turned_ref[:, 2 * wide :] = raw_ref[:, 2 * wide :].astype(turned_ref.dtype)
    rows = raw_ref.shape[0]
    bias = bias_ref[0]
    scale = HDIM**-0.5
    for head in range(heads):
        lanes = slice(head * HDIM, head * HDIM + HDIM)
        keys = turned_ref[:, wide + head * HDIM : wide + head * HDIM + HDIM]
        values = turned_ref[:, 2 * wide + head * HDIM : 2 * wide + head * HDIM + HDIM]
        stamp_key = stamp_ref[0, :, lanes].astype(jnp.float32)
        stamp_value = stamp_ref[
            0, :, wide + head * HDIM : wide + head * HDIM + HDIM
        ].astype(jnp.float32)

        def one(step, carry):
            place = pl.ds(pl.multiple_of(step * tile, tile), tile)
            query = turned_ref[place, lanes] * jnp.asarray(scale, turned_ref.dtype)
            scores = times_transposed(query, keys) + bias
            stamp_score = jnp.sum(query.astype(jnp.float32) * stamp_key, axis=1, keepdims=True)
            top = jnp.maximum(jnp.max(scores, axis=1, keepdims=True), stamp_score)
            expo = jnp.exp(scores - top)
            stamp_expo = jnp.exp(stamp_score - top)
            denom = jnp.sum(expo, axis=1, keepdims=True) + stamp_expo
            share = 1.0 / denom
            prob = (expo * share).astype(values.dtype)
            stamp_prob = (stamp_expo * share).astype(values.dtype).astype(jnp.float32)
            mixed = jnp.dot(prob, values, preferred_element_type=jnp.float32)
            out_ref[place, lanes] = (mixed + stamp_prob * stamp_value).astype(out_ref.dtype)
            lse_ref[place, head : head + 1] = top + jnp.log(denom)
            return carry

        lax.fori_loop(0, rows // tile, one, 0)

    pl.when(step == last)(end_swap)


def flash_forward(normed, matrix, stamps, bias, rotary, heads, ff_low, rows_of_clip, collective_id):
    clips, rows = bias.shape
    wide = heads * HDIM
    group, piece, features = rows_of_clip.shape
    owned, columns = ff_low.shape
    hidden = columns // (3 * group)
    like = lambda *shape: jax.ShapeDtypeStruct(shape, rows_of_clip.dtype)
    blocked = lambda lanes: pl.BlockSpec((rows, lanes), lambda clip: (clip, 0))
    return pl.pallas_call(
        functools.partial(flash_forward_body, heads, rows // 4),
        grid=(clips,),
        out_shape=[
            like(clips * rows, 3 * wide),
            like(clips * rows, wide),
            jax.ShapeDtypeStruct((clips * rows, 128), jnp.float32),
            like(group, owned, 2 * hidden),
            like(group, owned, hidden),
            like(group, piece, features),
        ],
        in_specs=[
            blocked(features),
            pl.BlockSpec(matrix.shape, lambda clip: (0, 0)),
            pl.BlockSpec((1, 1, 2 * wide), lambda clip: (clip, 0, 0)),
            pl.BlockSpec((1, 1, rows), lambda clip: (clip, 0, 0)),
            pl.BlockSpec((2, rows, 128), lambda clip: (0, 0, 0)),
            any_spec(),
            any_spec(),
        ],
        out_specs=[blocked(3 * wide), blocked(wide), blocked(128)] + [any_spec()] * 3,
        scratch_shapes=[pltpu.VMEM((rows, 3 * wide), jnp.float32)] + swap_beside_scratch(4),
        compiler_params=communicating(collective_id),
    )(normed, matrix, stamps[:, None], bias[:, None], rotary, ff_low, rows_of_clip)


def flash_backward_body(
    heads,
    tile,
    turned_ref,
    mixed_ref,
    grad_ref,
    lse_ref,
    stamp_ref,
    bias_ref,
    rotary_ref,
    cut_ref,
    normed_ref,
    stamp_normed_ref,
    out_ref,
    stamp_out_ref,
    mine_ref,
    outer_ref,
    query_grad,
    key_grad,
    value_grad,
    outer_total,
    *sems,
):
    place, depth, flip = plane_places()
    start_swap, end_swap = swap_beside(
        [(lambda other: cut_ref.at[other], lambda other: mine_ref.at[other])], *sems
    )

    @pl.when(pl.program_id(0) == 0)
    def _():
        greet([(flip(mask), depth) for mask in range(1, 8)])
        start_swap()

    wide = heads * HDIM
    rows = turned_ref.shape[0]
    scale = HDIM**-0.5
    low = turned_ref.dtype
    f32 = jnp.float32
    first_row = lax.broadcasted_iota(jnp.int32, (8, tile), 0) == 0
    ones = lambda count, width: jnp.ones((count, width), low)
    blank = lambda count, width: jnp.zeros((count, width), low)
    bias = bias_ref[0].astype(low)

    def widened(count, *parts):
        have = sum(part.shape[1] for part in parts)
        return jnp.concatenate(list(parts) + [blank(count, 128 - have)], axis=1)

    def negative_parts(column):
        parts, rest = [], -column
        for _ in range(3):
            parts.append(rest.astype(low))
            rest = rest - parts[-1].astype(f32)
        return parts

    for head in range(heads):
        lanes = slice(head * HDIM, head * HDIM + HDIM)
        later = slice(wide + head * HDIM, wide + head * HDIM + HDIM)
        keys = turned_ref[:, later]
        values = turned_ref[:, 2 * wide + head * HDIM : 2 * wide + head * HDIM + HDIM]
        keys_across = keys.astype(f32).T.astype(low)
        wide_keys = widened(rows, keys, bias, ones(rows, 3))
        wide_values = widened(rows, values, ones(rows, 3))
        stamp_key = jnp.broadcast_to(stamp_ref[0, :, lanes], (8, HDIM))
        stamp_value = jnp.broadcast_to(stamp_ref[0, :, later], (8, HDIM))
        wide_stamp_key = widened(8, stamp_key, blank(8, 1), ones(8, 3))
        wide_stamp_value = widened(8, stamp_value, ones(8, 3))
        stamp_column = stamp_ref[0, :, lanes].astype(f32).T
        key_total = jnp.zeros((rows, HDIM), f32)
        value_total = jnp.zeros((rows, HDIM), f32)
        stamp_key_total = jnp.zeros((8, HDIM), f32)
        stamp_value_total = jnp.zeros((8, HDIM), f32)
        for step in range(rows // tile):
            place = slice(step * tile, step * tile + tile)
            query = turned_ref[place, lanes] * jnp.asarray(scale, low)
            grad = grad_ref[place, lanes]
            delta = jnp.sum(
                grad.astype(f32) * mixed_ref[place, lanes].astype(f32), axis=1, keepdims=True
            )
            lse = lse_ref[place, head : head + 1]
            wide_query = widened(tile, query, ones(tile, 1), *negative_parts(lse))
            wide_grad = widened(tile, grad, *negative_parts(delta))
            prob = jnp.exp(times_transposed(wide_keys, wide_query))
            scores = (prob * times_transposed(wide_values, wide_grad)).astype(low)
            stamp_prob = jnp.exp(times_transposed(wide_stamp_key, wide_query))
            stamp_scores = stamp_prob * times_transposed(wide_stamp_value, wide_grad)
            stamp_scores = jnp.where(first_row, stamp_scores, 0.0).astype(low)
            value_total += jnp.dot(prob.astype(low), grad, preferred_element_type=f32)
            key_total += jnp.dot(scores, query, preferred_element_type=f32)
            across = jnp.dot(keys_across, scores, preferred_element_type=f32)
            across = across + stamp_column * stamp_scores[:1].astype(f32)
            query_grad[place, lanes] = across.T * scale
            stamp_key_total += jnp.dot(stamp_scores, query, preferred_element_type=f32)
            stamp_value_total += jnp.dot(
                jnp.where(first_row, stamp_prob, 0.0).astype(low), grad, preferred_element_type=f32
            )
        key_grad[:, lanes] = key_total
        value_grad[:, lanes] = value_total
        stamp_out_ref[0, :, lanes] = stamp_key_total[:1]
        stamp_out_ref[0, :, later] = stamp_value_total[:1]
    both = jnp.concatenate([query_grad[...], key_grad[...]], axis=1)
    for pair in range(2 * wide // 128):
        lanes = slice(pair * 128, pair * 128 + 128)
        out_ref[:, lanes] = turn_heads(both[:, lanes], rotary_ref[0], -rotary_ref[1]).astype(low)
    out_ref[:, 2 * wide :] = value_grad[...].astype(low)
    count = outer_total.shape[1]
    tile = 512
    for start in range(0, normed_ref.shape[1], tile):
        span = slice(start, start + tile)
        product = outer_sum(normed_ref[:, span], out_ref[...])
        stamp_part = stamp_normed_ref[0, span] * stamp_out_ref[0]
        product = product + jnp.concatenate(
            [jnp.zeros((tile, count - 2 * wide), f32), stamp_part], axis=1
        )

        @pl.when(pl.program_id(0) == 0)
        def _():
            outer_total[span] = product

        @pl.when(pl.program_id(0) > 0)
        def _():
            outer_total[span] += product

    @pl.when(pl.program_id(0) == pl.num_programs(0) - 1)
    def _():
        outer_ref[...] = outer_total[...].astype(outer_ref.dtype)
        end_swap()


def flash_backward(
    turned, mixed, grad, lse, stamps, bias, rotary, heads, cut, normed, stamp_normed, collective_id
):
    clips, rows = bias.shape
    wide = heads * HDIM
    blocked = lambda lanes: pl.BlockSpec((rows, lanes), lambda clip: (clip, 0))
    features = normed.shape[1]
    grads, stamp_grads, mine, outer = pl.pallas_call(
        functools.partial(flash_backward_body, heads, rows // 4),
        grid=(clips,),
        out_shape=[
            jax.ShapeDtypeStruct((clips * rows, 3 * wide), jnp.bfloat16),
            jax.ShapeDtypeStruct((clips, 1, 2 * wide), jnp.float32),
            jax.ShapeDtypeStruct(cut.shape, cut.dtype),
            jax.ShapeDtypeStruct((features, 3 * wide), jnp.bfloat16),
        ],
        in_specs=[
            blocked(3 * wide),
            blocked(wide),
            blocked(wide),
            blocked(128),
            pl.BlockSpec((1, 1, 2 * wide), lambda clip: (clip, 0, 0)),
            pl.BlockSpec((1, rows, 1), lambda clip: (clip, 0, 0)),
            pl.BlockSpec((2, rows, 128), lambda clip: (0, 0, 0)),
            any_spec(),
            blocked(features),
            pl.BlockSpec((1, features, 1), lambda clip: (clip, 0, 0)),
        ],
        out_specs=[
            blocked(3 * wide),
            pl.BlockSpec((1, 1, 2 * wide), lambda clip: (clip, 0, 0)),
            any_spec(),
            pl.BlockSpec((features, 3 * wide), lambda clip: (0, 0)),
        ],
        scratch_shapes=[pltpu.VMEM((rows, wide), jnp.float32)] * 3
        + [pltpu.VMEM((features, 3 * wide), jnp.float32)]
        + swap_beside_scratch(1),
        compiler_params=communicating(collective_id),
    )(
        turned,
        mixed,
        grad,
        lse,
        stamps[:, None],
        bias[:, :, None],
        rotary,
        cut,
        normed,
        stamp_normed.astype(jnp.float32)[:, :, None],
    )
    return grads, stamp_grads[:, 0], mine, outer


def adam_body(factor_ref, weight_ref, first_ref, second_ref, grad_ref, *outs):
    gradient = jnp.concatenate(
        [grad_ref[part] for part in range(grad_ref.shape[0])], axis=1
    ).astype(jnp.float32)
    results = adam_step(
        weight_ref[...],
        first_ref[...],
        second_ref[...],
        gradient * factor_ref[0, 0],
        matrix_rate,
        matrix_decay,
    )
    for out, result in zip(outs, results):
        out[...] = result


def adam_blocks_body(places, factor_ref, weight_ref, first_ref, second_ref, *refs):
    *owned_refs, weight_out, first_out, second_out = refs
    for block, (which, start, stop) in enumerate(places):

        @pl.when(pl.program_id(0) == block)
        def _(owned_ref=owned_refs[which], start=start, stop=stop):
            gradient = jnp.concatenate(
                [owned_ref[part, :, start:stop] for part in range(owned_ref.shape[0])], axis=1
            ).astype(jnp.float32)
            results = adam_step(
                weight_ref[...],
                first_ref[...],
                second_ref[...],
                gradient * factor_ref[0, 0],
                matrix_rate,
                matrix_decay,
            )
            weight_out[...], first_out[...], second_out[...] = results


def adam_blocks(factor, weight, first, second, owned, places):
    rows, columns = weight.shape
    group = owned[0].shape[0]
    blocks = len(places)
    width = columns // (group * blocks)
    piece = pl.BlockSpec((rows, group * width), lambda block: (0, block))
    whole = [pl.BlockSpec(pieces.shape, lambda block: (0, 0, 0)) for pieces in owned]
    return pl.pallas_call(
        functools.partial(adam_blocks_body, places),
        grid=(blocks,),
        out_shape=[jax.ShapeDtypeStruct(weight.shape, jnp.float32)] * 3,
        in_specs=[pl.BlockSpec(memory_space=pltpu.SMEM), piece, piece, piece] + whole,
        out_specs=[piece] * 3,
        compiler_params=pltpu.CompilerParams(vmem_limit_bytes=VMEM_LIMIT),
    )(factor, weight, first, second, *owned)


def adam_matrix(factor, weight, first, second, owned, width, parts):
    rows, columns = weight.shape
    group = owned.shape[0]
    steps = group // parts
    piece = pl.BlockSpec((rows, parts * width), lambda block, step: (0, block * steps + step))
    grads = pl.BlockSpec((parts, rows, width), lambda block, step: (step, 0, block))
    return pl.pallas_call(
        adam_body,
        grid=(columns // (group * width), steps),
        out_shape=[jax.ShapeDtypeStruct(weight.shape, jnp.float32)] * 3,
        in_specs=[pl.BlockSpec(memory_space=pltpu.SMEM), piece, piece, piece, grads],
        out_specs=[piece] * 3,
        compiler_params=pltpu.CompilerParams(vmem_limit_bytes=VMEM_LIMIT),
    )(factor, weight, first, second, owned)


def plane_device(
    frames,
    time_token,
    cond_ids,
    cond_mask,
    lengths,
    cond_table,
    cotangent,
    attn_weight,
    cross_weight,
    norm_param,
    ff_weight,
    attn_first,
    attn_second,
    cross_first,
    cross_second,
    norm_first,
    norm_second,
    ff_first,
    ff_second,
):
    group, planes = lax.axis_size("dp"), lax.axis_size("seq")
    place, depth = lax.axis_index("dp"), lax.axis_index("seq")
    clips = group // planes
    _, frame_rows, wide = frames.shape
    piece = frame_rows // group
    seq_frames = frame_rows * planes
    own_rows = planes * piece
    heads = HEADS // group
    head_wide = heads * HDIM
    ff_wide = FF // group
    owned = wide // (group * planes)
    cond_count, cond_wide = cond_ids.shape[1], cond_table.shape[1]
    cond_owned = cross_weight.shape[0]

    order = jnp.arange(wide).reshape(group, planes, owned).swapaxes(0, 1).reshape(wide)
    order_mat = (jnp.arange(wide)[:, None] == order[None, :]).astype(jnp.bfloat16)

    def to_plane_order(values):
        return jnp.dot(values, order_mat, preferred_element_type=jnp.float32).astype(jnp.bfloat16)

    def to_whole_order(values):
        return times_transposed(values, order_mat)

    attn_low = attn_weight.astype(jnp.bfloat16).reshape(owned, 6, group, head_wide)
    attn_cut = attn_low.transpose(2, 0, 1, 3).reshape(group, owned, 6 * head_wide)
    cross_low = cross_weight.astype(jnp.bfloat16).reshape(cond_owned, 2, group, head_wide)
    cross_cut = cross_low.transpose(2, 0, 1, 3).reshape(group, owned, -1)
    norm_block = norm_param.astype(jnp.bfloat16).astype(jnp.float32)
    norm_block = jnp.pad(norm_block, ((0, 2), (0, 128 - owned)))
    pack = jnp.concatenate(
        [
            time_token.astype(jnp.float32),
            jnp.pad(cond_ids.astype(jnp.float32), ((0, 0), (0, wide - cond_count))),
            jnp.pad(cond_mask.astype(jnp.float32), ((0, 0), (0, wide - cond_count))),
            jnp.broadcast_to(lengths.astype(jnp.float32)[:, None], (1, wide)),
            jnp.zeros((4, wide), jnp.float32),
        ],
        axis=0,
    )
    stream, gain_rows, packs, qkv_mine, rest_mine, ff_low = enter(
        to_plane_order(frames[0]).reshape(group, piece, wide),
        norm_block,
        pack,
        attn_cut[:, :, : 3 * head_wide],
        jnp.concatenate([attn_cut[:, :, 3 * head_wide :], cross_cut], axis=2),
        ff_weight,
        planes,
        1,
    )
    stream = stream.reshape(clips, own_rows, wide).astype(jnp.float32)

    def over_planes(block):
        return lax.all_gather(block.reshape(group * owned, -1), "seq", axis=0, tiled=True)

    w_qkv = over_planes(qkv_mine)
    w_rest = over_planes(rest_mine)
    of_self_out = (0, head_wide)
    of_cross_query = (head_wide, 2 * head_wide)
    of_cross_out = (2 * head_wide, 3 * head_wide)
    w_cond = w_rest[:, 3 * head_wide :].reshape(planes, group, cond_owned, -1)
    w_cond = jnp.swapaxes(w_cond, 0, 1).reshape(cond_wide, 2 * head_wide)
    plane_packs = lax.dynamic_slice_in_dim(packs, depth * clips, clips, axis=0)
    stamps = to_plane_order(plane_packs[:, 0].astype(jnp.bfloat16)).astype(jnp.float32)
    cond_keep = plane_packs[:, 2, :cond_count] > 0
    clip_lengths = plane_packs[:, 3, 0].astype(jnp.int32)
    share = cond_count // group
    all_ids = packs[:, 1, :cond_count].astype(jnp.int32)
    own_ids = lax.dynamic_slice_in_dim(all_ids, place * share, share, axis=1)
    vocab_rows = cond_table.shape[0]
    relative = own_ids - depth * vocab_rows
    inside = (relative >= 0) & (relative < vocab_rows)
    picked = jnp.take(cond_table, jnp.clip(relative, 0, vocab_rows - 1), axis=0)
    picked = jnp.where(inside[..., None], picked, jnp.zeros((), picked.dtype))
    picked = picked.reshape(planes, clips, share, cond_wide)
    positions = depth * frame_rows + jnp.arange(frame_rows)
    frame_valid = (positions[None, :] < lengths[:, None]).astype(cotangent.dtype)
    masked = to_plane_order((cotangent * frame_valid[..., None])[0])

    group_rows = clips * seq_frames
    row_place = np.arange(seq_frames)
    row_owner, row_rest = row_place // own_rows, row_place % own_rows
    true_place = (row_rest // piece) * frame_rows + row_owner * piece + row_rest % piece
    key_keep = true_place[None, :] < clip_lengths[:, None]
    group_shape = (clips, seq_frames, heads, HDIM)

    group_one, cond = gather_dot(stream, None, None, 5, gain_rows[0:2], picked)
    cond_flat = cond.swapaxes(0, 1).reshape(clips * cond_count, cond_wide)
    stamp_normed = layer_norm(stamps, gain_rows[0], gain_rows[1]).astype(jnp.bfloat16)
    stamp_pair = jnp.dot(stamp_normed, w_qkv[:, head_wide:], preferred_element_type=jnp.float32)
    stamp_pair = stamp_pair.astype(jnp.bfloat16)
    rotary = rotary_lanes(true_place)
    key_bias = jnp.where(key_keep, 0.0, masked_score)
    rotated, self_low, self_lse, gate_up_mine, down_mine, grad_out_mid = flash_forward(
        group_one,
        w_qkv,
        stamp_pair,
        key_bias,
        rotary,
        heads,
        ff_low,
        masked.reshape(group, piece, wide),
        2,
    )
    w_gate_up = over_planes(gate_up_mine)
    w_down = over_planes(down_mine)
    cond_pair = jnp.dot(cond_flat, w_cond, preferred_element_type=jnp.float32)
    cond_pair = cond_pair.astype(jnp.bfloat16).reshape(clips, cond_count, 2 * head_wide)
    cond_bias = jnp.where(cond_keep, 0.0, masked_score)[:, None]
    resid_one, group_two, cross_query, cross_out, grad_out_low = reduce_gather(
        self_low,
        w_rest,
        clips,
        6,
        stream,
        w_rest,
        span=of_self_out,
        gains=gain_rows[2:4],
        second_span=of_cross_query,
        pair=cond_pair,
        bias=cond_bias,
        passing=grad_out_mid,
    )
    grad_out_low = grad_out_low.reshape(clips, own_rows, wide)
    (resid_two,) = dot_reduce(cross_out, w_rest, clips, 8, resid_one, of_cross_out)
    group_three, gate_up = gather_dot(resid_two, w_gate_up, jnp.float32, 9, gain_rows[4:6])
    gate_up, grad_out_low = lax.optimization_barrier((gate_up, grad_out_low))
    group_grad_out, grad_gate_up, hidden = gather_dot(
        grad_out_low, w_down, None, 10, gate_up=gate_up
    )

    def over_rows(block):
        return lax.psum_scatter(
            block.astype(jnp.bfloat16), "seq", scatter_dimension=0, tiled=True
        ).reshape(group, owned, -1)

    layer_rows, ff_piece = ff_outer(
        grad_gate_up, hidden, w_down, group_three, group_grad_out, resid_two, 12
    )
    ff_piece, grad_gate_up = lax.optimization_barrier((ff_piece, grad_gate_up))
    ff_rows = over_rows(ff_piece)
    grad_two, stats_three = dot_reduce(
        grad_gate_up, w_gate_up, clips, 13, grad_out_low, back=(resid_two, gain_rows[4:5])
    )
    _, grad_cross_query, cond_grad, cross_piece = gather_dot(
        grad_two,
        w_rest,
        None,
        15,
        span=of_cross_out,
        pair=cond_pair,
        bias=cond_bias,
        query=cross_query,
        outer=(group_two, cross_out),
    )
    cond_grad = cond_grad.reshape(clips * cond_count, 2 * head_wide)
    cond_piece = split_outer(cond_flat, cond_grad)
    cond_piece = cond_piece.reshape(group, planes, cond_owned, 2 * head_wide)
    cond_piece = jnp.swapaxes(cond_piece, 0, 1).reshape(wide, head_wide).astype(jnp.bfloat16)
    grad_one, stats_two, _, grad_self_mixed, rest_piece, layer_out, cross_rows = reduce_gather(
        grad_cross_query,
        w_rest,
        clips,
        16,
        grad_two,
        w_rest,
        span=of_cross_query,
        back=(resid_one, gain_rows[2:3]),
        second_span=of_self_out,
        outer=(self_low, cond_piece),
        adding=cross_piece.reshape(planes, group * owned, 2 * head_wide),
        leaving=layer_rows.reshape(clips, planes, piece, wide),
    )
    layer_out = to_whole_order(layer_out.reshape(frame_rows, wide)).astype(jnp.bfloat16)
    layer_out = layer_out.reshape(frames.shape)
    rest_piece, ff_rows = lax.optimization_barrier((rest_piece, ff_rows))
    rest_rows = over_rows(rest_piece)
    grad_project, stamp_grad, ff_owned, qkv_piece = flash_backward(
        rotated,
        self_low,
        grad_self_mixed,
        self_lse,
        stamp_pair,
        key_bias,
        rotary,
        heads,
        ff_rows,
        group_one,
        stamp_normed,
        3,
    )
    grad_stamp_normed = split_times_transposed(stamp_grad, w_qkv[:, head_wide:])
    qkv_rows = over_rows(qkv_piece)
    grad_project, rest_rows = lax.optimization_barrier((grad_project, rest_rows))
    frames_grad, stats_one = dot_reduce(
        grad_project,
        w_qkv,
        clips,
        18,
        grad_one,
        back=(stream, gain_rows[0:1]),
        kind=jnp.bfloat16,
    )
    _, norm_stamp_back = jax.vjp(layer_norm, stamps, gain_rows[0], gain_rows[1])
    _, grad_gain_stamp, grad_bias_stamp = norm_stamp_back(grad_stamp_normed)
    stamp_stats = jnp.stack([grad_gain_stamp, grad_bias_stamp])
    norm_grad = jnp.concatenate([stats_one + stamp_stats, stats_two, stats_three], axis=0)
    norm_parts = norm_grad.reshape(6, planes, group, owned).transpose(2, 1, 0, 3)
    norm_parts = norm_parts.reshape(group * planes, 6, owned)
    norm_parts = jnp.pad(norm_parts, ((0, 0), (0, 2), (0, 128 - owned)))
    ff_squares = jnp.sum(jnp.square(ff_owned.astype(jnp.float32)))
    frames_grad, owned_pieces, norm_sum, total = leave(
        frames_grad.reshape(clips, planes, piece, wide),
        [qkv_rows, cross_rows.reshape(group, owned, -1), rest_rows],
        norm_parts,
        ff_squares.reshape(1, 1),
        20,
    )
    frames_grad = to_whole_order(frames_grad.reshape(frame_rows, wide)).reshape(frames.shape)
    cross_reduced = owned_pieces[2][:, :, head_wide:].reshape(group, cond_owned, 2, head_wide)
    cross_reduced = cross_reduced.transpose(1, 2, 0, 3).reshape(cross_weight.shape)
    cross_reduced = cross_reduced.astype(jnp.float32)
    norm_reduced = norm_sum[:6, :owned]
    grad_norm = jnp.sqrt(total[0, 0])
    factor = jnp.minimum(1.0, clip_limit / grad_norm)
    factor_block = factor.reshape(1, 1)
    attn_new, attn_first_new, attn_second_new = adam_blocks(
        factor_block,
        attn_weight,
        attn_first,
        attn_second,
        owned_pieces,
        [
            (which, block * head_wide, (block + 1) * head_wide)
            for which, block in ((0, 0), (0, 1), (0, 2), (2, 0), (1, 0), (1, 1))
        ],
    )
    cross_new, cross_first_new, cross_second_new = adam_step(
        cross_weight, cross_first, cross_second, cross_reduced * factor, matrix_rate, matrix_decay
    )
    norm_new, norm_first_new, norm_second_new = adam_step(
        norm_param, norm_first, norm_second, norm_reduced * factor, gain_rate, 0.0
    )
    ff_new, ff_first_new, ff_second_new = adam_matrix(
        factor_block, ff_weight, ff_first, ff_second, ff_owned, ff_wide, group // 2
    )
    return (
        layer_out,
        frames_grad,
        grad_norm,
        attn_new,
        cross_new,
        norm_new,
        ff_new,
        attn_first_new,
        cross_first_new,
        norm_first_new,
        ff_first_new,
        attn_second_new,
        cross_second_new,
        norm_second_new,
        ff_second_new,
    )


def solution(mesh):
    return jax.shard_map(
        plane_device if plane_fits(mesh) else per_device,
        mesh=mesh,
        in_specs=(
            P("dp", "seq", None),
            P("dp", None),
            P("dp", None),
            P("dp", None),
            P("dp"),
            P("seq", None),
            P("dp", "seq", None),
            P(("dp", "seq"), None),
            P(("dp", "seq"), None),
            P(None, ("dp", "seq")),
            P(("dp", "seq"), None),
            P(("dp", "seq"), None),
            P(("dp", "seq"), None),
            P(("dp", "seq"), None),
            P(("dp", "seq"), None),
            P(None, ("dp", "seq")),
            P(None, ("dp", "seq")),
            P(("dp", "seq"), None),
            P(("dp", "seq"), None),
        ),
        out_specs=(
            P("dp", "seq", None),
            P("dp", "seq", None),
            P(),
            P(("dp", "seq"), None),
            P(("dp", "seq"), None),
            P(None, ("dp", "seq")),
            P(("dp", "seq"), None),
            P(("dp", "seq"), None),
            P(("dp", "seq"), None),
            P(None, ("dp", "seq")),
            P(("dp", "seq"), None),
            P(("dp", "seq"), None),
            P(("dp", "seq"), None),
            P(None, ("dp", "seq")),
            P(("dp", "seq"), None),
        ),
        check_vma=False,
    )
```

```python
import functools

import jax
import jax.numpy as jnp
import numpy as np
from jax import lax
from jax.experimental import pallas as pl
from jax.experimental.pallas import tpu as pltpu
from jax.sharding import PartitionSpec as P

HEADS = 24
HDIM = 64
FF = 6144
UPDATE_STEP = 10


norm_eps = 1e-05
beta_first = 0.5
beta_second = 0.5
adam_eps = 1e-08
matrix_decay = 0.01
matrix_rate = 0.03
gain_rate = 0.25
clip_limit = 1.0
masked_score = -1e30


def layer_norm(values, gain_row, bias_row):
    center = values - jnp.mean(values, axis=-1, keepdims=True)
    spread = jnp.mean(center * center, axis=-1, keepdims=True)
    return center * lax.rsqrt(spread + norm_eps) * gain_row + bias_row


def rotary_tables(positions, head_size):
    half_size = head_size // 2
    frequency = 10000.0 ** (-jnp.arange(half_size, dtype=jnp.float32) / half_size)
    angles = positions.astype(jnp.float32)[:, None] * frequency[None, :]
    return (jnp.cos(angles)[:, None, :], jnp.sin(angles)[:, None, :])


def rotate(values, cosine_table, sine_table):
    half_size = values.shape[-1] // 2
    first_half = values[..., :half_size]
    second_half = values[..., half_size:]
    return jnp.concatenate(
        [
            first_half * cosine_table - second_half * sine_table,
            second_half * cosine_table + first_half * sine_table,
        ],
        axis=-1,
    )


def outer_sum(left_mat, right_mat):
    return lax.dot_general(
        left_mat, right_mat, (((0,), (0,)), ((), ())), preferred_element_type=jnp.float32
    )


def times_transposed(left_mat, right_mat):
    return lax.dot_general(
        left_mat, right_mat, (((1,), (1,)), ((), ())), preferred_element_type=jnp.float32
    )


def split_parts(values):
    upper = values.astype(jnp.bfloat16)
    lower = (values - upper.astype(jnp.float32)).astype(jnp.bfloat16)
    return (upper, lower)


def split_outer(left_low, right_full):
    upper, lower = split_parts(right_full)
    return outer_sum(left_low, upper) + outer_sum(left_low, lower)


def split_times_transposed(left_full, right_low):
    upper, lower = split_parts(left_full)
    return times_transposed(upper, right_low) + times_transposed(lower, right_low)


def self_scores(queries, keys, stamp_key, keep):
    score_scale = HDIM ** (-0.5)
    frame_part = (
        jnp.einsum("cqhd,ckhd->chqk", queries, keys, preferred_element_type=jnp.float32)
        * score_scale
    )
    frame_part = jnp.where(keep[:, None, None, :], frame_part, masked_score)
    stamp_part = (
        jnp.einsum("cqhd,chd->chq", queries, stamp_key, preferred_element_type=jnp.float32)
        * score_scale
    )
    return (frame_part, stamp_part)


def self_forward(queries, keys, values, stamp_key, stamp_value, keep):
    frame_scores, stamp_scores = self_scores(queries, keys, stamp_key, keep)
    top_score = jnp.maximum(jnp.max(frame_scores, axis=-1), stamp_scores)
    frame_expo = jnp.exp(frame_scores - top_score[..., None])
    stamp_expo = jnp.exp(stamp_scores - top_score)
    denom = jnp.sum(frame_expo, axis=-1) + stamp_expo
    self_lse = top_score + jnp.log(denom)
    frame_prob = (frame_expo / denom[..., None]).astype(jnp.bfloat16)
    stamp_prob = (stamp_expo / denom).astype(jnp.bfloat16)
    mixed = jnp.einsum(
        "chqk,ckhd->cqhd", frame_prob, values, preferred_element_type=jnp.float32
    ) + jnp.einsum("chq,chd->cqhd", stamp_prob, stamp_value, preferred_element_type=jnp.float32)
    return (mixed, self_lse)


def self_backward(queries, keys, values, stamp_key, stamp_value, keep, self_lse, grad_mixed):
    score_scale = HDIM ** (-0.5)
    frame_scores, stamp_scores = self_scores(queries, keys, stamp_key, keep)
    frame_prob = jnp.exp(frame_scores - self_lse[..., None])
    stamp_prob = jnp.exp(stamp_scores - self_lse)
    grad_frame_prob = jnp.einsum(
        "cqhd,ckhd->chqk", grad_mixed, values, preferred_element_type=jnp.float32
    )
    grad_stamp_prob = jnp.einsum(
        "cqhd,chd->chq", grad_mixed, stamp_value, preferred_element_type=jnp.float32
    )
    delta = jnp.sum(frame_prob * grad_frame_prob, axis=-1) + stamp_prob * grad_stamp_prob
    grad_frame_scores = (frame_prob * (grad_frame_prob - delta[..., None])).astype(jnp.bfloat16)
    grad_stamp_scores = (stamp_prob * (grad_stamp_prob - delta)).astype(jnp.bfloat16)
    grad_queries = (
        jnp.einsum("chqk,ckhd->cqhd", grad_frame_scores, keys, preferred_element_type=jnp.float32)
        + jnp.einsum(
            "chq,chd->cqhd", grad_stamp_scores, stamp_key, preferred_element_type=jnp.float32
        )
    ) * score_scale
    key_part = (
        jnp.einsum(
            "chqk,cqhd->ckhd", grad_frame_scores, queries, preferred_element_type=jnp.float32
        )
        * score_scale
    )
    value_part = jnp.einsum(
        "chqk,cqhd->ckhd",
        frame_prob.astype(jnp.bfloat16),
        grad_mixed,
        preferred_element_type=jnp.float32,
    )
    grad_stamp_key = (
        jnp.einsum("chq,cqhd->chd", grad_stamp_scores, queries, preferred_element_type=jnp.float32)
        * score_scale
    )
    grad_stamp_value = jnp.einsum(
        "chq,cqhd->chd",
        stamp_prob.astype(jnp.bfloat16),
        grad_mixed,
        preferred_element_type=jnp.float32,
    )
    return (grad_queries, key_part, value_part, grad_stamp_key, grad_stamp_value)


def cross_scores(query, keys, keep):
    score_scale = HDIM ** (-0.5)
    scores = (
        jnp.einsum("cqhd,ckhd->chqk", query, keys, preferred_element_type=jnp.float32) * score_scale
    )
    return jnp.where(keep[:, None, None, :], scores, masked_score)


def cross_forward(query, keys, values, keep):
    scores = cross_scores(query, keys, keep)
    top_score = jnp.max(scores, axis=-1)
    expo = jnp.exp(scores - top_score[..., None])
    denom = jnp.sum(expo, axis=-1)
    cross_lse = top_score + jnp.log(denom)
    prob = (expo / denom[..., None]).astype(jnp.bfloat16)
    mixed = jnp.einsum("chqk,ckhd->cqhd", prob, values, preferred_element_type=jnp.float32)
    return (mixed, cross_lse)


def cross_backward(query, keys, values, keep, cross_lse, grad_mixed):
    score_scale = HDIM ** (-0.5)
    prob = jnp.exp(cross_scores(query, keys, keep) - cross_lse[..., None])
    grad_prob = jnp.einsum(
        "cqhd,ckhd->chqk", grad_mixed, values, preferred_element_type=jnp.float32
    )
    delta = jnp.sum(prob * grad_prob, axis=-1)
    grad_scores = (prob * (grad_prob - delta[..., None])).astype(jnp.bfloat16)
    grad_query = (
        jnp.einsum("chqk,ckhd->cqhd", grad_scores, keys, preferred_element_type=jnp.float32)
        * score_scale
    )
    grad_keys = (
        jnp.einsum("chqk,cqhd->ckhd", grad_scores, query, preferred_element_type=jnp.float32)
        * score_scale
    )
    grad_values = jnp.einsum(
        "chqk,cqhd->ckhd", prob.astype(jnp.bfloat16), grad_mixed, preferred_element_type=jnp.float32
    )
    return (grad_query, grad_keys, grad_values)


def adam_step(weight, first, second, gradient, step_rate, decay_rate):
    first_new = beta_first * first + (1.0 - beta_first) * gradient
    second_new = beta_second * second + (1.0 - beta_second) * gradient * gradient
    fix_first = 1.0 - beta_first**UPDATE_STEP
    fix_second = 1.0 - beta_second**UPDATE_STEP
    normed_step = first_new / fix_first / (jnp.sqrt(second_new / fix_second) + adam_eps)
    return (weight - step_rate * (normed_step + decay_rate * weight), first_new, second_new)


def per_device(
    frames,
    time_token,
    cond_ids,
    cond_mask,
    lengths,
    cond_table,
    cotangent,
    attn_weight,
    cross_weight,
    norm_param,
    ff_weight,
    attn_first,
    attn_second,
    cross_first,
    cross_second,
    norm_first,
    norm_second,
    ff_first,
    ff_second,
):
    clip_count, frame_rows, wide = frames.shape
    hidden_width = FF
    token_count = clip_count * frame_rows
    seq_count = lax.axis_size("seq")
    seq_frames = frame_rows * seq_count
    seq_place = lax.axis_index("seq")
    vocab_rows = cond_table.shape[0]
    relative = cond_ids - seq_place * vocab_rows
    inside = (relative >= 0) & (relative < vocab_rows)
    picked = jnp.take(cond_table, jnp.clip(relative, 0, vocab_rows - 1), axis=0).astype(jnp.float32)
    picked = jnp.where(inside[..., None], picked, 0.0)
    cond = lax.psum(picked.astype(jnp.bfloat16), "seq")
    cond_count = cond.shape[1]
    cond_flat = cond.reshape(clip_count * cond_count, cond.shape[2])
    cond_width = cond.shape[2]
    cond_keep = cond_mask > 0
    attn_low = attn_weight.astype(jnp.bfloat16)
    cross_low = cross_weight.astype(jnp.bfloat16)
    norm_low = norm_param.astype(jnp.bfloat16)
    ff_low = ff_weight.astype(jnp.bfloat16)
    stream = frames.astype(jnp.float32).reshape(token_count, wide)
    stamps = time_token.astype(jnp.float32)
    positions = seq_place * frame_rows + jnp.arange(frame_rows)
    key_keep = jnp.arange(seq_frames)[None, :] < lengths[:, None]
    frame_valid = (positions[None, :] < lengths[:, None]).reshape(token_count)
    grad_out = cotangent.astype(jnp.float32).reshape(token_count, wide) * frame_valid[
        :, None
    ].astype(jnp.float32)
    grad_out_low = grad_out.astype(jnp.bfloat16)
    piece_heads = HEADS // seq_count
    piece_wide = wide // seq_count
    piece_ff = hidden_width // seq_count
    group_rows = clip_count * seq_frames

    def pieces():
        norm_copies = jnp.tile(norm_low[None], (1, 1, seq_count))
        moved_attn, moved_cross, moved_ff, moved_norm = (
            lax.all_to_all(
                attn_low.reshape(-1, 6, wide), "seq", split_axis=2, concat_axis=0, tiled=True
            ),
            lax.all_to_all(
                cross_low.reshape(-1, 2, wide), "seq", split_axis=2, concat_axis=0, tiled=True
            ),
            lax.all_to_all(
                ff_low.reshape(-1, 3, hidden_width), "seq", split_axis=2, concat_axis=0, tiled=True
            ),
            lax.all_to_all(norm_copies, "seq", split_axis=2, concat_axis=0, tiled=True),
        )
        attn_cols, cross_cols, ff_cols, norm_blocks = (
            lax.all_gather(moved_attn, "dp", axis=0, tiled=True),
            lax.all_gather(moved_cross, "dp", axis=0, tiled=True),
            lax.all_gather(moved_ff, "dp", axis=0, tiled=True),
            lax.all_gather(moved_norm, "dp", axis=0, tiled=True),
        )
        gains = norm_blocks.transpose(1, 0, 2).reshape(6, wide).astype(jnp.float32)
        return (attn_cols, cross_cols, ff_cols, gains)

    def collect(rows):
        whole = lax.all_gather(
            rows.reshape(clip_count, frame_rows, wide), "seq", axis=1, tiled=True
        )
        return whole.reshape(group_rows, wide)

    def spread(partial_value):
        mine = lax.psum_scatter(
            partial_value.reshape(clip_count, seq_frames, wide).astype(jnp.bfloat16),
            "seq",
            scatter_dimension=1,
            tiled=True,
        ).astype(jnp.float32)
        return mine.reshape(token_count, wide)

    attn_cols, cross_cols, ff_cols, gain_rows = pieces()
    group_shape = (clip_count, seq_frames, piece_heads, HDIM)
    cosine_table, sine_table = rotary_tables(jnp.arange(seq_frames), HDIM)
    normed_one = layer_norm(stream, gain_rows[0], gain_rows[1]).astype(jnp.bfloat16)
    group_one = collect(normed_one)
    projected = jnp.dot(
        group_one,
        attn_cols[:, :3].reshape(wide, 3 * piece_wide),
        preferred_element_type=jnp.float32,
    )
    queries = rotate(
        projected[:, :piece_wide].reshape(group_shape), cosine_table, sine_table
    ).astype(jnp.bfloat16)
    all_keys = rotate(
        projected[:, piece_wide : 2 * piece_wide].reshape(group_shape), cosine_table, sine_table
    ).astype(jnp.bfloat16)
    all_values = projected[:, 2 * piece_wide :].astype(jnp.bfloat16).reshape(group_shape)
    stamp_normed = layer_norm(stamps, gain_rows[0], gain_rows[1]).astype(jnp.bfloat16)
    stamp_pair = jnp.dot(
        stamp_normed,
        attn_cols[:, 1:3].reshape(wide, 2 * piece_wide),
        preferred_element_type=jnp.float32,
    )
    stamp_key = (
        stamp_pair[:, :piece_wide].astype(jnp.bfloat16).reshape(clip_count, piece_heads, HDIM)
    )
    stamp_value = (
        stamp_pair[:, piece_wide:].astype(jnp.bfloat16).reshape(clip_count, piece_heads, HDIM)
    )
    self_mixed, self_lse = self_forward(
        queries, all_keys, all_values, stamp_key, stamp_value, key_keep
    )
    self_low = self_mixed.astype(jnp.bfloat16).reshape(group_rows, piece_wide)
    resid_one = stream + spread(times_transposed(self_low, attn_cols[:, 3]))
    normed_two = layer_norm(resid_one, gain_rows[2], gain_rows[3]).astype(jnp.bfloat16)
    group_two = collect(normed_two)
    cross_query = jnp.dot(group_two, attn_cols[:, 4], preferred_element_type=jnp.float32)
    cross_query = cross_query.astype(jnp.bfloat16).reshape(group_shape)
    cond_pair = jnp.dot(
        cond_flat,
        cross_cols.reshape(cond_width, 2 * piece_wide),
        preferred_element_type=jnp.float32,
    )
    cond_shape = (clip_count, cond_count, piece_heads, HDIM)
    cross_keys = cond_pair[:, :piece_wide].astype(jnp.bfloat16).reshape(cond_shape)
    cross_values = cond_pair[:, piece_wide:].astype(jnp.bfloat16).reshape(cond_shape)
    cross_mixed, cross_lse = cross_forward(cross_query, cross_keys, cross_values, cond_keep)
    cross_low_out = cross_mixed.astype(jnp.bfloat16).reshape(group_rows, piece_wide)
    resid_two = resid_one + spread(times_transposed(cross_low_out, attn_cols[:, 5]))
    normed_three = layer_norm(resid_two, gain_rows[4], gain_rows[5]).astype(jnp.bfloat16)
    group_three = collect(normed_three)
    gate_up = jnp.dot(
        group_three, ff_cols[:, :2].reshape(wide, 2 * piece_ff), preferred_element_type=jnp.float32
    )
    gate_val = gate_up[:, :piece_ff]
    up_val = gate_up[:, piece_ff:]
    hidden = (jax.nn.silu(gate_val) * up_val).astype(jnp.bfloat16)
    branch = spread(times_transposed(hidden, ff_cols[:, 2]))
    layer_out = (resid_two + branch).astype(jnp.bfloat16).reshape(clip_count, frame_rows, wide)
    attn_cols, cross_cols, ff_cols, gain_rows = pieces()
    group_grad_out = collect(grad_out_low)
    grad_hidden = jnp.dot(group_grad_out, ff_cols[:, 2], preferred_element_type=jnp.float32)
    sigmoid_gate = jax.nn.sigmoid(gate_val)
    grad_gate = grad_hidden * up_val * sigmoid_gate * (1.0 + gate_val * (1.0 - sigmoid_gate))
    grad_up = grad_hidden * gate_val * sigmoid_gate
    grad_gate_up = jnp.concatenate([grad_gate, grad_up], axis=1).astype(jnp.bfloat16)
    grad_normed_three = spread(
        times_transposed(grad_gate_up, ff_cols[:, :2].reshape(wide, 2 * piece_ff))
    )
    _, norm_three_back = jax.vjp(layer_norm, resid_two, gain_rows[4], gain_rows[5])
    grad_two_part, grad_gain_three, grad_bias_three = norm_three_back(grad_normed_three)
    grad_two = grad_out + grad_two_part
    grad_cross_branch = grad_two.astype(jnp.bfloat16)
    group_cross_branch = collect(grad_cross_branch)
    grad_cross_mixed = jnp.dot(
        group_cross_branch, attn_cols[:, 5], preferred_element_type=jnp.float32
    )
    grad_cross_mixed = grad_cross_mixed.astype(jnp.bfloat16).reshape(group_shape)
    grad_cross_query, grad_cross_keys, grad_cross_values = cross_backward(
        cross_query, cross_keys, cross_values, cond_keep, cross_lse, grad_cross_mixed
    )
    grad_cross_query = grad_cross_query.astype(jnp.bfloat16).reshape(group_rows, piece_wide)
    grad_normed_two = spread(times_transposed(grad_cross_query, attn_cols[:, 4]))
    _, norm_two_back = jax.vjp(layer_norm, resid_one, gain_rows[2], gain_rows[3])
    grad_one_part, grad_gain_two, grad_bias_two = norm_two_back(grad_normed_two)
    grad_one = grad_two + grad_one_part
    grad_self_branch = grad_one.astype(jnp.bfloat16)
    group_self_branch = collect(grad_self_branch)
    grad_self_mixed = jnp.dot(
        group_self_branch, attn_cols[:, 3], preferred_element_type=jnp.float32
    )
    grad_self_mixed = grad_self_mixed.astype(jnp.bfloat16).reshape(group_shape)
    grad_queries, key_part, value_part, grad_stamp_key, grad_stamp_value = self_backward(
        queries, all_keys, all_values, stamp_key, stamp_value, key_keep, self_lse, grad_self_mixed
    )
    grad_query_raw = (
        rotate(grad_queries, cosine_table, -sine_table)
        .astype(jnp.bfloat16)
        .reshape(group_rows, piece_wide)
    )
    grad_key_raw = (
        rotate(key_part, cosine_table, -sine_table)
        .astype(jnp.bfloat16)
        .reshape(group_rows, piece_wide)
    )
    grad_value = value_part.astype(jnp.bfloat16).reshape(group_rows, piece_wide)
    grad_project = jnp.concatenate([grad_query_raw, grad_key_raw, grad_value], axis=1)
    grad_normed_one = spread(
        times_transposed(grad_project, attn_cols[:, :3].reshape(wide, 3 * piece_wide))
    )
    stamp_grad = jnp.concatenate(
        [
            grad_stamp_key.reshape(clip_count, piece_wide),
            grad_stamp_value.reshape(clip_count, piece_wide),
        ],
        axis=1,
    )
    grad_stamp_normed = split_times_transposed(
        stamp_grad, attn_cols[:, 1:3].reshape(wide, 2 * piece_wide)
    )
    _, norm_one_back = jax.vjp(layer_norm, stream, gain_rows[0], gain_rows[1])
    grad_zero_part, grad_gain_one, grad_bias_one = norm_one_back(grad_normed_one)
    _, norm_stamp_back = jax.vjp(layer_norm, stamps, gain_rows[0], gain_rows[1])
    _, grad_gain_stamp, grad_bias_stamp = norm_stamp_back(grad_stamp_normed)
    frames_grad = (grad_one + grad_zero_part).reshape(clip_count, frame_rows, wide)
    project_grad = outer_sum(group_one, grad_project)
    stamp_weight_grad = split_outer(stamp_normed, stamp_grad)
    attn_piece = jnp.stack(
        [
            project_grad[:, :piece_wide],
            project_grad[:, piece_wide : 2 * piece_wide] + stamp_weight_grad[:, :piece_wide],
            project_grad[:, 2 * piece_wide :] + stamp_weight_grad[:, piece_wide:],
            outer_sum(group_self_branch, self_low),
            outer_sum(group_two, grad_cross_query),
            outer_sum(group_cross_branch, cross_low_out),
        ],
        axis=1,
    )
    cond_grad = jnp.concatenate(
        [
            grad_cross_keys.reshape(clip_count * cond_count, piece_wide),
            grad_cross_values.reshape(clip_count * cond_count, piece_wide),
        ],
        axis=1,
    )
    cross_piece = split_outer(cond_flat, cond_grad).reshape(cond_width, 2, piece_wide)
    ff_piece = jnp.stack(
        [
            outer_sum(group_three, grad_gate_up[:, :piece_ff]),
            outer_sum(group_three, grad_gate_up[:, piece_ff:]),
            outer_sum(group_grad_out, hidden),
        ],
        axis=1,
    )
    norm_grad = jnp.stack(
        [
            grad_gain_one + grad_gain_stamp,
            grad_bias_one + grad_bias_stamp,
            grad_gain_two,
            grad_bias_two,
            grad_gain_three,
            grad_bias_three,
        ],
        axis=0,
    )
    norm_column = norm_grad.T[:, :, None]
    summed_attn, summed_cross, summed_ff, summed_norm = (
        lax.psum_scatter(
            attn_piece.astype(jnp.bfloat16), "dp", scatter_dimension=0, tiled=True
        ).astype(jnp.float32),
        lax.psum_scatter(
            cross_piece.astype(jnp.bfloat16), "dp", scatter_dimension=0, tiled=True
        ).astype(jnp.float32),
        lax.psum_scatter(
            ff_piece.astype(jnp.bfloat16), "dp", scatter_dimension=0, tiled=True
        ).astype(jnp.float32),
        lax.psum_scatter(
            norm_column.astype(jnp.bfloat16), "dp", scatter_dimension=0, tiled=True
        ).astype(jnp.float32),
    )
    owned_attn, owned_cross, owned_ff, owned_norm = (
        lax.all_to_all(
            summed_attn.astype(jnp.bfloat16), "seq", split_axis=0, concat_axis=2, tiled=True
        ).astype(summed_attn.dtype),
        lax.all_to_all(
            summed_cross.astype(jnp.bfloat16), "seq", split_axis=0, concat_axis=2, tiled=True
        ).astype(summed_cross.dtype),
        lax.all_to_all(
            summed_ff.astype(jnp.bfloat16), "seq", split_axis=0, concat_axis=2, tiled=True
        ).astype(summed_ff.dtype),
        lax.all_to_all(
            summed_norm.astype(jnp.bfloat16), "seq", split_axis=0, concat_axis=2, tiled=True
        ).astype(summed_norm.dtype),
    )
    attn_reduced = owned_attn.reshape(owned_attn.shape[0], 6 * wide)
    cross_reduced = owned_cross.reshape(owned_cross.shape[0], 2 * wide)
    ff_reduced = owned_ff.reshape(owned_ff.shape[0], 3 * hidden_width)
    norm_reduced = jnp.sum(owned_norm, axis=2).T
    local_squares = (
        jnp.sum(attn_reduced * attn_reduced)
        + jnp.sum(cross_reduced * cross_reduced)
        + jnp.sum(norm_reduced * norm_reduced)
        + jnp.sum(ff_reduced * ff_reduced)
    )
    total_squares = lax.psum(local_squares, ("dp", "seq"))
    grad_norm = jnp.sqrt(total_squares)
    factor = jnp.minimum(1.0, clip_limit / grad_norm)
    attn_new, attn_first_new, attn_second_new = adam_step(
        attn_weight, attn_first, attn_second, attn_reduced * factor, matrix_rate, matrix_decay
    )
    cross_new, cross_first_new, cross_second_new = adam_step(
        cross_weight, cross_first, cross_second, cross_reduced * factor, matrix_rate, matrix_decay
    )
    norm_new, norm_first_new, norm_second_new = adam_step(
        norm_param, norm_first, norm_second, norm_reduced * factor, gain_rate, 0.0
    )
    ff_new, ff_first_new, ff_second_new = adam_step(
        ff_weight, ff_first, ff_second, ff_reduced * factor, matrix_rate, matrix_decay
    )
    return (
        layer_out,
        frames_grad,
        grad_norm,
        attn_new,
        cross_new,
        norm_new,
        ff_new,
        attn_first_new,
        cross_first_new,
        norm_first_new,
        ff_first_new,
        attn_second_new,
        cross_second_new,
        norm_second_new,
        ff_second_new,
    )


MESH = pl.DeviceIdType.MESH
DMA = pltpu.SemaphoreType.DMA
VMEM_LIMIT = 60 * 2**20


def plane_fits(mesh):
    return mesh.shape["dp"] == 8 and mesh.shape["dp"] % mesh.shape["seq"] == 0


def plane_places():
    place = lax.axis_index("dp")
    return (place, lax.axis_index("seq"), lambda mask: jnp.bitwise_xor(place, mask))


def greet(partners):
    barrier = pltpu.get_barrier_semaphore()
    for partner in partners:
        pl.semaphore_signal(barrier, inc=1, device_id=partner, device_id_type=MESH)
    pl.semaphore_wait(barrier, len(partners))


def remote(source, goal, send_sem, recv_sem, device):
    return pltpu.make_async_remote_copy(
        src_ref=source,
        dst_ref=goal,
        send_sem=send_sem,
        recv_sem=recv_sem,
        device_id=device,
        device_id_type=MESH,
    )


def communicating(collective_id):
    return pltpu.CompilerParams(
        has_side_effects=True, collective_id=collective_id, vmem_limit_bytes=VMEM_LIMIT
    )


def any_spec():
    return pl.BlockSpec(memory_space=pl.ANY)


def greet_cross(group, planes):
    place, depth, flip = plane_places()
    greet(
        [(flip(mask), depth) for mask in range(1, group)]
        + [(place, lax.rem(depth + step, planes)) for step in range(1, planes)]
    )


def outward_steps(group, planes, kept_ref, own_ref, mid, *sems):
    far_send, far_recv, near_send, near_recv, local_sem = sems
    place, depth, flip = plane_places()
    per = group // planes
    first = []
    for step in range(1, planes):
        origin = lax.rem(depth + step, planes)
        for slot in range(per):
            clip = per * depth + slot
            copy = remote(
                kept_ref.at[slot, origin],
                mid.at[clip],
                far_send.at[slot, step],
                far_recv.at[clip],
                (place, origin),
            )
            copy.start()
            first.append(copy)
    second = []

    def hand_over(block, clip):
        index = len(second)
        away = remote(
            block, own_ref.at[place], near_send.at[index], near_recv.at[place], (clip, depth)
        )
        stay = pltpu.make_async_copy(block, own_ref.at[place], local_sem.at[index])
        pl.when(clip != place)(away.start)
        pl.when(clip == place)(stay.start)
        second.append((clip, away, stay))

    for slot in range(per):
        hand_over(kept_ref.at[slot, depth], per * depth + slot)
    yield
    for step in range(1, planes):
        source = lax.rem(depth + step, planes)
        for slot in range(per):
            clip = per * source + slot
            block = mid.at[clip]
            remote(
                block, block, far_send.at[0, 0], far_recv.at[clip], (place, source)
            ).wait_recv()
            hand_over(block, clip)
    yield
    for mask in range(1, group):
        other = flip(mask)
        block = own_ref.at[other]
        remote(block, block, near_send.at[0], near_recv.at[other], (other, depth)).wait_recv()
    for clip, away, stay in second:
        pl.when(clip != place)(away.wait_send)
        pl.when(clip == place)(stay.wait)
    for copy in first:
        copy.wait_send()
    yield


def outward_scratch(group, planes):
    return [
        DMA((group // planes, planes)),
        DMA((group,)),
        DMA((group,)),
        DMA((group,)),
        DMA((group,)),
    ]


def settle_body(group, planes, dones, kept_ref, cut_ref, parts_ref, squares_ref, *refs):
    done_refs, refs = refs[:dones], refs[dones:]
    own_ref, mine_ref, norm_ref, total_ref, mid, terms, block, blocks, *sems = refs
    part_send, part_recv, block_send, block_recv, *sems = sems
    place, depth, flip = plane_places()
    devices = [(flip(mask), lax.rem(depth + step, planes)) for mask, step in everyone(planes)]
    greet(devices)
    here = place * planes + depth
    start_swap, end_swap = swap_beside(
        [(lambda other: cut_ref.at[other], lambda other: mine_ref.at[other])], *sems[:3]
    )
    start_swap()
    copies = []
    for index, (other, plane) in enumerate(devices):
        copy = remote(
            parts_ref.at[other * planes + plane],
            terms.at[here],
            part_send.at[index],
            part_recv.at[here],
            (other, plane),
        )
        copy.start()
        copies.append(copy)
    rows = outward_steps(group, planes, kept_ref, own_ref, mid, *sems[3:])
    next(rows)
    terms[here] = parts_ref[here]

    def squares_of(array_ref):
        values = [array_ref[piece].astype(jnp.float32) for piece in range(array_ref.shape[0])]
        return jnp.sum(sum(value * value for value in values))

    squares = squares_ref[0, 0]
    for done_ref in done_refs:
        squares = squares + squares_of(done_ref)
    for other, plane in devices:
        source = other * planes + plane
        one = terms.at[source]
        remote(one, one, part_send.at[0], part_recv.at[source], (other, plane)).wait_recv()
    norm_sum = jnp.sum(terms[...], axis=0)
    norm_ref[...] = norm_sum
    squares = squares + jnp.sum(norm_sum * norm_sum)
    end_swap()
    squares = squares + squares_of(mine_ref)
    block[...] = jnp.full(block.shape, squares)
    blocks[here] = block[...]
    for index, (other, plane) in enumerate(devices):
        copy = remote(
            block, blocks.at[here], block_send.at[index], block_recv.at[here], (other, plane)
        )
        copy.start()
        copies.append(copy)
    next(rows)
    next(rows)
    for other, plane in devices:
        source = other * planes + plane
        one = blocks.at[source]
        remote(one, one, block_send.at[0], block_recv.at[source], (other, plane)).wait_recv()
    total_ref[...] = jnp.sum(blocks[...], axis=0)
    for copy in copies:
        copy.wait_send()


def settle(kept_rows, cut, done, norm_parts, squares, collective_id):
    per, planes, rows, wide = kept_rows.shape
    group = per * planes
    count = norm_parts.shape[0]
    inside = pl.BlockSpec(memory_space=pltpu.VMEM)
    like = lambda shape, array: jax.ShapeDtypeStruct(shape, array.dtype)
    *results, _ = pl.pallas_call(
        functools.partial(settle_body, group, planes, len(done)),
        out_shape=[
            like((group, rows, wide), kept_rows),
            like(cut.shape, cut),
            like(norm_parts.shape[1:], norm_parts),
            like((8, 128), norm_parts),
            like((group, rows, wide), kept_rows),
        ],
        in_specs=[any_spec(), any_spec(), inside, pl.BlockSpec(memory_space=pltpu.SMEM)]
        + [inside] * len(done),
        out_specs=[any_spec()] + [inside] * 3 + [any_spec()],
        scratch_shapes=[
            pltpu.VMEM(norm_parts.shape, jnp.float32),
            pltpu.VMEM((8, 128), jnp.float32),
            pltpu.VMEM((count, 8, 128), jnp.float32),
            DMA((count,)),
            DMA((count,)),
            DMA((count,)),
            DMA((count,)),
        ]
        + swap_beside_scratch(1)
        + outward_scratch(group, planes),
        compiler_params=communicating(collective_id),
    )(kept_rows, cut, norm_parts, squares, *done)
    return results


def everyone(planes):
    return [(mask, step) for mask in range(8) for step in range(planes) if mask or step]


def to_plane_features(values, group, planes):
    width = values.shape[1] // (group * planes)
    starts = [
        (owner * planes + plane) * width for plane in range(planes) for owner in range(group)
    ]
    return jnp.concatenate([values[:, start : start + width] for start in starts], axis=1)


def to_whole_features(values, group, planes):
    width = values.shape[1] // (group * planes)
    starts = [
        (plane * group + owner) * width for owner in range(group) for plane in range(planes)
    ]
    return jnp.concatenate([values[:, start : start + width] for start in starts], axis=1)


def enter_body(
    group,
    planes,
    frames_ref,
    grads_ref,
    valid_ref,
    norm_ref,
    pack_ref,
    attn_ref,
    cross_ref,
    ff_ref,
    kept_ref,
    gains_ref,
    packs_ref,
    first_mine_ref,
    rest_mine_ref,
    ff_low_ref,
    grads_mid_ref,
    mid,
    norms_ref,
    pieces,
    grad_pieces,
    attn_full,
    cross_full,
    first_cut,
    rest_cut,
    ff_full,
    ff_low,
    load_sem,
    near_send,
    near_recv,
    far_send,
    far_recv,
    local_sem,
    norm_send,
    norm_recv,
    swap_send,
    swap_recv,
    stay_sem,
):
    place, depth, flip = plane_places()
    per = group // planes
    low = pieces.dtype
    f32 = jnp.float32
    others = everyone(planes)
    loads = [
        pltpu.make_async_copy(source, goal, load_sem.at[which])
        for which, (source, goal) in enumerate(
            ((attn_ref, attn_full), (cross_ref, cross_full), (ff_ref, ff_full))
        )
    ]
    for copy in loads:
        copy.start()
    own = to_plane_features(frames_ref[...].astype(f32), group, planes).astype(low)
    pieces[...] = own.reshape(pieces.shape)
    greet([(flip(mask), lax.rem(depth + step, planes)) for mask, step in others])
    here = place * planes + depth
    first = []
    for mask in (6, 7, 2, 3, 4, 5, 1):
        other = flip(mask)
        copy = remote(
            pieces.at[other],
            mid.at[place],
            near_send.at[mask],
            near_recv.at[mask],
            (other, depth),
        )
        copy.start()
        first.append((mask, copy))
    small = []
    for index, (mask, step) in enumerate(others):
        copy = remote(
            norm_ref,
            norms_ref.at[here],
            norm_send.at[index],
            norm_recv.at[here],
            (flip(mask), lax.rem(depth + step, planes)),
        )
        copy.start()
        small.append(copy)
    swaps = []

    def swap(which, source, goal):
        for mask in (6, 7, 2, 3, 4, 5, 1):
            other = flip(mask)
            copy = remote(
                source(other),
                goal.at[place],
                swap_send.at[which, mask],
                swap_recv.at[which, mask],
                (other, depth),
            )
            copy.start()
            swaps.append(copy)
        stay = pltpu.make_async_copy(source(place), goal.at[place], stay_sem.at[which])
        stay.start()
        stays.append(stay)

    stays = []
    swap(0, lambda other: pack_ref, packs_ref)
    norms_ref[here] = norm_ref[...]
    loads[0].wait()
    loads[1].wait()
    wide = attn_full.shape[1] // 6
    piece = wide // group
    for device in range(group):
        for block in range(6):
            cut_ref = (first_cut, rest_cut)[block // 3]
            start = block * wide + device * piece
            cut_ref[device, :, block % 3 * piece : (block % 3 + 1) * piece] = attn_full[
                :, start : start + piece
            ].astype(low)
        keys = cross_full[:, device * piece : (device + 1) * piece]
        values = cross_full[:, wide + device * piece : wide + (device + 1) * piece]
        rest_cut[device, :, 3 * piece :] = jnp.concatenate([keys, values], axis=0).astype(low)
    swap(1, lambda other: first_cut.at[other], first_mine_ref)
    swap(2, lambda other: rest_cut.at[other], rest_mine_ref)
    second = []
    arrivals = dict(first)
    for mask in (0, 1, 2, 3, 4, 5, 6, 7):
        source = flip(mask)
        goal, slot = lax.div(source, per), lax.rem(source, per)
        block = pieces.at[place]
        if mask:
            arrivals[mask].wait_recv()
            block = mid.at[source]
        away = remote(
            block,
            kept_ref.at[slot, depth],
            far_send.at[mask],
            far_recv.at[slot, depth],
            (place, goal),
        )
        stay = pltpu.make_async_copy(block, kept_ref.at[slot, depth], local_sem.at[mask])
        pl.when(goal != depth)(away.start)
        pl.when(goal == depth)(stay.start)
        second.append((goal, away, stay))
    grads = to_plane_features(grads_ref[...].astype(f32) * valid_ref[...], group, planes)
    grad_pieces[...] = grads.astype(low).reshape(grad_pieces.shape)
    grads_store = pltpu.make_async_copy(grad_pieces, grads_mid_ref, stay_sem.at[3])
    grads_store.start()
    loads[2].wait()
    tile = ff_full.shape[1] // 24

    def round_tile(index, carry):
        lanes = pl.ds(pl.multiple_of(index * tile, 128), tile)
        ff_low[:, lanes] = ff_full[:, lanes].astype(low)
        return carry

    lax.fori_loop(0, 24, round_tile, 0)
    ff_store = pltpu.make_async_copy(ff_low, ff_low_ref, load_sem.at[3])
    ff_store.start()
    for mask, step in others:
        source = flip(mask) * planes + lax.rem(depth + step, planes)
        block = norms_ref.at[source]
        remote(
            block,
            block,
            norm_send.at[0],
            norm_recv.at[source],
            (flip(mask), lax.rem(depth + step, planes)),
        ).wait_recv()
    width = gains_ref.shape[1] // (group * planes)
    gains_ref[...] = jnp.concatenate(
        [
            norms_ref[owner * planes + plane, :, :width]
            for plane in range(planes)
            for owner in range(group)
        ],
        axis=1,
    )
    for slot in range(per):
        for origin in range(planes):
            block = kept_ref.at[slot, origin]
            pl.when(origin != depth)(
                remote(
                    block,
                    block,
                    far_send.at[0],
                    far_recv.at[slot, origin],
                    (place, lax.rem(depth + 1, planes)),
                ).wait_recv
            )
    ff_store.wait()
    grads_store.wait()
    for copy in swaps:
        copy.wait()
    for stay in stays:
        stay.wait()
    for goal, away, stay in second:
        pl.when(goal != depth)(away.wait_send)
        pl.when(goal == depth)(stay.wait)
    for mask, copy in first:
        copy.wait_send()
    for copy in small:
        copy.wait_send()


def enter(frames, grads, valid, norm_block, pack, attn, cross, ff, planes, collective_id):
    rows, wide = frames.shape
    group = 8
    count = group * planes
    piece = rows // group
    owned = attn.shape[0]
    third = attn.shape[1] // (2 * group)
    rest = third + cross.shape[0] * cross.shape[1] // (owned * group)
    low, f32 = jnp.bfloat16, jnp.float32
    inside = pl.BlockSpec(memory_space=pltpu.VMEM)
    like = jax.ShapeDtypeStruct
    *results, _ = pl.pallas_call(
        functools.partial(enter_body, group, planes),
        out_shape=[
            like((group // planes, planes, piece, wide), low),
            like((norm_block.shape[0], wide), f32),
            like((group,) + pack.shape, f32),
            like((group, owned, third), low),
            like((group, owned, rest), low),
            like(ff.shape, low),
            like((group, piece, wide), low),
            like((group, piece, wide), low),
        ],
        in_specs=[inside] * 4 + [any_spec()] * 4,
        out_specs=[any_spec(), inside] + [any_spec()] * 6,
        scratch_shapes=[
            pltpu.VMEM((count,) + norm_block.shape, f32),
            pltpu.VMEM((group, piece, wide), low),
            pltpu.VMEM((group, piece, wide), low),
            pltpu.VMEM(attn.shape, f32),
            pltpu.VMEM(cross.shape, f32),
            pltpu.VMEM((group, owned, third), low),
            pltpu.VMEM((group, owned, rest), low),
            pltpu.VMEM(ff.shape, f32),
            pltpu.VMEM(ff.shape, low),
            DMA((4,)),
            DMA((group,)),
            DMA((group,)),
            DMA((group,)),
            DMA((group // planes, planes)),
            DMA((group,)),
            DMA((count,)),
            DMA((count,)),
            DMA((4, group)),
            DMA((4, group)),
            DMA((4,)),
        ],
        compiler_params=communicating(collective_id),
    )(frames, grads, valid, norm_block, pack, attn, cross, ff)
    return results


def cond_steps(group, planes, pick_ref, cond_ref, parts, summed, *sems):
    part_send, part_recv, cond_send, cond_recv = sems
    place, depth, flip = plane_places()
    pushes = []
    for step in range(1, planes):
        goal = lax.rem(depth + step, planes)
        copy = remote(
            pick_ref.at[goal],
            parts.at[depth],
            part_send.at[step],
            part_recv.at[depth],
            (place, goal),
        )
        copy.start()
        pushes.append(copy)
    yield
    total = pick_ref[depth].astype(jnp.float32)
    for step in range(1, planes):
        source = lax.rem(depth + step, planes)
        block = parts.at[source]
        remote(
            block, block, part_send.at[0], part_recv.at[source], (place, source)
        ).wait_recv()
        total = total + parts[source].astype(jnp.float32)
    summed[...] = total.astype(summed.dtype)
    cond_ref[place] = total.astype(summed.dtype)
    for mask in range(1, group):
        copy = remote(
            summed,
            cond_ref.at[place],
            cond_send.at[mask],
            cond_recv.at[mask],
            (flip(mask), depth),
        )
        copy.start()
        pushes.append(copy)
    yield
    for mask in range(1, group):
        block = cond_ref.at[flip(mask)]
        remote(
            block, block, cond_send.at[0], cond_recv.at[mask], (flip(mask), depth)
        ).wait_recv()
    for copy in pushes:
        copy.wait_send()
    yield


def inward_over(group, planes, mid_ref, kept_ref, send_sem, recv_sem, local_sem):
    place, depth, flip = plane_places()
    per = group // planes

    def piece(source):
        goal, slot = lax.div(source, per), lax.rem(source, per)
        block = mid_ref.at[source]
        away = remote(
            block,
            kept_ref.at[slot, depth],
            send_sem.at[source],
            recv_sem.at[slot, depth],
            (place, goal),
        )
        stay = pltpu.make_async_copy(block, kept_ref.at[slot, depth], local_sem.at[source])
        return goal != depth, away, stay

    def begin():
        for source in range(group):
            leaves, away, stay = piece(source)
            pl.when(leaves)(away.start)
            pl.when(jnp.logical_not(leaves))(stay.start)

    def end():
        for slot in range(per):
            for origin in range(planes):
                block = kept_ref.at[slot, origin]
                pl.when(origin != depth)(
                    remote(
                        block,
                        block,
                        send_sem.at[0],
                        recv_sem.at[slot, origin],
                        (place, lax.rem(depth + 1, planes)),
                    ).wait_recv
                )
        for source in range(group):
            leaves, away, stay = piece(source)
            pl.when(leaves)(away.wait_send)
            pl.when(jnp.logical_not(leaves))(stay.wait)

    return begin, end


def dot_tiles(left, right_ref, span, transposed, width):
    first, last = span
    count = right_ref.shape[0] if transposed else last - first
    for start in range(0, count, width):
        stop = min(start + width, count)
        if transposed:
            yield start, stop, times_transposed(left, right_ref[start:stop, first:last])
        else:
            yield start, stop, jnp.dot(
                left, right_ref[:, first + start : first + stop], preferred_element_type=jnp.float32
            )


def window_of(matrix, span):
    first, last = span or (0, matrix.shape[1])
    start = first // 128 * 128
    while (matrix.shape[1] - start) * 2 > matrix.shape[1] and start and start % 384:
        start -= 128
    stop = min(-(-last // 128) * 128, matrix.shape[1])
    return (start, stop - start), (first - start, last - start)


def cross_shares(queries, pair_ref, bias_ref):
    wide = queries[0].shape[1]
    keys = [
        (clip, start, pair_ref[clip, :, start : start + HDIM])
        for clip in range(len(queries))
        for start in range(0, wide, HDIM)
    ]
    scores = [
        times_transposed(queries[clip][:, start : start + HDIM], key) * HDIM ** (-0.5)
        + bias_ref[clip]
        for clip, start, key in keys
    ]
    tops = [jnp.max(score, axis=1, keepdims=True) for score in scores]
    expos = [jnp.exp(score - top) for score, top in zip(scores, tops)]
    sums = [jnp.sum(expo, axis=1, keepdims=True) for expo in expos]
    return keys, [expo / total for expo, total in zip(expos, sums)]


def by_clip_of(results, clips, low):
    heads = len(results) // clips
    return [
        jnp.concatenate(results[clip * heads : (clip + 1) * heads], axis=1).astype(low)
        for clip in range(clips)
    ]


def cross_rows(queries, pair_ref, bias_ref):
    low, wide = queries[0].dtype, queries[0].shape[1]
    keys, shares = cross_shares(queries, pair_ref, bias_ref)
    mixed = [
        jnp.dot(
            share.astype(low),
            pair_ref[clip, :, wide + start : wide + start + HDIM],
            preferred_element_type=jnp.float32,
        )
        for (clip, start, _), share in zip(keys, shares)
    ]
    return by_clip_of(mixed, len(queries), low)


def cross_rows_back(queries, grads, pair_ref, bias_ref, pair_grad_ref):
    low, wide = queries[0].dtype, queries[0].shape[1]
    scale = HDIM ** (-0.5)
    keys, shares = cross_shares(queries, pair_ref, bias_ref)
    own_grads = [grads[clip][:, start : start + HDIM] for clip, start, _ in keys]
    grad_shares = [
        times_transposed(grad, pair_ref[clip, :, wide + start : wide + start + HDIM])
        for (clip, start, _), grad in zip(keys, own_grads)
    ]
    deltas = [
        jnp.sum(share * grad_share, axis=1, keepdims=True)
        for share, grad_share in zip(shares, grad_shares)
    ]
    scores = [
        (share * (grad_share - delta)).astype(low)
        for share, grad_share, delta in zip(shares, grad_shares, deltas)
    ]
    results = [
        jnp.dot(score, key, preferred_element_type=jnp.float32) * scale
        for score, (_, _, key) in zip(scores, keys)
    ]
    key_grads = [
        outer_sum(score, queries[clip][:, start : start + HDIM]) * scale
        for score, (clip, start, _) in zip(scores, keys)
    ]
    value_grads = [
        outer_sum(share.astype(low), grad) for share, grad in zip(shares, own_grads)
    ]
    heads = len(keys) // len(queries)
    for clip in range(len(queries)):
        mine = slice(clip * heads, (clip + 1) * heads)
        pair_grad_ref[clip] += jnp.concatenate(key_grads[mine] + value_grads[mine], axis=1)
    return by_clip_of(results, len(queries), low)


def outer_columns(out_ref, start, small, big):
    width = small.shape[-1]
    product = outer_sum(small.reshape(-1, width), big.reshape(-1, big.shape[-1]))
    out_ref[:, start : start + width] = product.T.astype(out_ref.dtype)


def by_slot_loads(source, goal, sem):
    clips = source.shape[0]
    return [
        pltpu.make_async_copy(source.at[clip, slot], goal.at[slot, clip], sem.at[slot, clip])
        for slot in range(8)
        for clip in range(clips)
    ]


def gather_parts(clips, rows, sub, mode, window, span, ins, outs_refs, scratch):
    ins, outs_refs, scratch = list(ins), list(outs_refs), list(scratch)
    mat_ref = ins.pop(0) if mode != "rows" else None
    gates_ref = ins.pop(0) if mode == "gates" else None
    pair_ref, bias_ref = (ins.pop(0), ins.pop(0)) if mode in ("cross", "cross_back") else (None, None)
    query_ref = ins.pop(0) if mode == "cross_back" else None
    all_ref = outs_refs.pop(0)
    pair_grad_ref = outs_refs.pop() if mode == "cross_back" else None
    prod_refs = outs_refs
    take = lambda count: [scratch.pop(0) for _ in range(count)]
    held, send_sem, recv_sem, all_sem = take(4)
    mat, mat_sem = take(2) if mode != "rows" else (None, None)
    stages = take(len(prod_refs))
    prod_sem = take(1)[0] if prod_refs else None
    gates, gates_sem = take(2) if mode == "gates" else (None, None)
    queries, query_sem = take(2) if mode == "cross_back" else (None, None)
    place, depth, flip = plane_places()
    core, beside_x, beside_y, across = flip(1), flip(2), flip(4), flip(6)
    loads = []
    gate_loads = {}
    if mode != "rows":
        loads.append(pltpu.make_async_copy(mat_ref.at[:, pl.ds(*window)], mat, mat_sem))
    if mode == "cross_back":
        loads.append(pltpu.make_async_copy(query_ref, queries, query_sem))
    if mode == "gates":
        for mask in (0, 1, 2, 4, 3, 5, 6, 7):
            slot = flip(mask)
            gate_loads[mask] = [
                pltpu.make_async_copy(
                    gates_ref.at[clip, slot], gates.at[slot, clip], gates_sem.at[slot, clip]
                )
                for clip in range(clips)
            ]

    def load():
        if mode == "cross_back":
            pair_grad_ref[...] = jnp.zeros_like(pair_grad_ref)
        for copy in loads + [copy for copies in gate_loads.values() for copy in copies]:
            copy.start()

    chunks = [(clip, part) for clip in range(clips) for part in range(rows // sub)]
    count = len(chunks)
    half = count // 2
    sends = []

    def view(slot, index):
        clip, part = chunks[index]
        return held.at[slot, clip, pl.ds(part * sub, sub)]

    def send(slot, index, device):
        block = view(slot, index)
        copy = remote(
            block, block, send_sem.at[len(sends)], recv_sem.at[slot, index], (device, depth)
        )
        copy.start()
        sends.append(copy)

    def arrived(slot, index):
        block = view(slot, index)
        remote(
            block, block, send_sem.at[0], recv_sem.at[slot, index], (core, depth)
        ).wait_recv()

    x_order = list(range(count))
    y_order = list(range(half, count)) + list(range(half))

    def put(index, values):
        clip, part = chunks[index]
        held[place, clip, pl.ds(part * sub, sub)] = values.astype(held.dtype)
        if index < half:
            send(place, index, beside_x)
        else:
            send(place, index, beside_y)
        send(place, index, core)
        if index == count - 1:
            for low in range(half):
                send(place, half + low, beside_x)
                send(place, low, beside_y)

    outs = []

    def leave_here(source, goal, sem, major):
        for clip in range(clips):
            there = goal.at[major, clip] if goal.shape[0] == 8 else goal.at[clip, major]
            copy = pltpu.make_async_copy(source.at[major, clip], there, sem.at[major, clip])
            copy.start()
            outs.append(copy)

    def multiply(mask):
        slot = flip(mask)
        leave_here(held, all_ref, all_sem, slot)
        if mode == "rows":
            return
        left = held[slot].reshape(clips * rows, held.shape[3])
        for copy in gate_loads.get(mask, ()):
            copy.wait()
        for start, stop, product in dot_tiles(
            left, mat, span, False, 256 * (1 if mode == "gates" else 3)
        ):
            product = product.reshape(clips, rows, stop - start)
            if mode == "cross":
                query = product.astype(stages[0].dtype)
                stages[0][slot] = query
                mixed = cross_rows([query[clip] for clip in range(clips)], pair_ref, bias_ref)
                for clip in range(clips):
                    stages[1][slot, clip] = mixed[clip]
                continue
            if mode == "cross_back":
                grad = product.astype(stages[0].dtype)
                results = cross_rows_back(
                    [queries[clip, slot] for clip in range(clips)],
                    [grad[clip] for clip in range(clips)],
                    pair_ref,
                    bias_ref,
                    pair_grad_ref,
                )
                for clip in range(clips):
                    stages[0][slot, clip] = results[clip]
                continue
            if mode == "dot":
                stages[0][slot, :, :, start:stop] = product.astype(stages[0].dtype)
                continue
            width = stages[1].shape[3]
            gate = gates[slot, :, :, start:stop]
            up = gates[slot, :, :, width + start : width + stop]
            sigmoid = jax.nn.sigmoid(gate)
            active = gate * sigmoid
            low = stages[0].dtype
            stages[0][slot, :, :, start:stop] = (
                product * up * sigmoid * (1.0 + gate * (1.0 - sigmoid))
            ).astype(low)
            stages[0][slot, :, :, width + start : width + stop] = (product * active).astype(low)
            stages[1][slot, :, :, start:stop] = (active * up).astype(low)
        for which, (stage, prod_ref) in enumerate(zip(stages, prod_refs)):
            leave_here(stage, prod_ref, prod_sem.at[which], slot)

    def run(late=lambda: None):
        for copy in loads:
            copy.wait()
        multiply(0)
        for step in range(count):
            x_index, y_index = x_order[step], y_order[step]
            arrived(beside_x, x_index)
            if x_index < half:
                send(beside_x, x_index, beside_y)
            send(beside_x, x_index, core)
            arrived(beside_y, y_index)
            if y_index >= half:
                send(beside_y, y_index, beside_x)
            send(beside_y, y_index, core)
            if step == 0:
                for index in range(count):
                    arrived(core, index)
                multiply(1)
        late()
        multiply(2)
        for step in range(half):
            for index in (x_order[step], y_order[step]):
                arrived(across, index)
                send(across, index, core)
            if step == 0:
                multiply(4)
        for mask in (3, 5):
            for index in range(count):
                arrived(flip(mask), index)
            multiply(mask)
        multiply(6)
        for index in range(count):
            arrived(flip(7), index)
        multiply(7)
        for copy in outs:
            copy.wait()
        for copy in sends:
            copy.wait_send()

    return load, put, run


def chunk_order(clips, rows, sub):
    half = clips * (rows // sub) // 2
    return [index for low in range(half) for index in (low, half + low)]


def gather_plan(clips, rows, wide, sub, matrix, kind, gate_up, span, pair, bias, query):
    count = clips * (rows // sub)
    low = jnp.bfloat16
    inside = pl.BlockSpec(memory_space=pltpu.VMEM)
    by_clip = lambda columns, of: jax.ShapeDtypeStruct((clips, 8, rows, columns), of)
    by_device = lambda columns, of: jax.ShapeDtypeStruct((8, clips, rows, columns), of)
    mode = "rows" if matrix is None else "dot"
    if gate_up is not None:
        mode = "gates"
    if pair is not None:
        mode = "cross" if query is None else "cross_back"
    window = inner = None
    args, in_specs = [], []
    outs = [by_device(wide, low) if mode == "gates" else by_clip(wide, low)]
    scratch = [
        pltpu.VMEM((8, clips, rows, wide), low),
        DMA((7 * count,)),
        DMA((8, count)),
        DMA((8, clips)),
    ]
    if mode != "rows":
        window, inner = window_of(matrix, span)
        columns = inner[1] - inner[0]
        args.append(matrix)
        in_specs.append(any_spec())
        scratch += [pltpu.VMEM((wide, window[1]), low), DMA(())]
    if mode == "dot":
        outs.append(by_clip(columns, kind))
        scratch += [pltpu.VMEM((8, clips, rows, columns), kind), DMA((1, 8, clips))]
    if mode == "gates":
        args.append(gate_up.reshape(clips, 8, rows, 2 * columns))
        in_specs.append(any_spec())
        outs += [by_clip(2 * columns, low), by_device(columns, low)]
        scratch += [
            pltpu.VMEM((8, clips, rows, 2 * columns), low),
            pltpu.VMEM((8, clips, rows, columns), low),
            DMA((2, 8, clips)),
            pltpu.VMEM((8, clips, rows, 2 * columns), jnp.float32),
            DMA((8, clips)),
        ]
    if mode == "cross":
        args += [pair, bias]
        in_specs += [inside] * 2
        outs += [by_clip(columns, low)] * 2
        scratch += [pltpu.VMEM((8, clips, rows, columns), low)] * 2 + [DMA((2, 8, clips))]
    out_specs = [any_spec()] * len(outs)
    if mode == "cross_back":
        args += [pair, bias, query.reshape(clips, 8, rows, columns)]
        in_specs += [inside, inside, any_spec()]
        outs += [by_clip(columns, low), jax.ShapeDtypeStruct(pair.shape, jnp.float32)]
        out_specs += [any_spec(), inside]
        scratch += [
            pltpu.VMEM((8, clips, rows, columns), low),
            DMA((1, 8, clips)),
            pltpu.VMEM((clips, 8, rows, columns), low),
            DMA(()),
        ]
    return (mode, window, inner), args, in_specs, outs, out_specs, scratch


def flat_rows(results):
    return [
        block.reshape(-1, block.shape[3]) if len(block.shape) == 4 else block for block in results
    ]


def gather_dot_body(clips, rows, sub, normed, plan, beside, outer, counts, own_ref, *refs):
    refs = list(refs)
    take = lambda count: [refs.pop(0) for _ in range(count)]
    gain_ref = take(1)[0] if normed else None
    ins = take(counts[0])
    pick_ref = take(1)[0] if beside else None
    past_ref, mixed_ref = take(2) if outer else (None, None)
    outs = take(counts[1])
    cond_ref = take(1)[0] if beside else None
    outer_ref = take(1)[0] if outer else None
    scratch = take(counts[2])
    load, put, run = gather_parts(clips, rows, sub, *plan, ins, outs, scratch)
    load()
    if outer:
        past, mixed, past_sem, mixed_sem = refs
        outer_loads = by_slot_loads(past_ref, past, past_sem)
        outer_loads += by_slot_loads(mixed_ref, mixed, mixed_sem)
        for copy in outer_loads:
            copy.start()
    place, depth, flip = plane_places()
    if beside:
        greet_cross(*beside)
        cond = cond_steps(*beside, pick_ref, cond_ref, *refs)
        next(cond)
    else:
        greet([(flip(1), depth), (flip(2), depth), (flip(4), depth)])
    for index in chunk_order(clips, rows, sub):
        clip, part = divmod(index, rows // sub)
        values = own_ref[clip, pl.ds(part * sub, sub)]
        if normed:
            values = layer_norm(values.astype(jnp.float32), gain_ref[0:1], gain_ref[1:2])
        put(index, values)
    if beside:
        run(lambda: next(cond))
        next(cond)
    else:
        run()
    if outer:
        for copy in outer_loads:
            copy.wait()
        held, queries = scratch[0], scratch[6]
        outer_columns(outer_ref, 0, queries[...], past[...])
        outer_columns(outer_ref, queries.shape[3], mixed[...], held[...])


def gather_dot(
    own_rows,
    matrix,
    kind,
    collective_id,
    gains=None,
    picked=None,
    gate_up=None,
    span=None,
    pair=None,
    bias=None,
    query=None,
    outer=None,
    sub=64,
):
    clips, rows, wide = own_rows.shape
    plan, args, in_specs, outs, out_specs, scratch = gather_plan(
        clips, rows, wide, sub, matrix, kind, gate_up, span, pair, bias, query
    )
    inside = pl.BlockSpec(memory_space=pltpu.VMEM)
    counts = (len(args), len(outs), len(scratch))
    if gains is not None:
        args, in_specs = [gains] + args, [inside] + in_specs
    args, in_specs = [own_rows] + args, [inside] + in_specs
    beside = None
    if picked is not None:
        planes, per, tokens, cond_wide = picked.shape
        beside = (planes * per, planes)
        args.append(picked)
        in_specs.append(inside)
        outs.append(jax.ShapeDtypeStruct((8, per, tokens, cond_wide), picked.dtype))
        out_specs.append(inside)
        scratch += [
            pltpu.VMEM(picked.shape, picked.dtype),
            pltpu.VMEM(picked.shape[1:], picked.dtype),
            DMA((planes,)),
            DMA((planes,)),
            DMA((8,)),
            DMA((8,)),
        ]
    if outer is not None:
        past, mixed = outer
        width = mixed.shape[1]
        args += [past.reshape(clips, 8, rows, wide), mixed.reshape(clips, 8, rows, width)]
        in_specs += [any_spec()] * 2
        outs.append(jax.ShapeDtypeStruct((wide, 2 * width), jnp.bfloat16))
        out_specs.append(inside)
        scratch += [
            pltpu.VMEM((8, clips, rows, wide), jnp.bfloat16),
            pltpu.VMEM((8, clips, rows, width), jnp.bfloat16),
            DMA((8, clips)),
            DMA((8, clips)),
        ]
    results = pl.pallas_call(
        functools.partial(
            gather_dot_body,
            clips,
            rows,
            sub,
            gains is not None,
            plan,
            beside,
            outer is not None,
            counts,
        ),
        out_shape=outs,
        in_specs=in_specs,
        out_specs=out_specs,
        scratch_shapes=scratch,
        compiler_params=communicating(collective_id),
    )(*args)
    return flat_rows(results[: counts[1]]) + list(results[counts[1] :])


def reduce_steps(clips, rows, sub, multiply, final, terms, pair, turn, from_x, from_y, *sems):
    send_sem, core_sem, turn_sem, x_sem, y_sem = sems
    place, depth, flip = plane_places()
    core, beside_x, beside_y = flip(1), flip(2), flip(4)
    chunks = [(clip, part) for clip in range(clips) for part in range(rows // sub)]
    count = len(chunks)
    half = count // 2
    sends = []

    def send(source, goal, recv_sem, device):
        copy = remote(source, goal, send_sem.at[len(sends)], recv_sem, (device, depth))
        copy.start()
        sends.append(copy)

    def arrived(block, recv_sem):
        remote(block, block, send_sem.at[0], recv_sem, (core, depth)).wait_recv()

    def term(number, index):
        clip, part = chunks[index]
        return terms.at[number, clip, pl.ds(part * sub, sub)]

    def give(number, chip):
        for index in range(count):
            send(term(number, index), pair.at[index, chip], core_sem.at[index, chip], core)

    def total(*blocks):
        return sum(block[...].astype(jnp.float32) for block in blocks)

    def add(block, other):
        block[...] = total(block, other).astype(terms.dtype)

    numbers = {3: 1, 1: 3, 2: 5, 0: 7}

    def combine(chip, index):
        arrived(pair.at[index, chip], core_sem.at[index, chip])
        block = term(numbers[chip], index)
        add(block, pair.at[index, chip])
        return block

    multiply(0)
    give(0, 3)
    multiply(1)
    multiply(2)
    give(2, 1)
    for low in range(half):
        high = half + low
        send(combine(3, low), turn.at[low], turn_sem.at[low], beside_x)
        send(combine(3, high), turn.at[high], turn_sem.at[high], beside_y)
    multiply(3)
    multiply(4)
    give(4, 2)
    for low in range(half):
        send(combine(1, low), from_x.at[low], x_sem.at[low], beside_x)
    multiply(5)
    for high in range(half, count):
        send(combine(2, high), from_y.at[high], y_sem.at[high], beside_y)
    multiply(6)
    give(6, 0)
    multiply(7)
    yield
    for low in range(half):
        high = half + low
        block = combine(2, low)
        arrived(turn.at[low], turn_sem.at[low])
        add(block, turn.at[low])
        send(block, from_y.at[low], y_sem.at[low], beside_y)
        block = combine(1, high)
        arrived(turn.at[high], turn_sem.at[high])
        add(block, turn.at[high])
        send(block, from_x.at[high], x_sem.at[high], beside_x)
    yield
    for index in chunk_order(clips, rows, sub):
        clip, part = chunks[index]
        arrived(pair.at[index, 0], core_sem.at[index, 0])
        arrived(from_x.at[index], x_sem.at[index])
        arrived(from_y.at[index], y_sem.at[index])
        result = total(term(7, index), pair.at[index, 0], from_x.at[index], from_y.at[index])
        final(index, clip, pl.ds(part * sub, sub), result)
    yield
    for copy in sends:
        copy.wait_send()
    yield


def plane_order():
    place, depth, flip = plane_places()
    return [flip(mask) for mask in (7, 6, 3, 2, 5, 4, 1, 0)]


def reduce_scratch(clips, rows, sub, wide):
    count = clips * (rows // sub)
    low = jnp.bfloat16
    return [
        pltpu.VMEM((8, clips, rows, wide), low),
        pltpu.VMEM((count, 4, sub, wide), low),
        pltpu.VMEM((count, sub, wide), low),
        pltpu.VMEM((count, sub, wide), low),
        pltpu.VMEM((count, sub, wide), low),
        DMA((7 * count,)),
        DMA((count, 4)),
        DMA((count,)),
        DMA((count,)),
        DMA((count,)),
    ]


def norm_back(values, gain, grad):
    center = values - jnp.mean(values, axis=1, keepdims=True)
    inverse = lax.rsqrt(jnp.mean(center * center, axis=1, keepdims=True) + norm_eps)
    unit = center * inverse
    stats = [
        jnp.sum(grad * unit, axis=0, keepdims=True),
        jnp.sum(grad, axis=0, keepdims=True),
    ]
    scaled = grad * gain
    result = inverse * (
        scaled
        - jnp.mean(scaled, axis=1, keepdims=True)
        - unit * jnp.mean(scaled * unit, axis=1, keepdims=True)
    )
    return result, stats


def final_back(values_ref, gain_ref, base_ref, sum_ref, stats_ref, order=None):
    def final(index, clip, span, result):
        if values_ref is not None:
            result, stats = norm_back(values_ref[clip, span], gain_ref[...], result)
            for which, row in enumerate(stats):
                row = row + stats_ref[which : which + 1] if index else row
                stats_ref[which : which + 1] = row
        result = base_ref[clip, span].astype(jnp.float32) + result
        if order:
            result = to_whole_features(result, *order)
        sum_ref[clip, span] = result.astype(sum_ref.dtype)
        return result

    return final


def terms_of(clips, rows, blocks, mat, span, terms):
    def multiply(number):
        block = blocks(number)
        block = block.reshape(clips * rows, block.shape[-1])
        for start, stop, product in dot_tiles(block, mat, span, True, 256 * 2):
            terms[number, :, :, start:stop] = product.astype(terms.dtype).reshape(
                clips, rows, stop - start
            )

    return multiply


def dot_reduce_body(clips, rows, sub, window, span, back, order, swapped, left_ref, mat_ref, base_ref, *refs):
    refs = list(refs)
    take = lambda count: [refs.pop(0) for _ in range(count)]
    values_ref, gain_ref = take(2) if back else (None, None)
    cut_ref = take(1)[0] if swapped else None
    sum_ref = take(1)[0]
    stats_ref = take(1)[0] if back else None
    mine_ref = take(1)[0] if swapped else None
    left, mat, mat_sem, left_sem = take(4)
    swap_sems = take(3) if swapped else None
    terms = refs[0]
    place, depth, flip = plane_places()
    load = pltpu.make_async_copy(mat_ref.at[:, pl.ds(*window)], mat, mat_sem)
    load.start()
    loads = {}
    for number, slot in enumerate(plane_order()):
        loads[number] = [
            pltpu.make_async_copy(
                left_ref.at[clip, slot], left.at[number, clip], left_sem.at[number, clip]
            )
            for clip in range(clips)
        ]
        for copy in loads[number]:
            copy.start()
    if swapped:
        start_swap, end_swap = swap_beside(
            [(lambda other: cut_ref.at[other], lambda other: mine_ref.at[other])], *swap_sems
        )
        greet([(flip(mask), depth) for mask in range(1, 8)])
        start_swap()
    else:
        greet([(flip(1), depth), (flip(2), depth), (flip(4), depth)])
    load.wait()

    def blocks(number):
        for copy in loads[number]:
            copy.wait()
        return left[number]

    steps = reduce_steps(
        clips,
        rows,
        sub,
        terms_of(clips, rows, blocks, mat, span, terms),
        final_back(values_ref, gain_ref, base_ref, sum_ref, stats_ref, order),
        *refs,
    )
    for _ in steps:
        pass
    if swapped:
        end_swap()


def dot_reduce(
    left,
    matrix,
    clips,
    collective_id,
    base,
    span=None,
    back=None,
    kind=jnp.float32,
    order=None,
    cut=None,
    sub=64,
):
    wide = matrix.shape[0]
    rows, inner = left.shape[0] // (8 * clips), left.shape[1]
    low = jnp.bfloat16
    window, span = window_of(matrix, span)
    inside = pl.BlockSpec(memory_space=pltpu.VMEM)
    args = [left.reshape(clips, 8, rows, inner), matrix, base]
    in_specs = [any_spec(), any_spec(), inside]
    outs, out_specs = [jax.ShapeDtypeStruct((clips, rows, wide), kind)], [inside]
    if back is not None:
        args += list(back)
        in_specs += [inside] * 2
        outs.append(jax.ShapeDtypeStruct((2, wide), jnp.float32))
        out_specs.append(inside)
    swap_sems = []
    if cut is not None:
        args.append(cut)
        in_specs.append(any_spec())
        outs.append(jax.ShapeDtypeStruct(cut.shape, cut.dtype))
        out_specs.append(any_spec())
        swap_sems = swap_beside_scratch(1)
    return pl.pallas_call(
        functools.partial(
            dot_reduce_body,
            clips,
            rows,
            sub,
            window,
            span,
            back is not None,
            order,
            cut is not None,
        ),
        out_shape=outs,
        in_specs=in_specs,
        out_specs=out_specs,
        scratch_shapes=[
            pltpu.VMEM((8, clips, rows, inner), low),
            pltpu.VMEM((wide, window[1]), low),
            DMA(()),
            DMA((8, clips)),
        ]
        + swap_sems
        + reduce_scratch(clips, rows, sub, wide),
        compiler_params=communicating(collective_id),
    )(*args)


def add_steps(parts_ref, sum_ref, landed, send_sem, recv_sem, local_sem):
    place, depth, flip = plane_places()
    planes = parts_ref.shape[0]
    copies = []
    for step in range(1, planes):
        goal = lax.rem(depth + step, planes)
        copy = remote(
            parts_ref.at[goal],
            landed.at[depth],
            send_sem.at[step],
            recv_sem.at[depth],
            (place, goal),
        )
        copy.start()
        copies.append(copy)
    stay = pltpu.make_async_copy(parts_ref.at[depth], landed.at[depth], local_sem)
    stay.start()
    yield
    stay.wait()
    for step in range(1, planes):
        source = lax.rem(depth + step, planes)
        block = landed.at[source]
        remote(block, block, send_sem.at[0], recv_sem.at[source], (place, source)).wait_recv()
    sum_ref[...] = jnp.sum(landed[...].astype(jnp.float32), axis=0).astype(sum_ref.dtype)
    for copy in copies:
        copy.wait_send()
    yield


def reduce_gather_body(
    clips, rows, sub, spans, back, normed, plan, counts, passing, outer, leaving, adding, left_ref, mat_ref, base_ref, *refs
):
    refs = list(refs)
    take = lambda count: [refs.pop(0) for _ in range(count)]
    values_ref, back_gain_ref = take(2) if back else (None, None)
    gain_ref = take(1)[0] if normed else None
    ins = take(counts[0])
    mid_ref = take(1)[0] if passing else None
    low_ref, ending_ref = take(2) if outer else (None, None)
    leaving_ref = take(1)[0] if leaving else None
    adding_ref = take(1)[0] if adding else None
    sum_ref = take(1)[0]
    stats_ref = take(1)[0] if back else None
    outs = take(counts[1])
    kept_ref = take(1)[0] if passing else None
    outer_ref = take(1)[0] if outer else None
    own_ref, own_mid = take(2) if leaving else (None, None)
    added_ref = take(1)[0] if adding else None
    left, mat, mat_sem, left_sem = take(4)
    terms, *others = reduce_refs = take(10)
    gather_scratch = take(counts[2])
    load, put, run = gather_parts(clips, rows, sub, *plan, ins, outs, gather_scratch)
    window, span = spans
    place, depth, flip = plane_places()
    mat_load = pltpu.make_async_copy(mat_ref.at[:, pl.ds(*window)], mat, mat_sem)
    mat_load.start()
    loads = {}
    for number, slot in enumerate(plane_order()):
        loads[number] = [
            pltpu.make_async_copy(
                left_ref.at[clip, slot], left.at[number, clip], left_sem.at[number, clip]
            )
            for clip in range(clips)
        ]
        for copy in loads[number]:
            copy.start()
    load()
    if outer:
        low, low_sem = take(2)
        outer_loads = by_slot_loads(low_ref, low, low_sem)
        for copy in outer_loads:
            copy.start()
    if adding:
        adder = add_steps(adding_ref, added_ref, *take(4))
    if passing:
        greet_cross(*passing)
        pass_rows, end_rows = inward_over(*passing, mid_ref, kept_ref, *refs)
        pass_rows()
    elif leaving:
        greet_cross(*leaving)
        going = outward_steps(*leaving, leaving_ref, own_ref, own_mid, *refs)
        next(going)
    else:
        greet([(flip(1), depth), (flip(2), depth), (flip(4), depth)])
    mat_load.wait()

    def blocks(number):
        for copy in loads[number]:
            copy.wait()
        return left[number]

    keep = final_back(values_ref, back_gain_ref, base_ref, sum_ref, stats_ref)

    def final(index, clip, span_rows, result):
        result = keep(index, clip, span_rows, result)
        if normed:
            result = layer_norm(result, gain_ref[0:1], gain_ref[1:2])
        put(index, result)

    steps = reduce_steps(
        clips,
        rows,
        sub,
        terms_of(clips, rows, blocks, mat, span, terms),
        final,
        *reduce_refs,
    )

    next(steps)
    next(steps)
    next(steps)
    if adding:
        next(adder)
    run((lambda: next(going)) if leaving else (lambda: None))
    if outer:
        for copy in outer_loads:
            copy.wait()
        outer_columns(outer_ref, 0, low[...], gather_scratch[0][...])
        outer_ref[:, low.shape[3] :] = ending_ref[...]
    next(steps)
    if passing:
        end_rows()
    if leaving:
        next(going)
    if adding:
        next(adder)


def reduce_gather(
    left,
    matrix,
    clips,
    collective_id,
    base,
    second,
    kind=jnp.bfloat16,
    span=None,
    back=None,
    gains=None,
    second_span=None,
    pair=None,
    bias=None,
    passing=None,
    outer=None,
    leaving=None,
    adding=None,
    sub=64,
):
    wide = matrix.shape[0]
    rows, inner = left.shape[0] // (8 * clips), left.shape[1]
    low = jnp.bfloat16
    spans = window_of(matrix, span)
    inside = pl.BlockSpec(memory_space=pltpu.VMEM)
    plan, more, more_specs, outs, out_specs, more_scratch = gather_plan(
        clips, rows, wide, sub, second, kind, None, second_span, pair, bias, None
    )
    counts = (len(more), len(outs), len(more_scratch))
    args = [left.reshape(clips, 8, rows, inner), matrix, base]
    in_specs = [any_spec(), any_spec(), inside]
    first_outs = [jax.ShapeDtypeStruct((clips, rows, wide), jnp.float32)]
    scratch = [
        pltpu.VMEM((8, clips, rows, inner), low),
        pltpu.VMEM((wide, spans[0][1]), low),
        DMA(()),
        DMA((8, clips)),
    ] + reduce_scratch(clips, rows, sub, wide)
    if back is not None:
        args += list(back)
        in_specs += [inside] * 2
        first_outs.append(jax.ShapeDtypeStruct((2, wide), jnp.float32))
    if gains is not None:
        args.append(gains)
        in_specs.append(inside)
    args += more
    in_specs += more_specs
    scratch += more_scratch
    outs = first_outs + outs
    out_specs = [inside] * len(first_outs) + out_specs
    flat = len(outs)
    if passing is not None:
        group, piece, _ = passing.shape
        planes = group // clips
        args.append(passing)
        in_specs.append(any_spec())
        outs.append(jax.ShapeDtypeStruct((clips, planes, piece, wide), passing.dtype))
        out_specs.append(any_spec())
        scratch += [DMA((group,)), DMA((clips, planes)), DMA((group,))]
    if outer is not None:
        low_rows, ending = outer
        columns = low_rows.shape[1]
        args += [low_rows.reshape(clips, 8, rows, columns), ending]
        in_specs += [any_spec(), inside]
        outs.append(jax.ShapeDtypeStruct((wide, columns + ending.shape[1]), low))
        out_specs.append(inside)
        scratch += [pltpu.VMEM((8, clips, rows, columns), low), DMA((8, clips))]
    if leaving is not None:
        per, planes, piece, _ = leaving.shape
        group = per * planes
        args.append(leaving)
        in_specs.append(any_spec())
        outs += [jax.ShapeDtypeStruct((group, piece, wide), leaving.dtype)] * 2
        leaving_mid = len(outs) - 1
        out_specs += [any_spec()] * 2
    if adding is not None:
        args.append(adding)
        in_specs.append(any_spec())
        outs.append(jax.ShapeDtypeStruct(adding.shape[1:], adding.dtype))
        out_specs.append(inside)
        scratch += [
            pltpu.VMEM(adding.shape, adding.dtype),
            DMA((adding.shape[0],)),
            DMA((adding.shape[0],)),
            DMA(()),
        ]
    if leaving is not None:
        scratch += outward_scratch(group, planes)
    results = pl.pallas_call(
        functools.partial(
            reduce_gather_body,
            clips,
            rows,
            sub,
            spans,
            back is not None,
            gains is not None,
            plan,
            counts,
            passing is not None and (group, planes),
            outer is not None,
            leaving is not None and (group, planes),
            adding is not None,
        ),
        out_shape=outs,
        in_specs=in_specs,
        out_specs=out_specs,
        scratch_shapes=scratch,
        compiler_params=communicating(collective_id),
    )(*args)
    first = len(first_outs)
    if leaving is not None:
        results = [block for which, block in enumerate(results) if which != leaving_mid]
    return list(results[:first]) + flat_rows(results[first:flat]) + list(results[flat:])


def ff_outer_body(
    order_of,
    clips,
    rows,
    sub,
    gates_ref,
    hidden_ref,
    down_ref,
    normed_ref,
    grads_ref,
    values_ref,
    layer_ref,
    outer_ref,
    gates,
    hidden,
    down,
    normed,
    grads,
    stage,
    load_sem,
    tile_sem,
    stage_sem,
    *reduce_refs,
):
    place, depth, flip = plane_places()
    order = plane_order()
    loads = [
        pltpu.make_async_copy(source, goal, load_sem.at[which])
        for which, (source, goal) in enumerate(
            ((down_ref, down), (hidden_ref, hidden), (gates_ref, gates))
        )
    ]
    for copy in loads:
        copy.start()
    tile = stage.shape[1]
    tiles = normed_ref.shape[3] // tile
    total_rows = 8 * clips * rows
    inner = gates.shape[3]

    def fetch(index):
        return [
            pltpu.make_async_copy(
                source.at[:, :, :, pl.ds(index * tile, tile)],
                goal.at[index % 2],
                tile_sem.at[which, index % 2],
            )
            for which, (source, goal) in enumerate(((normed_ref, normed), (grads_ref, grads)))
        ]

    def stored(index):
        return pltpu.make_async_copy(
            stage.at[index % 2],
            outer_ref.at[pl.ds(index * tile, tile)],
            stage_sem.at[index % 2],
        )

    def outer_tile(index):
        spot = index % 2
        if index >= 2:
            stored(index - 2).wait()
        for copy in fetch(index):
            copy.wait()
        stage[spot, :, :inner] = outer_sum(
            normed[spot].reshape(total_rows, tile), gates[...].reshape(total_rows, inner)
        ).astype(stage.dtype)
        stage[spot, :, inner:] = outer_sum(
            grads[spot].reshape(total_rows, tile),
            hidden[...].reshape(total_rows, hidden.shape[3]),
        ).astype(stage.dtype)
        stored(index).start()
        if index + 2 < tiles:
            for copy in fetch(index + 2):
                copy.start()

    for index in range(2):
        for copy in fetch(index):
            copy.start()
    greet([(flip(1), depth), (flip(2), depth), (flip(4), depth)])
    loads[0].wait()
    loads[1].wait()

    def layer_rows(index, clip, span, result):
        result = to_whole_features(values_ref[clip, span] + result, *order_of)
        layer_ref[clip, span] = result.astype(layer_ref.dtype)

    steps = reduce_steps(
        clips,
        rows,
        sub,
        terms_of(
            clips, rows, lambda number: hidden[order[number]], down, (0, down.shape[1]), reduce_refs[0]
        ),
        layer_rows,
        *reduce_refs,
    )
    next(steps)
    loads[2].wait()
    outer_tile(0)
    next(steps)
    for index in range(1, tiles):
        outer_tile(index)
    next(steps)
    for index in range(max(tiles - 2, 0), tiles):
        stored(index).wait()
    next(steps)


def ff_outer(gates, hidden, down, normed, grads, values, planes, collective_id, sub=64):
    clips, rows, wide = values.shape
    low = jnp.bfloat16
    inner, columns = gates.shape[1], gates.shape[1] + hidden.shape[1]
    tile = 512
    inside = pl.BlockSpec(memory_space=pltpu.VMEM)
    return pl.pallas_call(
        functools.partial(ff_outer_body, (8, planes), clips, rows, sub),
        out_shape=[
            jax.ShapeDtypeStruct((clips, rows, wide), low),
            jax.ShapeDtypeStruct((wide, columns), low),
        ],
        in_specs=[any_spec()] * 5 + [inside],
        out_specs=[inside, any_spec()],
        scratch_shapes=[
            pltpu.VMEM((clips, 8, rows, inner), low),
            pltpu.VMEM((8, clips, rows, hidden.shape[1]), low),
            pltpu.VMEM(down.shape, low),
            pltpu.VMEM((2, clips, 8, rows, tile), low),
            pltpu.VMEM((2, 8, clips, rows, tile), low),
            pltpu.VMEM((2, tile, columns), low),
            DMA((3,)),
            DMA((2, 2)),
            DMA((2,)),
        ]
        + reduce_scratch(clips, rows, sub, wide),
        compiler_params=communicating(collective_id),
    )(
        gates.reshape(clips, 8, rows, inner),
        hidden.reshape(8, clips, rows, hidden.shape[1]),
        down,
        normed.reshape(clips, 8, rows, wide),
        grads.reshape(8, clips, rows, wide),
        values,
    )


def rotary_lanes(places):
    half = HDIM // 2
    frequency = 10000.0 ** (-np.arange(half, dtype=np.float32) / np.float32(half))
    angles = places.astype(np.float32)[:, None] * frequency.astype(np.float32)[None, :]
    cosine, sine = np.cos(angles), np.sin(angles)
    both = [
        np.concatenate([cosine] * 4, axis=1),
        np.concatenate([-sine, sine, -sine, sine], axis=1),
    ]
    return jnp.asarray(np.stack(both).astype(np.float32))


def turn_heads(values, cosine, sine):
    lane = lax.broadcasted_iota(jnp.int32, values.shape, 1)
    half = HDIM // 2
    ahead = pltpu.roll(values, 2 * HDIM - half, 1)
    behind = pltpu.roll(values, half, 1)
    other = jnp.where(lax.rem(lane, HDIM) < half, ahead, behind)
    return values * cosine + other * sine


def swap_beside(pairs, send_sem, recv_sem, local_sem):
    place, depth, flip = plane_places()

    def each(act):
        for which, (source, goal) in enumerate(pairs):
            for mask in (6, 7, 2, 3, 4, 5, 1):
                other = flip(mask)
                act(
                    remote(
                        source(other),
                        goal(place),
                        send_sem.at[which, mask],
                        recv_sem.at[which, mask],
                        (other, depth),
                    )
                )

    stays = [
        pltpu.make_async_copy(source(place), goal(place), local_sem.at[which])
        for which, (source, goal) in enumerate(pairs)
    ]

    def begin():
        each(lambda copy: copy.start())
        for stay in stays:
            stay.start()

    def end():
        each(lambda copy: copy.wait())
        for stay in stays:
            stay.wait()

    return begin, end


def swap_beside_scratch(count):
    return [DMA((count, 8)), DMA((count, 8)), DMA((count,))]


def flash_forward_body(
    heads,
    tile,
    normed_ref,
    mat_ref,
    stamp_ref,
    bias_ref,
    rotary_ref,
    ff_ref,
    own_ref,
    turned_ref,
    out_ref,
    lse_ref,
    gate_up_ref,
    down_ref,
    mid_ref,
    raw_ref,
    *sems,
):
    group = gate_up_ref.shape[0]
    hidden = down_ref.shape[2]
    step, last = pl.program_id(0), pl.num_programs(0) - 1

    def columns(block):
        return lambda other: ff_ref.at[
            :, pl.ds(pl.multiple_of((block * group + other) * hidden, 128), hidden)
        ]

    start_swap, end_swap = swap_beside(
        [
            (lambda other: own_ref.at[other], lambda other: mid_ref.at[other]),
            (columns(0), lambda other: gate_up_ref.at[other, :, pl.ds(0, hidden)]),
            (columns(1), lambda other: gate_up_ref.at[other, :, pl.ds(hidden, hidden)]),
            (columns(2), lambda other: down_ref.at[other]),
        ],
        *sems,
    )
    place, depth, flip = plane_places()

    @pl.when(step == 0)
    def _():
        greet([(flip(mask), depth) for mask in range(1, group)])
        start_swap()

    def project(index, carry):
        place = pl.ds(pl.multiple_of(index * tile, tile), tile)
        raw_ref[place, :] = jnp.dot(
            normed_ref[place, :], mat_ref[...], preferred_element_type=jnp.float32
        )
        return carry

    lax.fori_loop(0, raw_ref.shape[0] // tile, project, 0)
    wide = heads * HDIM
    for pair in range(2 * wide // 128):
        lanes = slice(pair * 128, pair * 128 + 128)
        turned_ref[:, lanes] = turn_heads(
            raw_ref[:, lanes], rotary_ref[0], rotary_ref[1]
        ).astype(turned_ref.dtype)
    turned_ref[:, 2 * wide :] = raw_ref[:, 2 * wide :].astype(turned_ref.dtype)
    rows = raw_ref.shape[0]
    bias = bias_ref[0]
    scale = HDIM**-0.5
    for head in range(heads):
        lanes = slice(head * HDIM, head * HDIM + HDIM)
        keys = turned_ref[:, wide + head * HDIM : wide + head * HDIM + HDIM]
        values = turned_ref[:, 2 * wide + head * HDIM : 2 * wide + head * HDIM + HDIM]
        stamp_key = stamp_ref[0, :, lanes].astype(jnp.float32)
        stamp_value = stamp_ref[
            0, :, wide + head * HDIM : wide + head * HDIM + HDIM
        ].astype(jnp.float32)

        def one(step, carry):
            place = pl.ds(pl.multiple_of(step * tile, tile), tile)
            query = turned_ref[place, lanes] * jnp.asarray(scale, turned_ref.dtype)
            scores = times_transposed(query, keys) + bias
            stamp_score = jnp.sum(query.astype(jnp.float32) * stamp_key, axis=1, keepdims=True)
            top = jnp.maximum(jnp.max(scores, axis=1, keepdims=True), stamp_score)
            expo = jnp.exp(scores - top)
            stamp_expo = jnp.exp(stamp_score - top)
            denom = jnp.sum(expo, axis=1, keepdims=True) + stamp_expo
            share = 1.0 / denom
            prob = (expo * share).astype(values.dtype)
            stamp_prob = (stamp_expo * share).astype(values.dtype).astype(jnp.float32)
            mixed = jnp.dot(prob, values, preferred_element_type=jnp.float32)
            out_ref[place, lanes] = (mixed + stamp_prob * stamp_value).astype(out_ref.dtype)
            lse_ref[place, head : head + 1] = top + jnp.log(denom)
            return carry

        lax.fori_loop(0, rows // tile, one, 0)

    pl.when(step == last)(end_swap)


def flash_forward(normed, matrix, stamps, bias, rotary, heads, ff_low, rows_of_clip, collective_id):
    clips, rows = bias.shape
    wide = heads * HDIM
    group, piece, features = rows_of_clip.shape
    owned, columns = ff_low.shape
    hidden = columns // (3 * group)
    like = lambda *shape: jax.ShapeDtypeStruct(shape, rows_of_clip.dtype)
    blocked = lambda lanes: pl.BlockSpec((rows, lanes), lambda clip: (clip, 0))
    return pl.pallas_call(
        functools.partial(flash_forward_body, heads, rows // 4),
        grid=(clips,),
        out_shape=[
            like(clips * rows, 3 * wide),
            like(clips * rows, wide),
            jax.ShapeDtypeStruct((clips * rows, 128), jnp.float32),
            like(group, owned, 2 * hidden),
            like(group, owned, hidden),
            like(group, piece, features),
        ],
        in_specs=[
            blocked(features),
            pl.BlockSpec(matrix.shape, lambda clip: (0, 0)),
            pl.BlockSpec((1, 1, 2 * wide), lambda clip: (clip, 0, 0)),
            pl.BlockSpec((1, 1, rows), lambda clip: (clip, 0, 0)),
            pl.BlockSpec((2, rows, 128), lambda clip: (0, 0, 0)),
            any_spec(),
            any_spec(),
        ],
        out_specs=[blocked(3 * wide), blocked(wide), blocked(128)] + [any_spec()] * 3,
        scratch_shapes=[pltpu.VMEM((rows, 3 * wide), jnp.float32)] + swap_beside_scratch(4),
        compiler_params=communicating(collective_id),
    )(normed, matrix, stamps[:, None], bias[:, None], rotary, ff_low, rows_of_clip)


def flash_backward_body(
    heads,
    tile,
    turned_ref,
    mixed_ref,
    grad_ref,
    lse_ref,
    stamp_ref,
    bias_ref,
    rotary_ref,
    cut_ref,
    cross_cut_ref,
    normed_ref,
    stamp_normed_ref,
    out_ref,
    stamp_out_ref,
    mine_ref,
    cross_mine_ref,
    outer_ref,
    query_grad,
    key_grad,
    value_grad,
    outer_total,
    *sems,
):
    place, depth, flip = plane_places()
    start_swap, end_swap = swap_beside(
        [
            (lambda other: cut_ref.at[other], lambda other: mine_ref.at[other]),
            (lambda other: cross_cut_ref.at[other], lambda other: cross_mine_ref.at[other]),
        ],
        *sems,
    )

    @pl.when(pl.program_id(0) == 0)
    def _():
        greet([(flip(mask), depth) for mask in range(1, 8)])
        start_swap()

    wide = heads * HDIM
    rows = turned_ref.shape[0]
    scale = HDIM**-0.5
    low = turned_ref.dtype
    f32 = jnp.float32
    first_row = lax.broadcasted_iota(jnp.int32, (8, tile), 0) == 0
    ones = lambda count, width: jnp.ones((count, width), low)
    blank = lambda count, width: jnp.zeros((count, width), low)
    bias = bias_ref[0].astype(low)

    def widened(count, *parts):
        have = sum(part.shape[1] for part in parts)
        return jnp.concatenate(list(parts) + [blank(count, 128 - have)], axis=1)

    def negative_parts(column):
        parts, rest = [], -column
        for _ in range(3):
            parts.append(rest.astype(low))
            rest = rest - parts[-1].astype(f32)
        return parts

    for head in range(heads):
        lanes = slice(head * HDIM, head * HDIM + HDIM)
        later = slice(wide + head * HDIM, wide + head * HDIM + HDIM)
        keys = turned_ref[:, later]
        values = turned_ref[:, 2 * wide + head * HDIM : 2 * wide + head * HDIM + HDIM]
        keys_across = keys.astype(f32).T.astype(low)
        wide_keys = widened(rows, keys, bias, ones(rows, 3))
        wide_values = widened(rows, values, ones(rows, 3))
        stamp_key = jnp.broadcast_to(stamp_ref[0, :, lanes], (8, HDIM))
        stamp_value = jnp.broadcast_to(stamp_ref[0, :, later], (8, HDIM))
        wide_stamp_key = widened(8, stamp_key, blank(8, 1), ones(8, 3))
        wide_stamp_value = widened(8, stamp_value, ones(8, 3))
        stamp_column = stamp_ref[0, :, lanes].astype(f32).T
        key_total = jnp.zeros((rows, HDIM), f32)
        value_total = jnp.zeros((rows, HDIM), f32)
        stamp_key_total = jnp.zeros((8, HDIM), f32)
        stamp_value_total = jnp.zeros((8, HDIM), f32)
        for step in range(rows // tile):
            place = slice(step * tile, step * tile + tile)
            query = turned_ref[place, lanes] * jnp.asarray(scale, low)
            grad = grad_ref[place, lanes]
            delta = jnp.sum(
                grad.astype(f32) * mixed_ref[place, lanes].astype(f32), axis=1, keepdims=True
            )
            lse = lse_ref[place, head : head + 1]
            wide_query = widened(tile, query, ones(tile, 1), *negative_parts(lse))
            wide_grad = widened(tile, grad, *negative_parts(delta))
            prob = jnp.exp(times_transposed(wide_keys, wide_query))
            scores = (prob * times_transposed(wide_values, wide_grad)).astype(low)
            stamp_prob = jnp.exp(times_transposed(wide_stamp_key, wide_query))
            stamp_scores = stamp_prob * times_transposed(wide_stamp_value, wide_grad)
            stamp_scores = jnp.where(first_row, stamp_scores, 0.0).astype(low)
            value_total += jnp.dot(prob.astype(low), grad, preferred_element_type=f32)
            key_total += jnp.dot(scores, query, preferred_element_type=f32)
            across = jnp.dot(keys_across, scores, preferred_element_type=f32)
            across = across + stamp_column * stamp_scores[:1].astype(f32)
            query_grad[place, lanes] = across.T * scale
            stamp_key_total += jnp.dot(stamp_scores, query, preferred_element_type=f32)
            stamp_value_total += jnp.dot(
                jnp.where(first_row, stamp_prob, 0.0).astype(low), grad, preferred_element_type=f32
            )
        key_grad[:, lanes] = key_total
        value_grad[:, lanes] = value_total
        stamp_out_ref[0, :, lanes] = stamp_key_total[:1]
        stamp_out_ref[0, :, later] = stamp_value_total[:1]
    both = jnp.concatenate([query_grad[...], key_grad[...]], axis=1)
    for pair in range(2 * wide // 128):
        lanes = slice(pair * 128, pair * 128 + 128)
        out_ref[:, lanes] = turn_heads(both[:, lanes], rotary_ref[0], -rotary_ref[1]).astype(low)
    out_ref[:, 2 * wide :] = value_grad[...].astype(low)
    count = outer_total.shape[1]
    tile = 512
    for start in range(0, normed_ref.shape[1], tile):
        span = slice(start, start + tile)
        product = outer_sum(normed_ref[:, span], out_ref[...])
        stamp_part = stamp_normed_ref[0, span] * stamp_out_ref[0]
        product = product + jnp.concatenate(
            [jnp.zeros((tile, count - 2 * wide), f32), stamp_part], axis=1
        )

        @pl.when(pl.program_id(0) == 0)
        def _():
            outer_total[span] = product

        @pl.when(pl.program_id(0) > 0)
        def _():
            outer_total[span] += product

    @pl.when(pl.program_id(0) == pl.num_programs(0) - 1)
    def _():
        outer_ref[...] = outer_total[...].astype(outer_ref.dtype)
        end_swap()


def flash_backward(
    turned,
    mixed,
    grad,
    lse,
    stamps,
    bias,
    rotary,
    heads,
    cut,
    cross_cut,
    normed,
    stamp_normed,
    collective_id,
):
    clips, rows, _ = bias.shape
    wide = heads * HDIM
    blocked = lambda lanes: pl.BlockSpec((rows, lanes), lambda clip: (clip, 0))
    features = normed.shape[1]
    grads, stamp_grads, mine, cross_mine, outer = pl.pallas_call(
        functools.partial(flash_backward_body, heads, rows // 4),
        grid=(clips,),
        out_shape=[
            jax.ShapeDtypeStruct((clips * rows, 3 * wide), jnp.bfloat16),
            jax.ShapeDtypeStruct((clips, 1, 2 * wide), jnp.float32),
            jax.ShapeDtypeStruct(cut.shape, cut.dtype),
            jax.ShapeDtypeStruct(cross_cut.shape, cross_cut.dtype),
            jax.ShapeDtypeStruct((features, 3 * wide), jnp.bfloat16),
        ],
        in_specs=[
            blocked(3 * wide),
            blocked(wide),
            blocked(wide),
            blocked(128),
            pl.BlockSpec((1, 1, 2 * wide), lambda clip: (clip, 0, 0)),
            pl.BlockSpec((1, rows, 1), lambda clip: (clip, 0, 0)),
            pl.BlockSpec((2, rows, 128), lambda clip: (0, 0, 0)),
            any_spec(),
            any_spec(),
            blocked(features),
            pl.BlockSpec((1, features, 1), lambda clip: (clip, 0, 0)),
        ],
        out_specs=[
            blocked(3 * wide),
            pl.BlockSpec((1, 1, 2 * wide), lambda clip: (clip, 0, 0)),
            any_spec(),
            any_spec(),
            pl.BlockSpec((features, 3 * wide), lambda clip: (0, 0)),
        ],
        scratch_shapes=[pltpu.VMEM((rows, wide), jnp.float32)] * 3
        + [pltpu.VMEM((features, 3 * wide), jnp.float32)]
        + swap_beside_scratch(2),
        compiler_params=communicating(collective_id),
    )(
        turned,
        mixed,
        grad,
        lse,
        stamps[:, None],
        bias,
        rotary,
        cut,
        cross_cut,
        normed,
        stamp_normed,
    )
    return grads, stamp_grads[:, 0], mine, cross_mine, outer


def adam_body(ff_steps, places, *refs):
    refs = list(refs)
    take = lambda count: [refs.pop(0) for _ in range(count)]
    total_ref = take(1)[0]
    ff_refs, ff_grad_ref = take(3), take(1)[0]
    attn_refs = take(3)
    attn_grads = take(1 + max(which for which, _, _ in places))
    ff_outs, attn_outs = take(3), take(3)
    step = pl.program_id(0)
    factor = jnp.minimum(1.0, clip_limit / jnp.sqrt(total_ref[0:1, 0:1]))

    def update(olds, gradient, outs):
        results = adam_step(
            *[old[...] for old in olds],
            gradient.astype(jnp.float32) * factor,
            matrix_rate,
            matrix_decay,
        )
        for out, result in zip(outs, results):
            out[...] = result

    @pl.when(step < ff_steps)
    def _():
        gradient = jnp.concatenate(
            [ff_grad_ref[part] for part in range(ff_grad_ref.shape[0])], axis=1
        )
        update(ff_refs, gradient, ff_outs)

    for block, (which, start, stop) in enumerate(places):

        @pl.when(step == ff_steps + block)
        def _(owned_ref=attn_grads[which], start=start, stop=stop):
            gradient = jnp.concatenate(
                [owned_ref[part, :, start:stop] for part in range(owned_ref.shape[0])], axis=1
            )
            update(attn_refs, gradient, attn_outs)


def adam(total, ff, ff_grad, attn, attn_grads, places):
    rows, columns = ff[0].shape
    group, _, held = ff_grad.shape
    parts = group // 2
    width = columns // (3 * group)
    ff_steps = 3 * group // parts
    steps = ff_steps + len(places)
    ff_step = lambda step: jnp.minimum(step, ff_steps - 1)
    ff_piece = pl.BlockSpec((rows, parts * width), lambda step: (0, ff_step(step)))
    ff_grads = pl.BlockSpec(
        (parts, rows, width), lambda step: (lax.rem(ff_step(step), 2), 0, lax.div(ff_step(step), 2))
    )
    attn_piece = pl.BlockSpec(
        (rows, attn[0].shape[1] // len(places)), lambda step: (0, jnp.maximum(step - ff_steps, 0))
    )
    whole = [pl.BlockSpec(grad.shape, lambda step: (0, 0, 0)) for grad in attn_grads]
    f32 = jnp.float32
    results = pl.pallas_call(
        functools.partial(adam_body, ff_steps, places),
        grid=(steps,),
        out_shape=[jax.ShapeDtypeStruct(ff[0].shape, f32)] * 3
        + [jax.ShapeDtypeStruct(attn[0].shape, f32)] * 3,
        in_specs=[pl.BlockSpec((8, 128), lambda step: (0, 0))]
        + [ff_piece] * 3
        + [ff_grads]
        + [attn_piece] * 3
        + whole,
        out_specs=[ff_piece] * 3 + [attn_piece] * 3,
        compiler_params=pltpu.CompilerParams(vmem_limit_bytes=VMEM_LIMIT),
    )(total, *ff, ff_grad, *attn, *attn_grads)
    return results[:3], results[3:]


def plane_device(
    frames,
    time_token,
    cond_ids,
    cond_mask,
    lengths,
    cond_table,
    cotangent,
    attn_weight,
    cross_weight,
    norm_param,
    ff_weight,
    attn_first,
    attn_second,
    cross_first,
    cross_second,
    norm_first,
    norm_second,
    ff_first,
    ff_second,
):
    group, planes = lax.axis_size("dp"), lax.axis_size("seq")
    place, depth = lax.axis_index("dp"), lax.axis_index("seq")
    clips = group // planes
    _, frame_rows, wide = frames.shape
    piece = frame_rows // group
    seq_frames = frame_rows * planes
    own_rows = planes * piece
    heads = HEADS // group
    head_wide = heads * HDIM
    ff_wide = FF // group
    owned = wide // (group * planes)
    cond_count, cond_wide = cond_ids.shape[1], cond_table.shape[1]
    cond_owned = cross_weight.shape[0]

    norm_block = norm_param.astype(jnp.bfloat16).astype(jnp.float32)
    norm_block = jnp.pad(norm_block, ((0, 2), (0, 128 - owned)))
    pack = jnp.concatenate(
        [
            time_token.astype(jnp.float32),
            jnp.pad(cond_ids.astype(jnp.float32), ((0, 0), (0, wide - cond_count))),
            jnp.pad(cond_mask.astype(jnp.float32), ((0, 0), (0, wide - cond_count))),
            jnp.broadcast_to(lengths.astype(jnp.float32)[:, None], (1, wide)),
            jnp.zeros((4, wide), jnp.float32),
        ],
        axis=0,
    )
    positions = depth * frame_rows + jnp.arange(frame_rows)
    valid = (positions < lengths).astype(jnp.float32)[:, None]
    stream, gain_rows, packs, qkv_mine, rest_mine, ff_low, grad_pieces = enter(
        frames[0],
        cotangent[0],
        valid,
        norm_block,
        pack,
        attn_weight,
        cross_weight,
        ff_weight,
        planes,
        1,
    )
    stream = stream.reshape(clips, own_rows, wide).astype(jnp.float32)

    def over_planes(block):
        return lax.all_gather(block.reshape(group * owned, -1), "seq", axis=0, tiled=True)

    w_qkv = over_planes(qkv_mine)
    w_rest = over_planes(rest_mine)
    of_self_out = (0, head_wide)
    of_cross_query = (head_wide, 2 * head_wide)
    of_cross_out = (2 * head_wide, 3 * head_wide)
    w_cond = w_rest[:, 3 * head_wide :].reshape(planes, group, 2, cond_owned, head_wide)
    w_cond = w_cond.transpose(1, 0, 3, 2, 4).reshape(cond_wide, 2 * head_wide)
    plane_packs = lax.dynamic_slice_in_dim(packs, depth * clips, clips, axis=0)
    stamps = plane_packs[:, 0].reshape(clips, group, planes, owned)
    stamps = stamps.swapaxes(1, 2).reshape(clips, wide)
    cond_keep = plane_packs[:, 2, :cond_count] > 0
    clip_lengths = plane_packs[:, 3, 0].astype(jnp.int32)
    share = cond_count // group
    all_ids = packs[:, 1, :cond_count].astype(jnp.int32)
    own_ids = lax.dynamic_slice_in_dim(all_ids, place * share, share, axis=1)
    vocab_rows = cond_table.shape[0]
    relative = own_ids - depth * vocab_rows
    inside = (relative >= 0) & (relative < vocab_rows)
    picked = jnp.take(cond_table, jnp.clip(relative, 0, vocab_rows - 1), axis=0)
    picked = jnp.where(inside[..., None], picked, jnp.zeros((), picked.dtype))
    picked = picked.reshape(planes, clips, share, cond_wide)
    group_rows = clips * seq_frames
    row_place = np.arange(seq_frames)
    row_owner, row_rest = row_place // own_rows, row_place % own_rows
    true_place = (row_rest // piece) * frame_rows + row_owner * piece + row_rest % piece
    key_keep = true_place[None, :] < clip_lengths[:, None]
    group_shape = (clips, seq_frames, heads, HDIM)

    group_one, cond = gather_dot(stream, None, None, 5, gain_rows[0:2], picked)
    cond_flat = cond.swapaxes(0, 1).reshape(clips * cond_count, cond_wide)
    stamp_normed = layer_norm(stamps, gain_rows[0], gain_rows[1]).astype(jnp.bfloat16)
    stamp_pair = jnp.dot(stamp_normed, w_qkv[:, head_wide:], preferred_element_type=jnp.float32)
    stamp_pair = stamp_pair.astype(jnp.bfloat16)
    rotary = rotary_lanes(true_place)
    key_bias = jnp.where(key_keep, 0.0, masked_score)
    rotated, self_low, self_lse, gate_up_mine, down_mine, grad_out_mid = flash_forward(
        group_one,
        w_qkv,
        stamp_pair,
        key_bias,
        rotary,
        heads,
        ff_low,
        grad_pieces,
        2,
    )
    w_gate_up = over_planes(gate_up_mine)
    w_down = over_planes(down_mine)
    cond_pair = jnp.dot(cond_flat, w_cond, preferred_element_type=jnp.float32)
    cond_pair = cond_pair.astype(jnp.bfloat16).reshape(clips, cond_count, 2 * head_wide)
    cond_bias = jnp.where(cond_keep, 0.0, masked_score)[:, None]
    resid_one, group_two, cross_query, cross_out, grad_out_low = reduce_gather(
        self_low,
        w_rest,
        clips,
        6,
        stream,
        w_rest,
        span=of_self_out,
        gains=gain_rows[2:4],
        second_span=of_cross_query,
        pair=cond_pair,
        bias=cond_bias,
        passing=grad_out_mid,
    )
    grad_out_low = grad_out_low.reshape(clips, own_rows, wide)
    (resid_two,) = dot_reduce(cross_out, w_rest, clips, 8, resid_one, of_cross_out)
    group_three, gate_up = gather_dot(resid_two, w_gate_up, jnp.float32, 9, gain_rows[4:6])
    stamp_column = stamp_normed.astype(jnp.float32)[:, :, None]
    bias_column = key_bias[:, :, None]
    gate_up, grad_out_low, stamp_column, bias_column = lax.optimization_barrier(
        (gate_up, grad_out_low, stamp_column, bias_column)
    )
    group_grad_out, grad_gate_up, hidden = gather_dot(
        grad_out_low, w_down, None, 10, gate_up=gate_up
    )

    def over_rows(block):
        return lax.psum_scatter(
            block.astype(jnp.bfloat16), "seq", scatter_dimension=0, tiled=True
        ).reshape(group, owned, -1)

    layer_rows, ff_piece = ff_outer(
        grad_gate_up, hidden, w_down, group_three, group_grad_out, resid_two, planes, 12
    )
    ff_piece, grad_gate_up = lax.optimization_barrier((ff_piece, grad_gate_up))
    ff_rows = over_rows(ff_piece)
    grad_two, stats_three = dot_reduce(
        grad_gate_up, w_gate_up, clips, 13, grad_out_low, back=(resid_two, gain_rows[4:5])
    )
    _, grad_cross_query, cond_grad, cross_piece = gather_dot(
        grad_two,
        w_rest,
        None,
        15,
        span=of_cross_out,
        pair=cond_pair,
        bias=cond_bias,
        query=cross_query,
        outer=(group_two, cross_out),
    )
    cond_grad = cond_grad.reshape(clips * cond_count, 2 * head_wide)
    cond_piece = split_outer(cond_flat, cond_grad)
    cond_piece = cond_piece.reshape(group, planes, cond_owned, 2, head_wide)
    cond_piece = cond_piece.transpose(1, 0, 3, 2, 4).reshape(wide, head_wide)
    cond_piece = cond_piece.astype(jnp.bfloat16)
    grad_one, stats_two, _, grad_self_mixed, rest_piece, layer_out, cross_rows = reduce_gather(
        grad_cross_query,
        w_rest,
        clips,
        16,
        grad_two,
        w_rest,
        span=of_cross_query,
        back=(resid_one, gain_rows[2:3]),
        second_span=of_self_out,
        outer=(self_low, cond_piece),
        adding=cross_piece.reshape(planes, group * owned, 2 * head_wide),
        leaving=layer_rows.reshape(clips, planes, piece, wide),
    )
    rest_piece, ff_rows = lax.optimization_barrier((rest_piece, ff_rows))
    rest_rows = over_rows(rest_piece)
    grad_project, stamp_grad, ff_owned, cross_owned, qkv_piece = flash_backward(
        rotated,
        self_low,
        grad_self_mixed,
        self_lse,
        stamp_pair,
        bias_column,
        rotary,
        heads,
        ff_rows,
        cross_rows.reshape(group, owned, -1),
        group_one,
        stamp_column,
        3,
    )
    grad_stamp_normed = split_times_transposed(stamp_grad, w_qkv[:, head_wide:])
    qkv_rows = over_rows(qkv_piece)
    grad_project, rest_rows = lax.optimization_barrier((grad_project, rest_rows))
    frames_grad, stats_one, rest_owned = dot_reduce(
        grad_project,
        w_qkv,
        clips,
        18,
        grad_one,
        back=(stream, gain_rows[0:1]),
        kind=jnp.bfloat16,
        order=(group, planes),
        cut=rest_rows,
    )
    _, norm_stamp_back = jax.vjp(layer_norm, stamps, gain_rows[0], gain_rows[1])
    _, grad_gain_stamp, grad_bias_stamp = norm_stamp_back(grad_stamp_normed)
    stamp_stats = jnp.stack([grad_gain_stamp, grad_bias_stamp])
    norm_grad = jnp.concatenate([stats_one + stamp_stats, stats_two, stats_three], axis=0)
    norm_parts = norm_grad.reshape(6, planes, group, owned).transpose(2, 1, 0, 3)
    norm_parts = norm_parts.reshape(group * planes, 6, owned)
    norm_parts = jnp.pad(norm_parts, ((0, 0), (0, 2), (0, 128 - owned)))
    ff_squares = jnp.sum(jnp.square(ff_owned.astype(jnp.float32)))
    frames_grad, qkv_owned, norm_sum, total = settle(
        frames_grad.reshape(clips, planes, piece, wide),
        qkv_rows,
        [cross_owned, rest_owned],
        norm_parts,
        ff_squares.reshape(1, 1),
        20,
    )
    cross_reduced = rest_owned[:, :, head_wide:].reshape(group, 2, cond_owned, head_wide)
    cross_reduced = cross_reduced.transpose(2, 1, 0, 3).reshape(cross_weight.shape)
    cross_reduced = cross_reduced.astype(jnp.float32)
    norm_reduced = norm_sum[:6, :owned]
    grad_norm = jnp.sqrt(total[0, 0])
    factor = jnp.minimum(1.0, clip_limit / grad_norm)
    ff_results, attn_results = adam(
        total,
        (ff_weight, ff_first, ff_second),
        ff_owned,
        (attn_weight, attn_first, attn_second),
        [qkv_owned, cross_owned, rest_owned],
        [
            (which, block * head_wide, (block + 1) * head_wide)
            for which, block in ((0, 0), (0, 1), (0, 2), (2, 0), (1, 0), (1, 1))
        ],
    )
    ff_new, ff_first_new, ff_second_new = ff_results
    attn_new, attn_first_new, attn_second_new = attn_results
    frames_grad = frames_grad.reshape(frames.shape).astype(jnp.float32)
    layer_out = layer_out.reshape(frames.shape)
    cross_new, cross_first_new, cross_second_new = adam_step(
        cross_weight, cross_first, cross_second, cross_reduced * factor, matrix_rate, matrix_decay
    )
    norm_new, norm_first_new, norm_second_new = adam_step(
        norm_param, norm_first, norm_second, norm_reduced * factor, gain_rate, 0.0
    )
    return (
        layer_out,
        frames_grad,
        grad_norm,
        attn_new,
        cross_new,
        norm_new,
        ff_new,
        attn_first_new,
        cross_first_new,
        norm_first_new,
        ff_first_new,
        attn_second_new,
        cross_second_new,
        norm_second_new,
        ff_second_new,
    )


def solution(mesh):
    return jax.shard_map(
        plane_device if plane_fits(mesh) else per_device,
        mesh=mesh,
        in_specs=(
            P("dp", "seq", None),
            P("dp", None),
            P("dp", None),
            P("dp", None),
            P("dp"),
            P("seq", None),
            P("dp", "seq", None),
            P(("dp", "seq"), None),
            P(("dp", "seq"), None),
            P(None, ("dp", "seq")),
            P(("dp", "seq"), None),
            P(("dp", "seq"), None),
            P(("dp", "seq"), None),
            P(("dp", "seq"), None),
            P(("dp", "seq"), None),
            P(None, ("dp", "seq")),
            P(None, ("dp", "seq")),
            P(("dp", "seq"), None),
            P(("dp", "seq"), None),
        ),
        out_specs=(
            P("dp", "seq", None),
            P("dp", "seq", None),
            P(),
            P(("dp", "seq"), None),
            P(("dp", "seq"), None),
            P(None, ("dp", "seq")),
            P(("dp", "seq"), None),
            P(("dp", "seq"), None),
            P(("dp", "seq"), None),
            P(None, ("dp", "seq")),
            P(("dp", "seq"), None),
            P(("dp", "seq"), None),
            P(("dp", "seq"), None),
            P(None, ("dp", "seq")),
            P(("dp", "seq"), None),
        ),
        check_vma=False,
    )
```

```python
import functools

import jax
import jax.numpy as jnp
import numpy as np
from jax import lax
from jax.experimental import pallas as pl
from jax.experimental.pallas import tpu as pltpu
from jax.sharding import PartitionSpec as P

HEADS = 24
HDIM = 64
FF = 6144
UPDATE_STEP = 10


norm_eps = 1e-05
beta_first = 0.5
beta_second = 0.5
adam_eps = 1e-08
matrix_decay = 0.01
matrix_rate = 0.03
gain_rate = 0.25
clip_limit = 1.0
masked_score = -1e30


def layer_norm(values, gain_row, bias_row):
    center = values - jnp.mean(values, axis=-1, keepdims=True)
    spread = jnp.mean(center * center, axis=-1, keepdims=True)
    return center * lax.rsqrt(spread + norm_eps) * gain_row + bias_row


def rotary_tables(positions, head_size):
    half_size = head_size // 2
    frequency = 10000.0 ** (-jnp.arange(half_size, dtype=jnp.float32) / half_size)
    angles = positions.astype(jnp.float32)[:, None] * frequency[None, :]
    return (jnp.cos(angles)[:, None, :], jnp.sin(angles)[:, None, :])


def rotate(values, cosine_table, sine_table):
    half_size = values.shape[-1] // 2
    first_half = values[..., :half_size]
    second_half = values[..., half_size:]
    return jnp.concatenate(
        [
            first_half * cosine_table - second_half * sine_table,
            second_half * cosine_table + first_half * sine_table,
        ],
        axis=-1,
    )


def outer_sum(left_mat, right_mat):
    return lax.dot_general(
        left_mat, right_mat, (((0,), (0,)), ((), ())), preferred_element_type=jnp.float32
    )


def times_transposed(left_mat, right_mat):
    return lax.dot_general(
        left_mat, right_mat, (((1,), (1,)), ((), ())), preferred_element_type=jnp.float32
    )


def split_parts(values):
    upper = values.astype(jnp.bfloat16)
    lower = (values - upper.astype(jnp.float32)).astype(jnp.bfloat16)
    return (upper, lower)


def split_outer(left_low, right_full):
    upper, lower = split_parts(right_full)
    return outer_sum(left_low, upper) + outer_sum(left_low, lower)


def split_times_transposed(left_full, right_low):
    upper, lower = split_parts(left_full)
    return times_transposed(upper, right_low) + times_transposed(lower, right_low)


def self_scores(queries, keys, stamp_key, keep):
    score_scale = HDIM ** (-0.5)
    frame_part = (
        jnp.einsum("cqhd,ckhd->chqk", queries, keys, preferred_element_type=jnp.float32)
        * score_scale
    )
    frame_part = jnp.where(keep[:, None, None, :], frame_part, masked_score)
    stamp_part = (
        jnp.einsum("cqhd,chd->chq", queries, stamp_key, preferred_element_type=jnp.float32)
        * score_scale
    )
    return (frame_part, stamp_part)


def self_forward(queries, keys, values, stamp_key, stamp_value, keep):
    frame_scores, stamp_scores = self_scores(queries, keys, stamp_key, keep)
    top_score = jnp.maximum(jnp.max(frame_scores, axis=-1), stamp_scores)
    frame_expo = jnp.exp(frame_scores - top_score[..., None])
    stamp_expo = jnp.exp(stamp_scores - top_score)
    denom = jnp.sum(frame_expo, axis=-1) + stamp_expo
    self_lse = top_score + jnp.log(denom)
    frame_prob = (frame_expo / denom[..., None]).astype(jnp.bfloat16)
    stamp_prob = (stamp_expo / denom).astype(jnp.bfloat16)
    mixed = jnp.einsum(
        "chqk,ckhd->cqhd", frame_prob, values, preferred_element_type=jnp.float32
    ) + jnp.einsum("chq,chd->cqhd", stamp_prob, stamp_value, preferred_element_type=jnp.float32)
    return (mixed, self_lse)


def self_backward(queries, keys, values, stamp_key, stamp_value, keep, self_lse, grad_mixed):
    score_scale = HDIM ** (-0.5)
    frame_scores, stamp_scores = self_scores(queries, keys, stamp_key, keep)
    frame_prob = jnp.exp(frame_scores - self_lse[..., None])
    stamp_prob = jnp.exp(stamp_scores - self_lse)
    grad_frame_prob = jnp.einsum(
        "cqhd,ckhd->chqk", grad_mixed, values, preferred_element_type=jnp.float32
    )
    grad_stamp_prob = jnp.einsum(
        "cqhd,chd->chq", grad_mixed, stamp_value, preferred_element_type=jnp.float32
    )
    delta = jnp.sum(frame_prob * grad_frame_prob, axis=-1) + stamp_prob * grad_stamp_prob
    grad_frame_scores = (frame_prob * (grad_frame_prob - delta[..., None])).astype(jnp.bfloat16)
    grad_stamp_scores = (stamp_prob * (grad_stamp_prob - delta)).astype(jnp.bfloat16)
    grad_queries = (
        jnp.einsum("chqk,ckhd->cqhd", grad_frame_scores, keys, preferred_element_type=jnp.float32)
        + jnp.einsum(
            "chq,chd->cqhd", grad_stamp_scores, stamp_key, preferred_element_type=jnp.float32
        )
    ) * score_scale
    key_part = (
        jnp.einsum(
            "chqk,cqhd->ckhd", grad_frame_scores, queries, preferred_element_type=jnp.float32
        )
        * score_scale
    )
    value_part = jnp.einsum(
        "chqk,cqhd->ckhd",
        frame_prob.astype(jnp.bfloat16),
        grad_mixed,
        preferred_element_type=jnp.float32,
    )
    grad_stamp_key = (
        jnp.einsum("chq,cqhd->chd", grad_stamp_scores, queries, preferred_element_type=jnp.float32)
        * score_scale
    )
    grad_stamp_value = jnp.einsum(
        "chq,cqhd->chd",
        stamp_prob.astype(jnp.bfloat16),
        grad_mixed,
        preferred_element_type=jnp.float32,
    )
    return (grad_queries, key_part, value_part, grad_stamp_key, grad_stamp_value)


def cross_scores(query, keys, keep):
    score_scale = HDIM ** (-0.5)
    scores = (
        jnp.einsum("cqhd,ckhd->chqk", query, keys, preferred_element_type=jnp.float32) * score_scale
    )
    return jnp.where(keep[:, None, None, :], scores, masked_score)


def cross_forward(query, keys, values, keep):
    scores = cross_scores(query, keys, keep)
    top_score = jnp.max(scores, axis=-1)
    expo = jnp.exp(scores - top_score[..., None])
    denom = jnp.sum(expo, axis=-1)
    cross_lse = top_score + jnp.log(denom)
    prob = (expo / denom[..., None]).astype(jnp.bfloat16)
    mixed = jnp.einsum("chqk,ckhd->cqhd", prob, values, preferred_element_type=jnp.float32)
    return (mixed, cross_lse)


def cross_backward(query, keys, values, keep, cross_lse, grad_mixed):
    score_scale = HDIM ** (-0.5)
    prob = jnp.exp(cross_scores(query, keys, keep) - cross_lse[..., None])
    grad_prob = jnp.einsum(
        "cqhd,ckhd->chqk", grad_mixed, values, preferred_element_type=jnp.float32
    )
    delta = jnp.sum(prob * grad_prob, axis=-1)
    grad_scores = (prob * (grad_prob - delta[..., None])).astype(jnp.bfloat16)
    grad_query = (
        jnp.einsum("chqk,ckhd->cqhd", grad_scores, keys, preferred_element_type=jnp.float32)
        * score_scale
    )
    grad_keys = (
        jnp.einsum("chqk,cqhd->ckhd", grad_scores, query, preferred_element_type=jnp.float32)
        * score_scale
    )
    grad_values = jnp.einsum(
        "chqk,cqhd->ckhd", prob.astype(jnp.bfloat16), grad_mixed, preferred_element_type=jnp.float32
    )
    return (grad_query, grad_keys, grad_values)


def adam_step(weight, first, second, gradient, step_rate, decay_rate):
    first_new = beta_first * first + (1.0 - beta_first) * gradient
    second_new = beta_second * second + (1.0 - beta_second) * gradient * gradient
    fix_first = 1.0 - beta_first**UPDATE_STEP
    fix_second = 1.0 - beta_second**UPDATE_STEP
    normed_step = first_new / fix_first / (jnp.sqrt(second_new / fix_second) + adam_eps)
    return (weight - step_rate * (normed_step + decay_rate * weight), first_new, second_new)


def per_device(
    frames,
    time_token,
    cond_ids,
    cond_mask,
    lengths,
    cond_table,
    cotangent,
    attn_weight,
    cross_weight,
    norm_param,
    ff_weight,
    attn_first,
    attn_second,
    cross_first,
    cross_second,
    norm_first,
    norm_second,
    ff_first,
    ff_second,
):
    clip_count, frame_rows, wide = frames.shape
    hidden_width = FF
    token_count = clip_count * frame_rows
    seq_count = lax.axis_size("seq")
    seq_frames = frame_rows * seq_count
    seq_place = lax.axis_index("seq")
    vocab_rows = cond_table.shape[0]
    relative = cond_ids - seq_place * vocab_rows
    inside = (relative >= 0) & (relative < vocab_rows)
    picked = jnp.take(cond_table, jnp.clip(relative, 0, vocab_rows - 1), axis=0).astype(jnp.float32)
    picked = jnp.where(inside[..., None], picked, 0.0)
    cond = lax.psum(picked.astype(jnp.bfloat16), "seq")
    cond_count = cond.shape[1]
    cond_flat = cond.reshape(clip_count * cond_count, cond.shape[2])
    cond_width = cond.shape[2]
    cond_keep = cond_mask > 0
    attn_low = attn_weight.astype(jnp.bfloat16)
    cross_low = cross_weight.astype(jnp.bfloat16)
    norm_low = norm_param.astype(jnp.bfloat16)
    ff_low = ff_weight.astype(jnp.bfloat16)
    stream = frames.astype(jnp.float32).reshape(token_count, wide)
    stamps = time_token.astype(jnp.float32)
    positions = seq_place * frame_rows + jnp.arange(frame_rows)
    key_keep = jnp.arange(seq_frames)[None, :] < lengths[:, None]
    frame_valid = (positions[None, :] < lengths[:, None]).reshape(token_count)
    grad_out = cotangent.astype(jnp.float32).reshape(token_count, wide) * frame_valid[
        :, None
    ].astype(jnp.float32)
    grad_out_low = grad_out.astype(jnp.bfloat16)
    piece_heads = HEADS // seq_count
    piece_wide = wide // seq_count
    piece_ff = hidden_width // seq_count
    group_rows = clip_count * seq_frames

    def pieces():
        norm_copies = jnp.tile(norm_low[None], (1, 1, seq_count))
        moved_attn, moved_cross, moved_ff, moved_norm = (
            lax.all_to_all(
                attn_low.reshape(-1, 6, wide), "seq", split_axis=2, concat_axis=0, tiled=True
            ),
            lax.all_to_all(
                cross_low.reshape(-1, 2, wide), "seq", split_axis=2, concat_axis=0, tiled=True
            ),
            lax.all_to_all(
                ff_low.reshape(-1, 3, hidden_width), "seq", split_axis=2, concat_axis=0, tiled=True
            ),
            lax.all_to_all(norm_copies, "seq", split_axis=2, concat_axis=0, tiled=True),
        )
        attn_cols, cross_cols, ff_cols, norm_blocks = (
            lax.all_gather(moved_attn, "dp", axis=0, tiled=True),
            lax.all_gather(moved_cross, "dp", axis=0, tiled=True),
            lax.all_gather(moved_ff, "dp", axis=0, tiled=True),
            lax.all_gather(moved_norm, "dp", axis=0, tiled=True),
        )
        gains = norm_blocks.transpose(1, 0, 2).reshape(6, wide).astype(jnp.float32)
        return (attn_cols, cross_cols, ff_cols, gains)

    def collect(rows):
        whole = lax.all_gather(
            rows.reshape(clip_count, frame_rows, wide), "seq", axis=1, tiled=True
        )
        return whole.reshape(group_rows, wide)

    def spread(partial_value):
        mine = lax.psum_scatter(
            partial_value.reshape(clip_count, seq_frames, wide).astype(jnp.bfloat16),
            "seq",
            scatter_dimension=1,
            tiled=True,
        ).astype(jnp.float32)
        return mine.reshape(token_count, wide)

    attn_cols, cross_cols, ff_cols, gain_rows = pieces()
    group_shape = (clip_count, seq_frames, piece_heads, HDIM)
    cosine_table, sine_table = rotary_tables(jnp.arange(seq_frames), HDIM)
    normed_one = layer_norm(stream, gain_rows[0], gain_rows[1]).astype(jnp.bfloat16)
    group_one = collect(normed_one)
    projected = jnp.dot(
        group_one,
        attn_cols[:, :3].reshape(wide, 3 * piece_wide),
        preferred_element_type=jnp.float32,
    )
    queries = rotate(
        projected[:, :piece_wide].reshape(group_shape), cosine_table, sine_table
    ).astype(jnp.bfloat16)
    all_keys = rotate(
        projected[:, piece_wide : 2 * piece_wide].reshape(group_shape), cosine_table, sine_table
    ).astype(jnp.bfloat16)
    all_values = projected[:, 2 * piece_wide :].astype(jnp.bfloat16).reshape(group_shape)
    stamp_normed = layer_norm(stamps, gain_rows[0], gain_rows[1]).astype(jnp.bfloat16)
    stamp_pair = jnp.dot(
        stamp_normed,
        attn_cols[:, 1:3].reshape(wide, 2 * piece_wide),
        preferred_element_type=jnp.float32,
    )
    stamp_key = (
        stamp_pair[:, :piece_wide].astype(jnp.bfloat16).reshape(clip_count, piece_heads, HDIM)
    )
    stamp_value = (
        stamp_pair[:, piece_wide:].astype(jnp.bfloat16).reshape(clip_count, piece_heads, HDIM)
    )
    self_mixed, self_lse = self_forward(
        queries, all_keys, all_values, stamp_key, stamp_value, key_keep
    )
    self_low = self_mixed.astype(jnp.bfloat16).reshape(group_rows, piece_wide)
    resid_one = stream + spread(times_transposed(self_low, attn_cols[:, 3]))
    normed_two = layer_norm(resid_one, gain_rows[2], gain_rows[3]).astype(jnp.bfloat16)
    group_two = collect(normed_two)
    cross_query = jnp.dot(group_two, attn_cols[:, 4], preferred_element_type=jnp.float32)
    cross_query = cross_query.astype(jnp.bfloat16).reshape(group_shape)
    cond_pair = jnp.dot(
        cond_flat,
        cross_cols.reshape(cond_width, 2 * piece_wide),
        preferred_element_type=jnp.float32,
    )
    cond_shape = (clip_count, cond_count, piece_heads, HDIM)
    cross_keys = cond_pair[:, :piece_wide].astype(jnp.bfloat16).reshape(cond_shape)
    cross_values = cond_pair[:, piece_wide:].astype(jnp.bfloat16).reshape(cond_shape)
    cross_mixed, cross_lse = cross_forward(cross_query, cross_keys, cross_values, cond_keep)
    cross_low_out = cross_mixed.astype(jnp.bfloat16).reshape(group_rows, piece_wide)
    resid_two = resid_one + spread(times_transposed(cross_low_out, attn_cols[:, 5]))
    normed_three = layer_norm(resid_two, gain_rows[4], gain_rows[5]).astype(jnp.bfloat16)
    group_three = collect(normed_three)
    gate_up = jnp.dot(
        group_three, ff_cols[:, :2].reshape(wide, 2 * piece_ff), preferred_element_type=jnp.float32
    )
    gate_val = gate_up[:, :piece_ff]
    up_val = gate_up[:, piece_ff:]
    hidden = (jax.nn.silu(gate_val) * up_val).astype(jnp.bfloat16)
    branch = spread(times_transposed(hidden, ff_cols[:, 2]))
    layer_out = (resid_two + branch).astype(jnp.bfloat16).reshape(clip_count, frame_rows, wide)
    attn_cols, cross_cols, ff_cols, gain_rows = pieces()
    group_grad_out = collect(grad_out_low)
    grad_hidden = jnp.dot(group_grad_out, ff_cols[:, 2], preferred_element_type=jnp.float32)
    sigmoid_gate = jax.nn.sigmoid(gate_val)
    grad_gate = grad_hidden * up_val * sigmoid_gate * (1.0 + gate_val * (1.0 - sigmoid_gate))
    grad_up = grad_hidden * gate_val * sigmoid_gate
    grad_gate_up = jnp.concatenate([grad_gate, grad_up], axis=1).astype(jnp.bfloat16)
    grad_normed_three = spread(
        times_transposed(grad_gate_up, ff_cols[:, :2].reshape(wide, 2 * piece_ff))
    )
    _, norm_three_back = jax.vjp(layer_norm, resid_two, gain_rows[4], gain_rows[5])
    grad_two_part, grad_gain_three, grad_bias_three = norm_three_back(grad_normed_three)
    grad_two = grad_out + grad_two_part
    grad_cross_branch = grad_two.astype(jnp.bfloat16)
    group_cross_branch = collect(grad_cross_branch)
    grad_cross_mixed = jnp.dot(
        group_cross_branch, attn_cols[:, 5], preferred_element_type=jnp.float32
    )
    grad_cross_mixed = grad_cross_mixed.astype(jnp.bfloat16).reshape(group_shape)
    grad_cross_query, grad_cross_keys, grad_cross_values = cross_backward(
        cross_query, cross_keys, cross_values, cond_keep, cross_lse, grad_cross_mixed
    )
    grad_cross_query = grad_cross_query.astype(jnp.bfloat16).reshape(group_rows, piece_wide)
    grad_normed_two = spread(times_transposed(grad_cross_query, attn_cols[:, 4]))
    _, norm_two_back = jax.vjp(layer_norm, resid_one, gain_rows[2], gain_rows[3])
    grad_one_part, grad_gain_two, grad_bias_two = norm_two_back(grad_normed_two)
    grad_one = grad_two + grad_one_part
    grad_self_branch = grad_one.astype(jnp.bfloat16)
    group_self_branch = collect(grad_self_branch)
    grad_self_mixed = jnp.dot(
        group_self_branch, attn_cols[:, 3], preferred_element_type=jnp.float32
    )
    grad_self_mixed = grad_self_mixed.astype(jnp.bfloat16).reshape(group_shape)
    grad_queries, key_part, value_part, grad_stamp_key, grad_stamp_value = self_backward(
        queries, all_keys, all_values, stamp_key, stamp_value, key_keep, self_lse, grad_self_mixed
    )
    grad_query_raw = (
        rotate(grad_queries, cosine_table, -sine_table)
        .astype(jnp.bfloat16)
        .reshape(group_rows, piece_wide)
    )
    grad_key_raw = (
        rotate(key_part, cosine_table, -sine_table)
        .astype(jnp.bfloat16)
        .reshape(group_rows, piece_wide)
    )
    grad_value = value_part.astype(jnp.bfloat16).reshape(group_rows, piece_wide)
    grad_project = jnp.concatenate([grad_query_raw, grad_key_raw, grad_value], axis=1)
    grad_normed_one = spread(
        times_transposed(grad_project, attn_cols[:, :3].reshape(wide, 3 * piece_wide))
    )
    stamp_grad = jnp.concatenate(
        [
            grad_stamp_key.reshape(clip_count, piece_wide),
            grad_stamp_value.reshape(clip_count, piece_wide),
        ],
        axis=1,
    )
    grad_stamp_normed = split_times_transposed(
        stamp_grad, attn_cols[:, 1:3].reshape(wide, 2 * piece_wide)
    )
    _, norm_one_back = jax.vjp(layer_norm, stream, gain_rows[0], gain_rows[1])
    grad_zero_part, grad_gain_one, grad_bias_one = norm_one_back(grad_normed_one)
    _, norm_stamp_back = jax.vjp(layer_norm, stamps, gain_rows[0], gain_rows[1])
    _, grad_gain_stamp, grad_bias_stamp = norm_stamp_back(grad_stamp_normed)
    frames_grad = (grad_one + grad_zero_part).reshape(clip_count, frame_rows, wide)
    project_grad = outer_sum(group_one, grad_project)
    stamp_weight_grad = split_outer(stamp_normed, stamp_grad)
    attn_piece = jnp.stack(
        [
            project_grad[:, :piece_wide],
            project_grad[:, piece_wide : 2 * piece_wide] + stamp_weight_grad[:, :piece_wide],
            project_grad[:, 2 * piece_wide :] + stamp_weight_grad[:, piece_wide:],
            outer_sum(group_self_branch, self_low),
            outer_sum(group_two, grad_cross_query),
            outer_sum(group_cross_branch, cross_low_out),
        ],
        axis=1,
    )
    cond_grad = jnp.concatenate(
        [
            grad_cross_keys.reshape(clip_count * cond_count, piece_wide),
            grad_cross_values.reshape(clip_count * cond_count, piece_wide),
        ],
        axis=1,
    )
    cross_piece = split_outer(cond_flat, cond_grad).reshape(cond_width, 2, piece_wide)
    ff_piece = jnp.stack(
        [
            outer_sum(group_three, grad_gate_up[:, :piece_ff]),
            outer_sum(group_three, grad_gate_up[:, piece_ff:]),
            outer_sum(group_grad_out, hidden),
        ],
        axis=1,
    )
    norm_grad = jnp.stack(
        [
            grad_gain_one + grad_gain_stamp,
            grad_bias_one + grad_bias_stamp,
            grad_gain_two,
            grad_bias_two,
            grad_gain_three,
            grad_bias_three,
        ],
        axis=0,
    )
    norm_column = norm_grad.T[:, :, None]
    summed_attn, summed_cross, summed_ff, summed_norm = (
        lax.psum_scatter(
            attn_piece.astype(jnp.bfloat16), "dp", scatter_dimension=0, tiled=True
        ).astype(jnp.float32),
        lax.psum_scatter(
            cross_piece.astype(jnp.bfloat16), "dp", scatter_dimension=0, tiled=True
        ).astype(jnp.float32),
        lax.psum_scatter(
            ff_piece.astype(jnp.bfloat16), "dp", scatter_dimension=0, tiled=True
        ).astype(jnp.float32),
        lax.psum_scatter(
            norm_column.astype(jnp.bfloat16), "dp", scatter_dimension=0, tiled=True
        ).astype(jnp.float32),
    )
    owned_attn, owned_cross, owned_ff, owned_norm = (
        lax.all_to_all(
            summed_attn.astype(jnp.bfloat16), "seq", split_axis=0, concat_axis=2, tiled=True
        ).astype(summed_attn.dtype),
        lax.all_to_all(
            summed_cross.astype(jnp.bfloat16), "seq", split_axis=0, concat_axis=2, tiled=True
        ).astype(summed_cross.dtype),
        lax.all_to_all(
            summed_ff.astype(jnp.bfloat16), "seq", split_axis=0, concat_axis=2, tiled=True
        ).astype(summed_ff.dtype),
        lax.all_to_all(
            summed_norm.astype(jnp.bfloat16), "seq", split_axis=0, concat_axis=2, tiled=True
        ).astype(summed_norm.dtype),
    )
    attn_reduced = owned_attn.reshape(owned_attn.shape[0], 6 * wide)
    cross_reduced = owned_cross.reshape(owned_cross.shape[0], 2 * wide)
    ff_reduced = owned_ff.reshape(owned_ff.shape[0], 3 * hidden_width)
    norm_reduced = jnp.sum(owned_norm, axis=2).T
    local_squares = (
        jnp.sum(attn_reduced * attn_reduced)
        + jnp.sum(cross_reduced * cross_reduced)
        + jnp.sum(norm_reduced * norm_reduced)
        + jnp.sum(ff_reduced * ff_reduced)
    )
    total_squares = lax.psum(local_squares, ("dp", "seq"))
    grad_norm = jnp.sqrt(total_squares)
    factor = jnp.minimum(1.0, clip_limit / grad_norm)
    attn_new, attn_first_new, attn_second_new = adam_step(
        attn_weight, attn_first, attn_second, attn_reduced * factor, matrix_rate, matrix_decay
    )
    cross_new, cross_first_new, cross_second_new = adam_step(
        cross_weight, cross_first, cross_second, cross_reduced * factor, matrix_rate, matrix_decay
    )
    norm_new, norm_first_new, norm_second_new = adam_step(
        norm_param, norm_first, norm_second, norm_reduced * factor, gain_rate, 0.0
    )
    ff_new, ff_first_new, ff_second_new = adam_step(
        ff_weight, ff_first, ff_second, ff_reduced * factor, matrix_rate, matrix_decay
    )
    return (
        layer_out,
        frames_grad,
        grad_norm,
        attn_new,
        cross_new,
        norm_new,
        ff_new,
        attn_first_new,
        cross_first_new,
        norm_first_new,
        ff_first_new,
        attn_second_new,
        cross_second_new,
        norm_second_new,
        ff_second_new,
    )


MESH = pl.DeviceIdType.MESH
DMA = pltpu.SemaphoreType.DMA
VMEM_LIMIT = 60 * 2**20


def plane_fits(mesh):
    return mesh.shape["dp"] == 8 and mesh.shape["dp"] % mesh.shape["seq"] == 0


def plane_places():
    place = lax.axis_index("dp")
    return (place, lax.axis_index("seq"), lambda mask: jnp.bitwise_xor(place, mask))


def greet(partners):
    barrier = pltpu.get_barrier_semaphore()
    for partner in partners:
        pl.semaphore_signal(barrier, inc=1, device_id=partner, device_id_type=MESH)
    pl.semaphore_wait(barrier, len(partners))


def remote(source, goal, send_sem, recv_sem, device):
    return pltpu.make_async_remote_copy(
        src_ref=source,
        dst_ref=goal,
        send_sem=send_sem,
        recv_sem=recv_sem,
        device_id=device,
        device_id_type=MESH,
    )


def communicating(collective_id):
    return pltpu.CompilerParams(
        has_side_effects=True, collective_id=collective_id, vmem_limit_bytes=VMEM_LIMIT
    )


def any_spec():
    return pl.BlockSpec(memory_space=pl.ANY)


def greet_cross(group, planes):
    place, depth, flip = plane_places()
    greet(
        [(flip(mask), depth) for mask in range(1, group)]
        + [(place, lax.rem(depth + step, planes)) for step in range(1, planes)]
    )


def outward_steps(group, planes, kept_ref, own_ref, mid, *sems):
    far_send, far_recv, near_send, near_recv, local_sem = sems
    place, depth, flip = plane_places()
    per = group // planes
    first = []
    for step in range(1, planes):
        origin = lax.rem(depth + step, planes)
        for slot in range(per):
            clip = per * depth + slot
            copy = remote(
                kept_ref.at[slot, origin],
                mid.at[clip],
                far_send.at[slot, step],
                far_recv.at[clip],
                (place, origin),
            )
            copy.start()
            first.append(copy)
    second = []

    def hand_over(block, clip):
        index = len(second)
        away = remote(
            block, own_ref.at[place], near_send.at[index], near_recv.at[place], (clip, depth)
        )
        stay = pltpu.make_async_copy(block, own_ref.at[place], local_sem.at[index])
        pl.when(clip != place)(away.start)
        pl.when(clip == place)(stay.start)
        second.append((clip, away, stay))

    for slot in range(per):
        hand_over(kept_ref.at[slot, depth], per * depth + slot)
    yield
    for step in range(1, planes):
        source = lax.rem(depth + step, planes)
        for slot in range(per):
            clip = per * source + slot
            block = mid.at[clip]
            remote(
                block, block, far_send.at[0, 0], far_recv.at[clip], (place, source)
            ).wait_recv()
            hand_over(block, clip)
    yield
    for mask in range(1, group):
        other = flip(mask)
        block = own_ref.at[other]
        remote(block, block, near_send.at[0], near_recv.at[other], (other, depth)).wait_recv()
    for clip, away, stay in second:
        pl.when(clip != place)(away.wait_send)
        pl.when(clip == place)(stay.wait)
    for copy in first:
        copy.wait_send()
    yield


def outward_scratch(group, planes):
    return [
        DMA((group // planes, planes)),
        DMA((group,)),
        DMA((group,)),
        DMA((group,)),
        DMA((group,)),
    ]


def settle_body(group, planes, dones, kept_ref, cut_ref, parts_ref, squares_ref, *refs):
    done_refs, refs = refs[:dones], refs[dones:]
    own_ref, mine_ref, norm_ref, total_ref, mid, terms, block, blocks, *sems = refs
    part_send, part_recv, block_send, block_recv, *sems = sems
    place, depth, flip = plane_places()
    devices = [(flip(mask), lax.rem(depth + step, planes)) for mask, step in everyone(planes)]
    greet(devices)
    here = place * planes + depth
    start_swap, end_swap = swap_beside(
        [(lambda other: cut_ref.at[other], lambda other: mine_ref.at[other])], *sems[:3]
    )
    start_swap()
    copies = []
    for index, (other, plane) in enumerate(devices):
        copy = remote(
            parts_ref.at[other * planes + plane],
            terms.at[here],
            part_send.at[index],
            part_recv.at[here],
            (other, plane),
        )
        copy.start()
        copies.append(copy)
    rows = outward_steps(group, planes, kept_ref, own_ref, mid, *sems[3:])
    next(rows)
    terms[here] = parts_ref[here]

    def squares_of(array_ref):
        values = [array_ref[piece].astype(jnp.float32) for piece in range(array_ref.shape[0])]
        return jnp.sum(sum(value * value for value in values))

    squares = squares_ref[0, 0]
    for done_ref in done_refs:
        squares = squares + squares_of(done_ref)
    for other, plane in devices:
        source = other * planes + plane
        one = terms.at[source]
        remote(one, one, part_send.at[0], part_recv.at[source], (other, plane)).wait_recv()
    norm_sum = jnp.sum(terms[...], axis=0)
    norm_ref[...] = norm_sum
    squares = squares + jnp.sum(norm_sum * norm_sum)
    end_swap()
    squares = squares + squares_of(mine_ref)
    block[...] = jnp.full(block.shape, squares)
    blocks[here] = block[...]
    for index, (other, plane) in enumerate(devices):
        copy = remote(
            block, blocks.at[here], block_send.at[index], block_recv.at[here], (other, plane)
        )
        copy.start()
        copies.append(copy)
    next(rows)
    next(rows)
    for other, plane in devices:
        source = other * planes + plane
        one = blocks.at[source]
        remote(one, one, block_send.at[0], block_recv.at[source], (other, plane)).wait_recv()
    total_ref[...] = jnp.sum(blocks[...], axis=0)
    for copy in copies:
        copy.wait_send()


def settle(kept_rows, cut, done, norm_parts, squares, collective_id):
    per, planes, rows, wide = kept_rows.shape
    group = per * planes
    count = norm_parts.shape[0]
    inside = pl.BlockSpec(memory_space=pltpu.VMEM)
    like = lambda shape, array: jax.ShapeDtypeStruct(shape, array.dtype)
    *results, _ = pl.pallas_call(
        functools.partial(settle_body, group, planes, len(done)),
        out_shape=[
            like((group, rows, wide), kept_rows),
            like(cut.shape, cut),
            like(norm_parts.shape[1:], norm_parts),
            like((8, 128), norm_parts),
            like((group, rows, wide), kept_rows),
        ],
        in_specs=[any_spec(), any_spec(), inside, pl.BlockSpec(memory_space=pltpu.SMEM)]
        + [inside] * len(done),
        out_specs=[any_spec()] + [inside] * 3 + [any_spec()],
        scratch_shapes=[
            pltpu.VMEM(norm_parts.shape, jnp.float32),
            pltpu.VMEM((8, 128), jnp.float32),
            pltpu.VMEM((count, 8, 128), jnp.float32),
            DMA((count,)),
            DMA((count,)),
            DMA((count,)),
            DMA((count,)),
        ]
        + swap_beside_scratch(1)
        + outward_scratch(group, planes),
        compiler_params=communicating(collective_id),
    )(kept_rows, cut, norm_parts, squares, *done)
    return results


def everyone(planes):
    return [(mask, step) for mask in range(8) for step in range(planes) if mask or step]


def to_plane_features(values, group, planes):
    width = values.shape[1] // (group * planes)
    starts = [
        (owner * planes + plane) * width for plane in range(planes) for owner in range(group)
    ]
    return jnp.concatenate([values[:, start : start + width] for start in starts], axis=1)


def to_whole_features(values, group, planes):
    width = values.shape[1] // (group * planes)
    starts = [
        (plane * group + owner) * width for owner in range(group) for plane in range(planes)
    ]
    return jnp.concatenate([values[:, start : start + width] for start in starts], axis=1)


def enter_body(
    group,
    planes,
    frames_ref,
    grads_ref,
    valid_ref,
    norm_ref,
    pack_ref,
    attn_ref,
    cross_ref,
    ff_ref,
    kept_ref,
    gains_ref,
    packs_ref,
    first_mine_ref,
    rest_mine_ref,
    ff_low_ref,
    grads_mid_ref,
    mid,
    norms_ref,
    pieces,
    grad_pieces,
    attn_full,
    cross_full,
    first_cut,
    rest_cut,
    ff_full,
    ff_low,
    load_sem,
    near_send,
    near_recv,
    far_send,
    far_recv,
    local_sem,
    norm_send,
    norm_recv,
    swap_send,
    swap_recv,
    stay_sem,
):
    place, depth, flip = plane_places()
    per = group // planes
    low = pieces.dtype
    f32 = jnp.float32
    others = everyone(planes)
    loads = [
        pltpu.make_async_copy(source, goal, load_sem.at[which])
        for which, (source, goal) in enumerate(
            ((attn_ref, attn_full), (cross_ref, cross_full), (ff_ref, ff_full))
        )
    ]
    for copy in loads:
        copy.start()
    own = to_plane_features(frames_ref[...].astype(f32), group, planes).astype(low)
    pieces[...] = own.reshape(pieces.shape)
    greet([(flip(mask), lax.rem(depth + step, planes)) for mask, step in others])
    here = place * planes + depth
    first = []
    for mask in (6, 7, 2, 3, 4, 5, 1):
        other = flip(mask)
        copy = remote(
            pieces.at[other],
            mid.at[place],
            near_send.at[mask],
            near_recv.at[mask],
            (other, depth),
        )
        copy.start()
        first.append((mask, copy))
    small = []
    for index, (mask, step) in enumerate(others):
        copy = remote(
            norm_ref,
            norms_ref.at[here],
            norm_send.at[index],
            norm_recv.at[here],
            (flip(mask), lax.rem(depth + step, planes)),
        )
        copy.start()
        small.append(copy)
    swaps = []

    def swap(which, source, goal):
        for mask in (6, 7, 2, 3, 4, 5, 1):
            other = flip(mask)
            copy = remote(
                source(other),
                goal.at[place],
                swap_send.at[which, mask],
                swap_recv.at[which, mask],
                (other, depth),
            )
            copy.start()
            swaps.append(copy)
        stay = pltpu.make_async_copy(source(place), goal.at[place], stay_sem.at[which])
        stay.start()
        stays.append(stay)

    stays = []
    swap(0, lambda other: pack_ref, packs_ref)
    norms_ref[here] = norm_ref[...]
    loads[0].wait()
    loads[1].wait()
    wide = attn_full.shape[1] // 6
    piece = wide // group
    for device in range(group):
        for block in range(6):
            cut_ref = (first_cut, rest_cut)[block // 3]
            start = block * wide + device * piece
            cut_ref[device, :, block % 3 * piece : (block % 3 + 1) * piece] = attn_full[
                :, start : start + piece
            ].astype(low)
        keys = cross_full[:, device * piece : (device + 1) * piece]
        values = cross_full[:, wide + device * piece : wide + (device + 1) * piece]
        rest_cut[device, :, 3 * piece :] = jnp.concatenate([keys, values], axis=0).astype(low)
    swap(1, lambda other: first_cut.at[other], first_mine_ref)
    swap(2, lambda other: rest_cut.at[other], rest_mine_ref)
    second = []
    arrivals = dict(first)
    for mask in (0, 1, 2, 3, 4, 5, 6, 7):
        source = flip(mask)
        goal, slot = lax.div(source, per), lax.rem(source, per)
        block = pieces.at[place]
        if mask:
            arrivals[mask].wait_recv()
            block = mid.at[source]
        away = remote(
            block,
            kept_ref.at[slot, depth],
            far_send.at[mask],
            far_recv.at[slot, depth],
            (place, goal),
        )
        stay = pltpu.make_async_copy(block, kept_ref.at[slot, depth], local_sem.at[mask])
        pl.when(goal != depth)(away.start)
        pl.when(goal == depth)(stay.start)
        second.append((goal, away, stay))
    grads = to_plane_features(grads_ref[...].astype(f32) * valid_ref[...], group, planes)
    grad_pieces[...] = grads.astype(low).reshape(grad_pieces.shape)
    grads_store = pltpu.make_async_copy(grad_pieces, grads_mid_ref, stay_sem.at[3])
    grads_store.start()
    loads[2].wait()
    tile = ff_full.shape[1] // 24

    def round_tile(index, carry):
        lanes = pl.ds(pl.multiple_of(index * tile, 128), tile)
        ff_low[:, lanes] = ff_full[:, lanes].astype(low)
        return carry

    lax.fori_loop(0, 24, round_tile, 0)
    ff_store = pltpu.make_async_copy(ff_low, ff_low_ref, load_sem.at[3])
    ff_store.start()
    for mask, step in others:
        source = flip(mask) * planes + lax.rem(depth + step, planes)
        block = norms_ref.at[source]
        remote(
            block,
            block,
            norm_send.at[0],
            norm_recv.at[source],
            (flip(mask), lax.rem(depth + step, planes)),
        ).wait_recv()
    width = gains_ref.shape[1] // (group * planes)
    gains_ref[...] = jnp.concatenate(
        [
            norms_ref[owner * planes + plane, :, :width]
            for plane in range(planes)
            for owner in range(group)
        ],
        axis=1,
    )
    for slot in range(per):
        for origin in range(planes):
            block = kept_ref.at[slot, origin]
            pl.when(origin != depth)(
                remote(
                    block,
                    block,
                    far_send.at[0],
                    far_recv.at[slot, origin],
                    (place, lax.rem(depth + 1, planes)),
                ).wait_recv
            )
    ff_store.wait()
    grads_store.wait()
    for copy in swaps:
        copy.wait()
    for stay in stays:
        stay.wait()
    for goal, away, stay in second:
        pl.when(goal != depth)(away.wait_send)
        pl.when(goal == depth)(stay.wait)
    for mask, copy in first:
        copy.wait_send()
    for copy in small:
        copy.wait_send()


def enter(frames, grads, valid, norm_block, pack, attn, cross, ff, planes, collective_id):
    rows, wide = frames.shape
    group = 8
    count = group * planes
    piece = rows // group
    owned = attn.shape[0]
    third = attn.shape[1] // (2 * group)
    rest = third + cross.shape[0] * cross.shape[1] // (owned * group)
    low, f32 = jnp.bfloat16, jnp.float32
    inside = pl.BlockSpec(memory_space=pltpu.VMEM)
    like = jax.ShapeDtypeStruct
    *results, _ = pl.pallas_call(
        functools.partial(enter_body, group, planes),
        out_shape=[
            like((group // planes, planes, piece, wide), low),
            like((norm_block.shape[0], wide), f32),
            like((group,) + pack.shape, f32),
            like((group, owned, third), low),
            like((group, owned, rest), low),
            like(ff.shape, low),
            like((group, piece, wide), low),
            like((group, piece, wide), low),
        ],
        in_specs=[inside] * 4 + [any_spec()] * 4,
        out_specs=[any_spec(), inside] + [any_spec()] * 6,
        scratch_shapes=[
            pltpu.VMEM((count,) + norm_block.shape, f32),
            pltpu.VMEM((group, piece, wide), low),
            pltpu.VMEM((group, piece, wide), low),
            pltpu.VMEM(attn.shape, f32),
            pltpu.VMEM(cross.shape, f32),
            pltpu.VMEM((group, owned, third), low),
            pltpu.VMEM((group, owned, rest), low),
            pltpu.VMEM(ff.shape, f32),
            pltpu.VMEM(ff.shape, low),
            DMA((4,)),
            DMA((group,)),
            DMA((group,)),
            DMA((group,)),
            DMA((group // planes, planes)),
            DMA((group,)),
            DMA((count,)),
            DMA((count,)),
            DMA((4, group)),
            DMA((4, group)),
            DMA((4,)),
        ],
        compiler_params=communicating(collective_id),
    )(frames, grads, valid, norm_block, pack, attn, cross, ff)
    return results


def cond_steps(group, planes, pick_ref, cond_ref, parts, summed, *sems):
    part_send, part_recv, cond_send, cond_recv = sems
    place, depth, flip = plane_places()
    pushes = []
    for step in range(1, planes):
        goal = lax.rem(depth + step, planes)
        copy = remote(
            pick_ref.at[goal],
            parts.at[depth],
            part_send.at[step],
            part_recv.at[depth],
            (place, goal),
        )
        copy.start()
        pushes.append(copy)
    yield
    total = pick_ref[depth].astype(jnp.float32)
    for step in range(1, planes):
        source = lax.rem(depth + step, planes)
        block = parts.at[source]
        remote(
            block, block, part_send.at[0], part_recv.at[source], (place, source)
        ).wait_recv()
        total = total + parts[source].astype(jnp.float32)
    summed[...] = total.astype(summed.dtype)
    cond_ref[place] = total.astype(summed.dtype)
    for mask in range(1, group):
        copy = remote(
            summed,
            cond_ref.at[place],
            cond_send.at[mask],
            cond_recv.at[mask],
            (flip(mask), depth),
        )
        copy.start()
        pushes.append(copy)
    yield
    for mask in range(1, group):
        block = cond_ref.at[flip(mask)]
        remote(
            block, block, cond_send.at[0], cond_recv.at[mask], (flip(mask), depth)
        ).wait_recv()
    for copy in pushes:
        copy.wait_send()
    yield


def inward_over(group, planes, mid_ref, kept_ref, send_sem, recv_sem, local_sem):
    place, depth, flip = plane_places()
    per = group // planes

    def piece(source):
        goal, slot = lax.div(source, per), lax.rem(source, per)
        block = mid_ref.at[source]
        away = remote(
            block,
            kept_ref.at[slot, depth],
            send_sem.at[source],
            recv_sem.at[slot, depth],
            (place, goal),
        )
        stay = pltpu.make_async_copy(block, kept_ref.at[slot, depth], local_sem.at[source])
        return goal != depth, away, stay

    def begin():
        for source in range(group):
            leaves, away, stay = piece(source)
            pl.when(leaves)(away.start)
            pl.when(jnp.logical_not(leaves))(stay.start)

    def end():
        for slot in range(per):
            for origin in range(planes):
                block = kept_ref.at[slot, origin]
                pl.when(origin != depth)(
                    remote(
                        block,
                        block,
                        send_sem.at[0],
                        recv_sem.at[slot, origin],
                        (place, lax.rem(depth + 1, planes)),
                    ).wait_recv
                )
        for source in range(group):
            leaves, away, stay = piece(source)
            pl.when(leaves)(away.wait_send)
            pl.when(jnp.logical_not(leaves))(stay.wait)

    return begin, end


def dot_tiles(left, right_ref, span, transposed, width):
    first, last = span
    count = right_ref.shape[0] if transposed else last - first
    for start in range(0, count, width):
        stop = min(start + width, count)
        if transposed:
            yield start, stop, times_transposed(left, right_ref[start:stop, first:last])
        else:
            yield start, stop, jnp.dot(
                left, right_ref[:, first + start : first + stop], preferred_element_type=jnp.float32
            )


def window_of(matrix, span):
    first, last = span or (0, matrix.shape[1])
    start = first // 128 * 128
    while (matrix.shape[1] - start) * 2 > matrix.shape[1] and start and start % 384:
        start -= 128
    stop = min(-(-last // 128) * 128, matrix.shape[1])
    return (start, stop - start), (first - start, last - start)


def cross_shares(queries, pair_ref, bias_ref):
    wide = queries[0].shape[1]
    keys = [
        (clip, start, pair_ref[clip, :, start : start + HDIM])
        for clip in range(len(queries))
        for start in range(0, wide, HDIM)
    ]
    scores = [
        times_transposed(queries[clip][:, start : start + HDIM], key) * HDIM ** (-0.5)
        + bias_ref[clip]
        for clip, start, key in keys
    ]
    tops = [jnp.max(score, axis=1, keepdims=True) for score in scores]
    expos = [jnp.exp(score - top) for score, top in zip(scores, tops)]
    sums = [jnp.sum(expo, axis=1, keepdims=True) for expo in expos]
    return keys, [expo / total for expo, total in zip(expos, sums)]


def by_clip_of(results, clips, low):
    heads = len(results) // clips
    return [
        jnp.concatenate(results[clip * heads : (clip + 1) * heads], axis=1).astype(low)
        for clip in range(clips)
    ]


def cross_rows(queries, pair_ref, bias_ref):
    low, wide = queries[0].dtype, queries[0].shape[1]
    keys, shares = cross_shares(queries, pair_ref, bias_ref)
    mixed = [
        jnp.dot(
            share.astype(low),
            pair_ref[clip, :, wide + start : wide + start + HDIM],
            preferred_element_type=jnp.float32,
        )
        for (clip, start, _), share in zip(keys, shares)
    ]
    return by_clip_of(mixed, len(queries), low)


def cross_rows_back(queries, grads, pair_ref, bias_ref, pair_grad_ref):
    low, wide = queries[0].dtype, queries[0].shape[1]
    scale = HDIM ** (-0.5)
    keys, shares = cross_shares(queries, pair_ref, bias_ref)
    own_grads = [grads[clip][:, start : start + HDIM] for clip, start, _ in keys]
    grad_shares = [
        times_transposed(grad, pair_ref[clip, :, wide + start : wide + start + HDIM])
        for (clip, start, _), grad in zip(keys, own_grads)
    ]
    deltas = [
        jnp.sum(share * grad_share, axis=1, keepdims=True)
        for share, grad_share in zip(shares, grad_shares)
    ]
    scores = [
        (share * (grad_share - delta)).astype(low)
        for share, grad_share, delta in zip(shares, grad_shares, deltas)
    ]
    results = [
        jnp.dot(score, key, preferred_element_type=jnp.float32) * scale
        for score, (_, _, key) in zip(scores, keys)
    ]
    key_grads = [
        outer_sum(score, queries[clip][:, start : start + HDIM]) * scale
        for score, (clip, start, _) in zip(scores, keys)
    ]
    value_grads = [
        outer_sum(share.astype(low), grad) for share, grad in zip(shares, own_grads)
    ]
    heads = len(keys) // len(queries)
    for clip in range(len(queries)):
        mine = slice(clip * heads, (clip + 1) * heads)
        pair_grad_ref[clip] += jnp.concatenate(key_grads[mine] + value_grads[mine], axis=1)
    return by_clip_of(results, len(queries), low)


def outer_columns(out_ref, start, small, big):
    width = small.shape[-1]
    product = outer_sum(small.reshape(-1, width), big.reshape(-1, big.shape[-1]))
    out_ref[:, start : start + width] = product.T.astype(out_ref.dtype)


def by_slot_loads(source, goal, sem):
    clips = source.shape[0]
    return [
        pltpu.make_async_copy(source.at[clip, slot], goal.at[slot, clip], sem.at[slot, clip])
        for slot in range(8)
        for clip in range(clips)
    ]


def gather_parts(clips, rows, sub, mode, window, span, ins, outs_refs, scratch):
    ins, outs_refs, scratch = list(ins), list(outs_refs), list(scratch)
    mat_ref = ins.pop(0) if mode != "rows" else None
    gates_ref = ins.pop(0) if mode == "gates" else None
    pair_ref, bias_ref = (ins.pop(0), ins.pop(0)) if mode in ("cross", "cross_back") else (None, None)
    query_ref = ins.pop(0) if mode == "cross_back" else None
    all_ref = outs_refs.pop(0)
    pair_grad_ref = outs_refs.pop() if mode == "cross_back" else None
    prod_refs = outs_refs
    take = lambda count: [scratch.pop(0) for _ in range(count)]
    held, send_sem, recv_sem, all_sem = take(4)
    mat, mat_sem = take(2) if mode != "rows" else (None, None)
    stages = take(len(prod_refs))
    prod_sem = take(1)[0] if prod_refs else None
    gates, gates_sem = take(2) if mode == "gates" else (None, None)
    queries, query_sem = take(2) if mode == "cross_back" else (None, None)
    place, depth, flip = plane_places()
    core, beside_x, beside_y, across = flip(1), flip(2), flip(4), flip(6)
    loads = []
    gate_loads = {}
    if mode != "rows":
        loads.append(pltpu.make_async_copy(mat_ref.at[:, pl.ds(*window)], mat, mat_sem))
    if mode == "cross_back":
        loads.append(pltpu.make_async_copy(query_ref, queries, query_sem))
    if mode == "gates":
        for mask in (0, 1, 2, 4, 3, 5, 6, 7):
            slot = flip(mask)
            gate_loads[mask] = [
                pltpu.make_async_copy(
                    gates_ref.at[clip, slot], gates.at[slot, clip], gates_sem.at[slot, clip]
                )
                for clip in range(clips)
            ]

    def load():
        if mode == "cross_back":
            pair_grad_ref[...] = jnp.zeros_like(pair_grad_ref)
        for copy in loads + [copy for copies in gate_loads.values() for copy in copies]:
            copy.start()

    chunks = [(clip, part) for clip in range(clips) for part in range(rows // sub)]
    count = len(chunks)
    half = count // 2
    sends = []

    def view(slot, index):
        clip, part = chunks[index]
        return held.at[slot, clip, pl.ds(part * sub, sub)]

    def send(slot, index, device):
        block = view(slot, index)
        copy = remote(
            block, block, send_sem.at[len(sends)], recv_sem.at[slot, index], (device, depth)
        )
        copy.start()
        sends.append(copy)

    def arrived(slot, index):
        block = view(slot, index)
        remote(
            block, block, send_sem.at[0], recv_sem.at[slot, index], (core, depth)
        ).wait_recv()

    x_order = list(range(count))
    y_order = list(range(half, count)) + list(range(half))

    def put(index, values):
        clip, part = chunks[index]
        held[place, clip, pl.ds(part * sub, sub)] = values.astype(held.dtype)
        if index < half:
            send(place, index, beside_x)
        else:
            send(place, index, beside_y)
        send(place, index, core)
        if index == count - 1:
            for low in range(half):
                send(place, half + low, beside_x)
                send(place, low, beside_y)

    outs = []

    def leave_here(source, goal, sem, major):
        for clip in range(clips):
            there = goal.at[major, clip] if goal.shape[0] == 8 else goal.at[clip, major]
            copy = pltpu.make_async_copy(source.at[major, clip], there, sem.at[major, clip])
            copy.start()
            outs.append(copy)

    def multiply(mask):
        slot = flip(mask)
        leave_here(held, all_ref, all_sem, slot)
        if mode == "rows":
            return
        left = held[slot].reshape(clips * rows, held.shape[3])
        for copy in gate_loads.get(mask, ()):
            copy.wait()
        for start, stop, product in dot_tiles(
            left, mat, span, False, 256 * (1 if mode == "gates" else 3)
        ):
            product = product.reshape(clips, rows, stop - start)
            if mode == "cross":
                query = product.astype(stages[0].dtype)
                stages[0][slot] = query
                mixed = cross_rows([query[clip] for clip in range(clips)], pair_ref, bias_ref)
                for clip in range(clips):
                    stages[1][slot, clip] = mixed[clip]
                continue
            if mode == "cross_back":
                grad = product.astype(stages[0].dtype)
                results = cross_rows_back(
                    [queries[clip, slot] for clip in range(clips)],
                    [grad[clip] for clip in range(clips)],
                    pair_ref,
                    bias_ref,
                    pair_grad_ref,
                )
                for clip in range(clips):
                    stages[0][slot, clip] = results[clip]
                continue
            if mode == "dot":
                stages[0][slot, :, :, start:stop] = product.astype(stages[0].dtype)
                continue
            width = stages[1].shape[3]
            gate = gates[slot, :, :, start:stop]
            up = gates[slot, :, :, width + start : width + stop]
            sigmoid = jax.nn.sigmoid(gate)
            active = gate * sigmoid
            low = stages[0].dtype
            stages[0][slot, :, :, start:stop] = (
                product * up * sigmoid * (1.0 + gate * (1.0 - sigmoid))
            ).astype(low)
            stages[0][slot, :, :, width + start : width + stop] = (product * active).astype(low)
            stages[1][slot, :, :, start:stop] = (active * up).astype(low)
        for which, (stage, prod_ref) in enumerate(zip(stages, prod_refs)):
            leave_here(stage, prod_ref, prod_sem.at[which], slot)

    def run(late=lambda: None):
        for copy in loads:
            copy.wait()
        multiply(0)
        for step in range(count):
            x_index, y_index = x_order[step], y_order[step]
            arrived(beside_x, x_index)
            if x_index < half:
                send(beside_x, x_index, beside_y)
            send(beside_x, x_index, core)
            arrived(beside_y, y_index)
            if y_index >= half:
                send(beside_y, y_index, beside_x)
            send(beside_y, y_index, core)
            if step == 0:
                for index in range(count):
                    arrived(core, index)
                multiply(1)
        late()
        multiply(2)
        for step in range(half):
            for index in (x_order[step], y_order[step]):
                arrived(across, index)
                send(across, index, core)
            if step == 0:
                multiply(4)
        for mask in (3, 5):
            for index in range(count):
                arrived(flip(mask), index)
            multiply(mask)
        multiply(6)
        for index in range(count):
            arrived(flip(7), index)
        multiply(7)
        for copy in outs:
            copy.wait()
        for copy in sends:
            copy.wait_send()

    return load, put, run


def chunk_order(clips, rows, sub):
    half = clips * (rows // sub) // 2
    return [index for low in range(half) for index in (low, half + low)]


def gather_plan(clips, rows, wide, sub, matrix, kind, gate_up, span, pair, bias, query):
    count = clips * (rows // sub)
    low = jnp.bfloat16
    inside = pl.BlockSpec(memory_space=pltpu.VMEM)
    by_clip = lambda columns, of: jax.ShapeDtypeStruct((clips, 8, rows, columns), of)
    by_device = lambda columns, of: jax.ShapeDtypeStruct((8, clips, rows, columns), of)
    mode = "rows" if matrix is None else "dot"
    if gate_up is not None:
        mode = "gates"
    if pair is not None:
        mode = "cross" if query is None else "cross_back"
    window = inner = None
    args, in_specs = [], []
    outs = [by_device(wide, low) if mode == "gates" else by_clip(wide, low)]
    scratch = [
        pltpu.VMEM((8, clips, rows, wide), low),
        DMA((7 * count,)),
        DMA((8, count)),
        DMA((8, clips)),
    ]
    if mode != "rows":
        window, inner = window_of(matrix, span)
        columns = inner[1] - inner[0]
        args.append(matrix)
        in_specs.append(any_spec())
        scratch += [pltpu.VMEM((wide, window[1]), low), DMA(())]
    if mode == "dot":
        outs.append(by_clip(columns, kind))
        scratch += [pltpu.VMEM((8, clips, rows, columns), kind), DMA((1, 8, clips))]
    if mode == "gates":
        args.append(gate_up.reshape(clips, 8, rows, 2 * columns))
        in_specs.append(any_spec())
        outs += [by_clip(2 * columns, low), by_device(columns, low)]
        scratch += [
            pltpu.VMEM((8, clips, rows, 2 * columns), low),
            pltpu.VMEM((8, clips, rows, columns), low),
            DMA((2, 8, clips)),
            pltpu.VMEM((8, clips, rows, 2 * columns), jnp.float32),
            DMA((8, clips)),
        ]
    if mode == "cross":
        args += [pair, bias]
        in_specs += [inside] * 2
        outs += [by_clip(columns, low)] * 2
        scratch += [pltpu.VMEM((8, clips, rows, columns), low)] * 2 + [DMA((2, 8, clips))]
    out_specs = [any_spec()] * len(outs)
    if mode == "cross_back":
        args += [pair, bias, query.reshape(clips, 8, rows, columns)]
        in_specs += [inside, inside, any_spec()]
        outs += [by_clip(columns, low), jax.ShapeDtypeStruct(pair.shape, jnp.float32)]
        out_specs += [any_spec(), inside]
        scratch += [
            pltpu.VMEM((8, clips, rows, columns), low),
            DMA((1, 8, clips)),
            pltpu.VMEM((clips, 8, rows, columns), low),
            DMA(()),
        ]
    return (mode, window, inner), args, in_specs, outs, out_specs, scratch


def flat_rows(results):
    return [
        block.reshape(-1, block.shape[3]) if len(block.shape) == 4 else block for block in results
    ]


def gather_dot_body(clips, rows, sub, normed, plan, beside, outer, counts, own_ref, *refs):
    refs = list(refs)
    take = lambda count: [refs.pop(0) for _ in range(count)]
    gain_ref = take(1)[0] if normed else None
    ins = take(counts[0])
    pick_ref = take(1)[0] if beside else None
    past_ref, mixed_ref = take(2) if outer else (None, None)
    outs = take(counts[1])
    cond_ref = take(1)[0] if beside else None
    outer_ref = take(1)[0] if outer else None
    scratch = take(counts[2])
    load, put, run = gather_parts(clips, rows, sub, *plan, ins, outs, scratch)
    load()
    if outer:
        past, mixed, past_sem, mixed_sem = refs
        outer_loads = by_slot_loads(past_ref, past, past_sem)
        outer_loads += by_slot_loads(mixed_ref, mixed, mixed_sem)
        for copy in outer_loads:
            copy.start()
    place, depth, flip = plane_places()
    if beside:
        greet_cross(*beside)
        cond = cond_steps(*beside, pick_ref, cond_ref, *refs)
        next(cond)
    else:
        greet([(flip(1), depth), (flip(2), depth), (flip(4), depth)])
    for index in chunk_order(clips, rows, sub):
        clip, part = divmod(index, rows // sub)
        values = own_ref[clip, pl.ds(part * sub, sub)]
        if normed:
            values = layer_norm(values.astype(jnp.float32), gain_ref[0:1], gain_ref[1:2])
        put(index, values)
    if beside:
        run(lambda: next(cond))
        next(cond)
    else:
        run()
    if outer:
        for copy in outer_loads:
            copy.wait()
        held, queries = scratch[0], scratch[6]
        outer_columns(outer_ref, 0, queries[...], past[...])
        outer_columns(outer_ref, queries.shape[3], mixed[...], held[...])


def gather_dot(
    own_rows,
    matrix,
    kind,
    collective_id,
    gains=None,
    picked=None,
    gate_up=None,
    span=None,
    pair=None,
    bias=None,
    query=None,
    outer=None,
    sub=64,
):
    clips, rows, wide = own_rows.shape
    plan, args, in_specs, outs, out_specs, scratch = gather_plan(
        clips, rows, wide, sub, matrix, kind, gate_up, span, pair, bias, query
    )
    inside = pl.BlockSpec(memory_space=pltpu.VMEM)
    counts = (len(args), len(outs), len(scratch))
    if gains is not None:
        args, in_specs = [gains] + args, [inside] + in_specs
    args, in_specs = [own_rows] + args, [inside] + in_specs
    beside = None
    if picked is not None:
        planes, per, tokens, cond_wide = picked.shape
        beside = (planes * per, planes)
        args.append(picked)
        in_specs.append(inside)
        outs.append(jax.ShapeDtypeStruct((8, per, tokens, cond_wide), picked.dtype))
        out_specs.append(inside)
        scratch += [
            pltpu.VMEM(picked.shape, picked.dtype),
            pltpu.VMEM(picked.shape[1:], picked.dtype),
            DMA((planes,)),
            DMA((planes,)),
            DMA((8,)),
            DMA((8,)),
        ]
    if outer is not None:
        past, mixed = outer
        width = mixed.shape[1]
        args += [past.reshape(clips, 8, rows, wide), mixed.reshape(clips, 8, rows, width)]
        in_specs += [any_spec()] * 2
        outs.append(jax.ShapeDtypeStruct((wide, 2 * width), jnp.bfloat16))
        out_specs.append(inside)
        scratch += [
            pltpu.VMEM((8, clips, rows, wide), jnp.bfloat16),
            pltpu.VMEM((8, clips, rows, width), jnp.bfloat16),
            DMA((8, clips)),
            DMA((8, clips)),
        ]
    results = pl.pallas_call(
        functools.partial(
            gather_dot_body,
            clips,
            rows,
            sub,
            gains is not None,
            plan,
            beside,
            outer is not None,
            counts,
        ),
        out_shape=outs,
        in_specs=in_specs,
        out_specs=out_specs,
        scratch_shapes=scratch,
        compiler_params=communicating(collective_id),
    )(*args)
    return flat_rows(results[: counts[1]]) + list(results[counts[1] :])


def reduce_steps(clips, rows, sub, multiply, final, terms, pair, turn, from_x, from_y, *sems):
    send_sem, core_sem, turn_sem, x_sem, y_sem = sems
    place, depth, flip = plane_places()
    core, beside_x, beside_y = flip(1), flip(2), flip(4)
    chunks = [(clip, part) for clip in range(clips) for part in range(rows // sub)]
    count = len(chunks)
    half = count // 2
    sends = []

    def send(source, goal, recv_sem, device):
        copy = remote(source, goal, send_sem.at[len(sends)], recv_sem, (device, depth))
        copy.start()
        sends.append(copy)

    def arrived(block, recv_sem):
        remote(block, block, send_sem.at[0], recv_sem, (core, depth)).wait_recv()

    def term(number, index):
        clip, part = chunks[index]
        return terms.at[number, clip, pl.ds(part * sub, sub)]

    def give(number, chip):
        for index in range(count):
            send(term(number, index), pair.at[index, chip], core_sem.at[index, chip], core)

    def total(*blocks):
        return sum(block[...].astype(jnp.float32) for block in blocks)

    def add(block, other):
        block[...] = total(block, other).astype(terms.dtype)

    numbers = {3: 1, 1: 3, 2: 5, 0: 7}

    def combine(chip, index):
        arrived(pair.at[index, chip], core_sem.at[index, chip])
        block = term(numbers[chip], index)
        add(block, pair.at[index, chip])
        return block

    multiply(0)
    give(0, 3)
    multiply(1)
    multiply(2)
    give(2, 1)
    for low in range(half):
        high = half + low
        send(combine(3, low), turn.at[low], turn_sem.at[low], beside_x)
        send(combine(3, high), turn.at[high], turn_sem.at[high], beside_y)
    multiply(3)
    multiply(4)
    give(4, 2)
    for low in range(half):
        send(combine(1, low), from_x.at[low], x_sem.at[low], beside_x)
    multiply(5)
    for high in range(half, count):
        send(combine(2, high), from_y.at[high], y_sem.at[high], beside_y)
    multiply(6)
    give(6, 0)
    multiply(7)
    yield
    for low in range(half):
        high = half + low
        block = combine(2, low)
        arrived(turn.at[low], turn_sem.at[low])
        add(block, turn.at[low])
        send(block, from_y.at[low], y_sem.at[low], beside_y)
        block = combine(1, high)
        arrived(turn.at[high], turn_sem.at[high])
        add(block, turn.at[high])
        send(block, from_x.at[high], x_sem.at[high], beside_x)
    yield
    for index in chunk_order(clips, rows, sub):
        clip, part = chunks[index]
        arrived(pair.at[index, 0], core_sem.at[index, 0])
        arrived(from_x.at[index], x_sem.at[index])
        arrived(from_y.at[index], y_sem.at[index])
        result = total(term(7, index), pair.at[index, 0], from_x.at[index], from_y.at[index])
        final(index, clip, pl.ds(part * sub, sub), result)
    yield
    for copy in sends:
        copy.wait_send()
    yield


def plane_order():
    place, depth, flip = plane_places()
    return [flip(mask) for mask in (7, 6, 3, 2, 5, 4, 1, 0)]


def reduce_scratch(clips, rows, sub, wide):
    count = clips * (rows // sub)
    low = jnp.bfloat16
    return [
        pltpu.VMEM((8, clips, rows, wide), low),
        pltpu.VMEM((count, 4, sub, wide), low),
        pltpu.VMEM((count, sub, wide), low),
        pltpu.VMEM((count, sub, wide), low),
        pltpu.VMEM((count, sub, wide), low),
        DMA((7 * count,)),
        DMA((count, 4)),
        DMA((count,)),
        DMA((count,)),
        DMA((count,)),
    ]


def norm_back(values, gain, grad):
    center = values - jnp.mean(values, axis=1, keepdims=True)
    inverse = lax.rsqrt(jnp.mean(center * center, axis=1, keepdims=True) + norm_eps)
    unit = center * inverse
    stats = [
        jnp.sum(grad * unit, axis=0, keepdims=True),
        jnp.sum(grad, axis=0, keepdims=True),
    ]
    scaled = grad * gain
    result = inverse * (
        scaled
        - jnp.mean(scaled, axis=1, keepdims=True)
        - unit * jnp.mean(scaled * unit, axis=1, keepdims=True)
    )
    return result, stats


def final_back(values_ref, gain_ref, base_ref, sum_ref, stats_ref, order=None):
    def final(index, clip, span, result):
        if values_ref is not None:
            result, stats = norm_back(values_ref[clip, span], gain_ref[...], result)
            for which, row in enumerate(stats):
                row = row + stats_ref[which : which + 1] if index else row
                stats_ref[which : which + 1] = row
        result = base_ref[clip, span].astype(jnp.float32) + result
        if order:
            result = to_whole_features(result, *order)
        sum_ref[clip, span] = result.astype(sum_ref.dtype)
        return result

    return final


def terms_of(clips, rows, blocks, mat, span, terms):
    def multiply(number):
        block = blocks(number)
        block = block.reshape(clips * rows, block.shape[-1])
        for start, stop, product in dot_tiles(block, mat, span, True, 256 * 2):
            terms[number, :, :, start:stop] = product.astype(terms.dtype).reshape(
                clips, rows, stop - start
            )

    return multiply


def dot_reduce_body(clips, rows, sub, window, span, back, order, swapped, left_ref, mat_ref, base_ref, *refs):
    refs = list(refs)
    take = lambda count: [refs.pop(0) for _ in range(count)]
    values_ref, gain_ref = take(2) if back else (None, None)
    cut_ref = take(1)[0] if swapped else None
    sum_ref = take(1)[0]
    stats_ref = take(1)[0] if back else None
    mine_ref = take(1)[0] if swapped else None
    left, mat, mat_sem, left_sem = take(4)
    swap_sems = take(3) if swapped else None
    terms = refs[0]
    place, depth, flip = plane_places()
    load = pltpu.make_async_copy(mat_ref.at[:, pl.ds(*window)], mat, mat_sem)
    load.start()
    loads = {}
    for number, slot in enumerate(plane_order()):
        loads[number] = [
            pltpu.make_async_copy(
                left_ref.at[clip, slot], left.at[number, clip], left_sem.at[number, clip]
            )
            for clip in range(clips)
        ]
        for copy in loads[number]:
            copy.start()
    if swapped:
        start_swap, end_swap = swap_beside(
            [(lambda other: cut_ref.at[other], lambda other: mine_ref.at[other])], *swap_sems
        )
        greet([(flip(mask), depth) for mask in range(1, 8)])
        start_swap()
    else:
        greet([(flip(1), depth), (flip(2), depth), (flip(4), depth)])
    load.wait()

    def blocks(number):
        for copy in loads[number]:
            copy.wait()
        return left[number]

    steps = reduce_steps(
        clips,
        rows,
        sub,
        terms_of(clips, rows, blocks, mat, span, terms),
        final_back(values_ref, gain_ref, base_ref, sum_ref, stats_ref, order),
        *refs,
    )
    for _ in steps:
        pass
    if swapped:
        end_swap()


def dot_reduce(
    left,
    matrix,
    clips,
    collective_id,
    base,
    span=None,
    back=None,
    kind=jnp.float32,
    order=None,
    cut=None,
    sub=64,
):
    wide = matrix.shape[0]
    rows, inner = left.shape[0] // (8 * clips), left.shape[1]
    low = jnp.bfloat16
    window, span = window_of(matrix, span)
    inside = pl.BlockSpec(memory_space=pltpu.VMEM)
    args = [left.reshape(clips, 8, rows, inner), matrix, base]
    in_specs = [any_spec(), any_spec(), inside]
    outs, out_specs = [jax.ShapeDtypeStruct((clips, rows, wide), kind)], [inside]
    if back is not None:
        args += list(back)
        in_specs += [inside] * 2
        outs.append(jax.ShapeDtypeStruct((2, wide), jnp.float32))
        out_specs.append(inside)
    swap_sems = []
    if cut is not None:
        args.append(cut)
        in_specs.append(any_spec())
        outs.append(jax.ShapeDtypeStruct(cut.shape, cut.dtype))
        out_specs.append(any_spec())
        swap_sems = swap_beside_scratch(1)
    return pl.pallas_call(
        functools.partial(
            dot_reduce_body,
            clips,
            rows,
            sub,
            window,
            span,
            back is not None,
            order,
            cut is not None,
        ),
        out_shape=outs,
        in_specs=in_specs,
        out_specs=out_specs,
        scratch_shapes=[
            pltpu.VMEM((8, clips, rows, inner), low),
            pltpu.VMEM((wide, window[1]), low),
            DMA(()),
            DMA((8, clips)),
        ]
        + swap_sems
        + reduce_scratch(clips, rows, sub, wide),
        compiler_params=communicating(collective_id),
    )(*args)


def add_steps(parts_ref, sum_ref, landed, send_sem, recv_sem, local_sem):
    place, depth, flip = plane_places()
    planes = parts_ref.shape[0]
    copies = []
    for step in range(1, planes):
        goal = lax.rem(depth + step, planes)
        copy = remote(
            parts_ref.at[goal],
            landed.at[depth],
            send_sem.at[step],
            recv_sem.at[depth],
            (place, goal),
        )
        copy.start()
        copies.append(copy)
    stay = pltpu.make_async_copy(parts_ref.at[depth], landed.at[depth], local_sem)
    stay.start()
    yield
    stay.wait()
    for step in range(1, planes):
        source = lax.rem(depth + step, planes)
        block = landed.at[source]
        remote(block, block, send_sem.at[0], recv_sem.at[source], (place, source)).wait_recv()
    sum_ref[...] = jnp.sum(landed[...].astype(jnp.float32), axis=0).astype(sum_ref.dtype)
    for copy in copies:
        copy.wait_send()
    yield


def reduce_gather_body(
    clips, rows, sub, spans, back, normed, plan, counts, passing, outer, leaving, adding, left_ref, mat_ref, base_ref, *refs
):
    refs = list(refs)
    take = lambda count: [refs.pop(0) for _ in range(count)]
    values_ref, back_gain_ref = take(2) if back else (None, None)
    gain_ref = take(1)[0] if normed else None
    ins = take(counts[0])
    mid_ref = take(1)[0] if passing else None
    low_ref, ending_ref = take(2) if outer else (None, None)
    leaving_ref = take(1)[0] if leaving else None
    adding_ref = take(1)[0] if adding else None
    sum_ref = take(1)[0]
    stats_ref = take(1)[0] if back else None
    outs = take(counts[1])
    kept_ref = take(1)[0] if passing else None
    outer_ref = take(1)[0] if outer else None
    own_ref, own_mid = take(2) if leaving else (None, None)
    added_ref = take(1)[0] if adding else None
    left, mat, mat_sem, left_sem = take(4)
    terms, *others = reduce_refs = take(10)
    gather_scratch = take(counts[2])
    load, put, run = gather_parts(clips, rows, sub, *plan, ins, outs, gather_scratch)
    window, span = spans
    place, depth, flip = plane_places()
    mat_load = pltpu.make_async_copy(mat_ref.at[:, pl.ds(*window)], mat, mat_sem)
    mat_load.start()
    loads = {}
    for number, slot in enumerate(plane_order()):
        loads[number] = [
            pltpu.make_async_copy(
                left_ref.at[clip, slot], left.at[number, clip], left_sem.at[number, clip]
            )
            for clip in range(clips)
        ]
        for copy in loads[number]:
            copy.start()
    load()
    if outer:
        low, low_sem = take(2)
        outer_loads = by_slot_loads(low_ref, low, low_sem)
        for copy in outer_loads:
            copy.start()
    if adding:
        adder = add_steps(adding_ref, added_ref, *take(4))
    if passing:
        greet_cross(*passing)
        pass_rows, end_rows = inward_over(*passing, mid_ref, kept_ref, *refs)
        pass_rows()
    elif leaving:
        greet_cross(*leaving)
        going = outward_steps(*leaving, leaving_ref, own_ref, own_mid, *refs)
        next(going)
    else:
        greet([(flip(1), depth), (flip(2), depth), (flip(4), depth)])
    mat_load.wait()

    def blocks(number):
        for copy in loads[number]:
            copy.wait()
        return left[number]

    keep = final_back(values_ref, back_gain_ref, base_ref, sum_ref, stats_ref)

    def final(index, clip, span_rows, result):
        result = keep(index, clip, span_rows, result)
        if normed:
            result = layer_norm(result, gain_ref[0:1], gain_ref[1:2])
        put(index, result)

    steps = reduce_steps(
        clips,
        rows,
        sub,
        terms_of(clips, rows, blocks, mat, span, terms),
        final,
        *reduce_refs,
    )

    next(steps)
    next(steps)
    next(steps)
    if adding:
        next(adder)
    run((lambda: next(going)) if leaving else (lambda: None))
    if outer:
        for copy in outer_loads:
            copy.wait()
        outer_columns(outer_ref, 0, low[...], gather_scratch[0][...])
        outer_ref[:, low.shape[3] :] = ending_ref[...]
    next(steps)
    if passing:
        end_rows()
    if leaving:
        next(going)
    if adding:
        next(adder)


def reduce_gather(
    left,
    matrix,
    clips,
    collective_id,
    base,
    second,
    kind=jnp.bfloat16,
    span=None,
    back=None,
    gains=None,
    second_span=None,
    pair=None,
    bias=None,
    passing=None,
    outer=None,
    leaving=None,
    adding=None,
    sub=64,
):
    wide = matrix.shape[0]
    rows, inner = left.shape[0] // (8 * clips), left.shape[1]
    low = jnp.bfloat16
    spans = window_of(matrix, span)
    inside = pl.BlockSpec(memory_space=pltpu.VMEM)
    plan, more, more_specs, outs, out_specs, more_scratch = gather_plan(
        clips, rows, wide, sub, second, kind, None, second_span, pair, bias, None
    )
    counts = (len(more), len(outs), len(more_scratch))
    args = [left.reshape(clips, 8, rows, inner), matrix, base]
    in_specs = [any_spec(), any_spec(), inside]
    first_outs = [jax.ShapeDtypeStruct((clips, rows, wide), jnp.float32)]
    scratch = [
        pltpu.VMEM((8, clips, rows, inner), low),
        pltpu.VMEM((wide, spans[0][1]), low),
        DMA(()),
        DMA((8, clips)),
    ] + reduce_scratch(clips, rows, sub, wide)
    if back is not None:
        args += list(back)
        in_specs += [inside] * 2
        first_outs.append(jax.ShapeDtypeStruct((2, wide), jnp.float32))
    if gains is not None:
        args.append(gains)
        in_specs.append(inside)
    args += more
    in_specs += more_specs
    scratch += more_scratch
    outs = first_outs + outs
    out_specs = [inside] * len(first_outs) + out_specs
    flat = len(outs)
    if passing is not None:
        group, piece, _ = passing.shape
        planes = group // clips
        args.append(passing)
        in_specs.append(any_spec())
        outs.append(jax.ShapeDtypeStruct((clips, planes, piece, wide), passing.dtype))
        out_specs.append(any_spec())
        scratch += [DMA((group,)), DMA((clips, planes)), DMA((group,))]
    if outer is not None:
        low_rows, ending = outer
        columns = low_rows.shape[1]
        args += [low_rows.reshape(clips, 8, rows, columns), ending]
        in_specs += [any_spec(), inside]
        outs.append(jax.ShapeDtypeStruct((wide, columns + ending.shape[1]), low))
        out_specs.append(inside)
        scratch += [pltpu.VMEM((8, clips, rows, columns), low), DMA((8, clips))]
    if leaving is not None:
        per, planes, piece, _ = leaving.shape
        group = per * planes
        args.append(leaving)
        in_specs.append(any_spec())
        outs += [jax.ShapeDtypeStruct((group, piece, wide), leaving.dtype)] * 2
        leaving_mid = len(outs) - 1
        out_specs += [any_spec()] * 2
    if adding is not None:
        args.append(adding)
        in_specs.append(any_spec())
        outs.append(jax.ShapeDtypeStruct(adding.shape[1:], adding.dtype))
        out_specs.append(inside)
        scratch += [
            pltpu.VMEM(adding.shape, adding.dtype),
            DMA((adding.shape[0],)),
            DMA((adding.shape[0],)),
            DMA(()),
        ]
    if leaving is not None:
        scratch += outward_scratch(group, planes)
    results = pl.pallas_call(
        functools.partial(
            reduce_gather_body,
            clips,
            rows,
            sub,
            spans,
            back is not None,
            gains is not None,
            plan,
            counts,
            passing is not None and (group, planes),
            outer is not None,
            leaving is not None and (group, planes),
            adding is not None,
        ),
        out_shape=outs,
        in_specs=in_specs,
        out_specs=out_specs,
        scratch_shapes=scratch,
        compiler_params=communicating(collective_id),
    )(*args)
    first = len(first_outs)
    if leaving is not None:
        results = [block for which, block in enumerate(results) if which != leaving_mid]
    return list(results[:first]) + flat_rows(results[first:flat]) + list(results[flat:])


def ff_outer_body(
    order_of,
    clips,
    rows,
    sub,
    gates_ref,
    hidden_ref,
    down_ref,
    normed_ref,
    grads_ref,
    values_ref,
    layer_ref,
    outer_ref,
    gates,
    hidden,
    down,
    normed,
    grads,
    stage,
    load_sem,
    tile_sem,
    stage_sem,
    *reduce_refs,
):
    place, depth, flip = plane_places()
    order = plane_order()
    loads = [
        pltpu.make_async_copy(source, goal, load_sem.at[which])
        for which, (source, goal) in enumerate(
            ((down_ref, down), (hidden_ref, hidden), (gates_ref, gates))
        )
    ]
    for copy in loads:
        copy.start()
    tile = stage.shape[1]
    tiles = normed_ref.shape[3] // tile
    total_rows = 8 * clips * rows
    inner = gates.shape[3]

    def fetch(index):
        return [
            pltpu.make_async_copy(
                source.at[:, :, :, pl.ds(index * tile, tile)],
                goal.at[index % 2],
                tile_sem.at[which, index % 2],
            )
            for which, (source, goal) in enumerate(((normed_ref, normed), (grads_ref, grads)))
        ]

    def stored(index):
        return pltpu.make_async_copy(
            stage.at[index % 2],
            outer_ref.at[pl.ds(index * tile, tile)],
            stage_sem.at[index % 2],
        )

    def outer_tile(index):
        spot = index % 2
        if index >= 2:
            stored(index - 2).wait()
        for copy in fetch(index):
            copy.wait()
        stage[spot, :, :inner] = outer_sum(
            normed[spot].reshape(total_rows, tile), gates[...].reshape(total_rows, inner)
        ).astype(stage.dtype)
        stage[spot, :, inner:] = outer_sum(
            grads[spot].reshape(total_rows, tile),
            hidden[...].reshape(total_rows, hidden.shape[3]),
        ).astype(stage.dtype)
        stored(index).start()
        if index + 2 < tiles:
            for copy in fetch(index + 2):
                copy.start()

    for index in range(2):
        for copy in fetch(index):
            copy.start()
    greet([(flip(1), depth), (flip(2), depth), (flip(4), depth)])
    loads[0].wait()
    loads[1].wait()

    def layer_rows(index, clip, span, result):
        result = to_whole_features(values_ref[clip, span] + result, *order_of)
        layer_ref[clip, span] = result.astype(layer_ref.dtype)

    steps = reduce_steps(
        clips,
        rows,
        sub,
        terms_of(
            clips, rows, lambda number: hidden[order[number]], down, (0, down.shape[1]), reduce_refs[0]
        ),
        layer_rows,
        *reduce_refs,
    )
    next(steps)
    loads[2].wait()
    outer_tile(0)
    next(steps)
    for index in range(1, tiles):
        outer_tile(index)
    next(steps)
    for index in range(max(tiles - 2, 0), tiles):
        stored(index).wait()
    next(steps)


def ff_outer(gates, hidden, down, normed, grads, values, planes, collective_id, sub=64):
    clips, rows, wide = values.shape
    low = jnp.bfloat16
    inner, columns = gates.shape[1], gates.shape[1] + hidden.shape[1]
    tile = 512
    inside = pl.BlockSpec(memory_space=pltpu.VMEM)
    return pl.pallas_call(
        functools.partial(ff_outer_body, (8, planes), clips, rows, sub),
        out_shape=[
            jax.ShapeDtypeStruct((clips, rows, wide), low),
            jax.ShapeDtypeStruct((wide, columns), low),
        ],
        in_specs=[any_spec()] * 5 + [inside],
        out_specs=[inside, any_spec()],
        scratch_shapes=[
            pltpu.VMEM((clips, 8, rows, inner), low),
            pltpu.VMEM((8, clips, rows, hidden.shape[1]), low),
            pltpu.VMEM(down.shape, low),
            pltpu.VMEM((2, clips, 8, rows, tile), low),
            pltpu.VMEM((2, 8, clips, rows, tile), low),
            pltpu.VMEM((2, tile, columns), low),
            DMA((3,)),
            DMA((2, 2)),
            DMA((2,)),
        ]
        + reduce_scratch(clips, rows, sub, wide),
        compiler_params=communicating(collective_id),
    )(
        gates.reshape(clips, 8, rows, inner),
        hidden.reshape(8, clips, rows, hidden.shape[1]),
        down,
        normed.reshape(clips, 8, rows, wide),
        grads.reshape(8, clips, rows, wide),
        values,
    )


def rotary_lanes(places):
    half = HDIM // 2
    frequency = 10000.0 ** (-np.arange(half, dtype=np.float32) / np.float32(half))
    angles = places.astype(np.float32)[:, None] * frequency.astype(np.float32)[None, :]
    cosine, sine = np.cos(angles), np.sin(angles)
    both = [
        np.concatenate([cosine] * 4, axis=1),
        np.concatenate([-sine, sine, -sine, sine], axis=1),
    ]
    return jnp.asarray(np.stack(both).astype(np.float32))


def turn_heads(values, cosine, sine):
    lane = lax.broadcasted_iota(jnp.int32, values.shape, 1)
    half = HDIM // 2
    ahead = pltpu.roll(values, 2 * HDIM - half, 1)
    behind = pltpu.roll(values, half, 1)
    other = jnp.where(lax.rem(lane, HDIM) < half, ahead, behind)
    return values * cosine + other * sine


def swap_beside(pairs, send_sem, recv_sem, local_sem):
    place, depth, flip = plane_places()

    def each(act):
        for which, (source, goal) in enumerate(pairs):
            for mask in (6, 7, 2, 3, 4, 5, 1):
                other = flip(mask)
                act(
                    remote(
                        source(other),
                        goal(place),
                        send_sem.at[which, mask],
                        recv_sem.at[which, mask],
                        (other, depth),
                    )
                )

    stays = [
        pltpu.make_async_copy(source(place), goal(place), local_sem.at[which])
        for which, (source, goal) in enumerate(pairs)
    ]

    def begin():
        each(lambda copy: copy.start())
        for stay in stays:
            stay.start()

    def end():
        each(lambda copy: copy.wait())
        for stay in stays:
            stay.wait()

    return begin, end


def swap_beside_scratch(count):
    return [DMA((count, 8)), DMA((count, 8)), DMA((count,))]


def flash_forward_body(
    heads,
    tile,
    normed_ref,
    mat_ref,
    stamp_ref,
    bias_ref,
    rotary_ref,
    ff_ref,
    own_ref,
    turned_ref,
    out_ref,
    lse_ref,
    gate_up_ref,
    down_ref,
    mid_ref,
    raw_ref,
    *sems,
):
    group = gate_up_ref.shape[0]
    hidden = down_ref.shape[2]
    step, last = pl.program_id(0), pl.num_programs(0) - 1

    def columns(block):
        return lambda other: ff_ref.at[
            :, pl.ds(pl.multiple_of((block * group + other) * hidden, 128), hidden)
        ]

    start_swap, end_swap = swap_beside(
        [
            (lambda other: own_ref.at[other], lambda other: mid_ref.at[other]),
            (columns(0), lambda other: gate_up_ref.at[other, :, pl.ds(0, hidden)]),
            (columns(1), lambda other: gate_up_ref.at[other, :, pl.ds(hidden, hidden)]),
            (columns(2), lambda other: down_ref.at[other]),
        ],
        *sems,
    )
    place, depth, flip = plane_places()

    @pl.when(step == 0)
    def _():
        greet([(flip(mask), depth) for mask in range(1, group)])
        start_swap()

    def project(index, carry):
        place = pl.ds(pl.multiple_of(index * tile, tile), tile)
        raw_ref[place, :] = jnp.dot(
            normed_ref[place, :], mat_ref[...], preferred_element_type=jnp.float32
        )
        return carry

    lax.fori_loop(0, raw_ref.shape[0] // tile, project, 0)
    wide = heads * HDIM
    for pair in range(2 * wide // 128):
        lanes = slice(pair * 128, pair * 128 + 128)
        turned_ref[:, lanes] = turn_heads(
            raw_ref[:, lanes], rotary_ref[0], rotary_ref[1]
        ).astype(turned_ref.dtype)
    turned_ref[:, 2 * wide :] = raw_ref[:, 2 * wide :].astype(turned_ref.dtype)
    rows = raw_ref.shape[0]
    bias = bias_ref[0]
    scale = HDIM**-0.5
    for head in range(heads):
        lanes = slice(head * HDIM, head * HDIM + HDIM)
        keys = turned_ref[:, wide + head * HDIM : wide + head * HDIM + HDIM]
        values = turned_ref[:, 2 * wide + head * HDIM : 2 * wide + head * HDIM + HDIM]
        stamp_key = stamp_ref[0, :, lanes].astype(jnp.float32)
        stamp_value = stamp_ref[
            0, :, wide + head * HDIM : wide + head * HDIM + HDIM
        ].astype(jnp.float32)

        def one(step, carry):
            place = pl.ds(pl.multiple_of(step * tile, tile), tile)
            query = turned_ref[place, lanes] * jnp.asarray(scale, turned_ref.dtype)
            scores = times_transposed(query, keys) + bias
            stamp_score = jnp.sum(query.astype(jnp.float32) * stamp_key, axis=1, keepdims=True)
            top = jnp.maximum(jnp.max(scores, axis=1, keepdims=True), stamp_score)
            expo = jnp.exp(scores - top)
            stamp_expo = jnp.exp(stamp_score - top)
            denom = jnp.sum(expo, axis=1, keepdims=True) + stamp_expo
            share = 1.0 / denom
            prob = (expo * share).astype(values.dtype)
            stamp_prob = (stamp_expo * share).astype(values.dtype).astype(jnp.float32)
            mixed = jnp.dot(prob, values, preferred_element_type=jnp.float32)
            out_ref[place, lanes] = (mixed + stamp_prob * stamp_value).astype(out_ref.dtype)
            lse_ref[place, head : head + 1] = top + jnp.log(denom)
            return carry

        lax.fori_loop(0, rows // tile, one, 0)

    pl.when(step == last)(end_swap)


def flash_forward(normed, matrix, stamps, bias, rotary, heads, ff_low, rows_of_clip, collective_id):
    clips, rows = bias.shape
    wide = heads * HDIM
    group, piece, features = rows_of_clip.shape
    owned, columns = ff_low.shape
    hidden = columns // (3 * group)
    like = lambda *shape: jax.ShapeDtypeStruct(shape, rows_of_clip.dtype)
    blocked = lambda lanes: pl.BlockSpec((rows, lanes), lambda clip: (clip, 0))
    return pl.pallas_call(
        functools.partial(flash_forward_body, heads, rows // 4),
        grid=(clips,),
        out_shape=[
            like(clips * rows, 3 * wide),
            like(clips * rows, wide),
            jax.ShapeDtypeStruct((clips * rows, 128), jnp.float32),
            like(group, owned, 2 * hidden),
            like(group, owned, hidden),
            like(group, piece, features),
        ],
        in_specs=[
            blocked(features),
            pl.BlockSpec(matrix.shape, lambda clip: (0, 0)),
            pl.BlockSpec((1, 1, 2 * wide), lambda clip: (clip, 0, 0)),
            pl.BlockSpec((1, 1, rows), lambda clip: (clip, 0, 0)),
            pl.BlockSpec((2, rows, 128), lambda clip: (0, 0, 0)),
            any_spec(),
            any_spec(),
        ],
        out_specs=[blocked(3 * wide), blocked(wide), blocked(128)] + [any_spec()] * 3,
        scratch_shapes=[pltpu.VMEM((rows, 3 * wide), jnp.float32)] + swap_beside_scratch(4),
        compiler_params=communicating(collective_id),
    )(normed, matrix, stamps[:, None], bias[:, None], rotary, ff_low, rows_of_clip)


def flash_backward_body(
    heads,
    tile,
    turned_ref,
    mixed_ref,
    grad_ref,
    lse_ref,
    stamp_ref,
    bias_ref,
    rotary_ref,
    cut_ref,
    cross_cut_ref,
    normed_ref,
    stamp_normed_ref,
    out_ref,
    stamp_out_ref,
    mine_ref,
    cross_mine_ref,
    outer_ref,
    query_grad,
    key_grad,
    value_grad,
    outer_total,
    *sems,
):
    place, depth, flip = plane_places()
    start_swap, end_swap = swap_beside(
        [
            (lambda other: cut_ref.at[other], lambda other: mine_ref.at[other]),
            (lambda other: cross_cut_ref.at[other], lambda other: cross_mine_ref.at[other]),
        ],
        *sems,
    )

    @pl.when(pl.program_id(0) == 0)
    def _():
        greet([(flip(mask), depth) for mask in range(1, 8)])
        start_swap()

    wide = heads * HDIM
    rows = turned_ref.shape[0]
    scale = HDIM**-0.5
    low = turned_ref.dtype
    f32 = jnp.float32
    first_row = lax.broadcasted_iota(jnp.int32, (8, tile), 0) == 0
    ones = lambda count, width: jnp.ones((count, width), low)
    blank = lambda count, width: jnp.zeros((count, width), low)
    bias = bias_ref[0].astype(low)

    def widened(count, *parts):
        have = sum(part.shape[1] for part in parts)
        return jnp.concatenate(list(parts) + [blank(count, 128 - have)], axis=1)

    def negative_parts(column):
        parts, rest = [], -column
        for _ in range(3):
            parts.append(rest.astype(low))
            rest = rest - parts[-1].astype(f32)
        return parts

    for head in range(heads):
        lanes = slice(head * HDIM, head * HDIM + HDIM)
        later = slice(wide + head * HDIM, wide + head * HDIM + HDIM)
        keys = turned_ref[:, later]
        values = turned_ref[:, 2 * wide + head * HDIM : 2 * wide + head * HDIM + HDIM]
        keys_across = keys.astype(f32).T.astype(low)
        wide_keys = widened(rows, keys, bias, ones(rows, 3))
        wide_values = widened(rows, values, ones(rows, 3))
        stamp_key = jnp.broadcast_to(stamp_ref[0, :, lanes], (8, HDIM))
        stamp_value = jnp.broadcast_to(stamp_ref[0, :, later], (8, HDIM))
        wide_stamp_key = widened(8, stamp_key, blank(8, 1), ones(8, 3))
        wide_stamp_value = widened(8, stamp_value, ones(8, 3))
        stamp_column = stamp_ref[0, :, lanes].astype(f32).T
        key_total = jnp.zeros((rows, HDIM), f32)
        value_total = jnp.zeros((rows, HDIM), f32)
        stamp_key_total = jnp.zeros((8, HDIM), f32)
        stamp_value_total = jnp.zeros((8, HDIM), f32)
        for step in range(rows // tile):
            place = slice(step * tile, step * tile + tile)
            query = turned_ref[place, lanes] * jnp.asarray(scale, low)
            grad = grad_ref[place, lanes]
            delta = jnp.sum(
                grad.astype(f32) * mixed_ref[place, lanes].astype(f32), axis=1, keepdims=True
            )
            lse = lse_ref[place, head : head + 1]
            wide_query = widened(tile, query, ones(tile, 1), *negative_parts(lse))
            wide_grad = widened(tile, grad, *negative_parts(delta))
            prob = jnp.exp(times_transposed(wide_keys, wide_query))
            scores = (prob * times_transposed(wide_values, wide_grad)).astype(low)
            stamp_prob = jnp.exp(times_transposed(wide_stamp_key, wide_query))
            stamp_scores = stamp_prob * times_transposed(wide_stamp_value, wide_grad)
            stamp_scores = jnp.where(first_row, stamp_scores, 0.0).astype(low)
            value_total += jnp.dot(prob.astype(low), grad, preferred_element_type=f32)
            key_total += jnp.dot(scores, query, preferred_element_type=f32)
            across = jnp.dot(keys_across, scores, preferred_element_type=f32)
            across = across + stamp_column * stamp_scores[:1].astype(f32)
            query_grad[place, lanes] = across.T * scale
            stamp_key_total += jnp.dot(stamp_scores, query, preferred_element_type=f32)
            stamp_value_total += jnp.dot(
                jnp.where(first_row, stamp_prob, 0.0).astype(low), grad, preferred_element_type=f32
            )
        key_grad[:, lanes] = key_total
        value_grad[:, lanes] = value_total
        stamp_out_ref[0, :, lanes] = stamp_key_total[:1]
        stamp_out_ref[0, :, later] = stamp_value_total[:1]
    both = jnp.concatenate([query_grad[...], key_grad[...]], axis=1)
    for pair in range(2 * wide // 128):
        lanes = slice(pair * 128, pair * 128 + 128)
        out_ref[:, lanes] = turn_heads(both[:, lanes], rotary_ref[0], -rotary_ref[1]).astype(low)
    out_ref[:, 2 * wide :] = value_grad[...].astype(low)
    count = outer_total.shape[1]
    tile = 512
    for start in range(0, normed_ref.shape[1], tile):
        span = slice(start, start + tile)
        product = outer_sum(normed_ref[:, span], out_ref[...])
        stamp_part = stamp_normed_ref[0, span] * stamp_out_ref[0]
        product = product + jnp.concatenate(
            [jnp.zeros((tile, count - 2 * wide), f32), stamp_part], axis=1
        )

        @pl.when(pl.program_id(0) == 0)
        def _():
            outer_total[span] = product

        @pl.when(pl.program_id(0) > 0)
        def _():
            outer_total[span] += product

    @pl.when(pl.program_id(0) == pl.num_programs(0) - 1)
    def _():
        outer_ref[...] = outer_total[...].astype(outer_ref.dtype)
        end_swap()


def flash_backward(
    turned,
    mixed,
    grad,
    lse,
    stamps,
    bias,
    rotary,
    heads,
    cut,
    cross_cut,
    normed,
    stamp_normed,
    collective_id,
):
    clips, rows, _ = bias.shape
    wide = heads * HDIM
    blocked = lambda lanes: pl.BlockSpec((rows, lanes), lambda clip: (clip, 0))
    features = normed.shape[1]
    grads, stamp_grads, mine, cross_mine, outer = pl.pallas_call(
        functools.partial(flash_backward_body, heads, rows // 4),
        grid=(clips,),
        out_shape=[
            jax.ShapeDtypeStruct((clips * rows, 3 * wide), jnp.bfloat16),
            jax.ShapeDtypeStruct((clips, 1, 2 * wide), jnp.float32),
            jax.ShapeDtypeStruct(cut.shape, cut.dtype),
            jax.ShapeDtypeStruct(cross_cut.shape, cross_cut.dtype),
            jax.ShapeDtypeStruct((features, 3 * wide), jnp.bfloat16),
        ],
        in_specs=[
            blocked(3 * wide),
            blocked(wide),
            blocked(wide),
            blocked(128),
            pl.BlockSpec((1, 1, 2 * wide), lambda clip: (clip, 0, 0)),
            pl.BlockSpec((1, rows, 1), lambda clip: (clip, 0, 0)),
            pl.BlockSpec((2, rows, 128), lambda clip: (0, 0, 0)),
            any_spec(),
            any_spec(),
            blocked(features),
            pl.BlockSpec((1, features, 1), lambda clip: (clip, 0, 0)),
        ],
        out_specs=[
            blocked(3 * wide),
            pl.BlockSpec((1, 1, 2 * wide), lambda clip: (clip, 0, 0)),
            any_spec(),
            any_spec(),
            pl.BlockSpec((features, 3 * wide), lambda clip: (0, 0)),
        ],
        scratch_shapes=[pltpu.VMEM((rows, wide), jnp.float32)] * 3
        + [pltpu.VMEM((features, 3 * wide), jnp.float32)]
        + swap_beside_scratch(2),
        compiler_params=communicating(collective_id),
    )(
        turned,
        mixed,
        grad,
        lse,
        stamps[:, None],
        bias,
        rotary,
        cut,
        cross_cut,
        normed,
        stamp_normed,
    )
    return grads, stamp_grads[:, 0], mine, cross_mine, outer


def matrix_step(weight, first, second, gradient):
    first_new = beta_first * first + (1.0 - beta_first) * gradient
    second_new = beta_second * second + (1.0 - beta_second) * (gradient * gradient)
    over_first = matrix_rate / (1.0 - beta_first**UPDATE_STEP)
    over_second = 1.0 / (1.0 - beta_second**UPDATE_STEP)
    change = first_new * over_first / (jnp.sqrt(second_new * over_second) + adam_eps)
    return (weight * (1.0 - matrix_rate * matrix_decay) - change, first_new, second_new)


def adam_body(ff_steps, places, *refs):
    refs = list(refs)
    take = lambda count: [refs.pop(0) for _ in range(count)]
    total_ref = take(1)[0]
    ff_refs, ff_grad_ref = take(3), take(1)[0]
    attn_refs = take(3)
    attn_grads = take(1 + max(which for which, _, _ in places))
    ff_outs, attn_outs = take(3), take(3)
    step = pl.program_id(0)
    factor = jnp.minimum(1.0, clip_limit / jnp.sqrt(total_ref[0:1, 0:1]))

    def update(olds, gradient, outs):
        results = matrix_step(
            *[old[...] for old in olds], gradient.astype(jnp.float32) * factor
        )
        for out, result in zip(outs, results):
            out[...] = result

    @pl.when(step < ff_steps)
    def _():
        gradient = jnp.concatenate(
            [ff_grad_ref[part] for part in range(ff_grad_ref.shape[0])], axis=1
        )
        update(ff_refs, gradient, ff_outs)

    for block, (which, start, stop) in enumerate(places):

        @pl.when(step == ff_steps + block)
        def _(owned_ref=attn_grads[which], start=start, stop=stop):
            gradient = jnp.concatenate(
                [owned_ref[part, :, start:stop] for part in range(owned_ref.shape[0])], axis=1
            )
            update(attn_refs, gradient, attn_outs)


def adam(total, ff, ff_grad, attn, attn_grads, places):
    rows, columns = ff[0].shape
    group, _, held = ff_grad.shape
    parts = group // 2
    width = columns // (3 * group)
    ff_steps = 3 * group // parts
    steps = ff_steps + len(places)
    ff_step = lambda step: jnp.minimum(step, ff_steps - 1)
    ff_piece = pl.BlockSpec((rows, parts * width), lambda step: (0, ff_step(step)))
    ff_grads = pl.BlockSpec(
        (parts, rows, width), lambda step: (lax.rem(ff_step(step), 2), 0, lax.div(ff_step(step), 2))
    )
    attn_piece = pl.BlockSpec(
        (rows, attn[0].shape[1] // len(places)), lambda step: (0, jnp.maximum(step - ff_steps, 0))
    )
    whole = [pl.BlockSpec(grad.shape, lambda step: (0, 0, 0)) for grad in attn_grads]
    f32 = jnp.float32
    results = pl.pallas_call(
        functools.partial(adam_body, ff_steps, places),
        grid=(steps,),
        out_shape=[jax.ShapeDtypeStruct(ff[0].shape, f32)] * 3
        + [jax.ShapeDtypeStruct(attn[0].shape, f32)] * 3,
        in_specs=[pl.BlockSpec((8, 128), lambda step: (0, 0))]
        + [ff_piece] * 3
        + [ff_grads]
        + [attn_piece] * 3
        + whole,
        out_specs=[ff_piece] * 3 + [attn_piece] * 3,
        compiler_params=pltpu.CompilerParams(vmem_limit_bytes=VMEM_LIMIT),
    )(total, *ff, ff_grad, *attn, *attn_grads)
    return results[:3], results[3:]


def plane_device(
    frames,
    time_token,
    cond_ids,
    cond_mask,
    lengths,
    cond_table,
    cotangent,
    attn_weight,
    cross_weight,
    norm_param,
    ff_weight,
    attn_first,
    attn_second,
    cross_first,
    cross_second,
    norm_first,
    norm_second,
    ff_first,
    ff_second,
):
    group, planes = lax.axis_size("dp"), lax.axis_size("seq")
    place, depth = lax.axis_index("dp"), lax.axis_index("seq")
    clips = group // planes
    _, frame_rows, wide = frames.shape
    piece = frame_rows // group
    seq_frames = frame_rows * planes
    own_rows = planes * piece
    heads = HEADS // group
    head_wide = heads * HDIM
    ff_wide = FF // group
    owned = wide // (group * planes)
    cond_count, cond_wide = cond_ids.shape[1], cond_table.shape[1]
    cond_owned = cross_weight.shape[0]

    norm_block = norm_param.astype(jnp.bfloat16).astype(jnp.float32)
    norm_block = jnp.pad(norm_block, ((0, 2), (0, 128 - owned)))
    pack = jnp.concatenate(
        [
            time_token.astype(jnp.float32),
            jnp.pad(cond_ids.astype(jnp.float32), ((0, 0), (0, wide - cond_count))),
            jnp.pad(cond_mask.astype(jnp.float32), ((0, 0), (0, wide - cond_count))),
            jnp.broadcast_to(lengths.astype(jnp.float32)[:, None], (1, wide)),
            jnp.zeros((4, wide), jnp.float32),
        ],
        axis=0,
    )
    positions = depth * frame_rows + jnp.arange(frame_rows)
    valid = (positions < lengths).astype(jnp.float32)[:, None]
    stream, gain_rows, packs, qkv_mine, rest_mine, ff_low, grad_pieces = enter(
        frames[0],
        cotangent[0],
        valid,
        norm_block,
        pack,
        attn_weight,
        cross_weight,
        ff_weight,
        planes,
        1,
    )
    stream = stream.reshape(clips, own_rows, wide).astype(jnp.float32)

    def over_planes(block):
        return lax.all_gather(block.reshape(group * owned, -1), "seq", axis=0, tiled=True)

    w_qkv = over_planes(qkv_mine)
    w_rest = over_planes(rest_mine)
    of_self_out = (0, head_wide)
    of_cross_query = (head_wide, 2 * head_wide)
    of_cross_out = (2 * head_wide, 3 * head_wide)
    w_cond = w_rest[:, 3 * head_wide :].reshape(planes, group, 2, cond_owned, head_wide)
    w_cond = w_cond.transpose(1, 0, 3, 2, 4).reshape(cond_wide, 2 * head_wide)
    plane_packs = lax.dynamic_slice_in_dim(packs, depth * clips, clips, axis=0)
    stamps = plane_packs[:, 0].reshape(clips, group, planes, owned)
    stamps = stamps.swapaxes(1, 2).reshape(clips, wide)
    cond_keep = plane_packs[:, 2, :cond_count] > 0
    clip_lengths = plane_packs[:, 3, 0].astype(jnp.int32)
    share = cond_count // group
    all_ids = packs[:, 1, :cond_count].astype(jnp.int32)
    own_ids = lax.dynamic_slice_in_dim(all_ids, place * share, share, axis=1)
    vocab_rows = cond_table.shape[0]
    relative = own_ids - depth * vocab_rows
    inside = (relative >= 0) & (relative < vocab_rows)
    picked = jnp.take(cond_table, jnp.clip(relative, 0, vocab_rows - 1), axis=0)
    picked = jnp.where(inside[..., None], picked, jnp.zeros((), picked.dtype))
    picked = picked.reshape(planes, clips, share, cond_wide)
    group_rows = clips * seq_frames
    row_place = np.arange(seq_frames)
    row_owner, row_rest = row_place // own_rows, row_place % own_rows
    true_place = (row_rest // piece) * frame_rows + row_owner * piece + row_rest % piece
    key_keep = true_place[None, :] < clip_lengths[:, None]
    group_shape = (clips, seq_frames, heads, HDIM)

    group_one, cond = gather_dot(stream, None, None, 5, gain_rows[0:2], picked)
    cond_flat = cond.swapaxes(0, 1).reshape(clips * cond_count, cond_wide)
    stamp_normed = layer_norm(stamps, gain_rows[0], gain_rows[1]).astype(jnp.bfloat16)
    stamp_pair = jnp.dot(stamp_normed, w_qkv[:, head_wide:], preferred_element_type=jnp.float32)
    stamp_pair = stamp_pair.astype(jnp.bfloat16)
    rotary = rotary_lanes(true_place)
    key_bias = jnp.where(key_keep, 0.0, masked_score)
    rotated, self_low, self_lse, gate_up_mine, down_mine, grad_out_mid = flash_forward(
        group_one,
        w_qkv,
        stamp_pair,
        key_bias,
        rotary,
        heads,
        ff_low,
        grad_pieces,
        2,
    )
    w_gate_up = over_planes(gate_up_mine)
    w_down = over_planes(down_mine)
    cond_pair = jnp.dot(cond_flat, w_cond, preferred_element_type=jnp.float32)
    cond_pair = cond_pair.astype(jnp.bfloat16).reshape(clips, cond_count, 2 * head_wide)
    cond_bias = jnp.where(cond_keep, 0.0, masked_score)[:, None]
    resid_one, group_two, cross_query, cross_out, grad_out_low = reduce_gather(
        self_low,
        w_rest,
        clips,
        6,
        stream,
        w_rest,
        span=of_self_out,
        gains=gain_rows[2:4],
        second_span=of_cross_query,
        pair=cond_pair,
        bias=cond_bias,
        passing=grad_out_mid,
    )
    grad_out_low = grad_out_low.reshape(clips, own_rows, wide)
    (resid_two,) = dot_reduce(cross_out, w_rest, clips, 8, resid_one, of_cross_out)
    group_three, gate_up = gather_dot(resid_two, w_gate_up, jnp.float32, 9, gain_rows[4:6])
    stamp_column = stamp_normed.astype(jnp.float32)[:, :, None]
    bias_column = key_bias[:, :, None]
    gate_up, grad_out_low, stamp_column, bias_column = lax.optimization_barrier(
        (gate_up, grad_out_low, stamp_column, bias_column)
    )
    group_grad_out, grad_gate_up, hidden = gather_dot(
        grad_out_low, w_down, None, 10, gate_up=gate_up
    )

    def over_rows(block):
        return lax.psum_scatter(
            block.astype(jnp.bfloat16), "seq", scatter_dimension=0, tiled=True
        ).reshape(group, owned, -1)

    layer_rows, ff_piece = ff_outer(
        grad_gate_up, hidden, w_down, group_three, group_grad_out, resid_two, planes, 12
    )
    ff_piece, grad_gate_up = lax.optimization_barrier((ff_piece, grad_gate_up))
    ff_rows = over_rows(ff_piece)
    grad_two, stats_three = dot_reduce(
        grad_gate_up, w_gate_up, clips, 13, grad_out_low, back=(resid_two, gain_rows[4:5])
    )
    _, grad_cross_query, cond_grad, cross_piece = gather_dot(
        grad_two,
        w_rest,
        None,
        15,
        span=of_cross_out,
        pair=cond_pair,
        bias=cond_bias,
        query=cross_query,
        outer=(group_two, cross_out),
    )
    cond_grad = cond_grad.reshape(clips * cond_count, 2 * head_wide)
    cond_piece = split_outer(cond_flat, cond_grad)
    cond_piece = cond_piece.reshape(group, planes, cond_owned, 2, head_wide)
    cond_piece = cond_piece.transpose(1, 0, 3, 2, 4).reshape(wide, head_wide)
    cond_piece = cond_piece.astype(jnp.bfloat16)
    grad_one, stats_two, _, grad_self_mixed, rest_piece, layer_out, cross_rows = reduce_gather(
        grad_cross_query,
        w_rest,
        clips,
        16,
        grad_two,
        w_rest,
        span=of_cross_query,
        back=(resid_one, gain_rows[2:3]),
        second_span=of_self_out,
        outer=(self_low, cond_piece),
        adding=cross_piece.reshape(planes, group * owned, 2 * head_wide),
        leaving=layer_rows.reshape(clips, planes, piece, wide),
    )
    rest_piece, ff_rows = lax.optimization_barrier((rest_piece, ff_rows))
    rest_rows = over_rows(rest_piece)
    grad_project, stamp_grad, ff_owned, cross_owned, qkv_piece = flash_backward(
        rotated,
        self_low,
        grad_self_mixed,
        self_lse,
        stamp_pair,
        bias_column,
        rotary,
        heads,
        ff_rows,
        cross_rows.reshape(group, owned, -1),
        group_one,
        stamp_column,
        3,
    )
    grad_stamp_normed = split_times_transposed(stamp_grad, w_qkv[:, head_wide:])
    qkv_rows = over_rows(qkv_piece)
    grad_project, rest_rows = lax.optimization_barrier((grad_project, rest_rows))
    frames_grad, stats_one, rest_owned = dot_reduce(
        grad_project,
        w_qkv,
        clips,
        18,
        grad_one,
        back=(stream, gain_rows[0:1]),
        kind=jnp.bfloat16,
        order=(group, planes),
        cut=rest_rows,
    )
    _, norm_stamp_back = jax.vjp(layer_norm, stamps, gain_rows[0], gain_rows[1])
    _, grad_gain_stamp, grad_bias_stamp = norm_stamp_back(grad_stamp_normed)
    stamp_stats = jnp.stack([grad_gain_stamp, grad_bias_stamp])
    norm_grad = jnp.concatenate([stats_one + stamp_stats, stats_two, stats_three], axis=0)
    norm_parts = norm_grad.reshape(6, planes, group, owned).transpose(2, 1, 0, 3)
    norm_parts = norm_parts.reshape(group * planes, 6, owned)
    norm_parts = jnp.pad(norm_parts, ((0, 0), (0, 2), (0, 128 - owned)))
    ff_squares = jnp.sum(jnp.square(ff_owned.astype(jnp.float32)))
    frames_grad, qkv_owned, norm_sum, total = settle(
        frames_grad.reshape(clips, planes, piece, wide),
        qkv_rows,
        [cross_owned, rest_owned],
        norm_parts,
        ff_squares.reshape(1, 1),
        20,
    )
    cross_reduced = rest_owned[:, :, head_wide:].reshape(group, 2, cond_owned, head_wide)
    cross_reduced = cross_reduced.transpose(2, 1, 0, 3).reshape(cross_weight.shape)
    cross_reduced = cross_reduced.astype(jnp.float32)
    norm_reduced = norm_sum[:6, :owned]
    grad_norm = jnp.sqrt(total[0, 0])
    factor = jnp.minimum(1.0, clip_limit / grad_norm)
    ff_results, attn_results = adam(
        total,
        (ff_weight, ff_first, ff_second),
        ff_owned,
        (attn_weight, attn_first, attn_second),
        [qkv_owned, cross_owned, rest_owned],
        [
            (which, block * head_wide, (block + 1) * head_wide)
            for which, block in ((0, 0), (0, 1), (0, 2), (2, 0), (1, 0), (1, 1))
        ],
    )
    ff_new, ff_first_new, ff_second_new = ff_results
    attn_new, attn_first_new, attn_second_new = attn_results
    frames_grad = frames_grad.reshape(frames.shape).astype(jnp.float32)
    layer_out = layer_out.reshape(frames.shape)
    cross_new, cross_first_new, cross_second_new = adam_step(
        cross_weight, cross_first, cross_second, cross_reduced * factor, matrix_rate, matrix_decay
    )
    norm_new, norm_first_new, norm_second_new = adam_step(
        norm_param, norm_first, norm_second, norm_reduced * factor, gain_rate, 0.0
    )
    return (
        layer_out,
        frames_grad,
        grad_norm,
        attn_new,
        cross_new,
        norm_new,
        ff_new,
        attn_first_new,
        cross_first_new,
        norm_first_new,
        ff_first_new,
        attn_second_new,
        cross_second_new,
        norm_second_new,
        ff_second_new,
    )


def solution(mesh):
    return jax.shard_map(
        plane_device if plane_fits(mesh) else per_device,
        mesh=mesh,
        in_specs=(
            P("dp", "seq", None),
            P("dp", None),
            P("dp", None),
            P("dp", None),
            P("dp"),
            P("seq", None),
            P("dp", "seq", None),
            P(("dp", "seq"), None),
            P(("dp", "seq"), None),
            P(None, ("dp", "seq")),
            P(("dp", "seq"), None),
            P(("dp", "seq"), None),
            P(("dp", "seq"), None),
            P(("dp", "seq"), None),
            P(("dp", "seq"), None),
            P(None, ("dp", "seq")),
            P(None, ("dp", "seq")),
            P(("dp", "seq"), None),
            P(("dp", "seq"), None),
        ),
        out_specs=(
            P("dp", "seq", None),
            P("dp", "seq", None),
            P(),
            P(("dp", "seq"), None),
            P(("dp", "seq"), None),
            P(None, ("dp", "seq")),
            P(("dp", "seq"), None),
            P(("dp", "seq"), None),
            P(("dp", "seq"), None),
            P(None, ("dp", "seq")),
            P(("dp", "seq"), None),
            P(("dp", "seq"), None),
            P(("dp", "seq"), None),
            P(None, ("dp", "seq")),
            P(("dp", "seq"), None),
        ),
        check_vma=False,
    )
```

```python
import functools

import jax
import jax.numpy as jnp
import numpy as np
from jax import lax
from jax.experimental import pallas as pl
from jax.experimental.pallas import tpu as pltpu
from jax.sharding import PartitionSpec as P

HEADS = 24
HDIM = 64
FF = 6144
UPDATE_STEP = 10


norm_eps = 1e-05
beta_first = 0.5
beta_second = 0.5
adam_eps = 1e-08
matrix_decay = 0.01
matrix_rate = 0.03
gain_rate = 0.25
clip_limit = 1.0
masked_score = -1e30


def layer_norm(values, gain_row, bias_row):
    center = values - jnp.mean(values, axis=-1, keepdims=True)
    spread = jnp.mean(center * center, axis=-1, keepdims=True)
    return center * lax.rsqrt(spread + norm_eps) * gain_row + bias_row


def rotary_tables(positions, head_size):
    half_size = head_size // 2
    frequency = 10000.0 ** (-jnp.arange(half_size, dtype=jnp.float32) / half_size)
    angles = positions.astype(jnp.float32)[:, None] * frequency[None, :]
    return (jnp.cos(angles)[:, None, :], jnp.sin(angles)[:, None, :])


def rotate(values, cosine_table, sine_table):
    half_size = values.shape[-1] // 2
    first_half = values[..., :half_size]
    second_half = values[..., half_size:]
    return jnp.concatenate(
        [
            first_half * cosine_table - second_half * sine_table,
            second_half * cosine_table + first_half * sine_table,
        ],
        axis=-1,
    )


def outer_sum(left_mat, right_mat):
    return lax.dot_general(
        left_mat, right_mat, (((0,), (0,)), ((), ())), preferred_element_type=jnp.float32
    )


def times_transposed(left_mat, right_mat):
    return lax.dot_general(
        left_mat, right_mat, (((1,), (1,)), ((), ())), preferred_element_type=jnp.float32
    )


def split_parts(values):
    upper = values.astype(jnp.bfloat16)
    lower = (values - upper.astype(jnp.float32)).astype(jnp.bfloat16)
    return (upper, lower)


def split_outer(left_low, right_full):
    upper, lower = split_parts(right_full)
    return outer_sum(left_low, upper) + outer_sum(left_low, lower)


def split_times_transposed(left_full, right_low):
    upper, lower = split_parts(left_full)
    return times_transposed(upper, right_low) + times_transposed(lower, right_low)


def self_scores(queries, keys, stamp_key, keep):
    score_scale = HDIM ** (-0.5)
    frame_part = (
        jnp.einsum("cqhd,ckhd->chqk", queries, keys, preferred_element_type=jnp.float32)
        * score_scale
    )
    frame_part = jnp.where(keep[:, None, None, :], frame_part, masked_score)
    stamp_part = (
        jnp.einsum("cqhd,chd->chq", queries, stamp_key, preferred_element_type=jnp.float32)
        * score_scale
    )
    return (frame_part, stamp_part)


def self_forward(queries, keys, values, stamp_key, stamp_value, keep):
    frame_scores, stamp_scores = self_scores(queries, keys, stamp_key, keep)
    top_score = jnp.maximum(jnp.max(frame_scores, axis=-1), stamp_scores)
    frame_expo = jnp.exp(frame_scores - top_score[..., None])
    stamp_expo = jnp.exp(stamp_scores - top_score)
    denom = jnp.sum(frame_expo, axis=-1) + stamp_expo
    self_lse = top_score + jnp.log(denom)
    frame_prob = (frame_expo / denom[..., None]).astype(jnp.bfloat16)
    stamp_prob = (stamp_expo / denom).astype(jnp.bfloat16)
    mixed = jnp.einsum(
        "chqk,ckhd->cqhd", frame_prob, values, preferred_element_type=jnp.float32
    ) + jnp.einsum("chq,chd->cqhd", stamp_prob, stamp_value, preferred_element_type=jnp.float32)
    return (mixed, self_lse)


def self_backward(queries, keys, values, stamp_key, stamp_value, keep, self_lse, grad_mixed):
    score_scale = HDIM ** (-0.5)
    frame_scores, stamp_scores = self_scores(queries, keys, stamp_key, keep)
    frame_prob = jnp.exp(frame_scores - self_lse[..., None])
    stamp_prob = jnp.exp(stamp_scores - self_lse)
    grad_frame_prob = jnp.einsum(
        "cqhd,ckhd->chqk", grad_mixed, values, preferred_element_type=jnp.float32
    )
    grad_stamp_prob = jnp.einsum(
        "cqhd,chd->chq", grad_mixed, stamp_value, preferred_element_type=jnp.float32
    )
    delta = jnp.sum(frame_prob * grad_frame_prob, axis=-1) + stamp_prob * grad_stamp_prob
    grad_frame_scores = (frame_prob * (grad_frame_prob - delta[..., None])).astype(jnp.bfloat16)
    grad_stamp_scores = (stamp_prob * (grad_stamp_prob - delta)).astype(jnp.bfloat16)
    grad_queries = (
        jnp.einsum("chqk,ckhd->cqhd", grad_frame_scores, keys, preferred_element_type=jnp.float32)
        + jnp.einsum(
            "chq,chd->cqhd", grad_stamp_scores, stamp_key, preferred_element_type=jnp.float32
        )
    ) * score_scale
    key_part = (
        jnp.einsum(
            "chqk,cqhd->ckhd", grad_frame_scores, queries, preferred_element_type=jnp.float32
        )
        * score_scale
    )
    value_part = jnp.einsum(
        "chqk,cqhd->ckhd",
        frame_prob.astype(jnp.bfloat16),
        grad_mixed,
        preferred_element_type=jnp.float32,
    )
    grad_stamp_key = (
        jnp.einsum("chq,cqhd->chd", grad_stamp_scores, queries, preferred_element_type=jnp.float32)
        * score_scale
    )
    grad_stamp_value = jnp.einsum(
        "chq,cqhd->chd",
        stamp_prob.astype(jnp.bfloat16),
        grad_mixed,
        preferred_element_type=jnp.float32,
    )
    return (grad_queries, key_part, value_part, grad_stamp_key, grad_stamp_value)


def cross_scores(query, keys, keep):
    score_scale = HDIM ** (-0.5)
    scores = (
        jnp.einsum("cqhd,ckhd->chqk", query, keys, preferred_element_type=jnp.float32) * score_scale
    )
    return jnp.where(keep[:, None, None, :], scores, masked_score)


def cross_forward(query, keys, values, keep):
    scores = cross_scores(query, keys, keep)
    top_score = jnp.max(scores, axis=-1)
    expo = jnp.exp(scores - top_score[..., None])
    denom = jnp.sum(expo, axis=-1)
    cross_lse = top_score + jnp.log(denom)
    prob = (expo / denom[..., None]).astype(jnp.bfloat16)
    mixed = jnp.einsum("chqk,ckhd->cqhd", prob, values, preferred_element_type=jnp.float32)
    return (mixed, cross_lse)


def cross_backward(query, keys, values, keep, cross_lse, grad_mixed):
    score_scale = HDIM ** (-0.5)
    prob = jnp.exp(cross_scores(query, keys, keep) - cross_lse[..., None])
    grad_prob = jnp.einsum(
        "cqhd,ckhd->chqk", grad_mixed, values, preferred_element_type=jnp.float32
    )
    delta = jnp.sum(prob * grad_prob, axis=-1)
    grad_scores = (prob * (grad_prob - delta[..., None])).astype(jnp.bfloat16)
    grad_query = (
        jnp.einsum("chqk,ckhd->cqhd", grad_scores, keys, preferred_element_type=jnp.float32)
        * score_scale
    )
    grad_keys = (
        jnp.einsum("chqk,cqhd->ckhd", grad_scores, query, preferred_element_type=jnp.float32)
        * score_scale
    )
    grad_values = jnp.einsum(
        "chqk,cqhd->ckhd", prob.astype(jnp.bfloat16), grad_mixed, preferred_element_type=jnp.float32
    )
    return (grad_query, grad_keys, grad_values)


def adam_step(weight, first, second, gradient, step_rate, decay_rate):
    first_new = beta_first * first + (1.0 - beta_first) * gradient
    second_new = beta_second * second + (1.0 - beta_second) * gradient * gradient
    fix_first = 1.0 - beta_first**UPDATE_STEP
    fix_second = 1.0 - beta_second**UPDATE_STEP
    normed_step = first_new / fix_first / (jnp.sqrt(second_new / fix_second) + adam_eps)
    return (weight - step_rate * (normed_step + decay_rate * weight), first_new, second_new)


def per_device(
    frames,
    time_token,
    cond_ids,
    cond_mask,
    lengths,
    cond_table,
    cotangent,
    attn_weight,
    cross_weight,
    norm_param,
    ff_weight,
    attn_first,
    attn_second,
    cross_first,
    cross_second,
    norm_first,
    norm_second,
    ff_first,
    ff_second,
):
    clip_count, frame_rows, wide = frames.shape
    hidden_width = FF
    token_count = clip_count * frame_rows
    seq_count = lax.axis_size("seq")
    seq_frames = frame_rows * seq_count
    seq_place = lax.axis_index("seq")
    vocab_rows = cond_table.shape[0]
    relative = cond_ids - seq_place * vocab_rows
    inside = (relative >= 0) & (relative < vocab_rows)
    picked = jnp.take(cond_table, jnp.clip(relative, 0, vocab_rows - 1), axis=0).astype(jnp.float32)
    picked = jnp.where(inside[..., None], picked, 0.0)
    cond = lax.psum(picked.astype(jnp.bfloat16), "seq")
    cond_count = cond.shape[1]
    cond_flat = cond.reshape(clip_count * cond_count, cond.shape[2])
    cond_width = cond.shape[2]
    cond_keep = cond_mask > 0
    attn_low = attn_weight.astype(jnp.bfloat16)
    cross_low = cross_weight.astype(jnp.bfloat16)
    norm_low = norm_param.astype(jnp.bfloat16)
    ff_low = ff_weight.astype(jnp.bfloat16)
    stream = frames.astype(jnp.float32).reshape(token_count, wide)
    stamps = time_token.astype(jnp.float32)
    positions = seq_place * frame_rows + jnp.arange(frame_rows)
    key_keep = jnp.arange(seq_frames)[None, :] < lengths[:, None]
    frame_valid = (positions[None, :] < lengths[:, None]).reshape(token_count)
    grad_out = cotangent.astype(jnp.float32).reshape(token_count, wide) * frame_valid[
        :, None
    ].astype(jnp.float32)
    grad_out_low = grad_out.astype(jnp.bfloat16)
    piece_heads = HEADS // seq_count
    piece_wide = wide // seq_count
    piece_ff = hidden_width // seq_count
    group_rows = clip_count * seq_frames

    def pieces():
        norm_copies = jnp.tile(norm_low[None], (1, 1, seq_count))
        moved_attn, moved_cross, moved_ff, moved_norm = (
            lax.all_to_all(
                attn_low.reshape(-1, 6, wide), "seq", split_axis=2, concat_axis=0, tiled=True
            ),
            lax.all_to_all(
                cross_low.reshape(-1, 2, wide), "seq", split_axis=2, concat_axis=0, tiled=True
            ),
            lax.all_to_all(
                ff_low.reshape(-1, 3, hidden_width), "seq", split_axis=2, concat_axis=0, tiled=True
            ),
            lax.all_to_all(norm_copies, "seq", split_axis=2, concat_axis=0, tiled=True),
        )
        attn_cols, cross_cols, ff_cols, norm_blocks = (
            lax.all_gather(moved_attn, "dp", axis=0, tiled=True),
            lax.all_gather(moved_cross, "dp", axis=0, tiled=True),
            lax.all_gather(moved_ff, "dp", axis=0, tiled=True),
            lax.all_gather(moved_norm, "dp", axis=0, tiled=True),
        )
        gains = norm_blocks.transpose(1, 0, 2).reshape(6, wide).astype(jnp.float32)
        return (attn_cols, cross_cols, ff_cols, gains)

    def collect(rows):
        whole = lax.all_gather(
            rows.reshape(clip_count, frame_rows, wide), "seq", axis=1, tiled=True
        )
        return whole.reshape(group_rows, wide)

    def spread(partial_value):
        mine = lax.psum_scatter(
            partial_value.reshape(clip_count, seq_frames, wide).astype(jnp.bfloat16),
            "seq",
            scatter_dimension=1,
            tiled=True,
        ).astype(jnp.float32)
        return mine.reshape(token_count, wide)

    attn_cols, cross_cols, ff_cols, gain_rows = pieces()
    group_shape = (clip_count, seq_frames, piece_heads, HDIM)
    cosine_table, sine_table = rotary_tables(jnp.arange(seq_frames), HDIM)
    normed_one = layer_norm(stream, gain_rows[0], gain_rows[1]).astype(jnp.bfloat16)
    group_one = collect(normed_one)
    projected = jnp.dot(
        group_one,
        attn_cols[:, :3].reshape(wide, 3 * piece_wide),
        preferred_element_type=jnp.float32,
    )
    queries = rotate(
        projected[:, :piece_wide].reshape(group_shape), cosine_table, sine_table
    ).astype(jnp.bfloat16)
    all_keys = rotate(
        projected[:, piece_wide : 2 * piece_wide].reshape(group_shape), cosine_table, sine_table
    ).astype(jnp.bfloat16)
    all_values = projected[:, 2 * piece_wide :].astype(jnp.bfloat16).reshape(group_shape)
    stamp_normed = layer_norm(stamps, gain_rows[0], gain_rows[1]).astype(jnp.bfloat16)
    stamp_pair = jnp.dot(
        stamp_normed,
        attn_cols[:, 1:3].reshape(wide, 2 * piece_wide),
        preferred_element_type=jnp.float32,
    )
    stamp_key = (
        stamp_pair[:, :piece_wide].astype(jnp.bfloat16).reshape(clip_count, piece_heads, HDIM)
    )
    stamp_value = (
        stamp_pair[:, piece_wide:].astype(jnp.bfloat16).reshape(clip_count, piece_heads, HDIM)
    )
    self_mixed, self_lse = self_forward(
        queries, all_keys, all_values, stamp_key, stamp_value, key_keep
    )
    self_low = self_mixed.astype(jnp.bfloat16).reshape(group_rows, piece_wide)
    resid_one = stream + spread(times_transposed(self_low, attn_cols[:, 3]))
    normed_two = layer_norm(resid_one, gain_rows[2], gain_rows[3]).astype(jnp.bfloat16)
    group_two = collect(normed_two)
    cross_query = jnp.dot(group_two, attn_cols[:, 4], preferred_element_type=jnp.float32)
    cross_query = cross_query.astype(jnp.bfloat16).reshape(group_shape)
    cond_pair = jnp.dot(
        cond_flat,
        cross_cols.reshape(cond_width, 2 * piece_wide),
        preferred_element_type=jnp.float32,
    )
    cond_shape = (clip_count, cond_count, piece_heads, HDIM)
    cross_keys = cond_pair[:, :piece_wide].astype(jnp.bfloat16).reshape(cond_shape)
    cross_values = cond_pair[:, piece_wide:].astype(jnp.bfloat16).reshape(cond_shape)
    cross_mixed, cross_lse = cross_forward(cross_query, cross_keys, cross_values, cond_keep)
    cross_low_out = cross_mixed.astype(jnp.bfloat16).reshape(group_rows, piece_wide)
    resid_two = resid_one + spread(times_transposed(cross_low_out, attn_cols[:, 5]))
    normed_three = layer_norm(resid_two, gain_rows[4], gain_rows[5]).astype(jnp.bfloat16)
    group_three = collect(normed_three)
    gate_up = jnp.dot(
        group_three, ff_cols[:, :2].reshape(wide, 2 * piece_ff), preferred_element_type=jnp.float32
    )
    gate_val = gate_up[:, :piece_ff]
    up_val = gate_up[:, piece_ff:]
    hidden = (jax.nn.silu(gate_val) * up_val).astype(jnp.bfloat16)
    branch = spread(times_transposed(hidden, ff_cols[:, 2]))
    layer_out = (resid_two + branch).astype(jnp.bfloat16).reshape(clip_count, frame_rows, wide)
    attn_cols, cross_cols, ff_cols, gain_rows = pieces()
    group_grad_out = collect(grad_out_low)
    grad_hidden = jnp.dot(group_grad_out, ff_cols[:, 2], preferred_element_type=jnp.float32)
    sigmoid_gate = jax.nn.sigmoid(gate_val)
    grad_gate = grad_hidden * up_val * sigmoid_gate * (1.0 + gate_val * (1.0 - sigmoid_gate))
    grad_up = grad_hidden * gate_val * sigmoid_gate
    grad_gate_up = jnp.concatenate([grad_gate, grad_up], axis=1).astype(jnp.bfloat16)
    grad_normed_three = spread(
        times_transposed(grad_gate_up, ff_cols[:, :2].reshape(wide, 2 * piece_ff))
    )
    _, norm_three_back = jax.vjp(layer_norm, resid_two, gain_rows[4], gain_rows[5])
    grad_two_part, grad_gain_three, grad_bias_three = norm_three_back(grad_normed_three)
    grad_two = grad_out + grad_two_part
    grad_cross_branch = grad_two.astype(jnp.bfloat16)
    group_cross_branch = collect(grad_cross_branch)
    grad_cross_mixed = jnp.dot(
        group_cross_branch, attn_cols[:, 5], preferred_element_type=jnp.float32
    )
    grad_cross_mixed = grad_cross_mixed.astype(jnp.bfloat16).reshape(group_shape)
    grad_cross_query, grad_cross_keys, grad_cross_values = cross_backward(
        cross_query, cross_keys, cross_values, cond_keep, cross_lse, grad_cross_mixed
    )
    grad_cross_query = grad_cross_query.astype(jnp.bfloat16).reshape(group_rows, piece_wide)
    grad_normed_two = spread(times_transposed(grad_cross_query, attn_cols[:, 4]))
    _, norm_two_back = jax.vjp(layer_norm, resid_one, gain_rows[2], gain_rows[3])
    grad_one_part, grad_gain_two, grad_bias_two = norm_two_back(grad_normed_two)
    grad_one = grad_two + grad_one_part
    grad_self_branch = grad_one.astype(jnp.bfloat16)
    group_self_branch = collect(grad_self_branch)
    grad_self_mixed = jnp.dot(
        group_self_branch, attn_cols[:, 3], preferred_element_type=jnp.float32
    )
    grad_self_mixed = grad_self_mixed.astype(jnp.bfloat16).reshape(group_shape)
    grad_queries, key_part, value_part, grad_stamp_key, grad_stamp_value = self_backward(
        queries, all_keys, all_values, stamp_key, stamp_value, key_keep, self_lse, grad_self_mixed
    )
    grad_query_raw = (
        rotate(grad_queries, cosine_table, -sine_table)
        .astype(jnp.bfloat16)
        .reshape(group_rows, piece_wide)
    )
    grad_key_raw = (
        rotate(key_part, cosine_table, -sine_table)
        .astype(jnp.bfloat16)
        .reshape(group_rows, piece_wide)
    )
    grad_value = value_part.astype(jnp.bfloat16).reshape(group_rows, piece_wide)
    grad_project = jnp.concatenate([grad_query_raw, grad_key_raw, grad_value], axis=1)
    grad_normed_one = spread(
        times_transposed(grad_project, attn_cols[:, :3].reshape(wide, 3 * piece_wide))
    )
    stamp_grad = jnp.concatenate(
        [
            grad_stamp_key.reshape(clip_count, piece_wide),
            grad_stamp_value.reshape(clip_count, piece_wide),
        ],
        axis=1,
    )
    grad_stamp_normed = split_times_transposed(
        stamp_grad, attn_cols[:, 1:3].reshape(wide, 2 * piece_wide)
    )
    _, norm_one_back = jax.vjp(layer_norm, stream, gain_rows[0], gain_rows[1])
    grad_zero_part, grad_gain_one, grad_bias_one = norm_one_back(grad_normed_one)
    _, norm_stamp_back = jax.vjp(layer_norm, stamps, gain_rows[0], gain_rows[1])
    _, grad_gain_stamp, grad_bias_stamp = norm_stamp_back(grad_stamp_normed)
    frames_grad = (grad_one + grad_zero_part).reshape(clip_count, frame_rows, wide)
    project_grad = outer_sum(group_one, grad_project)
    stamp_weight_grad = split_outer(stamp_normed, stamp_grad)
    attn_piece = jnp.stack(
        [
            project_grad[:, :piece_wide],
            project_grad[:, piece_wide : 2 * piece_wide] + stamp_weight_grad[:, :piece_wide],
            project_grad[:, 2 * piece_wide :] + stamp_weight_grad[:, piece_wide:],
            outer_sum(group_self_branch, self_low),
            outer_sum(group_two, grad_cross_query),
            outer_sum(group_cross_branch, cross_low_out),
        ],
        axis=1,
    )
    cond_grad = jnp.concatenate(
        [
            grad_cross_keys.reshape(clip_count * cond_count, piece_wide),
            grad_cross_values.reshape(clip_count * cond_count, piece_wide),
        ],
        axis=1,
    )
    cross_piece = split_outer(cond_flat, cond_grad).reshape(cond_width, 2, piece_wide)
    ff_piece = jnp.stack(
        [
            outer_sum(group_three, grad_gate_up[:, :piece_ff]),
            outer_sum(group_three, grad_gate_up[:, piece_ff:]),
            outer_sum(group_grad_out, hidden),
        ],
        axis=1,
    )
    norm_grad = jnp.stack(
        [
            grad_gain_one + grad_gain_stamp,
            grad_bias_one + grad_bias_stamp,
            grad_gain_two,
            grad_bias_two,
            grad_gain_three,
            grad_bias_three,
        ],
        axis=0,
    )
    norm_column = norm_grad.T[:, :, None]
    summed_attn, summed_cross, summed_ff, summed_norm = (
        lax.psum_scatter(
            attn_piece.astype(jnp.bfloat16), "dp", scatter_dimension=0, tiled=True
        ).astype(jnp.float32),
        lax.psum_scatter(
            cross_piece.astype(jnp.bfloat16), "dp", scatter_dimension=0, tiled=True
        ).astype(jnp.float32),
        lax.psum_scatter(
            ff_piece.astype(jnp.bfloat16), "dp", scatter_dimension=0, tiled=True
        ).astype(jnp.float32),
        lax.psum_scatter(
            norm_column.astype(jnp.bfloat16), "dp", scatter_dimension=0, tiled=True
        ).astype(jnp.float32),
    )
    owned_attn, owned_cross, owned_ff, owned_norm = (
        lax.all_to_all(
            summed_attn.astype(jnp.bfloat16), "seq", split_axis=0, concat_axis=2, tiled=True
        ).astype(summed_attn.dtype),
        lax.all_to_all(
            summed_cross.astype(jnp.bfloat16), "seq", split_axis=0, concat_axis=2, tiled=True
        ).astype(summed_cross.dtype),
        lax.all_to_all(
            summed_ff.astype(jnp.bfloat16), "seq", split_axis=0, concat_axis=2, tiled=True
        ).astype(summed_ff.dtype),
        lax.all_to_all(
            summed_norm.astype(jnp.bfloat16), "seq", split_axis=0, concat_axis=2, tiled=True
        ).astype(summed_norm.dtype),
    )
    attn_reduced = owned_attn.reshape(owned_attn.shape[0], 6 * wide)
    cross_reduced = owned_cross.reshape(owned_cross.shape[0], 2 * wide)
    ff_reduced = owned_ff.reshape(owned_ff.shape[0], 3 * hidden_width)
    norm_reduced = jnp.sum(owned_norm, axis=2).T
    local_squares = (
        jnp.sum(attn_reduced * attn_reduced)
        + jnp.sum(cross_reduced * cross_reduced)
        + jnp.sum(norm_reduced * norm_reduced)
        + jnp.sum(ff_reduced * ff_reduced)
    )
    total_squares = lax.psum(local_squares, ("dp", "seq"))
    grad_norm = jnp.sqrt(total_squares)
    factor = jnp.minimum(1.0, clip_limit / grad_norm)
    attn_new, attn_first_new, attn_second_new = adam_step(
        attn_weight, attn_first, attn_second, attn_reduced * factor, matrix_rate, matrix_decay
    )
    cross_new, cross_first_new, cross_second_new = adam_step(
        cross_weight, cross_first, cross_second, cross_reduced * factor, matrix_rate, matrix_decay
    )
    norm_new, norm_first_new, norm_second_new = adam_step(
        norm_param, norm_first, norm_second, norm_reduced * factor, gain_rate, 0.0
    )
    ff_new, ff_first_new, ff_second_new = adam_step(
        ff_weight, ff_first, ff_second, ff_reduced * factor, matrix_rate, matrix_decay
    )
    return (
        layer_out,
        frames_grad,
        grad_norm,
        attn_new,
        cross_new,
        norm_new,
        ff_new,
        attn_first_new,
        cross_first_new,
        norm_first_new,
        ff_first_new,
        attn_second_new,
        cross_second_new,
        norm_second_new,
        ff_second_new,
    )


MESH = pl.DeviceIdType.MESH
DMA = pltpu.SemaphoreType.DMA
VMEM_LIMIT = 60 * 2**20


def plane_fits(mesh):
    return mesh.shape["dp"] == 8 and mesh.shape["dp"] % mesh.shape["seq"] == 0


def plane_places():
    place = lax.axis_index("dp")
    return (place, lax.axis_index("seq"), lambda mask: jnp.bitwise_xor(place, mask))


def greet(partners):
    barrier = pltpu.get_barrier_semaphore()
    for partner in partners:
        pl.semaphore_signal(barrier, inc=1, device_id=partner, device_id_type=MESH)
    pl.semaphore_wait(barrier, len(partners))


def remote(source, goal, send_sem, recv_sem, device):
    return pltpu.make_async_remote_copy(
        src_ref=source,
        dst_ref=goal,
        send_sem=send_sem,
        recv_sem=recv_sem,
        device_id=device,
        device_id_type=MESH,
    )


def communicating(collective_id):
    return pltpu.CompilerParams(
        has_side_effects=True, collective_id=collective_id, vmem_limit_bytes=VMEM_LIMIT
    )


def any_spec():
    return pl.BlockSpec(memory_space=pl.ANY)


def greet_cross(group, planes):
    place, depth, flip = plane_places()
    greet(
        [(flip(mask), depth) for mask in range(1, group)]
        + [(place, lax.rem(depth + step, planes)) for step in range(1, planes)]
    )


def by_distance(planes, depth):
    low = [jnp.where(which >= depth, which + 1, which) for which in range(planes - 1)]
    return [
        jnp.where(depth < planes // 2, up, down) for up, down in zip(low, reversed(low))
    ]


def outward_steps(group, planes, kept_ref, own_ref, mid, *sems):
    far_send, far_recv, near_send, near_recv, local_sem = sems
    place, depth, flip = plane_places()
    per = group // planes
    first = []
    others = by_distance(planes, depth)
    for step, origin in reversed(list(enumerate(others))):
        for slot in range(per):
            clip = per * depth + slot
            copy = remote(
                kept_ref.at[slot, origin],
                mid.at[clip],
                far_send.at[slot, step],
                far_recv.at[clip],
                (place, origin),
            )
            copy.start()
            first.append(copy)
    second = []

    def hand_over(block, clip):
        index = len(second)
        away = remote(
            block, own_ref.at[place], near_send.at[index], near_recv.at[place], (clip, depth)
        )
        stay = pltpu.make_async_copy(block, own_ref.at[place], local_sem.at[index])
        pl.when(clip != place)(away.start)
        pl.when(clip == place)(stay.start)
        second.append((clip, away, stay))

    for slot in range(per):
        hand_over(kept_ref.at[slot, depth], per * depth + slot)
    yield
    for source in others:
        for slot in range(per):
            clip = per * source + slot
            block = mid.at[clip]
            remote(
                block, block, far_send.at[0, 0], far_recv.at[clip], (place, source)
            ).wait_recv()
            hand_over(block, clip)
    yield
    for mask in range(1, group):
        other = flip(mask)
        block = own_ref.at[other]
        remote(block, block, near_send.at[0], near_recv.at[other], (other, depth)).wait_recv()
    for clip, away, stay in second:
        pl.when(clip != place)(away.wait_send)
        pl.when(clip == place)(stay.wait)
    for copy in first:
        copy.wait_send()
    yield


def outward_scratch(group, planes):
    return [
        DMA((group // planes, planes)),
        DMA((group,)),
        DMA((group,)),
        DMA((group,)),
        DMA((group,)),
    ]


def settle_body(group, planes, dones, kept_ref, cut_ref, parts_ref, squares_ref, *refs):
    done_refs, refs = refs[:dones], refs[dones:]
    own_ref, mine_ref, norm_ref, total_ref, mid, terms, block, blocks, *sems = refs
    part_send, part_recv, block_send, block_recv, *sems = sems
    place, depth, flip = plane_places()
    devices = [(flip(mask), lax.rem(depth + step, planes)) for mask, step in everyone(planes)]
    greet(devices)
    here = place * planes + depth
    start_swap, end_swap = swap_beside(
        [(lambda other: cut_ref.at[other], lambda other: mine_ref.at[other])], *sems[:3]
    )
    start_swap()
    copies = []
    for index, (other, plane) in enumerate(devices):
        copy = remote(
            parts_ref.at[other * planes + plane],
            terms.at[here],
            part_send.at[index],
            part_recv.at[here],
            (other, plane),
        )
        copy.start()
        copies.append(copy)
    rows = outward_steps(group, planes, kept_ref, own_ref, mid, *sems[3:])
    next(rows)
    terms[here] = parts_ref[here]

    def squares_of(array_ref):
        values = [array_ref[piece].astype(jnp.float32) for piece in range(array_ref.shape[0])]
        return jnp.sum(sum(value * value for value in values))

    squares = squares_ref[0, 0]
    for done_ref in done_refs:
        squares = squares + squares_of(done_ref)
    for other, plane in devices:
        source = other * planes + plane
        one = terms.at[source]
        remote(one, one, part_send.at[0], part_recv.at[source], (other, plane)).wait_recv()
    norm_sum = jnp.sum(terms[...], axis=0)
    norm_ref[...] = norm_sum
    squares = squares + jnp.sum(norm_sum * norm_sum)
    end_swap()
    squares = squares + squares_of(mine_ref)
    block[...] = jnp.full(block.shape, squares)
    blocks[here] = block[...]
    for index, (other, plane) in enumerate(devices):
        copy = remote(
            block, blocks.at[here], block_send.at[index], block_recv.at[here], (other, plane)
        )
        copy.start()
        copies.append(copy)
    next(rows)
    next(rows)
    for other, plane in devices:
        source = other * planes + plane
        one = blocks.at[source]
        remote(one, one, block_send.at[0], block_recv.at[source], (other, plane)).wait_recv()
    total_ref[...] = jnp.sum(blocks[...], axis=0)
    for copy in copies:
        copy.wait_send()


def settle(kept_rows, cut, done, norm_parts, squares, collective_id):
    per, planes, rows, wide = kept_rows.shape
    group = per * planes
    count = norm_parts.shape[0]
    inside = pl.BlockSpec(memory_space=pltpu.VMEM)
    like = lambda shape, array: jax.ShapeDtypeStruct(shape, array.dtype)
    *results, _ = pl.pallas_call(
        functools.partial(settle_body, group, planes, len(done)),
        out_shape=[
            like((group, rows, wide), kept_rows),
            like(cut.shape, cut),
            like(norm_parts.shape[1:], norm_parts),
            like((8, 128), norm_parts),
            like((group, rows, wide), kept_rows),
        ],
        in_specs=[any_spec(), any_spec(), inside, pl.BlockSpec(memory_space=pltpu.SMEM)]
        + [inside] * len(done),
        out_specs=[any_spec()] + [inside] * 3 + [any_spec()],
        scratch_shapes=[
            pltpu.VMEM(norm_parts.shape, jnp.float32),
            pltpu.VMEM((8, 128), jnp.float32),
            pltpu.VMEM((count, 8, 128), jnp.float32),
            DMA((count,)),
            DMA((count,)),
            DMA((count,)),
            DMA((count,)),
        ]
        + swap_beside_scratch(1)
        + outward_scratch(group, planes),
        compiler_params=communicating(collective_id),
    )(kept_rows, cut, norm_parts, squares, *done)
    return results


def everyone(planes):
    return [(mask, step) for mask in range(8) for step in range(planes) if mask or step]


def to_plane_features(values, group, planes):
    width = values.shape[1] // (group * planes)
    starts = [
        (owner * planes + plane) * width for plane in range(planes) for owner in range(group)
    ]
    return jnp.concatenate([values[:, start : start + width] for start in starts], axis=1)


def to_whole_features(values, group, planes):
    width = values.shape[1] // (group * planes)
    starts = [
        (plane * group + owner) * width for owner in range(group) for plane in range(planes)
    ]
    return jnp.concatenate([values[:, start : start + width] for start in starts], axis=1)


def enter_body(
    group,
    planes,
    frames_ref,
    grads_ref,
    valid_ref,
    norm_ref,
    pack_ref,
    attn_ref,
    cross_ref,
    ff_ref,
    kept_ref,
    gains_ref,
    packs_ref,
    first_mine_ref,
    rest_mine_ref,
    ff_low_ref,
    grads_mid_ref,
    mid,
    norms_ref,
    pieces,
    grad_pieces,
    attn_full,
    cross_full,
    first_cut,
    rest_cut,
    ff_full,
    ff_low,
    load_sem,
    near_send,
    near_recv,
    far_send,
    far_recv,
    local_sem,
    norm_send,
    norm_recv,
    swap_send,
    swap_recv,
    stay_sem,
):
    place, depth, flip = plane_places()
    per = group // planes
    low = pieces.dtype
    f32 = jnp.float32
    others = everyone(planes)
    loads = [
        pltpu.make_async_copy(source, goal, load_sem.at[which])
        for which, (source, goal) in enumerate(
            ((attn_ref, attn_full), (cross_ref, cross_full), (ff_ref, ff_full))
        )
    ]
    for copy in loads:
        copy.start()
    own = to_plane_features(frames_ref[...].astype(f32), group, planes).astype(low)
    pieces[...] = own.reshape(pieces.shape)
    greet([(flip(mask), lax.rem(depth + step, planes)) for mask, step in others])
    here = place * planes + depth
    first = []
    for mask in (6, 7, 2, 3, 4, 5, 1):
        other = flip(mask)
        copy = remote(
            pieces.at[other],
            mid.at[place],
            near_send.at[mask],
            near_recv.at[mask],
            (other, depth),
        )
        copy.start()
        first.append((mask, copy))
    small = []
    for index, (mask, step) in enumerate(others):
        copy = remote(
            norm_ref,
            norms_ref.at[here],
            norm_send.at[index],
            norm_recv.at[here],
            (flip(mask), lax.rem(depth + step, planes)),
        )
        copy.start()
        small.append(copy)
    swaps = []

    def swap(which, source, goal):
        for mask in (6, 7, 2, 3, 4, 5, 1):
            other = flip(mask)
            copy = remote(
                source(other),
                goal.at[place],
                swap_send.at[which, mask],
                swap_recv.at[which, mask],
                (other, depth),
            )
            copy.start()
            swaps.append(copy)
        stay = pltpu.make_async_copy(source(place), goal.at[place], stay_sem.at[which])
        stay.start()
        stays.append(stay)

    stays = []
    swap(0, lambda other: pack_ref, packs_ref)
    norms_ref[here] = norm_ref[...]
    loads[0].wait()
    loads[1].wait()
    wide = attn_full.shape[1] // 6
    piece = wide // group
    for device in range(group):
        for block in range(6):
            cut_ref = (first_cut, rest_cut)[block // 3]
            start = block * wide + device * piece
            cut_ref[device, :, block % 3 * piece : (block % 3 + 1) * piece] = attn_full[
                :, start : start + piece
            ].astype(low)
        keys = cross_full[:, device * piece : (device + 1) * piece]
        values = cross_full[:, wide + device * piece : wide + (device + 1) * piece]
        rest_cut[device, :, 3 * piece :] = jnp.concatenate([keys, values], axis=0).astype(low)
    swap(1, lambda other: first_cut.at[other], first_mine_ref)
    swap(2, lambda other: rest_cut.at[other], rest_mine_ref)
    second = []
    arrivals = dict(first)
    for mask in (0, 1, 2, 3, 4, 5, 6, 7):
        source = flip(mask)
        goal, slot = lax.div(source, per), lax.rem(source, per)
        block = pieces.at[place]
        if mask:
            arrivals[mask].wait_recv()
            block = mid.at[source]
        away = remote(
            block,
            kept_ref.at[slot, depth],
            far_send.at[mask],
            far_recv.at[slot, depth],
            (place, goal),
        )
        stay = pltpu.make_async_copy(block, kept_ref.at[slot, depth], local_sem.at[mask])
        pl.when(goal != depth)(away.start)
        pl.when(goal == depth)(stay.start)
        second.append((goal, away, stay))
    grads = to_plane_features(grads_ref[...].astype(f32) * valid_ref[...], group, planes)
    grad_pieces[...] = grads.astype(low).reshape(grad_pieces.shape)
    grads_store = pltpu.make_async_copy(grad_pieces, grads_mid_ref, stay_sem.at[3])
    grads_store.start()
    loads[2].wait()
    tile = ff_full.shape[1] // 24

    def round_tile(index, carry):
        lanes = pl.ds(pl.multiple_of(index * tile, 128), tile)
        ff_low[:, lanes] = ff_full[:, lanes].astype(low)
        return carry

    lax.fori_loop(0, 24, round_tile, 0)
    ff_store = pltpu.make_async_copy(ff_low, ff_low_ref, load_sem.at[3])
    ff_store.start()
    for mask, step in others:
        source = flip(mask) * planes + lax.rem(depth + step, planes)
        block = norms_ref.at[source]
        remote(
            block,
            block,
            norm_send.at[0],
            norm_recv.at[source],
            (flip(mask), lax.rem(depth + step, planes)),
        ).wait_recv()
    width = gains_ref.shape[1] // (group * planes)
    gains_ref[...] = jnp.concatenate(
        [
            norms_ref[owner * planes + plane, :, :width]
            for plane in range(planes)
            for owner in range(group)
        ],
        axis=1,
    )
    for slot in range(per):
        for origin in range(planes):
            block = kept_ref.at[slot, origin]
            pl.when(origin != depth)(
                remote(
                    block,
                    block,
                    far_send.at[0],
                    far_recv.at[slot, origin],
                    (place, lax.rem(depth + 1, planes)),
                ).wait_recv
            )
    ff_store.wait()
    grads_store.wait()
    for copy in swaps:
        copy.wait()
    for stay in stays:
        stay.wait()
    for goal, away, stay in second:
        pl.when(goal != depth)(away.wait_send)
        pl.when(goal == depth)(stay.wait)
    for mask, copy in first:
        copy.wait_send()
    for copy in small:
        copy.wait_send()


def enter(frames, grads, valid, norm_block, pack, attn, cross, ff, planes, collective_id):
    rows, wide = frames.shape
    group = 8
    count = group * planes
    piece = rows // group
    owned = attn.shape[0]
    third = attn.shape[1] // (2 * group)
    rest = third + cross.shape[0] * cross.shape[1] // (owned * group)
    low, f32 = jnp.bfloat16, jnp.float32
    inside = pl.BlockSpec(memory_space=pltpu.VMEM)
    like = jax.ShapeDtypeStruct
    *results, _ = pl.pallas_call(
        functools.partial(enter_body, group, planes),
        out_shape=[
            like((group // planes, planes, piece, wide), low),
            like((norm_block.shape[0], wide), f32),
            like((group,) + pack.shape, f32),
            like((group, owned, third), low),
            like((group, owned, rest), low),
            like(ff.shape, low),
            like((group, piece, wide), low),
            like((group, piece, wide), low),
        ],
        in_specs=[inside] * 4 + [any_spec()] * 4,
        out_specs=[any_spec(), inside] + [any_spec()] * 6,
        scratch_shapes=[
            pltpu.VMEM((count,) + norm_block.shape, f32),
            pltpu.VMEM((group, piece, wide), low),
            pltpu.VMEM((group, piece, wide), low),
            pltpu.VMEM(attn.shape, f32),
            pltpu.VMEM(cross.shape, f32),
            pltpu.VMEM((group, owned, third), low),
            pltpu.VMEM((group, owned, rest), low),
            pltpu.VMEM(ff.shape, f32),
            pltpu.VMEM(ff.shape, low),
            DMA((4,)),
            DMA((group,)),
            DMA((group,)),
            DMA((group,)),
            DMA((group // planes, planes)),
            DMA((group,)),
            DMA((count,)),
            DMA((count,)),
            DMA((4, group)),
            DMA((4, group)),
            DMA((4,)),
        ],
        compiler_params=communicating(collective_id),
    )(frames, grads, valid, norm_block, pack, attn, cross, ff)
    return results


def cond_steps(group, planes, pick_ref, cond_ref, parts, summed, *sems):
    part_send, part_recv, cond_send, cond_recv = sems
    place, depth, flip = plane_places()
    pushes = []
    for step in range(1, planes):
        goal = lax.rem(depth + step, planes)
        copy = remote(
            pick_ref.at[goal],
            parts.at[depth],
            part_send.at[step],
            part_recv.at[depth],
            (place, goal),
        )
        copy.start()
        pushes.append(copy)
    yield
    total = pick_ref[depth].astype(jnp.float32)
    for step in range(1, planes):
        source = lax.rem(depth + step, planes)
        block = parts.at[source]
        remote(
            block, block, part_send.at[0], part_recv.at[source], (place, source)
        ).wait_recv()
        total = total + parts[source].astype(jnp.float32)
    summed[...] = total.astype(summed.dtype)
    cond_ref[place] = total.astype(summed.dtype)
    for mask in range(1, group):
        copy = remote(
            summed,
            cond_ref.at[place],
            cond_send.at[mask],
            cond_recv.at[mask],
            (flip(mask), depth),
        )
        copy.start()
        pushes.append(copy)
    yield
    for mask in range(1, group):
        block = cond_ref.at[flip(mask)]
        remote(
            block, block, cond_send.at[0], cond_recv.at[mask], (flip(mask), depth)
        ).wait_recv()
    for copy in pushes:
        copy.wait_send()
    yield


def inward_over(group, planes, mid_ref, kept_ref, send_sem, recv_sem, local_sem):
    place, depth, flip = plane_places()
    per = group // planes

    def piece(source):
        goal, slot = lax.div(source, per), lax.rem(source, per)
        block = mid_ref.at[source]
        away = remote(
            block,
            kept_ref.at[slot, depth],
            send_sem.at[source],
            recv_sem.at[slot, depth],
            (place, goal),
        )
        stay = pltpu.make_async_copy(block, kept_ref.at[slot, depth], local_sem.at[source])
        return goal != depth, away, stay

    def begin():
        for source in range(group):
            leaves, away, stay = piece(source)
            pl.when(leaves)(away.start)
            pl.when(jnp.logical_not(leaves))(stay.start)

    def end():
        for slot in range(per):
            for origin in range(planes):
                block = kept_ref.at[slot, origin]
                pl.when(origin != depth)(
                    remote(
                        block,
                        block,
                        send_sem.at[0],
                        recv_sem.at[slot, origin],
                        (place, lax.rem(depth + 1, planes)),
                    ).wait_recv
                )
        for source in range(group):
            leaves, away, stay = piece(source)
            pl.when(leaves)(away.wait_send)
            pl.when(jnp.logical_not(leaves))(stay.wait)

    return begin, end


def dot_tiles(left, right_ref, span, transposed, width):
    first, last = span
    count = right_ref.shape[0] if transposed else last - first
    for start in range(0, count, width):
        stop = min(start + width, count)
        if transposed:
            yield start, stop, times_transposed(left, right_ref[start:stop, first:last])
        else:
            yield start, stop, jnp.dot(
                left, right_ref[:, first + start : first + stop], preferred_element_type=jnp.float32
            )


def window_of(matrix, span):
    first, last = span or (0, matrix.shape[1])
    start = first // 128 * 128
    while (matrix.shape[1] - start) * 2 > matrix.shape[1] and start and start % 384:
        start -= 128
    stop = min(-(-last // 128) * 128, matrix.shape[1])
    return (start, stop - start), (first - start, last - start)


def cross_shares(queries, pair_ref, bias_ref):
    wide = queries[0].shape[1]
    keys = [
        (clip, start, pair_ref[clip, :, start : start + HDIM])
        for clip in range(len(queries))
        for start in range(0, wide, HDIM)
    ]
    scores = [
        times_transposed(queries[clip][:, start : start + HDIM], key) * HDIM ** (-0.5)
        + bias_ref[clip]
        for clip, start, key in keys
    ]
    tops = [jnp.max(score, axis=1, keepdims=True) for score in scores]
    expos = [jnp.exp(score - top) for score, top in zip(scores, tops)]
    sums = [jnp.sum(expo, axis=1, keepdims=True) for expo in expos]
    return keys, [expo / total for expo, total in zip(expos, sums)]


def by_clip_of(results, clips, low):
    heads = len(results) // clips
    return [
        jnp.concatenate(results[clip * heads : (clip + 1) * heads], axis=1).astype(low)
        for clip in range(clips)
    ]


def cross_rows(queries, pair_ref, bias_ref):
    low, wide = queries[0].dtype, queries[0].shape[1]
    keys, shares = cross_shares(queries, pair_ref, bias_ref)
    mixed = [
        jnp.dot(
            share.astype(low),
            pair_ref[clip, :, wide + start : wide + start + HDIM],
            preferred_element_type=jnp.float32,
        )
        for (clip, start, _), share in zip(keys, shares)
    ]
    return by_clip_of(mixed, len(queries), low)


def cross_rows_back(queries, grads, pair_ref, bias_ref, pair_grad_ref):
    low, wide = queries[0].dtype, queries[0].shape[1]
    scale = HDIM ** (-0.5)
    keys, shares = cross_shares(queries, pair_ref, bias_ref)
    own_grads = [grads[clip][:, start : start + HDIM] for clip, start, _ in keys]
    grad_shares = [
        times_transposed(grad, pair_ref[clip, :, wide + start : wide + start + HDIM])
        for (clip, start, _), grad in zip(keys, own_grads)
    ]
    deltas = [
        jnp.sum(share * grad_share, axis=1, keepdims=True)
        for share, grad_share in zip(shares, grad_shares)
    ]
    scores = [
        (share * (grad_share - delta)).astype(low)
        for share, grad_share, delta in zip(shares, grad_shares, deltas)
    ]
    results = [
        jnp.dot(score, key, preferred_element_type=jnp.float32) * scale
        for score, (_, _, key) in zip(scores, keys)
    ]
    key_grads = [
        outer_sum(score, queries[clip][:, start : start + HDIM]) * scale
        for score, (clip, start, _) in zip(scores, keys)
    ]
    value_grads = [
        outer_sum(share.astype(low), grad) for share, grad in zip(shares, own_grads)
    ]
    heads = len(keys) // len(queries)
    for clip in range(len(queries)):
        mine = slice(clip * heads, (clip + 1) * heads)
        pair_grad_ref[clip] += jnp.concatenate(key_grads[mine] + value_grads[mine], axis=1)
    return by_clip_of(results, len(queries), low)


def outer_columns(out_ref, start, small, big):
    width = small.shape[-1]
    product = outer_sum(small.reshape(-1, width), big.reshape(-1, big.shape[-1]))
    out_ref[:, start : start + width] = product.T.astype(out_ref.dtype)


def by_slot_loads(source, goal, sem):
    clips = source.shape[0]
    return [
        pltpu.make_async_copy(source.at[clip, slot], goal.at[slot, clip], sem.at[slot, clip])
        for slot in range(8)
        for clip in range(clips)
    ]


def gather_parts(clips, rows, sub, mode, window, span, ins, outs_refs, scratch):
    ins, outs_refs, scratch = list(ins), list(outs_refs), list(scratch)
    mat_ref = ins.pop(0) if mode != "rows" else None
    gates_ref = ins.pop(0) if mode == "gates" else None
    pair_ref, bias_ref = (ins.pop(0), ins.pop(0)) if mode in ("cross", "cross_back") else (None, None)
    query_ref = ins.pop(0) if mode == "cross_back" else None
    all_ref = outs_refs.pop(0)
    pair_grad_ref = outs_refs.pop() if mode == "cross_back" else None
    prod_refs = outs_refs
    take = lambda count: [scratch.pop(0) for _ in range(count)]
    held, send_sem, recv_sem, all_sem = take(4)
    mat, mat_sem = take(2) if mode != "rows" else (None, None)
    stages = take(len(prod_refs))
    prod_sem = take(1)[0] if prod_refs else None
    gates, gates_sem = take(2) if mode == "gates" else (None, None)
    queries, query_sem = take(2) if mode == "cross_back" else (None, None)
    place, depth, flip = plane_places()
    core, beside_x, beside_y, across = flip(1), flip(2), flip(4), flip(6)
    loads = []
    gate_loads = {}
    if mode != "rows":
        loads.append(pltpu.make_async_copy(mat_ref.at[:, pl.ds(*window)], mat, mat_sem))
    if mode == "cross_back":
        loads.append(pltpu.make_async_copy(query_ref, queries, query_sem))
    if mode == "gates":
        for mask in (0, 1, 2, 4, 3, 5, 6, 7):
            slot = flip(mask)
            gate_loads[mask] = [
                pltpu.make_async_copy(
                    gates_ref.at[clip, slot], gates.at[slot, clip], gates_sem.at[slot, clip]
                )
                for clip in range(clips)
            ]

    def load():
        if mode == "cross_back":
            pair_grad_ref[...] = jnp.zeros_like(pair_grad_ref)
        for copy in loads + [copy for copies in gate_loads.values() for copy in copies]:
            copy.start()

    chunks = [(clip, part) for clip in range(clips) for part in range(rows // sub)]
    count = len(chunks)
    half = count // 2
    sends = []

    def view(slot, index):
        clip, part = chunks[index]
        return held.at[slot, clip, pl.ds(part * sub, sub)]

    def send(slot, index, device):
        block = view(slot, index)
        copy = remote(
            block, block, send_sem.at[len(sends)], recv_sem.at[slot, index], (device, depth)
        )
        copy.start()
        sends.append(copy)

    def arrived(slot, index):
        block = view(slot, index)
        remote(
            block, block, send_sem.at[0], recv_sem.at[slot, index], (core, depth)
        ).wait_recv()

    x_order = list(range(count))
    y_order = list(range(half, count)) + list(range(half))

    def put(index, values):
        clip, part = chunks[index]
        held[place, clip, pl.ds(part * sub, sub)] = values.astype(held.dtype)
        if index < half:
            send(place, index, beside_x)
        else:
            send(place, index, beside_y)
        send(place, index, core)
        if index == count - 1:
            for low in range(half):
                send(place, half + low, beside_x)
                send(place, low, beside_y)

    outs = []

    def leave_here(source, goal, sem, major):
        for clip in range(clips):
            there = goal.at[major, clip] if goal.shape[0] == 8 else goal.at[clip, major]
            copy = pltpu.make_async_copy(source.at[major, clip], there, sem.at[major, clip])
            copy.start()
            outs.append(copy)

    def multiply(mask):
        slot = flip(mask)
        leave_here(held, all_ref, all_sem, slot)
        if mode == "rows":
            return
        left = held[slot].reshape(clips * rows, held.shape[3])
        for copy in gate_loads.get(mask, ()):
            copy.wait()
        for start, stop, product in dot_tiles(
            left, mat, span, False, 256 * (1 if mode == "gates" else 3)
        ):
            product = product.reshape(clips, rows, stop - start)
            if mode == "cross":
                query = product.astype(stages[0].dtype)
                stages[0][slot] = query
                mixed = cross_rows([query[clip] for clip in range(clips)], pair_ref, bias_ref)
                for clip in range(clips):
                    stages[1][slot, clip] = mixed[clip]
                continue
            if mode == "cross_back":
                grad = product.astype(stages[0].dtype)
                results = cross_rows_back(
                    [queries[clip, slot] for clip in range(clips)],
                    [grad[clip] for clip in range(clips)],
                    pair_ref,
                    bias_ref,
                    pair_grad_ref,
                )
                for clip in range(clips):
                    stages[0][slot, clip] = results[clip]
                continue
            if mode == "dot":
                stages[0][slot, :, :, start:stop] = product.astype(stages[0].dtype)
                continue
            width = stages[1].shape[3]
            gate = gates[slot, :, :, start:stop]
            up = gates[slot, :, :, width + start : width + stop]
            sigmoid = jax.nn.sigmoid(gate)
            active = gate * sigmoid
            low = stages[0].dtype
            stages[0][slot, :, :, start:stop] = (
                product * up * sigmoid * (1.0 + gate * (1.0 - sigmoid))
            ).astype(low)
            stages[0][slot, :, :, width + start : width + stop] = (product * active).astype(low)
            stages[1][slot, :, :, start:stop] = (active * up).astype(low)
        for which, (stage, prod_ref) in enumerate(zip(stages, prod_refs)):
            leave_here(stage, prod_ref, prod_sem.at[which], slot)

    def run(late=lambda: None):
        for copy in loads:
            copy.wait()
        multiply(0)
        for step in range(count):
            x_index, y_index = x_order[step], y_order[step]
            arrived(beside_x, x_index)
            if x_index < half:
                send(beside_x, x_index, beside_y)
            send(beside_x, x_index, core)
            arrived(beside_y, y_index)
            if y_index >= half:
                send(beside_y, y_index, beside_x)
            send(beside_y, y_index, core)
            if step == 0:
                for index in range(count):
                    arrived(core, index)
                multiply(1)
        late()
        multiply(2)
        for step in range(half):
            for index in (x_order[step], y_order[step]):
                arrived(across, index)
                send(across, index, core)
            if step == 0:
                multiply(4)
        for mask in (3, 5):
            for index in range(count):
                arrived(flip(mask), index)
            multiply(mask)
        multiply(6)
        for index in range(count):
            arrived(flip(7), index)
        multiply(7)
        for copy in outs:
            copy.wait()
        for copy in sends:
            copy.wait_send()

    return load, put, run


def chunk_order(clips, rows, sub):
    half = clips * (rows // sub) // 2
    return [index for low in range(half) for index in (low, half + low)]


def gather_plan(clips, rows, wide, sub, matrix, kind, gate_up, span, pair, bias, query):
    count = clips * (rows // sub)
    low = jnp.bfloat16
    inside = pl.BlockSpec(memory_space=pltpu.VMEM)
    by_clip = lambda columns, of: jax.ShapeDtypeStruct((clips, 8, rows, columns), of)
    by_device = lambda columns, of: jax.ShapeDtypeStruct((8, clips, rows, columns), of)
    mode = "rows" if matrix is None else "dot"
    if gate_up is not None:
        mode = "gates"
    if pair is not None:
        mode = "cross" if query is None else "cross_back"
    window = inner = None
    args, in_specs = [], []
    outs = [by_device(wide, low) if mode == "gates" else by_clip(wide, low)]
    scratch = [
        pltpu.VMEM((8, clips, rows, wide), low),
        DMA((7 * count,)),
        DMA((8, count)),
        DMA((8, clips)),
    ]
    if mode != "rows":
        window, inner = window_of(matrix, span)
        columns = inner[1] - inner[0]
        args.append(matrix)
        in_specs.append(any_spec())
        scratch += [pltpu.VMEM((wide, window[1]), low), DMA(())]
    if mode == "dot":
        outs.append(by_clip(columns, kind))
        scratch += [pltpu.VMEM((8, clips, rows, columns), kind), DMA((1, 8, clips))]
    if mode == "gates":
        args.append(gate_up.reshape(clips, 8, rows, 2 * columns))
        in_specs.append(any_spec())
        outs += [by_clip(2 * columns, low), by_device(columns, low)]
        scratch += [
            pltpu.VMEM((8, clips, rows, 2 * columns), low),
            pltpu.VMEM((8, clips, rows, columns), low),
            DMA((2, 8, clips)),
            pltpu.VMEM((8, clips, rows, 2 * columns), jnp.float32),
            DMA((8, clips)),
        ]
    if mode == "cross":
        args += [pair, bias]
        in_specs += [inside] * 2
        outs += [by_clip(columns, low)] * 2
        scratch += [pltpu.VMEM((8, clips, rows, columns), low)] * 2 + [DMA((2, 8, clips))]
    out_specs = [any_spec()] * len(outs)
    if mode == "cross_back":
        args += [pair, bias, query.reshape(clips, 8, rows, columns)]
        in_specs += [inside, inside, any_spec()]
        outs += [by_clip(columns, low), jax.ShapeDtypeStruct(pair.shape, jnp.float32)]
        out_specs += [any_spec(), inside]
        scratch += [
            pltpu.VMEM((8, clips, rows, columns), low),
            DMA((1, 8, clips)),
            pltpu.VMEM((clips, 8, rows, columns), low),
            DMA(()),
        ]
    return (mode, window, inner), args, in_specs, outs, out_specs, scratch


def flat_rows(results):
    return [
        block.reshape(-1, block.shape[3]) if len(block.shape) == 4 else block for block in results
    ]


def gather_dot_body(clips, rows, sub, normed, plan, beside, outer, counts, own_ref, *refs):
    refs = list(refs)
    take = lambda count: [refs.pop(0) for _ in range(count)]
    gain_ref = take(1)[0] if normed else None
    ins = take(counts[0])
    pick_ref = take(1)[0] if beside else None
    past_ref, mixed_ref = take(2) if outer else (None, None)
    outs = take(counts[1])
    cond_ref = take(1)[0] if beside else None
    outer_ref = take(1)[0] if outer else None
    scratch = take(counts[2])
    load, put, run = gather_parts(clips, rows, sub, *plan, ins, outs, scratch)
    load()
    if outer:
        past, mixed, past_sem, mixed_sem = refs
        outer_loads = by_slot_loads(past_ref, past, past_sem)
        outer_loads += by_slot_loads(mixed_ref, mixed, mixed_sem)
        for copy in outer_loads:
            copy.start()
    place, depth, flip = plane_places()
    if beside:
        greet_cross(*beside)
        cond = cond_steps(*beside, pick_ref, cond_ref, *refs)
        next(cond)
    else:
        greet([(flip(1), depth), (flip(2), depth), (flip(4), depth)])
    for index in chunk_order(clips, rows, sub):
        clip, part = divmod(index, rows // sub)
        values = own_ref[clip, pl.ds(part * sub, sub)]
        if normed:
            values = layer_norm(values.astype(jnp.float32), gain_ref[0:1], gain_ref[1:2])
        put(index, values)
    if beside:
        run(lambda: next(cond))
        next(cond)
    else:
        run()
    if outer:
        for copy in outer_loads:
            copy.wait()
        held, queries = scratch[0], scratch[6]
        outer_columns(outer_ref, 0, queries[...], past[...])
        outer_columns(outer_ref, queries.shape[3], mixed[...], held[...])


def gather_dot(
    own_rows,
    matrix,
    kind,
    collective_id,
    gains=None,
    picked=None,
    gate_up=None,
    span=None,
    pair=None,
    bias=None,
    query=None,
    outer=None,
    sub=64,
):
    clips, rows, wide = own_rows.shape
    plan, args, in_specs, outs, out_specs, scratch = gather_plan(
        clips, rows, wide, sub, matrix, kind, gate_up, span, pair, bias, query
    )
    inside = pl.BlockSpec(memory_space=pltpu.VMEM)
    counts = (len(args), len(outs), len(scratch))
    if gains is not None:
        args, in_specs = [gains] + args, [inside] + in_specs
    args, in_specs = [own_rows] + args, [inside] + in_specs
    beside = None
    if picked is not None:
        planes, per, tokens, cond_wide = picked.shape
        beside = (planes * per, planes)
        args.append(picked)
        in_specs.append(inside)
        outs.append(jax.ShapeDtypeStruct((8, per, tokens, cond_wide), picked.dtype))
        out_specs.append(inside)
        scratch += [
            pltpu.VMEM(picked.shape, picked.dtype),
            pltpu.VMEM(picked.shape[1:], picked.dtype),
            DMA((planes,)),
            DMA((planes,)),
            DMA((8,)),
            DMA((8,)),
        ]
    if outer is not None:
        past, mixed = outer
        width = mixed.shape[1]
        args += [past.reshape(clips, 8, rows, wide), mixed.reshape(clips, 8, rows, width)]
        in_specs += [any_spec()] * 2
        outs.append(jax.ShapeDtypeStruct((wide, 2 * width), jnp.bfloat16))
        out_specs.append(inside)
        scratch += [
            pltpu.VMEM((8, clips, rows, wide), jnp.bfloat16),
            pltpu.VMEM((8, clips, rows, width), jnp.bfloat16),
            DMA((8, clips)),
            DMA((8, clips)),
        ]
    results = pl.pallas_call(
        functools.partial(
            gather_dot_body,
            clips,
            rows,
            sub,
            gains is not None,
            plan,
            beside,
            outer is not None,
            counts,
        ),
        out_shape=outs,
        in_specs=in_specs,
        out_specs=out_specs,
        scratch_shapes=scratch,
        compiler_params=communicating(collective_id),
    )(*args)
    return flat_rows(results[: counts[1]]) + list(results[counts[1] :])


def reduce_steps(clips, rows, sub, multiply, final, terms, pair, turn, from_x, from_y, *sems):
    send_sem, core_sem, turn_sem, x_sem, y_sem = sems
    place, depth, flip = plane_places()
    core, beside_x, beside_y = flip(1), flip(2), flip(4)
    chunks = [(clip, part) for clip in range(clips) for part in range(rows // sub)]
    count = len(chunks)
    half = count // 2
    sends = []

    def send(source, goal, recv_sem, device):
        copy = remote(source, goal, send_sem.at[len(sends)], recv_sem, (device, depth))
        copy.start()
        sends.append(copy)

    def arrived(block, recv_sem):
        remote(block, block, send_sem.at[0], recv_sem, (core, depth)).wait_recv()

    def term(number, index):
        clip, part = chunks[index]
        return terms.at[number, clip, pl.ds(part * sub, sub)]

    def give(number, chip):
        for index in range(count):
            send(term(number, index), pair.at[index, chip], core_sem.at[index, chip], core)

    def total(*blocks):
        return sum(block[...].astype(jnp.float32) for block in blocks)

    def add(block, other):
        block[...] = total(block, other).astype(terms.dtype)

    numbers = {3: 1, 1: 3, 2: 5, 0: 7}

    def combine(chip, index):
        arrived(pair.at[index, chip], core_sem.at[index, chip])
        block = term(numbers[chip], index)
        add(block, pair.at[index, chip])
        return block

    multiply(0)
    give(0, 3)
    multiply(1)
    multiply(2)
    give(2, 1)
    for low in range(half):
        high = half + low
        send(combine(3, low), turn.at[low], turn_sem.at[low], beside_x)
        send(combine(3, high), turn.at[high], turn_sem.at[high], beside_y)
    multiply(3)
    multiply(4)
    give(4, 2)
    for low in range(half):
        send(combine(1, low), from_x.at[low], x_sem.at[low], beside_x)
    multiply(5)
    for high in range(half, count):
        send(combine(2, high), from_y.at[high], y_sem.at[high], beside_y)
    multiply(6)
    give(6, 0)
    multiply(7)
    yield
    for low in range(half):
        high = half + low
        block = combine(2, low)
        arrived(turn.at[low], turn_sem.at[low])
        add(block, turn.at[low])
        send(block, from_y.at[low], y_sem.at[low], beside_y)
        block = combine(1, high)
        arrived(turn.at[high], turn_sem.at[high])
        add(block, turn.at[high])
        send(block, from_x.at[high], x_sem.at[high], beside_x)
    yield
    for index in chunk_order(clips, rows, sub):
        clip, part = chunks[index]
        arrived(pair.at[index, 0], core_sem.at[index, 0])
        arrived(from_x.at[index], x_sem.at[index])
        arrived(from_y.at[index], y_sem.at[index])
        result = total(term(7, index), pair.at[index, 0], from_x.at[index], from_y.at[index])
        final(index, clip, pl.ds(part * sub, sub), result)
    yield
    for copy in sends:
        copy.wait_send()
    yield


def plane_order():
    place, depth, flip = plane_places()
    return [flip(mask) for mask in (7, 6, 3, 2, 5, 4, 1, 0)]


def reduce_scratch(clips, rows, sub, wide):
    count = clips * (rows // sub)
    low = jnp.bfloat16
    return [
        pltpu.VMEM((8, clips, rows, wide), low),
        pltpu.VMEM((count, 4, sub, wide), low),
        pltpu.VMEM((count, sub, wide), low),
        pltpu.VMEM((count, sub, wide), low),
        pltpu.VMEM((count, sub, wide), low),
        DMA((7 * count,)),
        DMA((count, 4)),
        DMA((count,)),
        DMA((count,)),
        DMA((count,)),
    ]


def norm_back(values, gain, grad):
    center = values - jnp.mean(values, axis=1, keepdims=True)
    inverse = lax.rsqrt(jnp.mean(center * center, axis=1, keepdims=True) + norm_eps)
    unit = center * inverse
    stats = [
        jnp.sum(grad * unit, axis=0, keepdims=True),
        jnp.sum(grad, axis=0, keepdims=True),
    ]
    scaled = grad * gain
    result = inverse * (
        scaled
        - jnp.mean(scaled, axis=1, keepdims=True)
        - unit * jnp.mean(scaled * unit, axis=1, keepdims=True)
    )
    return result, stats


def final_back(values_ref, gain_ref, base_ref, sum_ref, stats_ref, order=None):
    def final(index, clip, span, result):
        if values_ref is not None:
            result, stats = norm_back(values_ref[clip, span], gain_ref[...], result)
            for which, row in enumerate(stats):
                row = row + stats_ref[which : which + 1] if index else row
                stats_ref[which : which + 1] = row
        result = base_ref[clip, span].astype(jnp.float32) + result
        if order:
            result = to_whole_features(result, *order)
        sum_ref[clip, span] = result.astype(sum_ref.dtype)
        return result

    return final


def terms_of(clips, rows, blocks, mat, span, terms):
    def multiply(number):
        block = blocks(number)
        block = block.reshape(clips * rows, block.shape[-1])
        for start, stop, product in dot_tiles(block, mat, span, True, 256 * 2):
            terms[number, :, :, start:stop] = product.astype(terms.dtype).reshape(
                clips, rows, stop - start
            )

    return multiply


def dot_reduce_body(clips, rows, sub, window, span, back, order, swapped, left_ref, mat_ref, base_ref, *refs):
    refs = list(refs)
    take = lambda count: [refs.pop(0) for _ in range(count)]
    values_ref, gain_ref = take(2) if back else (None, None)
    cut_ref = take(1)[0] if swapped else None
    sum_ref = take(1)[0]
    stats_ref = take(1)[0] if back else None
    mine_ref = take(1)[0] if swapped else None
    left, mat, mat_sem, left_sem = take(4)
    swap_sems = take(3) if swapped else None
    terms = refs[0]
    place, depth, flip = plane_places()
    load = pltpu.make_async_copy(mat_ref.at[:, pl.ds(*window)], mat, mat_sem)
    load.start()
    loads = {}
    for number, slot in enumerate(plane_order()):
        loads[number] = [
            pltpu.make_async_copy(
                left_ref.at[clip, slot], left.at[number, clip], left_sem.at[number, clip]
            )
            for clip in range(clips)
        ]
        for copy in loads[number]:
            copy.start()
    if swapped:
        start_swap, end_swap = swap_beside(
            [(lambda other: cut_ref.at[other], lambda other: mine_ref.at[other])], *swap_sems
        )
        greet([(flip(mask), depth) for mask in range(1, 8)])
        start_swap()
    else:
        greet([(flip(1), depth), (flip(2), depth), (flip(4), depth)])
    load.wait()

    def blocks(number):
        for copy in loads[number]:
            copy.wait()
        return left[number]

    steps = reduce_steps(
        clips,
        rows,
        sub,
        terms_of(clips, rows, blocks, mat, span, terms),
        final_back(values_ref, gain_ref, base_ref, sum_ref, stats_ref, order),
        *refs,
    )
    for _ in steps:
        pass
    if swapped:
        end_swap()


def dot_reduce(
    left,
    matrix,
    clips,
    collective_id,
    base,
    span=None,
    back=None,
    kind=jnp.float32,
    order=None,
    cut=None,
    sub=64,
):
    wide = matrix.shape[0]
    rows, inner = left.shape[0] // (8 * clips), left.shape[1]
    low = jnp.bfloat16
    window, span = window_of(matrix, span)
    inside = pl.BlockSpec(memory_space=pltpu.VMEM)
    args = [left.reshape(clips, 8, rows, inner), matrix, base]
    in_specs = [any_spec(), any_spec(), inside]
    outs, out_specs = [jax.ShapeDtypeStruct((clips, rows, wide), kind)], [inside]
    if back is not None:
        args += list(back)
        in_specs += [inside] * 2
        outs.append(jax.ShapeDtypeStruct((2, wide), jnp.float32))
        out_specs.append(inside)
    swap_sems = []
    if cut is not None:
        args.append(cut)
        in_specs.append(any_spec())
        outs.append(jax.ShapeDtypeStruct(cut.shape, cut.dtype))
        out_specs.append(any_spec())
        swap_sems = swap_beside_scratch(1)
    return pl.pallas_call(
        functools.partial(
            dot_reduce_body,
            clips,
            rows,
            sub,
            window,
            span,
            back is not None,
            order,
            cut is not None,
        ),
        out_shape=outs,
        in_specs=in_specs,
        out_specs=out_specs,
        scratch_shapes=[
            pltpu.VMEM((8, clips, rows, inner), low),
            pltpu.VMEM((wide, window[1]), low),
            DMA(()),
            DMA((8, clips)),
        ]
        + swap_sems
        + reduce_scratch(clips, rows, sub, wide),
        compiler_params=communicating(collective_id),
    )(*args)


def add_steps(parts_ref, sum_ref, landed, send_sem, recv_sem, local_sem):
    place, depth, flip = plane_places()
    planes = parts_ref.shape[0]
    copies = []
    for step in range(1, planes):
        goal = lax.rem(depth + step, planes)
        copy = remote(
            parts_ref.at[goal],
            landed.at[depth],
            send_sem.at[step],
            recv_sem.at[depth],
            (place, goal),
        )
        copy.start()
        copies.append(copy)
    stay = pltpu.make_async_copy(parts_ref.at[depth], landed.at[depth], local_sem)
    stay.start()
    yield
    stay.wait()
    for step in range(1, planes):
        source = lax.rem(depth + step, planes)
        block = landed.at[source]
        remote(block, block, send_sem.at[0], recv_sem.at[source], (place, source)).wait_recv()
    sum_ref[...] = jnp.sum(landed[...].astype(jnp.float32), axis=0).astype(sum_ref.dtype)
    for copy in copies:
        copy.wait_send()
    yield


def reduce_gather_body(
    clips, rows, sub, spans, back, normed, plan, counts, passing, outer, leaving, adding, left_ref, mat_ref, base_ref, *refs
):
    refs = list(refs)
    take = lambda count: [refs.pop(0) for _ in range(count)]
    values_ref, back_gain_ref = take(2) if back else (None, None)
    gain_ref = take(1)[0] if normed else None
    ins = take(counts[0])
    mid_ref = take(1)[0] if passing else None
    low_ref, ending_ref = take(2) if outer else (None, None)
    leaving_ref = take(1)[0] if leaving else None
    adding_ref = take(1)[0] if adding else None
    sum_ref = take(1)[0]
    stats_ref = take(1)[0] if back else None
    outs = take(counts[1])
    kept_ref = take(1)[0] if passing else None
    outer_ref = take(1)[0] if outer else None
    own_ref, own_mid = take(2) if leaving else (None, None)
    added_ref = take(1)[0] if adding else None
    left, mat, mat_sem, left_sem = take(4)
    terms, *others = reduce_refs = take(10)
    gather_scratch = take(counts[2])
    load, put, run = gather_parts(clips, rows, sub, *plan, ins, outs, gather_scratch)
    window, span = spans
    place, depth, flip = plane_places()
    mat_load = pltpu.make_async_copy(mat_ref.at[:, pl.ds(*window)], mat, mat_sem)
    mat_load.start()
    loads = {}
    for number, slot in enumerate(plane_order()):
        loads[number] = [
            pltpu.make_async_copy(
                left_ref.at[clip, slot], left.at[number, clip], left_sem.at[number, clip]
            )
            for clip in range(clips)
        ]
        for copy in loads[number]:
            copy.start()
    load()
    if outer:
        low, low_sem = take(2)
        outer_loads = by_slot_loads(low_ref, low, low_sem)
        for copy in outer_loads:
            copy.start()
    if adding:
        adder = add_steps(adding_ref, added_ref, *take(4))
    if passing:
        greet_cross(*passing)
        pass_rows, end_rows = inward_over(*passing, mid_ref, kept_ref, *refs)
        pass_rows()
    elif leaving:
        greet_cross(*leaving)
        going = outward_steps(*leaving, leaving_ref, own_ref, own_mid, *refs)
        next(going)
    else:
        greet([(flip(1), depth), (flip(2), depth), (flip(4), depth)])
    mat_load.wait()

    def blocks(number):
        for copy in loads[number]:
            copy.wait()
        return left[number]

    keep = final_back(values_ref, back_gain_ref, base_ref, sum_ref, stats_ref)

    def final(index, clip, span_rows, result):
        result = keep(index, clip, span_rows, result)
        if normed:
            result = layer_norm(result, gain_ref[0:1], gain_ref[1:2])
        put(index, result)

    steps = reduce_steps(
        clips,
        rows,
        sub,
        terms_of(clips, rows, blocks, mat, span, terms),
        final,
        *reduce_refs,
    )

    next(steps)
    next(steps)
    next(steps)
    if adding:
        next(adder)
    run((lambda: next(going)) if leaving else (lambda: None))
    if outer:
        for copy in outer_loads:
            copy.wait()
        outer_columns(outer_ref, 0, low[...], gather_scratch[0][...])
        outer_ref[:, low.shape[3] :] = ending_ref[...]
    next(steps)
    if passing:
        end_rows()
    if leaving:
        next(going)
    if adding:
        next(adder)


def reduce_gather(
    left,
    matrix,
    clips,
    collective_id,
    base,
    second,
    kind=jnp.bfloat16,
    span=None,
    back=None,
    gains=None,
    second_span=None,
    pair=None,
    bias=None,
    passing=None,
    outer=None,
    leaving=None,
    adding=None,
    sub=64,
):
    wide = matrix.shape[0]
    rows, inner = left.shape[0] // (8 * clips), left.shape[1]
    low = jnp.bfloat16
    spans = window_of(matrix, span)
    inside = pl.BlockSpec(memory_space=pltpu.VMEM)
    plan, more, more_specs, outs, out_specs, more_scratch = gather_plan(
        clips, rows, wide, sub, second, kind, None, second_span, pair, bias, None
    )
    counts = (len(more), len(outs), len(more_scratch))
    args = [left.reshape(clips, 8, rows, inner), matrix, base]
    in_specs = [any_spec(), any_spec(), inside]
    first_outs = [jax.ShapeDtypeStruct((clips, rows, wide), jnp.float32)]
    scratch = [
        pltpu.VMEM((8, clips, rows, inner), low),
        pltpu.VMEM((wide, spans[0][1]), low),
        DMA(()),
        DMA((8, clips)),
    ] + reduce_scratch(clips, rows, sub, wide)
    if back is not None:
        args += list(back)
        in_specs += [inside] * 2
        first_outs.append(jax.ShapeDtypeStruct((2, wide), jnp.float32))
    if gains is not None:
        args.append(gains)
        in_specs.append(inside)
    args += more
    in_specs += more_specs
    scratch += more_scratch
    outs = first_outs + outs
    out_specs = [inside] * len(first_outs) + out_specs
    flat = len(outs)
    if passing is not None:
        group, piece, _ = passing.shape
        planes = group // clips
        args.append(passing)
        in_specs.append(any_spec())
        outs.append(jax.ShapeDtypeStruct((clips, planes, piece, wide), passing.dtype))
        out_specs.append(any_spec())
        scratch += [DMA((group,)), DMA((clips, planes)), DMA((group,))]
    if outer is not None:
        low_rows, ending = outer
        columns = low_rows.shape[1]
        args += [low_rows.reshape(clips, 8, rows, columns), ending]
        in_specs += [any_spec(), inside]
        outs.append(jax.ShapeDtypeStruct((wide, columns + ending.shape[1]), low))
        out_specs.append(inside)
        scratch += [pltpu.VMEM((8, clips, rows, columns), low), DMA((8, clips))]
    if leaving is not None:
        per, planes, piece, _ = leaving.shape
        group = per * planes
        args.append(leaving)
        in_specs.append(any_spec())
        outs += [jax.ShapeDtypeStruct((group, piece, wide), leaving.dtype)] * 2
        leaving_mid = len(outs) - 1
        out_specs += [any_spec()] * 2
    if adding is not None:
        args.append(adding)
        in_specs.append(any_spec())
        outs.append(jax.ShapeDtypeStruct(adding.shape[1:], adding.dtype))
        out_specs.append(inside)
        scratch += [
            pltpu.VMEM(adding.shape, adding.dtype),
            DMA((adding.shape[0],)),
            DMA((adding.shape[0],)),
            DMA(()),
        ]
    if leaving is not None:
        scratch += outward_scratch(group, planes)
    results = pl.pallas_call(
        functools.partial(
            reduce_gather_body,
            clips,
            rows,
            sub,
            spans,
            back is not None,
            gains is not None,
            plan,
            counts,
            passing is not None and (group, planes),
            outer is not None,
            leaving is not None and (group, planes),
            adding is not None,
        ),
        out_shape=outs,
        in_specs=in_specs,
        out_specs=out_specs,
        scratch_shapes=scratch,
        compiler_params=communicating(collective_id),
    )(*args)
    first = len(first_outs)
    if leaving is not None:
        results = [block for which, block in enumerate(results) if which != leaving_mid]
    return list(results[:first]) + flat_rows(results[first:flat]) + list(results[flat:])


def ff_outer_body(
    order_of,
    clips,
    rows,
    sub,
    gates_ref,
    hidden_ref,
    down_ref,
    normed_ref,
    grads_ref,
    values_ref,
    layer_ref,
    outer_ref,
    gates,
    hidden,
    down,
    normed,
    grads,
    stage,
    load_sem,
    tile_sem,
    stage_sem,
    *reduce_refs,
):
    place, depth, flip = plane_places()
    order = plane_order()
    loads = [
        pltpu.make_async_copy(source, goal, load_sem.at[which])
        for which, (source, goal) in enumerate(
            ((down_ref, down), (hidden_ref, hidden), (gates_ref, gates))
        )
    ]
    for copy in loads:
        copy.start()
    tile = stage.shape[1]
    tiles = normed_ref.shape[3] // tile
    total_rows = 8 * clips * rows
    inner = gates.shape[3]

    def fetch(index):
        return [
            pltpu.make_async_copy(
                source.at[:, :, :, pl.ds(index * tile, tile)],
                goal.at[index % 2],
                tile_sem.at[which, index % 2],
            )
            for which, (source, goal) in enumerate(((normed_ref, normed), (grads_ref, grads)))
        ]

    def stored(index):
        return pltpu.make_async_copy(
            stage.at[index % 2],
            outer_ref.at[pl.ds(index * tile, tile)],
            stage_sem.at[index % 2],
        )

    def outer_tile(index):
        spot = index % 2
        if index >= 2:
            stored(index - 2).wait()
        for copy in fetch(index):
            copy.wait()
        stage[spot, :, :inner] = outer_sum(
            normed[spot].reshape(total_rows, tile), gates[...].reshape(total_rows, inner)
        ).astype(stage.dtype)
        stage[spot, :, inner:] = outer_sum(
            grads[spot].reshape(total_rows, tile),
            hidden[...].reshape(total_rows, hidden.shape[3]),
        ).astype(stage.dtype)
        stored(index).start()
        if index + 2 < tiles:
            for copy in fetch(index + 2):
                copy.start()

    for index in range(2):
        for copy in fetch(index):
            copy.start()
    greet([(flip(1), depth), (flip(2), depth), (flip(4), depth)])
    loads[0].wait()
    loads[1].wait()

    def layer_rows(index, clip, span, result):
        result = to_whole_features(values_ref[clip, span] + result, *order_of)
        layer_ref[clip, span] = result.astype(layer_ref.dtype)

    steps = reduce_steps(
        clips,
        rows,
        sub,
        terms_of(
            clips, rows, lambda number: hidden[order[number]], down, (0, down.shape[1]), reduce_refs[0]
        ),
        layer_rows,
        *reduce_refs,
    )
    next(steps)
    loads[2].wait()
    outer_tile(0)
    next(steps)
    for index in range(1, tiles):
        outer_tile(index)
    next(steps)
    for index in range(max(tiles - 2, 0), tiles):
        stored(index).wait()
    next(steps)


def ff_outer(gates, hidden, down, normed, grads, values, planes, collective_id, sub=64):
    clips, rows, wide = values.shape
    low = jnp.bfloat16
    inner, columns = gates.shape[1], gates.shape[1] + hidden.shape[1]
    tile = 512
    inside = pl.BlockSpec(memory_space=pltpu.VMEM)
    return pl.pallas_call(
        functools.partial(ff_outer_body, (8, planes), clips, rows, sub),
        out_shape=[
            jax.ShapeDtypeStruct((clips, rows, wide), low),
            jax.ShapeDtypeStruct((wide, columns), low),
        ],
        in_specs=[any_spec()] * 5 + [inside],
        out_specs=[inside, any_spec()],
        scratch_shapes=[
            pltpu.VMEM((clips, 8, rows, inner), low),
            pltpu.VMEM((8, clips, rows, hidden.shape[1]), low),
            pltpu.VMEM(down.shape, low),
            pltpu.VMEM((2, clips, 8, rows, tile), low),
            pltpu.VMEM((2, 8, clips, rows, tile), low),
            pltpu.VMEM((2, tile, columns), low),
            DMA((3,)),
            DMA((2, 2)),
            DMA((2,)),
        ]
        + reduce_scratch(clips, rows, sub, wide),
        compiler_params=communicating(collective_id),
    )(
        gates.reshape(clips, 8, rows, inner),
        hidden.reshape(8, clips, rows, hidden.shape[1]),
        down,
        normed.reshape(clips, 8, rows, wide),
        grads.reshape(8, clips, rows, wide),
        values,
    )


def rotary_lanes(places):
    half = HDIM // 2
    frequency = 10000.0 ** (-np.arange(half, dtype=np.float32) / np.float32(half))
    angles = places.astype(np.float32)[:, None] * frequency.astype(np.float32)[None, :]
    cosine, sine = np.cos(angles), np.sin(angles)
    both = [
        np.concatenate([cosine] * 4, axis=1),
        np.concatenate([-sine, sine, -sine, sine], axis=1),
    ]
    return jnp.asarray(np.stack(both).astype(np.float32))


def turn_heads(values, cosine, sine):
    lane = lax.broadcasted_iota(jnp.int32, values.shape, 1)
    half = HDIM // 2
    ahead = pltpu.roll(values, 2 * HDIM - half, 1)
    behind = pltpu.roll(values, half, 1)
    other = jnp.where(lax.rem(lane, HDIM) < half, ahead, behind)
    return values * cosine + other * sine


def swap_beside(pairs, send_sem, recv_sem, local_sem):
    place, depth, flip = plane_places()

    def each(act):
        for which, (source, goal) in enumerate(pairs):
            for mask in (6, 7, 2, 3, 4, 5, 1):
                other = flip(mask)
                act(
                    remote(
                        source(other),
                        goal(place),
                        send_sem.at[which, mask],
                        recv_sem.at[which, mask],
                        (other, depth),
                    )
                )

    stays = [
        pltpu.make_async_copy(source(place), goal(place), local_sem.at[which])
        for which, (source, goal) in enumerate(pairs)
    ]

    def begin():
        each(lambda copy: copy.start())
        for stay in stays:
            stay.start()

    def end():
        each(lambda copy: copy.wait())
        for stay in stays:
            stay.wait()

    return begin, end


def swap_beside_scratch(count):
    return [DMA((count, 8)), DMA((count, 8)), DMA((count,))]


def flash_forward_body(
    heads,
    tile,
    normed_ref,
    mat_ref,
    stamp_ref,
    bias_ref,
    rotary_ref,
    ff_ref,
    own_ref,
    turned_ref,
    out_ref,
    lse_ref,
    gate_up_ref,
    down_ref,
    mid_ref,
    raw_ref,
    *sems,
):
    group = gate_up_ref.shape[0]
    hidden = down_ref.shape[2]
    step, last = pl.program_id(0), pl.num_programs(0) - 1

    def columns(block):
        return lambda other: ff_ref.at[
            :, pl.ds(pl.multiple_of((block * group + other) * hidden, 128), hidden)
        ]

    start_swap, end_swap = swap_beside(
        [
            (lambda other: own_ref.at[other], lambda other: mid_ref.at[other]),
            (columns(0), lambda other: gate_up_ref.at[other, :, pl.ds(0, hidden)]),
            (columns(1), lambda other: gate_up_ref.at[other, :, pl.ds(hidden, hidden)]),
            (columns(2), lambda other: down_ref.at[other]),
        ],
        *sems,
    )
    place, depth, flip = plane_places()

    @pl.when(step == 0)
    def _():
        greet([(flip(mask), depth) for mask in range(1, group)])
        start_swap()

    def project(index, carry):
        place = pl.ds(pl.multiple_of(index * tile, tile), tile)
        raw_ref[place, :] = jnp.dot(
            normed_ref[place, :], mat_ref[...], preferred_element_type=jnp.float32
        )
        return carry

    lax.fori_loop(0, raw_ref.shape[0] // tile, project, 0)
    wide = heads * HDIM
    for pair in range(2 * wide // 128):
        lanes = slice(pair * 128, pair * 128 + 128)
        turned_ref[:, lanes] = turn_heads(
            raw_ref[:, lanes], rotary_ref[0], rotary_ref[1]
        ).astype(turned_ref.dtype)
    turned_ref[:, 2 * wide :] = raw_ref[:, 2 * wide :].astype(turned_ref.dtype)
    rows = raw_ref.shape[0]
    bias = bias_ref[0]
    scale = HDIM**-0.5
    for head in range(heads):
        lanes = slice(head * HDIM, head * HDIM + HDIM)
        keys = turned_ref[:, wide + head * HDIM : wide + head * HDIM + HDIM]
        values = turned_ref[:, 2 * wide + head * HDIM : 2 * wide + head * HDIM + HDIM]
        stamp_key = stamp_ref[0, :, lanes].astype(jnp.float32)
        stamp_value = stamp_ref[
            0, :, wide + head * HDIM : wide + head * HDIM + HDIM
        ].astype(jnp.float32)

        def one(step, carry):
            place = pl.ds(pl.multiple_of(step * tile, tile), tile)
            query = turned_ref[place, lanes] * jnp.asarray(scale, turned_ref.dtype)
            scores = times_transposed(query, keys) + bias
            stamp_score = jnp.sum(query.astype(jnp.float32) * stamp_key, axis=1, keepdims=True)
            top = jnp.maximum(jnp.max(scores, axis=1, keepdims=True), stamp_score)
            expo = jnp.exp(scores - top)
            stamp_expo = jnp.exp(stamp_score - top)
            denom = jnp.sum(expo, axis=1, keepdims=True) + stamp_expo
            share = 1.0 / denom
            prob = (expo * share).astype(values.dtype)
            stamp_prob = (stamp_expo * share).astype(values.dtype).astype(jnp.float32)
            mixed = jnp.dot(prob, values, preferred_element_type=jnp.float32)
            out_ref[place, lanes] = (mixed + stamp_prob * stamp_value).astype(out_ref.dtype)
            lse_ref[place, head : head + 1] = top + jnp.log(denom)
            return carry

        lax.fori_loop(0, rows // tile, one, 0)

    pl.when(step == last)(end_swap)


def flash_forward(normed, matrix, stamps, bias, rotary, heads, ff_low, rows_of_clip, collective_id):
    clips, rows = bias.shape
    wide = heads * HDIM
    group, piece, features = rows_of_clip.shape
    owned, columns = ff_low.shape
    hidden = columns // (3 * group)
    like = lambda *shape: jax.ShapeDtypeStruct(shape, rows_of_clip.dtype)
    blocked = lambda lanes: pl.BlockSpec((rows, lanes), lambda clip: (clip, 0))
    return pl.pallas_call(
        functools.partial(flash_forward_body, heads, rows // 4),
        grid=(clips,),
        out_shape=[
            like(clips * rows, 3 * wide),
            like(clips * rows, wide),
            jax.ShapeDtypeStruct((clips * rows, 128), jnp.float32),
            like(group, owned, 2 * hidden),
            like(group, owned, hidden),
            like(group, piece, features),
        ],
        in_specs=[
            blocked(features),
            pl.BlockSpec(matrix.shape, lambda clip: (0, 0)),
            pl.BlockSpec((1, 1, 2 * wide), lambda clip: (clip, 0, 0)),
            pl.BlockSpec((1, 1, rows), lambda clip: (clip, 0, 0)),
            pl.BlockSpec((2, rows, 128), lambda clip: (0, 0, 0)),
            any_spec(),
            any_spec(),
        ],
        out_specs=[blocked(3 * wide), blocked(wide), blocked(128)] + [any_spec()] * 3,
        scratch_shapes=[pltpu.VMEM((rows, 3 * wide), jnp.float32)] + swap_beside_scratch(4),
        compiler_params=communicating(collective_id),
    )(normed, matrix, stamps[:, None], bias[:, None], rotary, ff_low, rows_of_clip)


def flash_backward_body(
    heads,
    tile,
    turned_ref,
    mixed_ref,
    grad_ref,
    lse_ref,
    stamp_ref,
    bias_ref,
    rotary_ref,
    cut_ref,
    cross_cut_ref,
    normed_ref,
    stamp_normed_ref,
    out_ref,
    stamp_out_ref,
    mine_ref,
    cross_mine_ref,
    outer_ref,
    query_grad,
    key_grad,
    value_grad,
    all_grads,
    stamp_grads,
    *sems,
):
    place, depth, flip = plane_places()
    start_swap, end_swap = swap_beside(
        [
            (lambda other: cut_ref.at[other], lambda other: mine_ref.at[other]),
            (lambda other: cross_cut_ref.at[other], lambda other: cross_mine_ref.at[other]),
        ],
        *sems,
    )

    @pl.when(pl.program_id(0) == 0)
    def _():
        greet([(flip(mask), depth) for mask in range(1, 8)])
        start_swap()

    wide = heads * HDIM
    rows = turned_ref.shape[0]
    scale = HDIM**-0.5
    low = turned_ref.dtype
    f32 = jnp.float32
    first_row = lax.broadcasted_iota(jnp.int32, (8, tile), 0) == 0
    ones = lambda count, width: jnp.ones((count, width), low)
    blank = lambda count, width: jnp.zeros((count, width), low)
    bias = bias_ref[0].astype(low)

    def widened(count, *parts):
        have = sum(part.shape[1] for part in parts)
        return jnp.concatenate(list(parts) + [blank(count, 128 - have)], axis=1)

    def negative_parts(column):
        parts, rest = [], -column
        for _ in range(3):
            parts.append(rest.astype(low))
            rest = rest - parts[-1].astype(f32)
        return parts

    for head in range(heads):
        lanes = slice(head * HDIM, head * HDIM + HDIM)
        later = slice(wide + head * HDIM, wide + head * HDIM + HDIM)
        keys = turned_ref[:, later]
        values = turned_ref[:, 2 * wide + head * HDIM : 2 * wide + head * HDIM + HDIM]
        keys_across = keys.astype(f32).T.astype(low)
        wide_keys = widened(rows, keys, bias, ones(rows, 3))
        wide_values = widened(rows, values, ones(rows, 3))
        stamp_key = jnp.broadcast_to(stamp_ref[0, :, lanes], (8, HDIM))
        stamp_value = jnp.broadcast_to(stamp_ref[0, :, later], (8, HDIM))
        wide_stamp_key = widened(8, stamp_key, blank(8, 1), ones(8, 3))
        wide_stamp_value = widened(8, stamp_value, ones(8, 3))
        stamp_column = stamp_ref[0, :, lanes].astype(f32).T
        key_total = jnp.zeros((rows, HDIM), f32)
        value_total = jnp.zeros((rows, HDIM), f32)
        stamp_key_total = jnp.zeros((8, HDIM), f32)
        stamp_value_total = jnp.zeros((8, HDIM), f32)
        for step in range(rows // tile):
            place = slice(step * tile, step * tile + tile)
            query = turned_ref[place, lanes] * jnp.asarray(scale, low)
            grad = grad_ref[place, lanes]
            delta = jnp.sum(
                grad.astype(f32) * mixed_ref[place, lanes].astype(f32), axis=1, keepdims=True
            )
            lse = lse_ref[place, head : head + 1]
            wide_query = widened(tile, query, ones(tile, 1), *negative_parts(lse))
            wide_grad = widened(tile, grad, *negative_parts(delta))
            prob = jnp.exp(times_transposed(wide_keys, wide_query))
            scores = (prob * times_transposed(wide_values, wide_grad)).astype(low)
            stamp_prob = jnp.exp(times_transposed(wide_stamp_key, wide_query))
            stamp_scores = stamp_prob * times_transposed(wide_stamp_value, wide_grad)
            stamp_scores = jnp.where(first_row, stamp_scores, 0.0).astype(low)
            value_total += jnp.dot(prob.astype(low), grad, preferred_element_type=f32)
            key_total += jnp.dot(scores, query, preferred_element_type=f32)
            across = jnp.dot(keys_across, scores, preferred_element_type=f32)
            across = across + stamp_column * stamp_scores[:1].astype(f32)
            query_grad[place, lanes] = across.T * scale
            stamp_key_total += jnp.dot(stamp_scores, query, preferred_element_type=f32)
            stamp_value_total += jnp.dot(
                jnp.where(first_row, stamp_prob, 0.0).astype(low), grad, preferred_element_type=f32
            )
        key_grad[:, lanes] = key_total
        value_grad[:, lanes] = value_total
        stamp_out_ref[0, :, lanes] = stamp_key_total[:1]
        stamp_out_ref[0, :, later] = stamp_value_total[:1]
    both = jnp.concatenate([query_grad[...], key_grad[...]], axis=1)
    for pair in range(2 * wide // 128):
        lanes = slice(pair * 128, pair * 128 + 128)
        out_ref[:, lanes] = turn_heads(both[:, lanes], rotary_ref[0], -rotary_ref[1]).astype(low)
    out_ref[:, 2 * wide :] = value_grad[...].astype(low)
    count = all_grads.shape[1]
    tile = 512
    step = pl.program_id(0)
    all_grads[pl.ds(pl.multiple_of(step * rows, rows), rows)] = out_ref[...]
    stamp_grads[step] = stamp_out_ref[0]

    @pl.when(step == pl.num_programs(0) - 1)
    def _():
        for start in range(0, normed_ref.shape[1], tile):
            span = slice(start, start + tile)
            product = outer_sum(normed_ref[:, span], all_grads[...])
            stamp_part = sum(
                stamp_normed_ref[clip, span] * stamp_grads[clip]
                for clip in range(stamp_grads.shape[0])
            )
            outer_ref[span, : count - 2 * wide] = product[:, : count - 2 * wide].astype(low)
            outer_ref[span, count - 2 * wide :] = (
                product[:, count - 2 * wide :] + stamp_part
            ).astype(low)
        end_swap()


def flash_backward(
    turned,
    mixed,
    grad,
    lse,
    stamps,
    bias,
    rotary,
    heads,
    cut,
    cross_cut,
    normed,
    stamp_normed,
    collective_id,
):
    clips, rows, _ = bias.shape
    wide = heads * HDIM
    blocked = lambda lanes: pl.BlockSpec((rows, lanes), lambda clip: (clip, 0))
    features = normed.shape[1]
    grads, stamp_grads, mine, cross_mine, outer = pl.pallas_call(
        functools.partial(flash_backward_body, heads, rows // 4),
        grid=(clips,),
        out_shape=[
            jax.ShapeDtypeStruct((clips * rows, 3 * wide), jnp.bfloat16),
            jax.ShapeDtypeStruct((clips, 1, 2 * wide), jnp.float32),
            jax.ShapeDtypeStruct(cut.shape, cut.dtype),
            jax.ShapeDtypeStruct(cross_cut.shape, cross_cut.dtype),
            jax.ShapeDtypeStruct((features, 3 * wide), jnp.bfloat16),
        ],
        in_specs=[
            blocked(3 * wide),
            blocked(wide),
            blocked(wide),
            blocked(128),
            pl.BlockSpec((1, 1, 2 * wide), lambda clip: (clip, 0, 0)),
            pl.BlockSpec((1, rows, 1), lambda clip: (clip, 0, 0)),
            pl.BlockSpec((2, rows, 128), lambda clip: (0, 0, 0)),
            any_spec(),
            any_spec(),
            pl.BlockSpec(normed.shape, lambda clip: (0, 0)),
            pl.BlockSpec((clips, features, 1), lambda clip: (0, 0, 0)),
        ],
        out_specs=[
            blocked(3 * wide),
            pl.BlockSpec((1, 1, 2 * wide), lambda clip: (clip, 0, 0)),
            any_spec(),
            any_spec(),
            pl.BlockSpec((features, 3 * wide), lambda clip: (0, 0)),
        ],
        scratch_shapes=[pltpu.VMEM((rows, wide), jnp.float32)] * 3
        + [
            pltpu.VMEM((clips * rows, 3 * wide), jnp.bfloat16),
            pltpu.VMEM((clips, 1, 2 * wide), jnp.float32),
        ]
        + swap_beside_scratch(2),
        compiler_params=communicating(collective_id),
    )(
        turned,
        mixed,
        grad,
        lse,
        stamps[:, None],
        bias,
        rotary,
        cut,
        cross_cut,
        normed,
        stamp_normed,
    )
    return grads, stamp_grads[:, 0], mine, cross_mine, outer


def adam_body(ff_steps, places, *refs):
    refs = list(refs)
    take = lambda count: [refs.pop(0) for _ in range(count)]
    total_ref = take(1)[0]
    ff_refs, ff_grad_ref = take(3), take(1)[0]
    attn_refs = take(3)
    attn_grads = take(1 + max(which for which, _, _ in places))
    ff_outs, attn_outs = take(3), take(3)
    step = pl.program_id(0)
    factor = jnp.minimum(1.0, clip_limit / jnp.sqrt(total_ref[0:1, 0:1]))

    def update(olds, gradient, outs):
        results = adam_step(
            *[old[...] for old in olds],
            gradient.astype(jnp.float32) * factor,
            matrix_rate,
            matrix_decay,
        )
        for out, result in zip(outs, results):
            out[...] = result

    @pl.when(step < ff_steps)
    def _():
        gradient = jnp.concatenate(
            [ff_grad_ref[part] for part in range(ff_grad_ref.shape[0])], axis=1
        )
        update(ff_refs, gradient, ff_outs)

    for block, (which, start, stop) in enumerate(places):

        @pl.when(step == ff_steps + block)
        def _(owned_ref=attn_grads[which], start=start, stop=stop):
            gradient = jnp.concatenate(
                [owned_ref[part, :, start:stop] for part in range(owned_ref.shape[0])], axis=1
            )
            update(attn_refs, gradient, attn_outs)


def adam(total, ff, ff_grad, attn, attn_grads, places):
    rows, columns = ff[0].shape
    group, _, held = ff_grad.shape
    parts = group // 2
    width = columns // (3 * group)
    ff_steps = 3 * group // parts
    steps = ff_steps + len(places)
    ff_step = lambda step: jnp.minimum(step, ff_steps - 1)
    ff_piece = pl.BlockSpec((rows, parts * width), lambda step: (0, ff_step(step)))
    ff_grads = pl.BlockSpec(
        (parts, rows, width), lambda step: (lax.rem(ff_step(step), 2), 0, lax.div(ff_step(step), 2))
    )
    attn_piece = pl.BlockSpec(
        (rows, attn[0].shape[1] // len(places)), lambda step: (0, jnp.maximum(step - ff_steps, 0))
    )
    whole = [pl.BlockSpec(grad.shape, lambda step: (0, 0, 0)) for grad in attn_grads]
    f32 = jnp.float32
    results = pl.pallas_call(
        functools.partial(adam_body, ff_steps, places),
        grid=(steps,),
        out_shape=[jax.ShapeDtypeStruct(ff[0].shape, f32)] * 3
        + [jax.ShapeDtypeStruct(attn[0].shape, f32)] * 3,
        in_specs=[pl.BlockSpec((8, 128), lambda step: (0, 0))]
        + [ff_piece] * 3
        + [ff_grads]
        + [attn_piece] * 3
        + whole,
        out_specs=[ff_piece] * 3 + [attn_piece] * 3,
        compiler_params=pltpu.CompilerParams(vmem_limit_bytes=VMEM_LIMIT),
    )(total, *ff, ff_grad, *attn, *attn_grads)
    return results[:3], results[3:]


def plane_device(
    frames,
    time_token,
    cond_ids,
    cond_mask,
    lengths,
    cond_table,
    cotangent,
    attn_weight,
    cross_weight,
    norm_param,
    ff_weight,
    attn_first,
    attn_second,
    cross_first,
    cross_second,
    norm_first,
    norm_second,
    ff_first,
    ff_second,
):
    group, planes = lax.axis_size("dp"), lax.axis_size("seq")
    place, depth = lax.axis_index("dp"), lax.axis_index("seq")
    clips = group // planes
    _, frame_rows, wide = frames.shape
    piece = frame_rows // group
    seq_frames = frame_rows * planes
    own_rows = planes * piece
    heads = HEADS // group
    head_wide = heads * HDIM
    ff_wide = FF // group
    owned = wide // (group * planes)
    cond_count, cond_wide = cond_ids.shape[1], cond_table.shape[1]
    cond_owned = cross_weight.shape[0]

    norm_block = norm_param.astype(jnp.bfloat16).astype(jnp.float32)
    norm_block = jnp.pad(norm_block, ((0, 2), (0, 128 - owned)))
    pack = jnp.concatenate(
        [
            time_token.astype(jnp.float32),
            jnp.pad(cond_ids.astype(jnp.float32), ((0, 0), (0, wide - cond_count))),
            jnp.pad(cond_mask.astype(jnp.float32), ((0, 0), (0, wide - cond_count))),
            jnp.broadcast_to(lengths.astype(jnp.float32)[:, None], (1, wide)),
            jnp.zeros((4, wide), jnp.float32),
        ],
        axis=0,
    )
    positions = depth * frame_rows + jnp.arange(frame_rows)
    valid = (positions < lengths).astype(jnp.float32)[:, None]
    stream, gain_rows, packs, qkv_mine, rest_mine, ff_low, grad_pieces = enter(
        frames[0],
        cotangent[0],
        valid,
        norm_block,
        pack,
        attn_weight,
        cross_weight,
        ff_weight,
        planes,
        1,
    )
    stream = stream.reshape(clips, own_rows, wide).astype(jnp.float32)

    def over_planes(block):
        return lax.all_gather(block.reshape(group * owned, -1), "seq", axis=0, tiled=True)

    w_qkv = over_planes(qkv_mine)
    w_rest = over_planes(rest_mine)
    of_self_out = (0, head_wide)
    of_cross_query = (head_wide, 2 * head_wide)
    of_cross_out = (2 * head_wide, 3 * head_wide)
    w_cond = w_rest[:, 3 * head_wide :].reshape(planes, group, 2, cond_owned, head_wide)
    w_cond = w_cond.transpose(1, 0, 3, 2, 4).reshape(cond_wide, 2 * head_wide)
    plane_packs = lax.dynamic_slice_in_dim(packs, depth * clips, clips, axis=0)
    stamps = plane_packs[:, 0].reshape(clips, group, planes, owned)
    stamps = stamps.swapaxes(1, 2).reshape(clips, wide)
    cond_keep = plane_packs[:, 2, :cond_count] > 0
    clip_lengths = plane_packs[:, 3, 0].astype(jnp.int32)
    share = cond_count // group
    all_ids = packs[:, 1, :cond_count].astype(jnp.int32)
    own_ids = lax.dynamic_slice_in_dim(all_ids, place * share, share, axis=1)
    vocab_rows = cond_table.shape[0]
    relative = own_ids - depth * vocab_rows
    inside = (relative >= 0) & (relative < vocab_rows)
    picked = jnp.take(cond_table, jnp.clip(relative, 0, vocab_rows - 1), axis=0)
    picked = jnp.where(inside[..., None], picked, jnp.zeros((), picked.dtype))
    picked = picked.reshape(planes, clips, share, cond_wide)
    group_rows = clips * seq_frames
    row_place = np.arange(seq_frames)
    row_owner, row_rest = row_place // own_rows, row_place % own_rows
    true_place = (row_rest // piece) * frame_rows + row_owner * piece + row_rest % piece
    key_keep = true_place[None, :] < clip_lengths[:, None]
    group_shape = (clips, seq_frames, heads, HDIM)

    group_one, cond = gather_dot(stream, None, None, 5, gain_rows[0:2], picked)
    cond_flat = cond.swapaxes(0, 1).reshape(clips * cond_count, cond_wide)
    stamp_normed = layer_norm(stamps, gain_rows[0], gain_rows[1]).astype(jnp.bfloat16)
    stamp_pair = jnp.dot(stamp_normed, w_qkv[:, head_wide:], preferred_element_type=jnp.float32)
    stamp_pair = stamp_pair.astype(jnp.bfloat16)
    rotary = rotary_lanes(true_place)
    key_bias = jnp.where(key_keep, 0.0, masked_score)
    rotated, self_low, self_lse, gate_up_mine, down_mine, grad_out_mid = flash_forward(
        group_one,
        w_qkv,
        stamp_pair,
        key_bias,
        rotary,
        heads,
        ff_low,
        grad_pieces,
        2,
    )
    w_gate_up = over_planes(gate_up_mine)
    w_down = over_planes(down_mine)
    cond_pair = jnp.dot(cond_flat, w_cond, preferred_element_type=jnp.float32)
    cond_pair = cond_pair.astype(jnp.bfloat16).reshape(clips, cond_count, 2 * head_wide)
    cond_bias = jnp.where(cond_keep, 0.0, masked_score)[:, None]
    resid_one, group_two, cross_query, cross_out, grad_out_low = reduce_gather(
        self_low,
        w_rest,
        clips,
        6,
        stream,
        w_rest,
        span=of_self_out,
        gains=gain_rows[2:4],
        second_span=of_cross_query,
        pair=cond_pair,
        bias=cond_bias,
        passing=grad_out_mid,
    )
    grad_out_low = grad_out_low.reshape(clips, own_rows, wide)
    (resid_two,) = dot_reduce(cross_out, w_rest, clips, 8, resid_one, of_cross_out)
    group_three, gate_up = gather_dot(resid_two, w_gate_up, jnp.float32, 9, gain_rows[4:6])
    stamp_column = stamp_normed.astype(jnp.float32)[:, :, None]
    bias_column = key_bias[:, :, None]
    gate_up, grad_out_low, stamp_column, bias_column = lax.optimization_barrier(
        (gate_up, grad_out_low, stamp_column, bias_column)
    )
    group_grad_out, grad_gate_up, hidden = gather_dot(
        grad_out_low, w_down, None, 10, gate_up=gate_up
    )

    def over_rows(block):
        return lax.psum_scatter(
            block.astype(jnp.bfloat16), "seq", scatter_dimension=0, tiled=True
        ).reshape(group, owned, -1)

    layer_rows, ff_piece = ff_outer(
        grad_gate_up, hidden, w_down, group_three, group_grad_out, resid_two, planes, 12
    )
    ff_piece, grad_gate_up = lax.optimization_barrier((ff_piece, grad_gate_up))
    ff_rows = over_rows(ff_piece)
    grad_two, stats_three = dot_reduce(
        grad_gate_up, w_gate_up, clips, 13, grad_out_low, back=(resid_two, gain_rows[4:5])
    )
    _, grad_cross_query, cond_grad, cross_piece = gather_dot(
        grad_two,
        w_rest,
        None,
        15,
        span=of_cross_out,
        pair=cond_pair,
        bias=cond_bias,
        query=cross_query,
        outer=(group_two, cross_out),
    )
    cond_grad = cond_grad.reshape(clips * cond_count, 2 * head_wide)
    cond_piece = split_outer(cond_flat, cond_grad)
    cond_piece = cond_piece.reshape(group, planes, cond_owned, 2, head_wide)
    cond_piece = cond_piece.transpose(1, 0, 3, 2, 4).reshape(wide, head_wide)
    cond_piece = cond_piece.astype(jnp.bfloat16)
    grad_one, stats_two, _, grad_self_mixed, rest_piece, layer_out, cross_rows = reduce_gather(
        grad_cross_query,
        w_rest,
        clips,
        16,
        grad_two,
        w_rest,
        span=of_cross_query,
        back=(resid_one, gain_rows[2:3]),
        second_span=of_self_out,
        outer=(self_low, cond_piece),
        adding=cross_piece.reshape(planes, group * owned, 2 * head_wide),
        leaving=layer_rows.reshape(clips, planes, piece, wide),
    )
    rest_piece, ff_rows = lax.optimization_barrier((rest_piece, ff_rows))
    rest_rows = over_rows(rest_piece)
    grad_project, stamp_grad, ff_owned, cross_owned, qkv_piece = flash_backward(
        rotated,
        self_low,
        grad_self_mixed,
        self_lse,
        stamp_pair,
        bias_column,
        rotary,
        heads,
        ff_rows,
        cross_rows.reshape(group, owned, -1),
        group_one,
        stamp_column,
        3,
    )
    grad_stamp_normed = split_times_transposed(stamp_grad, w_qkv[:, head_wide:])
    qkv_rows = over_rows(qkv_piece)
    grad_project, rest_rows = lax.optimization_barrier((grad_project, rest_rows))
    frames_grad, stats_one, rest_owned = dot_reduce(
        grad_project,
        w_qkv,
        clips,
        18,
        grad_one,
        back=(stream, gain_rows[0:1]),
        kind=jnp.bfloat16,
        order=(group, planes),
        cut=rest_rows,
    )
    _, norm_stamp_back = jax.vjp(layer_norm, stamps, gain_rows[0], gain_rows[1])
    _, grad_gain_stamp, grad_bias_stamp = norm_stamp_back(grad_stamp_normed)
    stamp_stats = jnp.stack([grad_gain_stamp, grad_bias_stamp])
    norm_grad = jnp.concatenate([stats_one + stamp_stats, stats_two, stats_three], axis=0)
    norm_parts = norm_grad.reshape(6, planes, group, owned).transpose(2, 1, 0, 3)
    norm_parts = norm_parts.reshape(group * planes, 6, owned)
    norm_parts = jnp.pad(norm_parts, ((0, 0), (0, 2), (0, 128 - owned)))
    ff_squares = jnp.sum(jnp.square(ff_owned.astype(jnp.float32)))
    frames_grad, qkv_owned, norm_sum, total = settle(
        frames_grad.reshape(clips, planes, piece, wide),
        qkv_rows,
        [cross_owned, rest_owned],
        norm_parts,
        ff_squares.reshape(1, 1),
        20,
    )
    cross_reduced = rest_owned[:, :, head_wide:].reshape(group, 2, cond_owned, head_wide)
    cross_reduced = cross_reduced.transpose(2, 1, 0, 3).reshape(cross_weight.shape)
    cross_reduced = cross_reduced.astype(jnp.float32)
    norm_reduced = norm_sum[:6, :owned]
    grad_norm = jnp.sqrt(total[0, 0])
    factor = jnp.minimum(1.0, clip_limit / grad_norm)
    ff_results, attn_results = adam(
        total,
        (ff_weight, ff_first, ff_second),
        ff_owned,
        (attn_weight, attn_first, attn_second),
        [qkv_owned, cross_owned, rest_owned],
        [
            (which, block * head_wide, (block + 1) * head_wide)
            for which, block in ((0, 0), (0, 1), (0, 2), (2, 0), (1, 0), (1, 1))
        ],
    )
    ff_new, ff_first_new, ff_second_new = ff_results
    attn_new, attn_first_new, attn_second_new = attn_results
    frames_grad = frames_grad.reshape(frames.shape).astype(jnp.float32)
    layer_out = layer_out.reshape(frames.shape)
    cross_new, cross_first_new, cross_second_new = adam_step(
        cross_weight, cross_first, cross_second, cross_reduced * factor, matrix_rate, matrix_decay
    )
    norm_new, norm_first_new, norm_second_new = adam_step(
        norm_param, norm_first, norm_second, norm_reduced * factor, gain_rate, 0.0
    )
    return (
        layer_out,
        frames_grad,
        grad_norm,
        attn_new,
        cross_new,
        norm_new,
        ff_new,
        attn_first_new,
        cross_first_new,
        norm_first_new,
        ff_first_new,
        attn_second_new,
        cross_second_new,
        norm_second_new,
        ff_second_new,
    )


def solution(mesh):
    return jax.shard_map(
        plane_device if plane_fits(mesh) else per_device,
        mesh=mesh,
        in_specs=(
            P("dp", "seq", None),
            P("dp", None),
            P("dp", None),
            P("dp", None),
            P("dp"),
            P("seq", None),
            P("dp", "seq", None),
            P(("dp", "seq"), None),
            P(("dp", "seq"), None),
            P(None, ("dp", "seq")),
            P(("dp", "seq"), None),
            P(("dp", "seq"), None),
            P(("dp", "seq"), None),
            P(("dp", "seq"), None),
            P(("dp", "seq"), None),
            P(None, ("dp", "seq")),
            P(None, ("dp", "seq")),
            P(("dp", "seq"), None),
            P(("dp", "seq"), None),
        ),
        out_specs=(
            P("dp", "seq", None),
            P("dp", "seq", None),
            P(),
            P(("dp", "seq"), None),
            P(("dp", "seq"), None),
            P(None, ("dp", "seq")),
            P(("dp", "seq"), None),
            P(("dp", "seq"), None),
            P(("dp", "seq"), None),
            P(None, ("dp", "seq")),
            P(("dp", "seq"), None),
            P(("dp", "seq"), None),
            P(("dp", "seq"), None),
            P(None, ("dp", "seq")),
            P(("dp", "seq"), None),
        ),
        check_vma=False,
    )
```
